32 devices in a mesh: dp: 8 (over z, core), seq: 4 (over y, x).
Axes of the slice: x: 2, y: 2, z: 4, core: 2. Of those that a mesh axis runs over, the one named last changes fastest.
Arguments:
- tokens: bfloat16 [4096, 768], P(('dp', 'seq')), may hold values from -6 to 6
- cotangent: bfloat16 [4096, 768], P(('dp', 'seq')), may hold values from -6 to 6
- lengths: int32 [8, 4], P('dp'), may hold values from 1 to 509, as said below
- w_query: bfloat16 [768, 768], replicated, may hold values from -0.21875 to 0.21875
- b_query: float32 [768], replicated, may hold values from -2 to 2
- w_key: bfloat16 [768, 768], replicated, may hold values from -0.21875 to 0.21875
- b_key: float32 [768], replicated, may hold values from -2 to 2
- w_value: bfloat16 [768, 768], replicated, may hold values from -0.21875 to 0.21875
- b_value: float32 [768], replicated, may hold values from -2 to 2
- w_out: bfloat16 [768, 768], replicated, may hold values from -4 to 4
- b_out: float32 [768], replicated, may hold values from -2 to 2
- gain_one: float32 [768], replicated, may hold values from 0.25 to 1.75
- shift_one: float32 [768], replicated, may hold values from -2 to 2
- w_up: bfloat16 [768, 3072], replicated, may hold values from -0.21875 to 0.21875
- b_up: float32 [3072], replicated, may hold values from -2 to 2
- w_down: bfloat16 [3072, 768], replicated, may hold values from -0.109375 to 0.109375
- b_down: float32 [768], replicated, may hold values from -2 to 2
- gain_two: float32 [768], replicated, may hold values from 0.25 to 1.75
- shift_two: float32 [768], replicated, may hold values from -2 to 2
- rel_table: bfloat16 [512, 768], replicated, may hold values from -6 to 6
Outputs:
- output: bfloat16 [4096, 768], P(('dp', 'seq'))
- grad_tokens: float32 [4096, 768], P(('dp', 'seq'))
- grad_w_query: float32 [768, 768], P('seq')
- grad_b_query: float32 [768], P('seq')
- grad_w_key: float32 [768, 768], P('seq')
- grad_b_key: float32 [768], P('seq')
- grad_w_value: float32 [768, 768], P('seq')
- grad_b_value: float32 [768], P('seq')
- grad_w_out: float32 [768, 768], P('seq')
- grad_b_out: float32 [768], P('seq')
- grad_gain_one: float32 [768], P('seq')
- grad_shift_one: float32 [768], P('seq')
- grad_w_up: float32 [768, 3072], P('seq')
- grad_b_up: float32 [3072], P('seq')
- grad_w_down: float32 [3072, 768], P('seq')
- grad_b_down: float32 [768], P('seq')
- grad_gain_two: float32 [768], P('seq')
- grad_shift_two: float32 [768], P('seq')
- grad_rel_table: float32 [512, 768], replicated
The draws below stay inside these ranges and needn't reach their ends.
Inputs may be any that keep to these rules, and one draw needn't show every extreme that they name: `lengths`: A row holds its 4 documents end to end from its first position; at most 16 positions at its end are padding. The longest document of a row is its first or its second and covers positions of the row's first and of its last block of 128 tokens. In every draw one row has no padding and its other documents one token each.
All inputs are finite; a program needn't handle non-finite values.
Results may differ from the reference program's by a relative error of at most 0.03.
Values may be sent and summed in bfloat16 or wider, within the bound.
No kernel may reach another device: no remote copies, remote signals or barrier semaphores. Data moves between devices by JAX's collectives and lax.ppermute only.
A program may use at most 128 MiB of HBM per device.

```python
import math
import jax
import jax.numpy as jnp
from jax import lax

D = 768
HEADS = 12
HEAD = 64
FF = 3072
SPAN = 256
TOK_DEV = 128
DOCS = 4
RELROWS = 512
ROW = 512
ROWS = 8
TOKENS = 4096


def draw_lengths(key, part):
    key = jax.random.fold_in(key, 7)
    keys = jax.random.split(key, 4)
    tight = jax.random.randint(keys[3], (), 0, ROWS)
    is_tight = jnp.arange(ROWS) == tight
    shorts = jax.random.randint(keys[0], (ROWS, DOCS - 1), 1, TOK_DEV // 8 + 1)
    shorts = jnp.where(is_tight[:, None], 1, shorts)
    padding = jax.random.randint(keys[1], (ROWS,), 0, TOK_DEV // 8 + 1)
    padding = jnp.where(is_tight, 0, padding)
    longest = ROW - jnp.sum(shorts, axis=1) - padding
    first = jax.random.randint(keys[2], (ROWS,), 0, 2)
    leading = jnp.where(first == 0, longest, shorts[:, 0])
    second = jnp.where(first == 0, shorts[:, 0], longest)
    return jnp.concatenate([leading[:, None], second[:, None], shorts[:, 1:]], axis=1).astype(jnp.int32)


def steps_of(key, extent, cuts, low, largest):
    factor_of, own = 1.0, jax.random.fold_in(key, 6)
    for axis_at, shards_of in cuts:
        draws = jnp.exp(jax.random.uniform(jax.random.fold_in(own, axis_at), (shards_of,), jnp.float32, low / len(cuts), largest / len(cuts)))
        factor_of = factor_of * jnp.repeat(draws, extent[axis_at] // shards_of).reshape([-1 if axis == axis_at else 1 for axis in range(len(extent))])
    return factor_of


def noise(rng, extent, scale, bound, cuts=(), held_as=jnp.bfloat16):
    result = scale * jax.random.normal(rng, extent, jnp.float32)
    if cuts:
        result = result * steps_of(rng, extent, cuts, -0.22, 0.18)
    return jnp.clip(result, -bound, bound).astype(held_as)


def setup_inputs(seed: int = 0) -> dict:
    key_of = jax.random.split(jax.random.key(seed), 21)
    tokens = noise(key_of[0], (TOKENS, D), 1.0, 6.0, ((0, 32),))
    cotangent = noise(key_of[1], (TOKENS, D), 1.0, 6.0, ((0, 32),))
    lengths = draw_lengths(jax.random.fold_in(key_of[20], 71), 0)
    w_query = noise(key_of[3], (D, D), D ** -0.5, 0.21875)
    b_query = noise(key_of[4], (D,), 0.3, 2.0, (), jnp.float32)
    w_key = noise(key_of[5], (D, D), D ** -0.5, 0.21875)
    b_key = noise(key_of[6], (D,), 0.3, 2.0, (), jnp.float32)
    w_value = noise(key_of[7], (D, D), D ** -0.5, 0.21875)
    b_value = noise(key_of[8], (D,), 0.3, 2.0, (), jnp.float32)
    w_out = noise(key_of[9], (D, D), 2 ** -0.5, 4.0)
    b_out = noise(key_of[10], (D,), 0.3, 2.0, (), jnp.float32)
    gain_one = jnp.clip(1.0 + 0.15 * jax.random.normal(key_of[11], (D,), jnp.float32), 0.25, 1.75)
    shift_one = noise(key_of[12], (D,), 0.3, 2.0, (), jnp.float32)
    w_up = noise(key_of[13], (D, FF), D ** -0.5, 0.21875)
    b_up = noise(key_of[14], (FF,), 0.3, 2.0, (), jnp.float32)
    w_down = noise(key_of[15], (FF, D), FF ** -0.5, 0.109375)
    b_down = noise(key_of[16], (D,), 0.3, 2.0, (), jnp.float32)
    gain_two = jnp.clip(1.0 + 0.15 * jax.random.normal(key_of[17], (D,), jnp.float32), 0.25, 1.75)
    shift_two = noise(key_of[18], (D,), 0.3, 2.0, (), jnp.float32)
    rel_table = noise(key_of[19], (RELROWS, D), 1.0, 6.0)
    return dict(tokens=tokens, cotangent=cotangent, lengths=lengths, w_query=w_query, b_query=b_query, w_key=w_key, b_key=b_key, w_value=w_value, b_value=b_value, w_out=w_out, b_out=b_out, gain_one=gain_one, shift_one=shift_one, w_up=w_up, b_up=b_up, w_down=w_down, b_down=b_down, gain_two=gain_two, shift_two=shift_two, rel_table=rel_table)


@jax.custom_vjp
def low(v):
    return lax.optimization_barrier(v.astype(jnp.bfloat16)).astype(jnp.float32)

@jax.custom_vjp
def low_back(v):
    return v

def low_keep(v):
    return (low(v), None)

def low_pass(kept, grad):
    return (grad,)

def back_keep(v):
    return (v, None)

def back_low(kept, grad):
    return (low(grad),)
low.defvjp(low_keep, low_pass)
low_back.defvjp(back_keep, back_low)

def rounded_both(value):
    return low(low_back(value))

def product(left, right):
    return jnp.dot(left, right, precision=lax.Precision.HIGHEST, preferred_element_type=jnp.float32)

def layer_norm(resid, gain, shift):
    center = resid - lax.optimization_barrier(jnp.mean(resid, axis=-1, keepdims=True))
    spread = lax.optimization_barrier(jnp.mean(center * center, axis=-1, keepdims=True))
    return center * lax.rsqrt(spread + 1e-07) * gain + shift

def rel_index(first, second):
    return jnp.clip(first[:, None] - second[None, :] + SPAN, 0, 2 * SPAN - 1).astype(jnp.int32)

def band_pick(table, where_from):
    full_index = jnp.broadcast_to(where_from[None], (table.shape[0],) + where_from.shape)
    return jnp.take_along_axis(table, full_index, axis=2)

def row_attention(query_row, key_row, value_row, seg_row, pos_key, pos_query):
    scale = 1.0 / math.sqrt(3 * HEAD)
    query3 = query_row.reshape(ROW, HEADS, HEAD)
    key3 = key_row.reshape(ROW, HEADS, HEAD)
    value3 = value_row.reshape(ROW, HEADS, HEAD)
    high = lax.Precision.HIGHEST
    c2p_table = jnp.einsum('qhd,rhd->hqr', query3, pos_key.reshape(RELROWS, HEADS, HEAD), precision=high)
    p2c_table = jnp.einsum('khd,rhd->hkr', key3, pos_query.reshape(RELROWS, HEADS, HEAD), precision=high)
    key_pos = jnp.arange(ROW, dtype=jnp.int32)

    def query_block(start):
        query_pos = (start + jnp.arange(TOK_DEV, dtype=jnp.int32)).astype(jnp.int32)
        block3 = lax.dynamic_slice_in_dim(query3, start, TOK_DEV, 0)
        first_table = low_back(lax.dynamic_slice_in_dim(c2p_table, start, TOK_DEV, 1))
        second_table = low_back(p2c_table)
        direct = jnp.einsum('qhd,khd->hqk', block3, key3, precision=high)
        c2p = band_pick(first_table, rel_index(query_pos, key_pos))
        p2c = jnp.swapaxes(band_pick(second_table, rel_index(key_pos, query_pos)), 1, 2)
        score = low_back((direct + c2p + p2c) * scale)
        seg_query = lax.dynamic_slice_in_dim(seg_row, start, TOK_DEV, 0)
        allowed = seg_query[:, None] == seg_row[None, :]
        prob = jax.nn.softmax(jnp.where(allowed[None], score, -1e+30), axis=-1)
        context = jnp.einsum('hqk,khd->qhd', low(prob), value3, precision=high)
        return context.reshape(TOK_DEV, D)
    starts = (jnp.arange(ROW // TOK_DEV, dtype=jnp.int32) * TOK_DEV).astype(jnp.int32)
    return lax.map(jax.checkpoint(query_block), starts).reshape(ROW, D)

def layer(inputs, segments):
    tokens, w_query, b_query, w_key, b_key, w_value, b_value, w_out, b_out, gain_one, shift_one, w_up, b_up, w_down, b_down, gain_two, shift_two, rel_table = inputs
    query = rounded_both(product(tokens, w_query) + b_query)
    key_all = rounded_both(product(tokens, w_key) + b_key)
    value_all = rounded_both(product(tokens, w_value) + b_value)
    pos_key = rounded_both(product(rel_table, w_key) + b_key)
    pos_query = rounded_both(product(rel_table, w_query) + b_query)

    def one_row(items):
        return row_attention(items[0], items[1], items[2], items[3], pos_key, pos_query)
    context = lax.map(jax.checkpoint(one_row), (query.reshape(ROWS, ROW, D), key_all.reshape(ROWS, ROW, D), value_all.reshape(ROWS, ROW, D), segments))
    context = rounded_both(context.reshape(TOKENS, D))
    attn = low_back(product(context, w_out) + b_out)
    hidden_one = layer_norm(tokens + attn, gain_one, shift_one)
    up = low_back(product(low(hidden_one), w_up) + b_up)
    act = low(jax.nn.gelu(up, approximate=False))
    down = low_back(product(act, w_down) + b_down)
    return layer_norm(hidden_one + down, gain_two, shift_two)

def reference(tokens, cotangent, lengths, w_query, b_query, w_key, b_key, w_value, b_value, w_out, b_out, gain_one, shift_one, w_up, b_up, w_down, b_down, gain_two, shift_two, rel_table):
    positions = jnp.arange(ROW, dtype=jnp.int32)
    bounds = jnp.cumsum(lengths, axis=1).astype(jnp.int32)
    segments = lax.optimization_barrier(jnp.sum((positions[None, :, None] >= bounds[:, None, :]).astype(jnp.int32), axis=2)).astype(jnp.int32)
    valid = (positions[None, :] < bounds[:, -1:]).astype(jnp.float32).reshape(TOKENS, 1)
    inputs = (tokens.astype(jnp.float32), w_query.astype(jnp.float32), b_query, w_key.astype(jnp.float32), b_key, w_value.astype(jnp.float32), b_value, w_out.astype(jnp.float32), b_out, gain_one, shift_one, w_up.astype(jnp.float32), b_up, w_down.astype(jnp.float32), b_down, gain_two, shift_two, rel_table.astype(jnp.float32))

    def forward(*values):
        return layer(values, segments)
    output, pullback = jax.vjp(forward, *inputs)
    grads = pullback(cotangent.astype(jnp.float32) * valid)
    return (output.astype(jnp.bfloat16), grads[0], grads[1], grads[2], grads[3], grads[4], grads[5], grads[6], grads[7], grads[8], grads[9], grads[10], grads[11], grads[12], grads[13], grads[14], grads[15], grads[16], grads[17])
```

```python
import functools
import math

import jax
import jax.numpy as jnp
from jax import lax
from jax.experimental import pallas as pl
from jax.experimental.pallas import tpu as pltpu
from jax.sharding import PartitionSpec as P

D = 768
HEADS = 12
HEAD = 64
SPAN = 256
RELROWS = 512
BLOCK = 128
EXT = RELROWS + 2 * SPAN
PAIRS = HEADS // 2
SCALE = 1.0 / math.sqrt(3 * HEAD)
F32 = jnp.float32
BF16 = jnp.bfloat16


def layer_norm(resid, gain, shift):
    center = resid - jnp.mean(resid, axis=-1, keepdims=True)
    spread = jnp.mean(center * center, axis=-1, keepdims=True)
    return center * lax.rsqrt(spread + 1e-07) * gain + shift


def gelu_exact(hidden):
    return jax.nn.gelu(hidden, approximate=False)


def product(left, right):
    return jnp.dot(left, right, preferred_element_type=F32)


def product_left(left, right):
    return lax.dot_general(left, right, (((0,), (0,)), ((), ())), preferred_element_type=F32)


def product_right(left, right):
    return lax.dot_general(left, right, (((1,), (1,)), ((), ())), preferred_element_type=F32)


def segment_ids(lengths_row, positions):
    bounds = jnp.cumsum(lengths_row)
    return jnp.sum((positions[:, None] >= bounds[None, :]).astype(jnp.int32), axis=1)


def anti_identity():
    rows = lax.broadcasted_iota(jnp.int32, (BLOCK, BLOCK), 0)
    cols = lax.broadcasted_iota(jnp.int32, (BLOCK, BLOCK), 1)
    return (rows + cols == BLOCK - 1).astype(BF16)


def fill_reversed(ext_ref, table_ref, flip):
    parts = RELROWS // BLOCK
    for part in range(parts):
        block = table_ref[(parts - 1 - part) * BLOCK : (parts - part) * BLOCK, :]
        ext_ref[SPAN + part * BLOCK : SPAN + (part + 1) * BLOCK, :] = product(flip, block).astype(
            BF16
        )
    ext_ref[0:SPAN, :] = jnp.broadcast_to(ext_ref[SPAN : SPAN + 1, :], (SPAN, BLOCK))
    last = ext_ref[SPAN + RELROWS - 1 : SPAN + RELROWS, :]
    ext_ref[SPAN + RELROWS :, :] = jnp.broadcast_to(last, (SPAN, BLOCK))


def fill_straight(ext_ref, table_ref):
    ext_ref[SPAN : SPAN + RELROWS, :] = table_ref[...]
    ext_ref[0:SPAN, :] = jnp.broadcast_to(table_ref[0:1, :], (SPAN, BLOCK))
    last = table_ref[RELROWS - 1 : RELROWS, :]
    ext_ref[SPAN + RELROWS :, :] = jnp.broadcast_to(last, (SPAN, BLOCK))


def window_start(offset):
    return pl.multiple_of(jnp.clip(offset, 0, EXT - 2 * BLOCK), BLOCK)


def head_mask(head):
    lane = lax.broadcasted_iota(jnp.int32, (1, BLOCK), 1)
    return (lane >= head * HEAD) & (lane < (head + 1) * HEAD)


def forward_kernel(
    blocks, dist_ref, q_ref, k_ref, v_ref, pk_ref, pq_ref, bias_ref, ctx_ref, prob_ref, ek_ref, eq_ref, score_ref
):
    flip = anti_identity()
    fill_reversed(ek_ref, pk_ref, flip)
    fill_reversed(eq_ref, pq_ref, flip)
    q = q_ref[...]
    out = jnp.zeros((BLOCK, BLOCK), F32)
    for head in range(2):
        mask = head_mask(head)
        q_head = jnp.where(mask, q, jnp.zeros_like(q))
        top = jnp.full((1, BLOCK), -jnp.inf, F32)
        for block in range(blocks):
            dist = dist_ref[block]
            rows = slice(block * BLOCK, (block + 1) * BLOCK)
            k_block = k_ref[rows, :]
            k_head = jnp.where(mask, k_block, jnp.zeros_like(k_block))
            window_c = ek_ref[pl.ds(window_start(384 - dist * BLOCK), 2 * BLOCK), :]
            window_p = eq_ref[pl.ds(window_start(384 + dist * BLOCK), 2 * BLOCK), :]
            c2p = pltpu.roll(product_right(q_head, window_c), BLOCK + 1, 1, stride=1, stride_axis=0)
            p2c = pltpu.roll(product_right(k_head, window_p), BLOCK + 1, 1, stride=1, stride_axis=0)
            direct = product_right(k_head, q)
            score = (direct + p2c[:, :BLOCK] + c2p[:, :BLOCK].T) * SCALE + bias_ref[rows, :]
            score_ref[rows, :] = score
            top = jnp.maximum(top, jnp.max(score, axis=0, keepdims=True))
        total = jnp.zeros((1, BLOCK), F32)
        for block in range(blocks):
            rows = slice(block * BLOCK, (block + 1) * BLOCK)
            weight = jnp.exp(score_ref[rows, :] - top)
            score_ref[rows, :] = weight
            total = total + jnp.sum(weight, axis=0, keepdims=True)
        inverse = 1.0 / total
        prob = (score_ref[...] * inverse).astype(BF16)
        prob_ref[head] = prob
        v_head = jnp.where(mask, v_ref[...], jnp.zeros_like(v_ref[...]))
        out = out + product_left(prob, v_head)
    ctx_ref[...] = out.astype(BF16)


def attention_forward(dist, query, key, value, pos_key, pos_query, bias):
    keys = key.shape[0]
    blocks = keys // BLOCK
    pair = lambda rows: pl.BlockSpec((rows, BLOCK), lambda p, dist: (0, p))
    return pl.pallas_call(
        functools.partial(forward_kernel, blocks),
        grid_spec=pltpu.PrefetchScalarGridSpec(
            num_scalar_prefetch=1,
            grid=(PAIRS,),
            in_specs=[
                pair(BLOCK),
                pair(keys),
                pair(keys),
                pair(RELROWS),
                pair(RELROWS),
                pl.BlockSpec((keys, BLOCK), lambda p, dist: (0, 0)),
            ],
            out_specs=[
                pair(BLOCK),
                pl.BlockSpec((2, keys, BLOCK), lambda p, dist: (p, 0, 0)),
            ],
            scratch_shapes=[
                pltpu.VMEM((EXT, BLOCK), BF16),
                pltpu.VMEM((EXT, BLOCK), BF16),
                pltpu.VMEM((keys, BLOCK), F32),
            ],
        ),
        out_shape=[
            jax.ShapeDtypeStruct((BLOCK, D), BF16),
            jax.ShapeDtypeStruct((HEADS, keys, BLOCK), BF16),
        ],
        compiler_params=pltpu.CompilerParams(vmem_limit_bytes=24 * 2**20),
        name="attention_forward",
    )(dist, query, key, value, pos_key, pos_query, bias)


def fold_edges(acc_ref, flip, out_ref):
    head_sum = jnp.sum(acc_ref[:, 0:SPAN], axis=1, keepdims=True)
    tail_sum = jnp.sum(acc_ref[:, SPAN + RELROWS :], axis=1, keepdims=True)
    lane = lax.broadcasted_iota(jnp.int32, (BLOCK, BLOCK), 1)
    parts = RELROWS // BLOCK
    for part in range(parts):
        piece = acc_ref[:, SPAN + part * BLOCK : SPAN + (part + 1) * BLOCK]
        if part == 0:
            piece = piece + jnp.where(lane == 0, head_sum, 0.0)
        if part == parts - 1:
            piece = piece + jnp.where(lane == BLOCK - 1, tail_sum, 0.0)
        piece = piece.astype(BF16)
        if flip is None:
            out_ref[:, part * BLOCK : (part + 1) * BLOCK] = piece
        else:
            at = (parts - 1 - part) * BLOCK
            out_ref[:, at : at + BLOCK] = product(piece, flip).astype(BF16)


def backward_kernel(
    blocks,
    dist_ref,
    q_ref,
    k_ref,
    v_ref,
    pk_ref,
    pq_ref,
    prob_ref,
    gctx_ref,
    gq_ref,
    gk_ref,
    gv_ref,
    gpk_ref,
    gpq_ref,
    ek_ref,
    eq_ref,
    gprob_ref,
    acck_ref,
    accq_ref,
):
    flip = anti_identity()
    fill_straight(ek_ref, pk_ref)
    fill_reversed(eq_ref, pq_ref, flip)
    acck_ref[...] = jnp.zeros_like(acck_ref)
    accq_ref[...] = jnp.zeros_like(accq_ref)
    q = q_ref[...]
    gctx = gctx_ref[...]
    masks = [head_mask(head) for head in range(2)]
    zero = jnp.zeros_like(q)
    q_heads = [jnp.where(mask, q, zero) for mask in masks]
    g_heads = [jnp.where(mask, gctx, zero) for mask in masks]
    g_both = jnp.concatenate(g_heads, axis=0)
    row_masks = [
        (lax.broadcasted_iota(jnp.int32, (BLOCK, 1), 0) // HEAD) == head for head in range(2)
    ]
    q_turned = q.astype(F32).T.astype(BF16)
    q_turned = jnp.concatenate([jnp.where(mask, q_turned, zero) for mask in row_masks], axis=1)
    deltas = [jnp.zeros((1, BLOCK), F32) for head in range(2)]
    for block in range(blocks):
        rows = slice(block * BLOCK, (block + 1) * BLOCK)
        v_block = v_ref[rows, :]
        probs = [prob_ref[head, rows, :] for head in range(2)]
        for head in range(2):
            g_prob = product_right(v_block, g_heads[head])
            gprob_ref[head, rows, :] = g_prob
            deltas[head] = deltas[head] + jnp.sum(
                probs[head].astype(F32) * g_prob, axis=0, keepdims=True
            )
        gv_ref[rows, :] = product(jnp.concatenate(probs, axis=1), g_both).astype(BF16)
    g_query = jnp.zeros((BLOCK, BLOCK), F32)
    pad = jnp.zeros((BLOCK, BLOCK), F32)
    for block in range(blocks):
        dist = dist_ref[block]
        rows = slice(block * BLOCK, (block + 1) * BLOCK)
        k_back = product(flip, k_ref[rows, :])
        k_turned = k_back.T.astype(BF16)
        k_turned = jnp.concatenate([jnp.where(mask, k_turned, zero) for mask in row_masks], axis=1)
        k_back = k_back.astype(BF16)
        start = window_start(384 + dist * BLOCK)
        window_c = ek_ref[pl.ds(start, 2 * BLOCK), :]
        window_p = eq_ref[pl.ds(start, 2 * BLOCK), :]
        lefts_q, lefts_k, rights_q, rights_k, bands_c, bands_p = [], [], [], [], [], []
        for head in range(2):
            g_score = (
                prob_ref[head, rows, :].astype(F32)
                * (gprob_ref[head, rows, :] - deltas[head])
                * SCALE
            ).astype(BF16)
            back = product(flip, g_score)
            turned = back.T
            band_c = pltpu.roll(
                jnp.concatenate([turned, pad], axis=1), 1, 1, stride=1, stride_axis=0
            ).astype(BF16)
            band_p = pltpu.roll(
                jnp.concatenate([back, pad], axis=1), 0, 1, stride=1, stride_axis=0
            ).astype(BF16)
            mask = masks[head]
            lefts_q += [turned.astype(BF16), band_c]
            rights_q += [jnp.where(mask, k_back, zero), jnp.where(mask, window_c, jnp.zeros_like(window_c))]
            lefts_k += [back.astype(BF16), band_p]
            rights_k += [q_heads[head], jnp.where(mask, window_p, jnp.zeros_like(window_p))]
            bands_c.append(band_c)
            bands_p.append(band_p)
        g_query = g_query + product(
            jnp.concatenate(lefts_q, axis=1), jnp.concatenate(rights_q, axis=0)
        )
        g_key = product(jnp.concatenate(lefts_k, axis=1), jnp.concatenate(rights_k, axis=0))
        gk_ref[rows, :] = product(flip, g_key.astype(BF16)).astype(BF16)
        at = pl.ds(start, 2 * BLOCK)
        acck_ref[:, at] += product(q_turned, jnp.concatenate(bands_c, axis=0))
        accq_ref[:, at] += product(k_turned, jnp.concatenate(bands_p, axis=0))
    gq_ref[...] = g_query.astype(BF16)
    fold_edges(acck_ref, None, gpk_ref)
    fold_edges(accq_ref, flip, gpq_ref)


def attention_backward(dist, query, key, value, pos_key, pos_query, prob, g_context):
    keys = key.shape[0]
    blocks = keys // BLOCK
    pair = lambda rows: pl.BlockSpec((rows, BLOCK), lambda p, dist: (0, p))
    turned = pl.BlockSpec((BLOCK, RELROWS), lambda p, dist: (p, 0))
    return pl.pallas_call(
        functools.partial(backward_kernel, blocks),
        grid_spec=pltpu.PrefetchScalarGridSpec(
            num_scalar_prefetch=1,
            grid=(PAIRS,),
            in_specs=[
                pair(BLOCK),
                pair(keys),
                pair(keys),
                pair(RELROWS),
                pair(RELROWS),
                pl.BlockSpec((2, keys, BLOCK), lambda p, dist: (p, 0, 0)),
                pair(BLOCK),
            ],
            out_specs=[pair(BLOCK), pair(keys), pair(keys), turned, turned],
            scratch_shapes=[
                pltpu.VMEM((EXT, BLOCK), BF16),
                pltpu.VMEM((EXT, BLOCK), BF16),
                pltpu.VMEM((2, keys, BLOCK), F32),
                pltpu.VMEM((BLOCK, EXT), F32),
                pltpu.VMEM((BLOCK, EXT), F32),
            ],
        ),
        out_shape=[
            jax.ShapeDtypeStruct((BLOCK, D), BF16),
            jax.ShapeDtypeStruct((keys, D), BF16),
            jax.ShapeDtypeStruct((keys, D), BF16),
            jax.ShapeDtypeStruct((D, RELROWS), BF16),
            jax.ShapeDtypeStruct((D, RELROWS), BF16),
        ],
        compiler_params=pltpu.CompilerParams(vmem_limit_bytes=24 * 2**20),
        name="attention_backward",
    )(dist, query, key, value, pos_key, pos_query, prob, g_context)


def swapped(array, axis, bit):
    return lax.ppermute(array, axis, [(i, i ^ bit) for i in range(lax.axis_size(axis))])


def picked(array, index, axis):
    return lax.dynamic_index_in_dim(array, index, axis, keepdims=False)


def square_mesh():
    return lax.axis_size("seq") == 4 and lax.axis_size("dp") == 8


def row_blocks(tokens):
    cycle = lax.axis_size("seq")
    mine = lax.axis_index("seq")
    if square_mesh():
        parts = [tokens] + [swapped(tokens, "seq", bit) for bit in (1, 2, 3)]
        ids = mine ^ jnp.arange(cycle, dtype=jnp.int32)
        return jnp.concatenate(parts, axis=0), ids
    return lax.all_gather(tokens, "seq", axis=0, tiled=True), jnp.arange(cycle, dtype=jnp.int32)


def to_home(partial):
    rows = partial.shape[0] // lax.axis_size("seq")
    if square_mesh():
        part = partial.reshape(4, rows, D)
        first, second = part[:, : rows // 2], part[:, rows // 2 :]
        got_first = swapped(first[1::2], "seq", 1)
        got_second = swapped(second[2:], "seq", 2)
        first = first[0::2] + got_first
        second = second[:2] + got_second
        got_first = swapped(first[1], "seq", 2)
        got_second = swapped(second[1], "seq", 1)
        return jnp.concatenate([first[0] + got_first, second[0] + got_second], axis=0)
    return lax.psum_scatter(partial, "seq", scatter_dimension=0, tiled=True)


def core_index():
    return lax.axis_index("dp") % 2


def column_halves(array):
    core = core_index()
    half = array.shape[1] // 2
    return (
        lax.dynamic_slice_in_dim(array, core * half, half, 1),
        lax.dynamic_slice_in_dim(array, (1 - core) * half, half, 1),
    )


def reduced(own, others):
    other = swapped(others, "dp", 1)
    summed = (own + other.astype(F32)).astype(BF16)
    rows, cols = summed.shape[0] // 4, summed.shape[1]
    mine = lax.axis_index("seq")
    at_y, at_x = mine // 2, mine % 2
    grid = summed.reshape(2, 2, rows, cols)
    first, second = grid[:, :, : rows // 2], grid[:, :, rows // 2 :]
    got_first = swapped(picked(first, 1 - at_x, 1), "seq", 1)
    got_second = swapped(picked(second, 1 - at_y, 0), "seq", 2)
    first = picked(first, at_x, 1) + got_first
    second = picked(second, at_y, 0) + got_second
    got_first = swapped(picked(first, 1 - at_y, 0), "seq", 2)
    got_second = swapped(picked(second, 1 - at_x, 0), "seq", 1)
    first = picked(first, at_y, 0) + got_first
    second = picked(second, at_x, 0) + got_second
    share = jnp.concatenate([first, second], axis=0)
    return along_z(share)


def along_z(share):
    at_z = lax.axis_index("dp") // 2
    inward = lax.ppermute(share, "dp", [(0, 2), (1, 3), (6, 4), (7, 5)])
    share = share + inward
    across = lax.ppermute(share, "dp", [(2, 4), (3, 5), (4, 2), (5, 3)])
    share = share + across
    outward = lax.ppermute(share, "dp", [(2, 0), (3, 1), (4, 6), (5, 7)])
    inner = (at_z == 1) | (at_z == 2)
    return jnp.where(inner, share, outward)


def both_halves(share):
    other = swapped(share, "dp", 1)
    first = core_index() == 0
    return jnp.concatenate(
        [jnp.where(first, share, other), jnp.where(first, other, share)], axis=-1
    ).astype(F32)


def reduce_plain(partial):
    share = lax.psum_scatter(partial.astype(BF16), "seq", scatter_dimension=0, tiled=True)
    return lax.psum(share, "dp").astype(F32)


def local(
    tokens,
    cotangent,
    lengths,
    w_query,
    b_query,
    w_key,
    b_key,
    w_value,
    b_value,
    w_out,
    b_out,
    gain_one,
    shift_one,
    w_up,
    b_up,
    w_down,
    b_down,
    gain_two,
    shift_two,
    rel_table,
):
    rows = tokens.shape[0]
    cycle = lax.axis_size("seq")
    mine = lax.axis_index("seq")
    lengths_row = lengths[0]
    offsets = jnp.arange(rows, dtype=jnp.int32)
    query_pos = mine * rows + offsets
    query_seg = segment_ids(lengths_row, query_pos)
    valid = (query_pos < jnp.sum(lengths_row)).astype(F32)

    tokens_row, ids = row_blocks(tokens)
    key_pos = (ids[:, None] * rows + offsets[None, :]).reshape(-1)
    key_seg = segment_ids(lengths_row, key_pos)
    bias = jnp.where(key_seg[:, None] == query_seg[None, :], 0.0, -1e30).astype(F32)
    dist = (mine - ids).astype(jnp.int32)

    query = (product(tokens, w_query) + b_query).astype(BF16)
    pos_key = (product(rel_table, w_key) + b_key).astype(BF16)
    pos_query = (product(rel_table, w_query) + b_query).astype(BF16)
    key = (product(tokens_row, w_key) + b_key).astype(BF16)
    value = (product(tokens_row, w_value) + b_value).astype(BF16)
    context, prob = attention_forward(dist, query, key, value, pos_key, pos_query, bias)

    attn = product(context, w_out) + b_out
    resid_one = tokens.astype(F32) + attn
    hidden_one, norm_one_back = jax.vjp(layer_norm, resid_one, gain_one, shift_one)
    hidden_low = hidden_one.astype(BF16)
    up = product(hidden_low, w_up) + b_up
    act_value, gelu_back = jax.vjp(gelu_exact, up)
    act = act_value.astype(BF16)
    down = product(act, w_down) + b_down
    final, norm_two_back = jax.vjp(layer_norm, hidden_one + down, gain_two, shift_two)
    output = final.astype(BF16)
    g_out = cotangent.astype(F32) * valid[:, None]
    g_resid_two, grad_gain_two, grad_shift_two = norm_two_back(g_out)
    g_down = g_resid_two.astype(BF16)
    grad_b_down = jnp.sum(g_down.astype(F32), axis=0)
    g_act = product_right(g_down, w_down)
    g_up = gelu_back(g_act)[0].astype(BF16)
    grad_b_up = jnp.sum(g_up.astype(F32), axis=0)
    g_hidden_one = g_resid_two + product_right(g_up, w_up)
    g_resid_one, grad_gain_one, grad_shift_one = norm_one_back(g_hidden_one)
    g_attn = g_resid_one.astype(BF16)
    grad_b_out = jnp.sum(g_attn.astype(F32), axis=0)
    g_context = product_right(g_attn, w_out).astype(BF16)
    g_query, g_key, g_value, g_pos_key, g_pos_query = attention_backward(
        dist, query, key, value, pos_key, pos_query, prob, g_context
    )

    grad_home = to_home((product_right(g_key, w_key) + product_right(g_value, w_value)).astype(BF16))
    grad_tokens = g_resid_one + product_right(g_query, w_query) + grad_home.astype(F32)
    g_pos = (
        jnp.sum(g_pos_query.astype(F32), axis=1),
        jnp.sum(g_pos_key.astype(F32), axis=1),
    )
    biases = [
        jnp.sum(g_query.astype(F32), axis=0) + g_pos[0],
        jnp.sum(g_key.astype(F32), axis=0) + g_pos[1],
        jnp.sum(g_value.astype(F32), axis=0),
        grad_b_out,
        grad_gain_one,
        grad_shift_one,
        grad_b_down,
        grad_gain_two,
        grad_shift_two,
    ]

    def for_query(cols):
        return product_left(tokens, g_query[:, cols]) + product_right(
            rel_table.T, g_pos_query[cols]
        )

    if square_mesh():
        core = core_index()
        half = D // 2

        def halves(make):
            return make(core * half), make((1 - core) * half)

        def columns(array, at):
            return lax.dynamic_slice_in_dim(array, at, half, 1)

        def rows_of(array, at):
            return lax.dynamic_slice_in_dim(array, at, half, 0)

        own, others = column_halves(g_down)
        down_share = reduced(product_left(act, own), product_left(act, others).astype(BF16))
        own, others = column_halves(g_up)
        up_share = reduced(
            product_left(hidden_low, own), product_left(hidden_low, others).astype(BF16)
        )
        own, others = column_halves(g_attn)
        out_share = reduced(product_left(context, own), product_left(context, others).astype(BF16))

        share = D // 4
        packed = jnp.concatenate(
            [v.reshape(4, share) for v in biases] + [grad_b_up.reshape(4, D)], axis=1
        )
        packed = jnp.pad(packed, ((0, 0), (0, 16 * half - packed.shape[1]))).reshape(4, 16, half)

        def last_group(at):
            gq = columns(g_query, at)
            gk = columns(g_key, at)
            gv = columns(g_value, at)
            gpq = rows_of(g_pos_query, at)
            gpk = rows_of(g_pos_key, at)
            parts = [
                product_left(tokens, gq)
                + lax.dot_general(
                    rel_table, gpq, (((0,), (1,)), ((), ())), preferred_element_type=F32
                ),
                product_left(tokens_row, gk)
                + lax.dot_general(
                    rel_table, gpk, (((0,), (1,)), ((), ())), preferred_element_type=F32
                ),
                product_left(tokens_row, gv),
            ]
            parts = [part.reshape(4, share, half) for part in parts]
            wq = rows_of(w_query, at)
            wk = rows_of(w_key, at)
            rel = lax.dot_general(
                g_pos_key, wk, (((0,), (1,)), ((), ())), preferred_element_type=F32
            ) + lax.dot_general(
                g_pos_query, wq, (((0,), (1,)), ((), ())), preferred_element_type=F32
            )
            parts.append(rel.reshape(4, RELROWS // 4, half))
            parts.append(packed)
            joined = jnp.concatenate([part.astype(BF16) for part in parts], axis=1)
            return joined.reshape(-1, half)

        own, others = halves(last_group)
        last = reduced(own.astype(F32), others)
        bias_share = last[3 * share + RELROWS // 4 :].reshape(-1).astype(F32)
        last = both_halves(last[: 3 * share + RELROWS // 4])
        grads = [last[i * share : (i + 1) * share] for i in range(3)]
        rel_part = last[3 * share :].astype(BF16)
        grad_rel = jnp.zeros((RELROWS, D), BF16)
        pieces = [rel_part] + [swapped(rel_part, "seq", bit) for bit in (1, 2, 3)]
        for bit, piece in enumerate(pieces):
            grad_rel = lax.dynamic_update_slice_in_dim(
                grad_rel, piece, (mine ^ bit) * (RELROWS // 4), 0
            )
        grad_rel = grad_rel.astype(F32)
        grad_w_down = both_halves(down_share)
        grad_w_up = both_halves(up_share)
        grad_w_out = both_halves(out_share)
        vectors = [bias_share[i * share : (i + 1) * share] for i in range(len(biases))]
        grad_b_up = bias_share[len(biases) * share : len(biases) * share + D]
    else:
        grads = [
            reduce_plain(
                product_left(tokens, g_query)
                + lax.dot_general(
                    rel_table, g_pos_query, (((0,), (1,)), ((), ())), preferred_element_type=F32
                )
            ),
            reduce_plain(
                product_left(tokens_row, g_key)
                + lax.dot_general(
                    rel_table, g_pos_key, (((0,), (1,)), ((), ())), preferred_element_type=F32
                )
            ),
            reduce_plain(product_left(tokens_row, g_value)),
        ]
        grad_w_out = reduce_plain(product_left(context, g_attn))
        grad_w_up = reduce_plain(product_left(hidden_low, g_up))
        grad_w_down = reduce_plain(product_left(act, g_down))
        vectors = [reduce_plain(v) for v in biases]
        grad_b_up = reduce_plain(grad_b_up)
        rel = lax.dot_general(
            g_pos_key, w_key, (((0,), (1,)), ((), ())), preferred_element_type=F32
        ) + lax.dot_general(
            g_pos_query, w_query, (((0,), (1,)), ((), ())), preferred_element_type=F32
        )
        grad_rel = lax.psum(rel, ("dp", "seq"))
    return (
        output,
        grad_tokens,
        grads[0],
        vectors[0],
        grads[1],
        vectors[1],
        grads[2],
        vectors[2],
        grad_w_out,
        vectors[3],
        vectors[4],
        vectors[5],
        grad_w_up,
        grad_b_up,
        grad_w_down,
        vectors[6],
        vectors[7],
        vectors[8],
        grad_rel,
    )


def solution(mesh):
    return jax.shard_map(
        local,
        mesh=mesh,
        in_specs=(
            P(("dp", "seq"), None),
            P(("dp", "seq"), None),
            P("dp", None),
        )
        + (P(),) * 17,
        out_specs=(
            P(("dp", "seq"), None),
            P(("dp", "seq"), None),
            P("seq", None),
            P("seq"),
            P("seq", None),
            P("seq"),
            P("seq", None),
            P("seq"),
            P("seq", None),
            P("seq"),
            P("seq"),
            P("seq"),
            P("seq", None),
            P("seq"),
            P("seq", None),
            P("seq"),
            P("seq"),
            P("seq"),
            P(),
        ),
        check_vma=False,
    )
```

```python
import functools
import math

import jax
import jax.numpy as jnp
from jax import lax
from jax.experimental import pallas as pl
from jax.experimental.pallas import tpu as pltpu
from jax.sharding import PartitionSpec as P

D = 768
HEADS = 12
HEAD = 64
SPAN = 256
RELROWS = 512
BLOCK = 128
EXT = RELROWS + 2 * SPAN
PAIRS = HEADS // 2
SCALE = 1.0 / math.sqrt(3 * HEAD)
F32 = jnp.float32
BF16 = jnp.bfloat16
ROLLED = BF16


def layer_norm(resid, gain, shift):
    center = resid - jnp.mean(resid, axis=-1, keepdims=True)
    spread = jnp.mean(center * center, axis=-1, keepdims=True)
    return center * lax.rsqrt(spread + 1e-07) * gain + shift


def gelu_exact(hidden):
    return jax.nn.gelu(hidden, approximate=False)


def product(left, right):
    return jnp.dot(left, right, preferred_element_type=F32)


def product_left(left, right):
    return lax.dot_general(left, right, (((0,), (0,)), ((), ())), preferred_element_type=F32)


def product_right(left, right):
    return lax.dot_general(left, right, (((1,), (1,)), ((), ())), preferred_element_type=F32)


def segment_ids(lengths_row, positions):
    bounds = jnp.cumsum(lengths_row)
    return jnp.sum((positions[:, None] >= bounds[None, :]).astype(jnp.int32), axis=1)


def anti_identity():
    rows = lax.broadcasted_iota(jnp.int32, (BLOCK, BLOCK), 0)
    cols = lax.broadcasted_iota(jnp.int32, (BLOCK, BLOCK), 1)
    return (rows + cols == BLOCK - 1).astype(BF16)


def window_start(offset):
    return pl.multiple_of(jnp.clip(offset, 0, EXT - 2 * BLOCK), BLOCK)


def head_mask(head):
    lane = lax.broadcasted_iota(jnp.int32, (1, BLOCK), 1)
    return (lane >= head * HEAD) & (lane < (head + 1) * HEAD)


def band_roll(wide, shift):
    return pltpu.roll(wide, shift, 1, stride=1, stride_axis=0)


def by_head(pair):
    zero = jnp.zeros_like(pair)
    return jnp.concatenate([jnp.where(head_mask(head), pair, zero) for head in range(2)], axis=0)


def forward_kernel(
    blocks, dist_ref, q_ref, k_ref, v_ref, ek_ref, eq_ref, bias_ref, ctx_ref, prob_ref, score_ref
):
    q = q_ref[...]
    q_heads = by_head(q)
    tops = [jnp.full((1, BLOCK), -jnp.inf, F32) for head in range(2)]
    for block in range(blocks):
        dist = dist_ref[block]
        rows = slice(block * BLOCK, (block + 1) * BLOCK)
        k_heads = by_head(k_ref[rows, :])
        window_c = ek_ref[pl.ds(window_start(384 - dist * BLOCK), 2 * BLOCK), :]
        window_p = eq_ref[pl.ds(window_start(384 + dist * BLOCK), 2 * BLOCK), :]
        c2p = product_right(q_heads, window_c)
        p2c = product_right(k_heads, window_p)
        direct = product_right(k_heads, q)
        for head in range(2):
            own = slice(head * BLOCK, (head + 1) * BLOCK)
            first = band_roll(c2p[own].astype(ROLLED), BLOCK + 1)[:, :BLOCK].T
            second = band_roll(p2c[own].astype(ROLLED), BLOCK + 1)[:, :BLOCK]
            score = (direct[own] + first.astype(F32) + second.astype(F32)) * SCALE + bias_ref[rows, :]
            score_ref[head, rows, :] = score
            tops[head] = jnp.maximum(tops[head], jnp.max(score, axis=0, keepdims=True))
    probs = []
    for head in range(2):
        weight = jnp.exp(score_ref[head] - tops[head])
        total = jnp.sum(weight, axis=0, keepdims=True)
        prob = (weight * (1.0 / total)).astype(BF16)
        prob_ref[head] = prob
        probs.append(prob)
    v = v_ref[...]
    zero = jnp.zeros_like(v)
    out = product_left(probs[0], jnp.where(head_mask(0), v, zero)) + product_left(
        probs[1], jnp.where(head_mask(1), v, zero)
    )
    ctx_ref[...] = out.astype(BF16)


def attention_forward(dist, query, key, value, ext_key, ext_query, bias):
    keys = key.shape[0]
    blocks = keys // BLOCK
    pair = lambda rows: pl.BlockSpec((rows, BLOCK), lambda p, dist: (0, p))
    return pl.pallas_call(
        functools.partial(forward_kernel, blocks),
        grid_spec=pltpu.PrefetchScalarGridSpec(
            num_scalar_prefetch=1,
            grid=(PAIRS,),
            in_specs=[
                pair(BLOCK),
                pair(keys),
                pair(keys),
                pair(EXT),
                pair(EXT),
                pl.BlockSpec((keys, BLOCK), lambda p, dist: (0, 0)),
            ],
            out_specs=[
                pair(BLOCK),
                pl.BlockSpec((2, keys, BLOCK), lambda p, dist: (p, 0, 0)),
            ],
            scratch_shapes=[pltpu.VMEM((2, keys, BLOCK), F32)],
        ),
        out_shape=[
            jax.ShapeDtypeStruct((BLOCK, D), BF16),
            jax.ShapeDtypeStruct((HEADS, keys, BLOCK), BF16),
        ],
        compiler_params=pltpu.CompilerParams(vmem_limit_bytes=24 * 2**20),
        name="attention_forward",
    )(dist, query, key, value, ext_key, ext_query, bias)


def fold_edges(acc_ref):
    head_sum = jnp.sum(acc_ref[:, 0:SPAN], axis=1, keepdims=True)
    tail_sum = jnp.sum(acc_ref[:, SPAN + RELROWS :], axis=1, keepdims=True)
    lane = lax.broadcasted_iota(jnp.int32, (BLOCK, RELROWS), 1)
    middle = acc_ref[:, SPAN : SPAN + RELROWS]
    middle = middle + jnp.where(lane == 0, head_sum, 0.0)
    return (middle + jnp.where(lane == RELROWS - 1, tail_sum, 0.0)).astype(BF16)


def flipped_lanes(array, flip):
    parts = array.shape[1] // BLOCK
    return jnp.concatenate(
        [
            product(array[:, part * BLOCK : (part + 1) * BLOCK], flip).astype(BF16)
            for part in reversed(range(parts))
        ],
        axis=1,
    )


def place(order_ref, share, core, shares, each):
    at = (core ^ order_ref[0]) * shares + (share ^ order_ref[1])
    return pl.multiple_of(at * each, 16)


def place_rows(order_ref, into_ref, value, cores, shares):
    each = value.shape[0] // (cores * shares)
    for share in range(shares):
        for core in range(cores):
            at = (share * cores + core) * each
            into_ref[pl.ds(place(order_ref, share, core, shares, each), each), :] = value[
                at : at + each
            ]


def store_pieces(refs, at, value, lanes):
    shares = refs[0].shape[0]
    each = value.shape[0] // (len(refs) * shares)
    for core, ref in enumerate(refs):
        for share in range(shares):
            start = (core * shares + share) * each
            ref[share, at : at + each, lanes] = value[start : start + each]


def backward_kernel(
    blocks,
    cores,
    first,
    last,
    dist_ref,
    order_ref,
    q_ref,
    k_ref,
    v_ref,
    ek_ref,
    eq_ref,
    prob_ref,
    gctx_ref,
    tok_ref,
    rel_ref,
    wq_ref,
    wk_ref,
    wv_ref,
    vec_ref,
    extra_one_ref,
    extra_two_ref,
    *refs,
):
    pack_refs, refs = refs[:cores], refs[cores:]
    backward_body(
        blocks, first, last, dist_ref, order_ref, q_ref, k_ref, v_ref, ek_ref, eq_ref, prob_ref, gctx_ref,
        tok_ref, rel_ref, wq_ref, wk_ref, wv_ref, vec_ref, extra_one_ref, extra_two_ref, pack_refs, *refs
    )


def backward_body(
    blocks,
    first,
    last,
    dist_ref,
    order_ref,
    q_ref,
    k_ref,
    v_ref,
    ek_ref,
    eq_ref,
    prob_ref,
    gctx_ref,
    tok_ref,
    rel_ref,
    wq_ref,
    wk_ref,
    wv_ref,
    vec_ref,
    extra_one_ref,
    extra_two_ref,
    pack_refs,
    out_one_ref,
    out_two_ref,
    gprob_ref,
    gk_ref,
    gv_ref,
    acck_ref,
    accq_ref,
    tokt_ref,
    relt_ref,
    acc_tok_ref,
    acc_rel_ref,
    turn_ref,
):
    step = pl.program_id(0)
    cores, shares, half = len(pack_refs), pack_refs[0].shape[0], pack_refs[0].shape[2]
    share = D // cores // shares
    flip = anti_identity()

    @pl.when(step == 0)
    def _():
        place_rows(order_ref, tokt_ref, tok_ref[...].T, cores, shares)
        place_rows(order_ref, relt_ref, rel_ref[...].T, cores, shares)
        if first:
            acc_tok_ref[...] = jnp.zeros_like(acc_tok_ref)
            acc_rel_ref[...] = jnp.zeros_like(acc_rel_ref)
        else:
            acc_tok_ref[...] = extra_one_ref[...]
            acc_rel_ref[...] = extra_two_ref[...]

    acck_ref[...] = jnp.zeros_like(acck_ref)
    accq_ref[...] = jnp.zeros_like(accq_ref)
    q_heads = by_head(q_ref[...])
    g_heads = by_head(gctx_ref[...])
    row_masks = [
        (lax.broadcasted_iota(jnp.int32, (BLOCK, 1), 0) // HEAD) == head for head in range(2)
    ]

    def turned_heads(array):
        turned = array.T
        zero = jnp.zeros_like(turned)
        return jnp.concatenate([jnp.where(mask, turned, zero) for mask in row_masks], axis=1)

    q_turned = turned_heads(q_ref[...])
    delta = jnp.zeros((1, 2 * BLOCK), F32)
    for block in range(blocks):
        rows = slice(block * BLOCK, (block + 1) * BLOCK)
        probs = jnp.concatenate([prob_ref[head, rows, :] for head in range(2)], axis=1)
        g_prob = product_right(v_ref[rows, :], g_heads)
        gprob_ref[rows, :] = g_prob
        delta = delta + jnp.sum(probs.astype(F32) * g_prob, axis=0, keepdims=True)
        gv_ref[rows, :] = product(probs, g_heads).astype(BF16)
    g_query = jnp.zeros((BLOCK, BLOCK), F32)
    pad = jnp.zeros((BLOCK, BLOCK), BF16)
    for block in range(blocks):
        rows = slice(block * BLOCK, (block + 1) * BLOCK)
        k_back = product(flip, k_ref[rows, :]).astype(BF16)
        start = window_start(384 + dist_ref[block] * BLOCK)
        window_c = by_head(ek_ref[pl.ds(start, 2 * BLOCK), :])
        window_p = by_head(eq_ref[pl.ds(start, 2 * BLOCK), :])
        probs = jnp.concatenate([prob_ref[head, rows, :] for head in range(2)], axis=1)
        g_score = (probs.astype(F32) * (gprob_ref[rows, :] - delta) * SCALE).astype(BF16)
        backs = product(flip, g_score).astype(BF16)
        turns, bands_c, bands_p = [], [], []
        for head in range(2):
            back = backs[:, head * BLOCK : (head + 1) * BLOCK]
            turned = back.T
            turns.append(turned)
            bands_c.append(band_roll(jnp.concatenate([turned, pad], axis=1), 1))
            bands_p.append(band_roll(jnp.concatenate([back, pad], axis=1), 0))
        g_query = g_query + product(
            jnp.concatenate(turns + bands_c, axis=1),
            jnp.concatenate([by_head(k_back), window_c], axis=0),
        )
        g_key = product(
            jnp.concatenate([backs] + bands_p, axis=1),
            jnp.concatenate([q_heads, window_p], axis=0),
        )
        gk_ref[rows, :] = product(flip, g_key.astype(BF16)).astype(BF16)
        at = pl.ds(start, 2 * BLOCK)
        acck_ref[:, at] += product(q_turned, jnp.concatenate(bands_c, axis=0))
        accq_ref[:, at] += product(turned_heads(k_back), jnp.concatenate(bands_p, axis=0))

    g_query = g_query.astype(BF16)
    g_pos_key = fold_edges(acck_ref)
    g_pos_query = flipped_lanes(fold_edges(accq_ref), flip)
    g_key = gk_ref[...]
    g_value = gv_ref[...]
    lanes = pl.ds(pl.multiple_of(step * BLOCK, BLOCK), BLOCK)
    ones_tok = jnp.ones((16, tok_ref.shape[0]), BF16)
    ones_rel = jnp.ones((16, RELROWS), BF16)
    row = lax.broadcasted_iota(jnp.int32, (16, BLOCK), 0)
    vec = vec_ref[...]
    g_both = jnp.concatenate([g_key, g_value], axis=1)
    pos_both = jnp.concatenate([g_pos_key, g_pos_query], axis=0)
    from_tok = product(tokt_ref[...], g_both)
    from_rel = product_right(relt_ref[...], pos_both)
    from_own = product(tokt_ref[:, :BLOCK], g_query)
    sum_tok = product(ones_tok, g_both)
    sum_rel = product_right(ones_rel, pos_both)
    sum_own = product(ones_tok[:, :BLOCK], g_query)
    weights = [
        (from_own + from_rel[:, BLOCK:], sum_own + sum_rel[:, BLOCK:]),
        (from_tok[:, :BLOCK] + from_rel[:, :BLOCK], sum_tok[:, :BLOCK] + sum_rel[:, :BLOCK]),
        (from_tok[:, BLOCK:], sum_tok[:, BLOCK:]),
    ]
    for at, (weight, total) in enumerate(weights):
        store_pieces(pack_refs, at * share, weight.astype(BF16), lanes)
        vec = vec + jnp.where(row == at, total, 0.0)
    vec = vec.astype(BF16)
    for pack_ref in pack_refs:
        for part in range(shares):
            pack_ref[part, 3 * share : 3 * share + 16, lanes] = vec
    acc_tok_ref[...] += product_right(
        g_both,
        jnp.concatenate([wk_ref[...], wv_ref[...]], axis=1),
    )
    acc_tok_ref[0:BLOCK, :] += product_right(g_query, wq_ref[...])
    acc_rel_ref[...] += product(
        jnp.concatenate([wk_ref[...], wq_ref[...]], axis=1),
        pos_both,
    )

    @pl.when(step == pl.num_programs(0) - 1)
    def _():
        base = 3 * share + 16
        extra = None
        if last:
            out_one_ref[...] = acc_tok_ref[0:BLOCK, :]
            out_two_ref[...] = acc_tok_ref[BLOCK:, :].astype(BF16)
            place_rows(order_ref, turn_ref, acc_rel_ref[...].T.astype(BF16), cores, shares)
            extra = turn_ref[...]
        else:
            out_one_ref[...] = acc_tok_ref[...]
            out_two_ref[...] = acc_rel_ref[...]
        if first:
            place_rows(order_ref, turn_ref, extra_one_ref[...].T, cores, shares)
            extra = product(turn_ref[...], extra_two_ref[...]).astype(BF16)
        if extra is not None:
            each = extra.shape[0] // (cores * shares)
            for part in range(D // half):
                columns = extra[:, part * half : (part + 1) * half]
                store_pieces(pack_refs, base + part * each, columns, slice(None))


def attention_backward(
    start, pairs, cores, shares, dist, order, query, key, value, ext_key, ext_query, prob, g_context,
    tokens_row, rel_table, w_query, w_key, w_value, vectors, extra_one, extra_two,
):
    keys = key.shape[0]
    blocks = keys // BLOCK
    first, last = start == 0, start + pairs == PAIRS
    share = D // cores // shares
    half = pairs * BLOCK
    rows_extra = D if first else RELROWS if last else 0
    pack = (shares, 3 * share + 16 + rows_extra // cores // shares * (D // half), half)
    pair = lambda rows: pl.BlockSpec((rows, BLOCK), lambda p, *_: (0, p + start))
    whole = lambda *shape: pl.BlockSpec(
        shape, lambda p, *_: (0,) * len(shape), pipeline_mode=pl.Buffered(1)
    )
    if first:
        extras = [whole(BLOCK, D), whole(BLOCK, D)]
        turn = (D, BLOCK)
    else:
        extras = [whole(keys, D), whole(D, RELROWS)]
        turn = (RELROWS, D)
    if last:
        outs = [((BLOCK, D), F32), ((keys - BLOCK, D), BF16)]
    else:
        outs = [((keys, D), F32), ((D, RELROWS), F32)]
    return pl.pallas_call(
        functools.partial(backward_kernel, blocks, cores, first, last),
        grid_spec=pltpu.PrefetchScalarGridSpec(
            num_scalar_prefetch=2,
            grid=(pairs,),
            in_specs=[
                pair(BLOCK),
                pair(keys),
                pair(keys),
                pair(EXT),
                pair(EXT),
                pl.BlockSpec((2, keys, BLOCK), lambda p, *_: (p + start, 0, 0)),
                pair(BLOCK),
                whole(keys, D),
                whole(RELROWS, D),
                pair(D),
                pair(D),
                pair(D),
                pair(16),
            ]
            + extras,
            out_specs=[whole(*pack)] * cores + [whole(*shape) for shape, _ in outs],
            scratch_shapes=[
                pltpu.VMEM((keys, 2 * BLOCK), F32),
                pltpu.VMEM((keys, BLOCK), BF16),
                pltpu.VMEM((keys, BLOCK), BF16),
                pltpu.VMEM((BLOCK, EXT), F32),
                pltpu.VMEM((BLOCK, EXT), F32),
                pltpu.VMEM((D, keys), BF16),
                pltpu.VMEM((D, RELROWS), BF16),
                pltpu.VMEM((keys, D), F32),
                pltpu.VMEM((D, RELROWS), F32),
                pltpu.VMEM(turn, BF16),
            ],
        ),
        out_shape=[jax.ShapeDtypeStruct(pack, BF16)] * cores
        + [jax.ShapeDtypeStruct(shape, dtype) for shape, dtype in outs],
        compiler_params=pltpu.CompilerParams(vmem_limit_bytes=(40 if keys <= 1024 else 58) * 2**20),
        name="attention_backward",
    )(
        dist, order, query, key, value, ext_key, ext_query, prob, g_context,
        tokens_row, rel_table, w_query, w_key, w_value, vectors, extra_one, extra_two,
    )


def swapped(array, axis, bits):
    return lax.ppermute(array, axis, [(i, i ^ bits) for i in range(lax.axis_size(axis))])


def from_peers(arrays):
    return [swapped(array, "seq", bits) for bits, array in enumerate(arrays, 1)]


def picked(array, index, axis):
    return lax.dynamic_index_in_dim(array, index, axis, keepdims=False)


def together(*arrays):
    return lax.optimization_barrier(arrays)


def added(*arrays):
    return functools.reduce(jnp.add, [array.astype(F32) for array in arrays]).astype(BF16)


def square_mesh():
    return lax.axis_size("seq") == 4 and lax.axis_size("dp") == 8


def scatter(pack):
    return from_peers([pack[1], pack[2], pack[3]])


def inward(share):
    return lax.ppermute(share, "dp", [(0, 2), (1, 3), (6, 4), (7, 5)])


def across(share):
    return lax.ppermute(share, "dp", [(2, 4), (3, 5), (4, 2), (5, 3)])


def outward(share):
    return lax.ppermute(share, "dp", [(2, 0), (3, 1), (4, 6), (5, 7)])


def settled(share, got):
    at_z = lax.axis_index("dp") // 2
    return jnp.where((at_z == 1) | (at_z == 2), share, got)


def core_index():
    return lax.axis_index("dp") % 2


def both_cores(share, axis):
    other = swapped(share, "dp", 1)
    first = core_index() == 0
    return jnp.concatenate(
        [jnp.where(first, share, other), jnp.where(first, other, share)], axis=axis
    )


def reduce_plain(partial):
    share = lax.psum_scatter(partial.astype(BF16), "seq", scatter_dimension=0, tiled=True)
    return lax.psum(share, "dp").astype(F32)


def extended(table):
    return jnp.concatenate(
        [
            jnp.broadcast_to(table[:1], (SPAN, D)),
            table,
            jnp.broadcast_to(table[-1:], (SPAN, D)),
        ],
        axis=0,
    )


def local(
    tokens,
    cotangent,
    lengths,
    w_query,
    b_query,
    w_key,
    b_key,
    w_value,
    b_value,
    w_out,
    b_out,
    gain_one,
    shift_one,
    w_up,
    b_up,
    w_down,
    b_down,
    gain_two,
    shift_two,
    rel_table,
):
    rows = tokens.shape[0]
    cycle = lax.axis_size("seq")
    mine = lax.axis_index("seq")
    core = core_index()
    square = square_mesh()
    hidden_units = w_up.shape[1]
    share = D // cycle
    lengths_row = lengths[0]
    offsets = jnp.arange(rows, dtype=jnp.int32)
    query_pos = mine * rows + offsets
    query_seg = segment_ids(lengths_row, query_pos)
    valid = (query_pos < jnp.sum(lengths_row)).astype(F32)

    if square:
        tokens_row = jnp.concatenate([tokens] + from_peers([tokens] * 3), axis=0)
        ids = mine ^ jnp.arange(cycle, dtype=jnp.int32)
        order = jnp.stack([core, mine]).astype(jnp.int32)
        cores = 2
    else:
        tokens_all = lax.all_gather(tokens, "seq", axis=0, tiled=True)
        tokens_row = jnp.concatenate([tokens, tokens_all], axis=0)
        ids = jnp.concatenate([mine[None], jnp.arange(cycle, dtype=jnp.int32)])
        order = jnp.zeros((2,), jnp.int32)
        cores = 1
    key_pos = (ids[:, None] * rows + offsets[None, :]).reshape(-1)
    key_seg = segment_ids(lengths_row, key_pos)
    bias = jnp.where(key_seg[:, None] == query_seg[None, :], 0.0, -1e30).astype(F32)
    if not square:
        again = jnp.concatenate(
            [jnp.zeros((rows,), jnp.bool_), jnp.repeat(ids[1:] == mine, rows)]
        )
        bias = jnp.where(again[:, None], -1e30, bias)
    dist = (mine - ids).astype(jnp.int32)

    query = (product(tokens, w_query) + b_query).astype(BF16)
    places = jnp.arange(RELROWS, dtype=jnp.int32)
    turn = (places[:, None] + places[None, :] == RELROWS - 1).astype(BF16)
    rel_back = extended(product(turn, rel_table).astype(BF16))
    ext_key_back = (product(rel_back, w_key) + b_key).astype(BF16)
    ext_query_back = (product(rel_back, w_query) + b_query).astype(BF16)
    ext_key = (product(extended(rel_table), w_key) + b_key).astype(BF16)
    key = (product(tokens_row, w_key) + b_key).astype(BF16)
    value = (product(tokens_row, w_value) + b_value).astype(BF16)
    context, prob = attention_forward(dist, query, key, value, ext_key_back, ext_query_back, bias)

    attn = product(context, w_out) + b_out
    resid_one = tokens.astype(F32) + attn
    hidden_one, norm_one_back = jax.vjp(layer_norm, resid_one, gain_one, shift_one)
    hidden_low = hidden_one.astype(BF16)
    up = product(hidden_low, w_up) + b_up
    act_value, gelu_back = jax.vjp(gelu_exact, up)
    act = act_value.astype(BF16)
    if square:
        quarter = hidden_units // 4
        columns = lambda bits: lax.dynamic_slice_in_dim(act, (mine ^ bits) * quarter, quarter, 1)
        act_got = from_peers([columns(bits) for bits in (1, 2, 3)])
        act_own = columns(0)
    down = product(act, w_down) + b_down
    final, norm_two_back = jax.vjp(layer_norm, hidden_one + down, gain_two, shift_two)
    output = final.astype(BF16)
    g_out = cotangent.astype(F32) * valid[:, None]
    g_resid_two, grad_gain_two, grad_shift_two = norm_two_back(g_out)
    g_down = g_resid_two.astype(BF16)
    if square:
        g_down_got = from_peers([g_down] * 3)
    grad_b_down = jnp.sum(g_down.astype(F32), axis=0)
    g_act = product_right(g_down, w_down)
    g_up = gelu_back(g_act)[0].astype(BF16)
    if square:
        half = hidden_units // 2
        g_up_own = lax.dynamic_slice_in_dim(g_up, core * half, half, 1)
        g_up_other = lax.dynamic_slice_in_dim(g_up, (1 - core) * half, half, 1)
        up_got = swapped(product_left(hidden_low, g_up_other).astype(BF16), "dp", 1)
    grad_b_up = jnp.sum(g_up.astype(F32), axis=0)
    g_hidden_one = g_resid_two + product_right(g_up, w_up)
    g_resid_one, grad_gain_one, grad_shift_one = norm_one_back(g_hidden_one)
    g_attn = g_resid_one.astype(BF16)
    grad_b_out = jnp.sum(g_attn.astype(F32), axis=0)
    g_context = product_right(g_attn, w_out).astype(BF16)

    sums = [grad_b_out, grad_gain_one, grad_shift_one, grad_b_down, grad_gain_two, grad_shift_two]
    vectors = jnp.concatenate(
        [jnp.zeros((3, D), F32)] + [v[None] for v in sums] + [grad_b_up.reshape(-1, D)], axis=0
    )
    vectors = jnp.pad(vectors, ((0, 16 - vectors.shape[0]), (0, 0)))

    def backward(start, pairs, g_context, extra_one, extra_two):
        outs = attention_backward(
            start, pairs, cores, cycle, dist, order, query, key, value, ext_key, ext_query_back, prob,
            g_context, tokens_row, rel_table, w_query, w_key, w_value, vectors, extra_one, extra_two,
        )
        return outs[:cores], outs[cores:]

    def assembled(packs, grad_tokens, grad_w_up, grad_w_down):
        piece = share // cores
        whole_rows = lambda v, at, each: v[:, at : at + each].reshape(cores * each, -1)
        grads = [
            jnp.concatenate([whole_rows(v, at * piece, piece) for v in packs], axis=1).astype(F32)
            for at in range(3)
        ]
        base = 3 * piece
        vector_sums = jnp.concatenate([v[0, base : base + 16] for v in packs], axis=1).astype(F32)
        base += 16

        def unpacked(v, each):
            parts = D // v.shape[2]
            return jnp.concatenate(
                [whole_rows(v, base + part * each, each) for part in range(parts)], axis=1
            )

        grad_w_out = unpacked(packs[0], piece).astype(F32)
        rel_part = unpacked(packs[-1], RELROWS // cycle // cores)
        if square:
            grad_rel = jnp.zeros((RELROWS, D), F32)
            for bits, part in enumerate([rel_part] + from_peers([rel_part] * 3)):
                grad_rel = lax.dynamic_update_slice_in_dim(
                    grad_rel, part.astype(F32), (mine ^ bits) * (RELROWS // cycle), 0
                )
        else:
            grad_rel = lax.all_gather(rel_part, "seq", axis=0, tiled=True).astype(F32)
        vector_share = lax.dynamic_slice_in_dim(vector_sums, mine * share, share, 1)
        up_rows = hidden_units // D
        grad_b_up = lax.dynamic_slice_in_dim(
            vector_sums[9 : 9 + up_rows].reshape(-1), mine * (hidden_units // cycle), hidden_units // cycle, 0
        )
        return (
            output,
            grad_tokens,
            grads[0],
            vector_share[0],
            grads[1],
            vector_share[1],
            grads[2],
            vector_share[2],
            grad_w_out,
            vector_share[3],
            vector_share[4],
            vector_share[5],
            grad_w_up,
            grad_b_up,
            grad_w_down,
            vector_share[6],
            vector_share[7],
            vector_share[8],
            grad_rel,
        )

    if not square:
        (one,), carried = backward(0, 3, g_context, context, g_attn)
        (two,), (home, away) = backward(3, 3, g_context, *carried)
        packs = [
            lax.psum(lax.psum_scatter(v, "seq", scatter_dimension=0, tiled=True), "dp")
            for v in (one, two)
        ]
        got = lax.psum_scatter(away, "seq", scatter_dimension=0, tiled=True)
        return assembled(
            packs,
            g_resid_one + home + got.astype(F32),
            reduce_plain(product_left(hidden_low, g_up)),
            reduce_plain(product_left(act, g_down)),
        )

    at_y, at_x = mine // 2, mine % 2
    up_sum = added(product_left(hidden_low, g_up_own), up_got).reshape(2, 2, share, half)
    up_first, up_second = up_sum[:, :, : share // 2], up_sum[:, :, share // 2 :]
    up_first_got = swapped(picked(up_first, 1 - at_x, 1), "seq", 1)
    up_second_got = swapped(picked(up_second, 1 - at_y, 0), "seq", 2)
    g_context, up_sum = together(g_context, up_sum)
    one, carried = backward(0, 2, g_context, context, g_attn)

    act_got, g_down_got, up_first_got, up_second_got, one, carried = together(
        act_got, g_down_got, up_first_got, up_second_got, one, carried
    )
    one_got = swapped(one[1], "dp", 1)
    g_down_row = jnp.concatenate([g_down] + g_down_got, axis=0)
    act_row = jnp.concatenate([act_own] + act_got, axis=0)
    half_rows = quarter // 2
    act_mine = lax.dynamic_slice_in_dim(act_row, core * half_rows, half_rows, 1)
    act_other = lax.dynamic_slice_in_dim(act_row, (1 - core) * half_rows, half_rows, 1)
    down_got = swapped(product_left(act_other, g_down_row).astype(BF16), "dp", 1)
    down_share = added(product_left(act_mine, g_down_row), down_got)
    down_got = inward(down_share)
    up_first = added(picked(up_first, at_x, 1), up_first_got)
    up_second = added(picked(up_second, at_y, 0), up_second_got)
    up_first_got = swapped(picked(up_first, 1 - at_y, 0), "seq", 2)
    up_second_got = swapped(picked(up_second, 1 - at_x, 0), "seq", 1)
    one_share = added(one[0], one_got)
    one_got = scatter(one_share)
    carried, one_share, down_share, up_first, up_second = together(
        carried, one_share, down_share, up_first, up_second
    )
    two, carried = backward(2, 2, g_context, *carried)

    two, carried, one_got, down_got, up_first_got, up_second_got = together(
        two, carried, one_got, down_got, up_first_got, up_second_got
    )
    two_got = swapped(two[1], "dp", 1)
    down_share = added(down_share, down_got)
    down_got = across(down_share)
    up_share = jnp.concatenate(
        [
            added(picked(up_first, at_y, 0), up_first_got),
            added(picked(up_second, at_x, 0), up_second_got),
        ],
        axis=0,
    )
    up_got = inward(up_share)
    one_share = added(one_share[0], *one_got)
    one_got = inward(one_share)
    two_share = added(two[0], two_got)
    two_got = scatter(two_share)
    carried, one_share, two_share, down_share, up_share = together(
        carried, one_share, two_share, down_share, up_share
    )
    three, (home, away) = backward(4, 2, g_context, *carried)

    three, home, away, one_got, two_got, down_got, up_got = together(
        three, home, away, one_got, two_got, down_got, up_got
    )
    three_got = swapped(three[1], "dp", 1)
    away = away.reshape(3, rows, D)
    three_share = added(three[0], three_got)
    down_share = added(down_share, down_got)
    up_share = added(up_share, up_got)
    one_share = added(one_share, one_got)
    two_share = added(two_share[0], *two_got)
    three_share, down_share, up_share, one_share, two_share = together(
        three_share, down_share, up_share, one_share, two_share
    )
    three_got = scatter(three_share)
    down_got = outward(down_share)
    up_got = across(up_share)
    one_got = across(one_share)
    two_got = inward(two_share)
    home_got = from_peers([away[0], away[1], away[2]])

    three_share = added(three_share[0], *three_got)
    three_got = inward(three_share)
    up_share = added(up_share, up_got)
    up_got = outward(up_share)
    one_share = added(one_share, one_got)
    one_got = outward(one_share)
    two_share = added(two_share, two_got)
    two_got = across(two_share)

    three_share = added(three_share, three_got)
    three_got = across(three_share)
    two_share = added(two_share, two_got)
    two_got = outward(two_share)
    three_share = added(three_share, three_got)
    three_got = outward(three_share)

    grad_tokens = g_resid_one + functools.reduce(jnp.add, [v.astype(F32) for v in home_got], home)
    down_share = settled(down_share, down_got)
    up_share = settled(up_share, up_got)
    packs = [
        settled(one_share, one_got),
        settled(two_share, two_got),
        settled(three_share, three_got),
    ]
    return assembled(
        [both_cores(v[None], 0) for v in packs],
        grad_tokens,
        both_cores(up_share, 1).astype(F32),
        both_cores(down_share, 0).astype(F32),
    )


def solution(mesh):
    return jax.shard_map(
        local,
        mesh=mesh,
        in_specs=(
            P(("dp", "seq"), None),
            P(("dp", "seq"), None),
            P("dp", None),
        )
        + (P(),) * 17,
        out_specs=(
            P(("dp", "seq"), None),
            P(("dp", "seq"), None),
            P("seq", None),
            P("seq"),
            P("seq", None),
            P("seq"),
            P("seq", None),
            P("seq"),
            P("seq", None),
            P("seq"),
            P("seq"),
            P("seq"),
            P("seq", None),
            P("seq"),
            P("seq", None),
            P("seq"),
            P("seq"),
            P("seq"),
            P(),
        ),
        check_vma=False,
    )
```

```python
import functools
import math

import jax
import jax.numpy as jnp
from jax import lax
from jax.experimental import pallas as pl
from jax.experimental.pallas import tpu as pltpu
from jax.sharding import Mesh, PartitionSpec as P

D = 768
HEADS = 12
HEAD = 64
SPAN = 256
RELROWS = 512
BLOCK = 128
EXT = RELROWS + 2 * SPAN
PAIRS = HEADS // 2
VECTORS = 6
SCALE = 1.0 / math.sqrt(3 * HEAD)
F32 = jnp.float32
BF16 = jnp.bfloat16
ROLLED = BF16


def normalized(resid):
    center = resid - jnp.mean(resid, axis=-1, keepdims=True)
    inverse = lax.rsqrt(jnp.mean(center * center, axis=-1, keepdims=True) + 1e-07)
    return center * inverse, inverse


def normalized_back(grad, normal, inverse, gain):
    hat = grad * gain
    means = jnp.mean(hat, axis=-1, keepdims=True) + normal * jnp.mean(
        hat * normal, axis=-1, keepdims=True
    )
    total = lambda v: jnp.sum(v, axis=0, keepdims=True)
    return (hat - means) * inverse, total(grad * normal), total(grad)


def product(left, right):
    return jnp.dot(left, right, preferred_element_type=F32)


def product_left(left, right):
    return lax.dot_general(left, right, (((0,), (0,)), ((), ())), preferred_element_type=F32)


def product_right(left, right):
    return lax.dot_general(left, right, (((1,), (1,)), ((), ())), preferred_element_type=F32)


def segment_ids(lengths_row, positions):
    bounds = jnp.cumsum(lengths_row)
    return jnp.sum((positions[:, None] >= bounds[None, :]).astype(jnp.int32), axis=1)


def anti_identity():
    rows = lax.broadcasted_iota(jnp.int32, (BLOCK, BLOCK), 0)
    cols = lax.broadcasted_iota(jnp.int32, (BLOCK, BLOCK), 1)
    return (rows + cols == BLOCK - 1).astype(BF16)


def window_start(offset):
    return pl.multiple_of(jnp.clip(offset, 0, EXT - 2 * BLOCK), BLOCK)


def head_mask(head):
    lane = lax.broadcasted_iota(jnp.int32, (1, BLOCK), 1)
    return (lane >= head * HEAD) & (lane < (head + 1) * HEAD)


def band_roll(wide, shift):
    return pltpu.roll(wide, shift, 1, stride=1, stride_axis=0)


def by_head(pair):
    zero = jnp.zeros_like(pair)
    return jnp.concatenate([jnp.where(head_mask(head), pair, zero) for head in range(2)], axis=0)


def forward_kernel(
    parts, blocks, dist_ref, *refs
):
    part_refs, refs = refs[:parts], refs[parts:]
    wq_ref, wk_ref, wv_ref, bq_ref, bk_ref, bv_ref, ek_ref, eq_ref, bias_ref, *refs = refs
    ctx_ref, prob_ref, q_ref, k_ref, v_ref, tok_ref, score_ref = refs

    @pl.when(pl.program_id(0) == 0)
    def _():
        at = 0
        for ref in part_refs:
            tok_ref[at : at + ref.shape[0], :] = ref[...]
            at += ref.shape[0]

    both = product(tok_ref[...], jnp.concatenate([wk_ref[...], wv_ref[...]], axis=1))
    k_ref[...] = (both[:, :BLOCK] + bk_ref[...]).astype(BF16)
    v_ref[...] = (both[:, BLOCK:] + bv_ref[...]).astype(BF16)
    q = (product(tok_ref[:BLOCK, :], wq_ref[...]) + bq_ref[...]).astype(BF16)
    q_ref[...] = q
    q_heads = by_head(q)
    tops = [jnp.full((1, BLOCK), -jnp.inf, F32) for head in range(2)]
    for block in range(blocks):
        dist = dist_ref[block]
        rows = slice(block * BLOCK, (block + 1) * BLOCK)
        k_heads = by_head(k_ref[rows, :])
        window_c = ek_ref[pl.ds(window_start(384 - dist * BLOCK), 2 * BLOCK), :]
        window_p = eq_ref[pl.ds(window_start(384 + dist * BLOCK), 2 * BLOCK), :]
        c2p = product_right(q_heads, window_c)
        p2c = product_right(k_heads, window_p)
        direct = product_right(k_heads, q)
        for head in range(2):
            own = slice(head * BLOCK, (head + 1) * BLOCK)
            first = band_roll(c2p[own].astype(BF16), BLOCK + 1)[:, :BLOCK].T
            second = band_roll(p2c[own].astype(BF16), BLOCK + 1)[:, :BLOCK]
            score = (direct[own] + first.astype(F32) + second.astype(F32)) * SCALE + bias_ref[rows, :]
            score_ref[head, rows, :] = score
            tops[head] = jnp.maximum(tops[head], jnp.max(score, axis=0, keepdims=True))
    probs = []
    for head in range(2):
        weight = jnp.exp(score_ref[head] - tops[head])
        total = jnp.sum(weight, axis=0, keepdims=True)
        prob = (weight * (1.0 / total)).astype(BF16)
        prob_ref[head] = prob
        probs.append(prob)
    v = v_ref[...]
    zero = jnp.zeros_like(v)
    out = product_left(probs[0], jnp.where(head_mask(0), v, zero)) + product_left(
        probs[1], jnp.where(head_mask(1), v, zero)
    )
    ctx_ref[...] = out.astype(BF16)


def streamed(*arrays):
    return [pltpu.with_memory_space_constraint(array, pltpu.HBM) for array in arrays]


def once(*shape):
    return pl.BlockSpec(shape, lambda p, *_: (0,) * len(shape), pipeline_mode=pl.Buffered(1))


def attention_forward(dist, token_parts, weights, biases, ext_key, ext_query, bias):
    keys = sum(part.shape[0] for part in token_parts)
    blocks = keys // BLOCK
    pair = lambda rows: pl.BlockSpec((rows, BLOCK), lambda p, dist: (0, p))
    return pl.pallas_call(
        functools.partial(forward_kernel, len(token_parts), blocks),
        grid_spec=pltpu.PrefetchScalarGridSpec(
            num_scalar_prefetch=1,
            grid=(PAIRS,),
            in_specs=[once(*part.shape) for part in token_parts]
            + [pair(D)] * 3
            + [pair(1)] * 3
            + [pair(EXT), pair(EXT), once(keys, BLOCK)],
            out_specs=[
                pair(BLOCK),
                pl.BlockSpec((2, keys, BLOCK), lambda p, dist: (p, 0, 0)),
                pair(BLOCK),
                pair(keys),
                pair(keys),
                once(keys, D),
            ],
            scratch_shapes=[pltpu.VMEM((2, keys, BLOCK), F32)],
        ),
        out_shape=[
            jax.ShapeDtypeStruct((BLOCK, D), BF16),
            pltpu.HBM((HEADS, keys, BLOCK), BF16),
            pltpu.HBM((BLOCK, D), BF16),
            pltpu.HBM((keys, D), BF16),
            pltpu.HBM((keys, D), BF16),
            pltpu.HBM((keys, D), BF16),
        ],
        compiler_params=pltpu.CompilerParams(vmem_limit_bytes=(16 if keys <= 1024 else 40) * 2**20),
        name="attention_forward",
    )(dist, *token_parts, *streamed(*weights), *biases, *streamed(ext_key, ext_query), bias)


def fold_edges(acc_ref):
    head_sum = jnp.sum(acc_ref[:, 0:SPAN], axis=1, keepdims=True)
    tail_sum = jnp.sum(acc_ref[:, SPAN + RELROWS :], axis=1, keepdims=True)
    lane = lax.broadcasted_iota(jnp.int32, (BLOCK, RELROWS), 1)
    middle = acc_ref[:, SPAN : SPAN + RELROWS]
    middle = middle + jnp.where(lane == 0, head_sum, 0.0)
    return (middle + jnp.where(lane == RELROWS - 1, tail_sum, 0.0)).astype(BF16)


def flipped_lanes(array, flip):
    parts = array.shape[1] // BLOCK
    return jnp.concatenate(
        [
            product(array[:, part * BLOCK : (part + 1) * BLOCK], flip).astype(BF16)
            for part in reversed(range(parts))
        ],
        axis=1,
    )


def place(order_ref, share, core, shares, each):
    at = (core ^ order_ref[0]) * shares + (share ^ order_ref[1])
    return pl.multiple_of(at * each, 16)


def place_rows(order_ref, into_ref, value, cores, shares):
    each = value.shape[0] // (cores * shares)
    for share in range(shares):
        for core in range(cores):
            at = (share * cores + core) * each
            into_ref[pl.ds(place(order_ref, share, core, shares, each), each), :] = value[
                at : at + each
            ]


def store_pieces(refs, at, value, lanes):
    shares = refs[0].shape[0]
    each = value.shape[0] // (len(refs) * shares)
    for core, ref in enumerate(refs):
        for share in range(shares):
            start = (core * shares + share) * each
            ref[share, at : at + each, lanes] = value[start : start + each]


def backward_kernel(
    blocks,
    cores,
    first,
    last,
    dist_ref,
    order_ref,
    q_ref,
    k_ref,
    v_ref,
    ek_ref,
    eq_ref,
    prob_ref,
    gctx_ref,
    tok_ref,
    rel_ref,
    wq_ref,
    wk_ref,
    wv_ref,
    extra_one_ref,
    extra_two_ref,
    *refs,
):
    vec_refs, refs = refs[:VECTORS], refs[VECTORS:]
    pack_refs, refs = refs[:cores], refs[cores:]
    backward_body(
        blocks, first, last, dist_ref, order_ref, q_ref, k_ref, v_ref, ek_ref, eq_ref, prob_ref, gctx_ref,
        tok_ref, rel_ref, wq_ref, wk_ref, wv_ref, extra_one_ref, extra_two_ref, vec_refs, pack_refs, *refs
    )


def backward_body(
    blocks,
    first,
    last,
    dist_ref,
    order_ref,
    q_ref,
    k_ref,
    v_ref,
    ek_ref,
    eq_ref,
    prob_ref,
    gctx_ref,
    tok_ref,
    rel_ref,
    wq_ref,
    wk_ref,
    wv_ref,
    extra_one_ref,
    extra_two_ref,
    vec_refs,
    pack_refs,
    out_one_ref,
    out_two_ref,
    back_ref,
    gk_ref,
    gv_ref,
    acck_ref,
    accq_ref,
    tokt_ref,
    relt_ref,
    acc_tok_ref,
    acc_rel_ref,
    turn_ref,
):
    step = pl.program_id(0)
    cores, shares, half = len(pack_refs), pack_refs[0].shape[0], pack_refs[0].shape[2]
    share = D // cores // shares
    flip = anti_identity()

    @pl.when(step == 0)
    def _():
        place_rows(order_ref, tokt_ref, tok_ref[...].T, cores, shares)
        place_rows(order_ref, relt_ref, rel_ref[...].T, cores, shares)
        if first:
            acc_tok_ref[...] = jnp.zeros_like(acc_tok_ref)
            acc_rel_ref[...] = jnp.zeros_like(acc_rel_ref)
        else:
            acc_tok_ref[...] = extra_one_ref[...]
            acc_rel_ref[...] = extra_two_ref[...]

    acck_ref[...] = jnp.zeros_like(acck_ref)
    accq_ref[...] = jnp.zeros_like(accq_ref)
    g_heads = by_head(gctx_ref[...])
    first_rows = lax.broadcasted_iota(jnp.int32, (BLOCK, 1), 0) < HEAD
    first_lanes = head_mask(0)

    def turned_heads(array):
        turned = array.T
        zero = jnp.zeros_like(turned)
        return jnp.concatenate(
            [jnp.where(first_rows, turned, zero), jnp.where(first_rows, zero, turned)], axis=1
        )

    def of_heads(stacked):
        return jnp.where(first_lanes, stacked[:BLOCK], stacked[BLOCK:])

    q_back = product(flip, q_ref[...]).astype(BF16)
    q_turned = turned_heads(q_back)
    probs = jnp.concatenate([prob_ref[head] for head in range(2)], axis=1)
    g_prob = product_right(v_ref[...], g_heads)
    gv_ref[...] = product(probs, g_heads).astype(BF16)
    probs = probs.astype(F32)
    delta = jnp.sum(probs * g_prob, axis=0, keepdims=True)
    g_score = (probs * (g_prob - delta) * SCALE).astype(BF16)
    for head in range(2):
        lanes = slice(head * BLOCK, (head + 1) * BLOCK)
        back_ref[:, lanes] = product(g_score[:, lanes], flip).astype(BF16)
    g_query = jnp.zeros((2 * BLOCK, BLOCK), F32)
    pad = jnp.zeros((BLOCK, BLOCK), BF16)
    for block in range(blocks):
        rows = slice(block * BLOCK, (block + 1) * BLOCK)
        k_block = k_ref[rows, :]
        at = pl.ds(window_start(384 - dist_ref[block] * BLOCK), 2 * BLOCK)
        window_c = ek_ref[at, :]
        window_p = eq_ref[at, :]
        backs = [back_ref[rows, head * BLOCK : (head + 1) * BLOCK] for head in range(2)]
        turns = [back.T for back in backs]
        bands_c = [band_roll(jnp.concatenate([turn, pad], axis=1), 0) for turn in turns]
        bands_p = [band_roll(jnp.concatenate([back, pad], axis=1), 1) for back in backs]
        bands_c = jnp.concatenate(bands_c, axis=0)
        bands_p = jnp.concatenate(bands_p, axis=0)
        g_query = g_query + product(
            jnp.concatenate([jnp.concatenate(turns, axis=0), bands_c], axis=1),
            jnp.concatenate([k_block, window_c], axis=0),
        )
        g_key = product(
            jnp.concatenate([jnp.concatenate(backs, axis=0), bands_p], axis=1),
            jnp.concatenate([q_back, window_p], axis=0),
        )
        gk_ref[rows, :] = of_heads(g_key).astype(BF16)
        acck_ref[:, at] += product(q_turned, bands_c)
        accq_ref[:, at] += product(turned_heads(k_block), bands_p)

    g_query = product(flip, of_heads(g_query).astype(BF16)).astype(BF16)
    g_pos_key = flipped_lanes(fold_edges(acck_ref), flip)
    g_pos_query = fold_edges(accq_ref)
    g_key = gk_ref[...]
    g_value = gv_ref[...]
    lanes = pl.ds(pl.multiple_of(step * BLOCK, BLOCK), BLOCK)
    ones_tok = jnp.ones((16, tok_ref.shape[0]), BF16)
    ones_rel = jnp.ones((16, RELROWS), BF16)
    row = lax.broadcasted_iota(jnp.int32, (16, BLOCK), 0)
    vec = jnp.zeros((16, BLOCK), F32)
    for at, vec_ref in enumerate(vec_refs):
        vec = vec + jnp.where(row == 3 + at, vec_ref[...], 0.0)
    g_both = jnp.concatenate([g_key, g_value], axis=1)
    pos_both = jnp.concatenate([g_pos_key, g_pos_query], axis=0)
    from_tok = product(tokt_ref[...], g_both)
    from_rel = product_right(relt_ref[...], pos_both)
    from_own = product(tokt_ref[:, :BLOCK], g_query)
    sum_tok = product(ones_tok, g_both)
    sum_rel = product_right(ones_rel, pos_both)
    sum_own = product(ones_tok[:, :BLOCK], g_query)
    weights = [
        (from_own + from_rel[:, BLOCK:], sum_own + sum_rel[:, BLOCK:]),
        (from_tok[:, :BLOCK] + from_rel[:, :BLOCK], sum_tok[:, :BLOCK] + sum_rel[:, :BLOCK]),
        (from_tok[:, BLOCK:], sum_tok[:, BLOCK:]),
    ]
    for at, (weight, total) in enumerate(weights):
        store_pieces(pack_refs, at * share, weight.astype(BF16), lanes)
        vec = vec + jnp.where(row == at, total, 0.0)
    vec = vec.astype(BF16)
    for pack_ref in pack_refs:
        for part in range(shares):
            pack_ref[part, 3 * share : 3 * share + 16, lanes] = vec
    acc_tok_ref[...] += product_right(
        g_both,
        jnp.concatenate([wk_ref[...], wv_ref[...]], axis=1),
    )
    acc_tok_ref[0:BLOCK, :] += product_right(g_query, wq_ref[...])
    acc_rel_ref[...] += product(
        jnp.concatenate([wk_ref[...], wq_ref[...]], axis=1),
        pos_both,
    )

    @pl.when(step == pl.num_programs(0) - 1)
    def _():
        base = 3 * share + 16
        extra = None
        if last:
            out_one_ref[...] = acc_tok_ref[0:BLOCK, :]
            acc_tok_ref[0:BLOCK, :] = jnp.zeros((BLOCK, D), F32)
            for block in range(blocks - out_two_ref.shape[0] // BLOCK, blocks):
                rows = pl.ds(pl.multiple_of(dist_ref[blocks + block] * BLOCK, BLOCK), BLOCK)
                out_two_ref[rows, :] = acc_tok_ref[block * BLOCK : (block + 1) * BLOCK].astype(BF16)
            place_rows(order_ref, turn_ref, acc_rel_ref[...].T.astype(BF16), cores, shares)
            extra = turn_ref[...]
        else:
            out_one_ref[...] = acc_tok_ref[...]
            out_two_ref[...] = acc_rel_ref[...]
        if first:
            place_rows(order_ref, turn_ref, extra_one_ref[...].T, cores, shares)
            extra = product(turn_ref[...], extra_two_ref[...]).astype(BF16)
        if extra is not None:
            each = extra.shape[0] // (cores * shares)
            for part in range(D // half):
                columns = extra[:, part * half : (part + 1) * half]
                store_pieces(pack_refs, base + part * each, columns, slice(None))


def attention_backward(
    start, pairs, cores, shares, dist, order, query, key, value, ext_key, ext_query, prob, g_context,
    tokens_row, rel_table, w_query, w_key, w_value, extra_one, extra_two, vectors,
):
    keys = key.shape[0]
    blocks = keys // BLOCK
    first, last = start == 0, start + pairs == PAIRS
    share = D // cores // shares
    half = pairs * BLOCK
    rows_extra = D if first else RELROWS if last else 0
    pack = (shares, 3 * share + 16 + rows_extra // cores // shares * (D // half), half)
    pair = lambda rows: pl.BlockSpec((rows, BLOCK), lambda p, *_: (0, p + start))
    if first:
        extras = [once(BLOCK, D), once(BLOCK, D)]
        turn = (D, BLOCK)
    else:
        extras = [once(keys, D), once(D, RELROWS)]
        turn = (RELROWS, D)
    if last:
        outs = [((BLOCK, D), F32), ((shares * BLOCK, D), BF16)]
    else:
        outs = [((keys, D), F32), ((D, RELROWS), F32)]
    return pl.pallas_call(
        functools.partial(backward_kernel, blocks, cores, first, last),
        grid_spec=pltpu.PrefetchScalarGridSpec(
            num_scalar_prefetch=2,
            grid=(pairs,),
            in_specs=[
                pair(BLOCK),
                pair(keys),
                pair(keys),
                pair(EXT),
                pair(EXT),
                pl.BlockSpec((2, keys, BLOCK), lambda p, *_: (p + start, 0, 0)),
                pair(BLOCK),
                once(keys, D),
                once(RELROWS, D),
                pair(D),
                pair(D),
                pair(D),
            ]
            + extras
            + [pair(1)] * VECTORS,
            out_specs=[once(*pack)] * cores + [once(*shape) for shape, _ in outs],
            scratch_shapes=[
                pltpu.VMEM((keys, 2 * BLOCK), BF16),
                pltpu.VMEM((keys, BLOCK), BF16),
                pltpu.VMEM((keys, BLOCK), BF16),
                pltpu.VMEM((BLOCK, EXT), F32),
                pltpu.VMEM((BLOCK, EXT), F32),
                pltpu.VMEM((D, keys), BF16),
                pltpu.VMEM((D, RELROWS), BF16),
                pltpu.VMEM((keys, D), F32),
                pltpu.VMEM((D, RELROWS), F32),
                pltpu.VMEM(turn, BF16),
            ],
        ),
        out_shape=[jax.ShapeDtypeStruct(pack, BF16)] * cores
        + [jax.ShapeDtypeStruct(shape, dtype) for shape, dtype in outs],
        compiler_params=pltpu.CompilerParams(vmem_limit_bytes=(24 if keys <= 1024 else 58) * 2**20),
        name="attention_backward",
    )(
        dist, order, *streamed(query, key, value, ext_key, ext_query, prob), g_context,
        *streamed(tokens_row, rel_table, w_query, w_key, w_value), extra_one, extra_two, *vectors,
    )


def gelu_and_slope(x):
    below = 0.5 + 0.5 * lax.erf(x * math.sqrt(0.5))
    density = jnp.exp(-0.5 * x * x) * (1.0 / math.sqrt(2.0 * math.pi))
    return x * below, below + x * density


def feedforward_kernel(
    parts,
    order_ref,
    *refs,
):
    part_refs, refs = refs[:parts], refs[parts:]
    wup_ref, bup_ref, wdown_ref, down_own_ref, down_other_ref, up_own_ref, up_other_ref, *refs = refs
    hid_ref, gd_ref, hidt_ref, sums_ref = refs
    step = pl.program_id(0)
    shares = up_own_ref.shape[0]
    half = down_own_ref.shape[1]
    width = wup_ref.shape[1]

    @pl.when(step == 0)
    def _():
        for part in range(parts):
            rows = slice(part * BLOCK, (part + 1) * BLOCK)
            hid_ref[rows, :] = part_refs[part][:, :D]
            gd_ref[rows, :] = part_refs[part][:, D:]
        place_rows(order_ref, hidt_ref, hid_ref[...].T, 2, shares)

    lanes = pl.ds(pl.multiple_of(step * width, width), width)
    act, slope = gelu_and_slope(product(hid_ref[...], wup_ref[...]) + bup_ref[...])
    g_up = (product_right(gd_ref[...], wdown_ref[...]) * slope).astype(BF16)
    act_turned = act.astype(BF16).T
    for core, ref in enumerate((down_own_ref, down_other_ref)):
        columns = pl.ds(pl.multiple_of((order_ref[0] ^ core) * half, BLOCK), half)
        ref[lanes, :] = product(act_turned, gd_ref[:, columns]).astype(BF16)
    store_pieces((up_own_ref, up_other_ref), 0, product(hidt_ref[...], g_up).astype(BF16), lanes)
    sums_ref[:, lanes] = product(jnp.ones((16, hid_ref.shape[0]), BF16), g_up)

    @pl.when(step == pl.num_programs(0) - 1)
    def _():
        for core, ref in enumerate((down_own_ref, down_other_ref)):
            columns = pl.ds(pl.multiple_of((order_ref[0] ^ core) * half, BLOCK), half)
            ref[pl.ds(sums_ref.shape[1], 16), :] = sums_ref[:, columns].astype(BF16)


def feedforward_gradients(order, row_parts, w_up, b_up, w_down):
    shares = len(row_parts)
    tokens = shares * BLOCK
    units = w_up.shape[1] // shares
    width = 256
    steps = units // width
    down = (units + 16, D // 2)
    up = (shares, D // shares // 2, units)
    return pl.pallas_call(
        functools.partial(feedforward_kernel, shares),
        grid_spec=pltpu.PrefetchScalarGridSpec(
            num_scalar_prefetch=1,
            grid=(steps,),
            in_specs=[once(BLOCK, 2 * D)] * shares
            + [
                pl.BlockSpec((D, width), lambda p, order: (0, order[1] * steps + p)),
                pl.BlockSpec((1, width), lambda p, order: (0, order[1] * steps + p)),
                pl.BlockSpec((width, D), lambda p, order: (order[1] * steps + p, 0)),
            ],
            out_specs=[once(*down), once(*down), once(*up), once(*up)],
            scratch_shapes=[
                pltpu.VMEM((tokens, D), BF16),
                pltpu.VMEM((tokens, D), BF16),
                pltpu.VMEM((D, tokens), BF16),
                pltpu.VMEM((16, units), F32),
            ],
        ),
        out_shape=[jax.ShapeDtypeStruct(shape, BF16) for shape in (down, down, up, up)],
        compiler_params=pltpu.CompilerParams(vmem_limit_bytes=16 * 2**20),
        name="feedforward_gradients",
    )(order, *row_parts, *streamed(w_up), b_up, *streamed(w_down))


def swapped(array, axis, bits):
    return lax.ppermute(array, axis, [(i, i ^ bits) for i in range(lax.axis_size(axis))])


def from_peers(arrays):
    return [swapped(array, "seq", bits) for bits, array in enumerate(arrays, 1)]


def picked(array, index, axis):
    return lax.dynamic_index_in_dim(array, index, axis, keepdims=False)


def together(*arrays):
    return lax.optimization_barrier(arrays)


def added(*arrays):
    return functools.reduce(jnp.add, [array.astype(F32) for array in arrays]).astype(BF16)


def halves(pack):
    middle = pack.shape[1] // 32 * 16
    return pack[:, :middle], pack[:, middle:]


def in_row_order(pack, mine):
    return jnp.stack([picked(pack, mine ^ at, 0) for at in range(4)], axis=0)


def square_mesh():
    return lax.axis_size("seq") == 4 and lax.axis_size("z") == 4


def scatter(pack):
    return from_peers([pack[1], pack[2], pack[3]])


def inward(share):
    return lax.ppermute(share, "z", [(0, 1), (3, 2)])


def across(share):
    return lax.ppermute(share, "z", [(1, 2), (2, 1)])


def outward(share):
    return lax.ppermute(share, "z", [(1, 0), (2, 3)])


def settled(share, got):
    at_z = lax.axis_index("z")
    return jnp.where((at_z == 1) | (at_z == 2), share, got)


def core_index():
    return lax.axis_index("core")


def both_cores(share, axis):
    other = swapped(share, "core", 1)
    first = core_index() == 0
    return jnp.concatenate(
        [jnp.where(first, share, other), jnp.where(first, other, share)], axis=axis
    )


def reduce_plain(partial):
    share = lax.psum_scatter(partial.astype(BF16), "seq", scatter_dimension=0, tiled=True)
    return lax.psum(share, ("z", "core")).astype(F32)


def extended(table):
    return jnp.concatenate(
        [
            jnp.broadcast_to(table[:1], (SPAN, D)),
            table,
            jnp.broadcast_to(table[-1:], (SPAN, D)),
        ],
        axis=0,
    )


def local(
    tokens,
    cotangent,
    lengths,
    w_query,
    b_query,
    w_key,
    b_key,
    w_value,
    b_value,
    w_out,
    b_out,
    gain_one,
    shift_one,
    w_up,
    b_up,
    w_down,
    b_down,
    gain_two,
    shift_two,
    rel_table,
):
    rows = tokens.shape[0]
    cycle = lax.axis_size("seq")
    mine = lax.axis_index("seq")
    core = core_index()
    square = square_mesh()
    hidden_units = w_up.shape[1]
    share = D // cycle
    lengths_row = lengths[0]
    offsets = jnp.arange(rows, dtype=jnp.int32)
    query_pos = mine * rows + offsets
    query_seg = segment_ids(lengths_row, query_pos)
    valid = (query_pos < jnp.sum(lengths_row)).astype(F32)

    if square:
        token_parts = [tokens] + from_peers([tokens] * 3)
        ids = mine ^ jnp.arange(cycle, dtype=jnp.int32)
        order = jnp.stack([core, mine]).astype(jnp.int32)
        cores = 2
    else:
        token_parts = [tokens, lax.all_gather(tokens, "seq", axis=0, tiled=True)]
        ids = jnp.concatenate([mine[None], jnp.arange(cycle, dtype=jnp.int32)])
        order = jnp.zeros((2,), jnp.int32)
        cores = 1
    key_pos = (ids[:, None] * rows + offsets[None, :]).reshape(-1)
    key_seg = segment_ids(lengths_row, key_pos)
    bias = jnp.where(key_seg[:, None] == query_seg[None, :], 0.0, -1e30).astype(F32)
    if not square:
        again = jnp.concatenate(
            [jnp.zeros((rows,), jnp.bool_), jnp.repeat(ids[1:] == mine, rows)]
        )
        bias = jnp.where(again[:, None], -1e30, bias)
    dist = jnp.concatenate([mine - ids, ids]).astype(jnp.int32)

    places = jnp.arange(RELROWS, dtype=jnp.int32)
    turn = (places[:, None] + places[None, :] == RELROWS - 1).astype(BF16)
    rel_back = extended(product(turn, rel_table).astype(BF16))
    ext_key_back = (product(rel_back, w_key) + b_key).astype(BF16)
    ext_query_back = (product(rel_back, w_query) + b_query).astype(BF16)
    ext_query = (product(extended(rel_table), w_query) + b_query).astype(BF16)
    context, prob, query, key, value, tokens_row = attention_forward(
        dist,
        token_parts,
        [w_query, w_key, w_value],
        [v[None] for v in (b_query, b_key, b_value)],
        ext_key_back,
        ext_query_back,
        bias,
    )

    attn = product(context, w_out) + b_out
    normal_one, inverse_one = normalized(tokens.astype(F32) + attn)
    hidden_one = normal_one * gain_one + shift_one
    hidden_low = hidden_one.astype(BF16)
    act, slope = gelu_and_slope(product(hidden_low, w_up) + b_up)
    act = act.astype(BF16)
    down = product(act, w_down) + b_down
    normal_two, inverse_two = normalized(hidden_one + down)
    output = (normal_two * gain_two + shift_two).astype(BF16)
    g_out = cotangent.astype(F32) * valid[:, None]
    g_resid_two, grad_gain_two, grad_shift_two = normalized_back(
        g_out, normal_two, inverse_two, gain_two
    )
    g_down = g_resid_two.astype(BF16)
    if square:
        feed = jnp.concatenate([hidden_low, g_down], axis=1)
        row_parts = [feed] + from_peers([feed] * 3)
    grad_b_down = jnp.sum(g_down.astype(F32), axis=0, keepdims=True)
    g_up = (product_right(g_down, w_down) * slope).astype(BF16)
    g_hidden_one = g_resid_two + product_right(g_up, w_up)
    g_resid_one, grad_gain_one, grad_shift_one = normalized_back(
        g_hidden_one, normal_one, inverse_one, gain_one
    )
    g_attn = g_resid_one.astype(BF16)
    grad_b_out = jnp.sum(g_attn.astype(F32), axis=0, keepdims=True)
    g_context = product_right(g_attn, w_out).astype(BF16)
    vectors = [grad_b_out, grad_gain_one, grad_shift_one, grad_b_down, grad_gain_two, grad_shift_two]

    def backward(start, pairs, g_context, extra_one, extra_two):
        outs = attention_backward(
            start, pairs, cores, cycle, dist, order, query, key, value, ext_key_back, ext_query, prob,
            g_context, tokens_row, rel_table, w_query, w_key, w_value, extra_one, extra_two, vectors,
        )
        return outs[:cores], outs[cores:]

    def assembled(packs, grad_tokens, grad_w_up, grad_w_down, grad_b_up):
        piece = share // cores
        whole_rows = lambda v, at, each: v[:, at : at + each].reshape(cores * each, -1)
        grads = [
            jnp.concatenate([whole_rows(v, at * piece, piece) for v in packs], axis=1).astype(F32)
            for at in range(3)
        ]
        base = 3 * piece
        vector_sums = jnp.concatenate([v[0, base : base + 16] for v in packs], axis=1).astype(F32)
        base += 16

        def unpacked(v, each):
            parts = D // v.shape[2]
            return jnp.concatenate(
                [whole_rows(v, base + part * each, each) for part in range(parts)], axis=1
            )

        grad_w_out = unpacked(packs[0], piece).astype(F32)
        rel_part = unpacked(packs[-1], RELROWS // cycle // cores)
        if square:
            grad_rel = jnp.zeros((RELROWS, D), F32)
            for bits, part in enumerate([rel_part] + from_peers([rel_part] * 3)):
                grad_rel = lax.dynamic_update_slice_in_dim(
                    grad_rel, part.astype(F32), (mine ^ bits) * (RELROWS // cycle), 0
                )
        else:
            grad_rel = lax.all_gather(rel_part, "seq", axis=0, tiled=True).astype(F32)
        vector_share = lax.dynamic_slice_in_dim(vector_sums, mine * share, share, 1)
        return (
            output,
            grad_tokens,
            grads[0],
            vector_share[0],
            grads[1],
            vector_share[1],
            grads[2],
            vector_share[2],
            grad_w_out,
            vector_share[3],
            vector_share[4],
            vector_share[5],
            grad_w_up,
            grad_b_up,
            grad_w_down,
            vector_share[6],
            vector_share[7],
            vector_share[8],
            grad_rel,
        )

    if not square:
        (one,), carried = backward(0, 3, g_context, context, g_attn)
        (two,), (home, away) = backward(3, 3, g_context, *carried)
        packs = [
            lax.psum(lax.psum_scatter(v, "seq", scatter_dimension=0, tiled=True), ("z", "core"))
            for v in (one, two)
        ]
        got = lax.psum_scatter(away, "seq", scatter_dimension=0, tiled=True)
        return assembled(
            packs,
            g_resid_one + home + got.astype(F32),
            reduce_plain(product_left(hidden_low, g_up)),
            reduce_plain(product_left(act, g_down)),
            reduce_plain(jnp.sum(g_up.astype(F32), axis=0)),
        )

    one, carried = backward(0, 3, g_context, context, g_attn)

    row_parts, one, carried = together(row_parts, one, carried)
    one_got = swapped(one[1], "core", 1)
    down_own, down_other, up_own, up_other = feedforward_gradients(
        order, row_parts, w_up, b_up[None], w_down
    )

    one_got, down_own, down_other, up_own, up_other = together(
        one_got, down_own, down_other, up_own, up_other
    )
    down_got = swapped(down_other, "core", 1)
    up_got = swapped(up_other, "core", 1)
    one_share = added(one[0], one_got)
    down_share = added(down_own, down_got)
    up_share = added(up_own, up_got)
    down_got = inward(down_share)
    up_got = inward(up_share)
    one_first, one_second = halves(one_share)
    one_first_got = swapped(one_first[1::2], "seq", 1)
    one_second_got = swapped(one_second[2:], "seq", 2)
    g_context, down_share, up_share, one_share = together(g_context, down_share, up_share, one_share)
    two, (home, away) = backward(3, 3, g_context, *carried)

    two, home, away, one_first_got, one_second_got, down_got = together(
        two, home, away, one_first_got, one_second_got, down_got
    )
    two_got = swapped(two[1], "core", 1)
    one_first = added(one_first[0::2], one_first_got)
    one_second = added(one_second[:2], one_second_got)
    down_share = added(down_share, down_got)
    down_got = across(down_share)
    one_first_got = swapped(one_first[1], "seq", 2)
    one_second_got = swapped(one_second[1], "seq", 1)

    two_got, up_got, one_first, one_second, down_share, away = together(
        two_got, up_got, one_first, one_second, down_share, away
    )
    two_share = added(two[0], two_got)
    up_share = added(up_share, up_got)
    two_first, two_second = halves(two_share)
    two_first_got = swapped(two_first[1::2], "seq", 1)
    two_second_got = swapped(two_second[2:], "seq", 2)

    one_first_got, one_second_got, two_first, two_second, up_share = together(
        one_first_got, one_second_got, two_first, two_second, up_share
    )
    one_share = jnp.concatenate(
        [added(one_first[0], one_first_got), added(one_second[0], one_second_got)], axis=0
    )
    one_got = inward(one_share)

    two_first_got, two_second_got, one_share, down_got = together(
        two_first_got, two_second_got, one_share, down_got
    )
    two_first = added(two_first[0::2], two_first_got)
    two_second = added(two_second[:2], two_second_got)
    two_first_got = swapped(two_first[1], "seq", 2)
    two_second_got = swapped(two_second[1], "seq", 1)
    down_share = added(down_share, down_got)
    down_got = outward(down_share)
    up_got = across(up_share)
    away = lax.psum_scatter(away, "seq", scatter_dimension=0, tiled=True)

    one_got, two_first_got, two_second_got, down_share = together(
        one_got, two_first_got, two_second_got, down_share
    )
    two_share = jnp.concatenate(
        [added(two_first[0], two_first_got), added(two_second[0], two_second_got)], axis=0
    )
    two_got = inward(two_share)
    one_share = added(one_share, one_got)
    one_got = across(one_share)

    one_got, two_got, up_got = together(one_got, two_got, up_got)
    two_share = added(two_share, two_got)
    two_got = across(two_share)
    up_share = added(up_share, up_got)
    up_got = outward(up_share)
    one_share = added(one_share, one_got)
    one_got = outward(one_share)

    two_got, one_share, up_got, down_got = together(two_got, one_share, up_got, down_got)
    two_share = added(two_share, two_got)
    two_got = outward(two_share)
    up_share = settled(up_share, up_got)
    up_got = scatter(up_share)
    down_share = both_cores(settled(down_share, down_got), 1)

    one_got, away, two_got = together(one_got, away, two_got)
    grad_tokens = g_resid_one + home + away.astype(F32)
    packs = [both_cores(settled(v, got)[None], 0) for v, got in ((one_share, one_got), (two_share, two_got))]
    up_share = jnp.stack([up_share[0]] + up_got, axis=0)
    up_share = both_cores(up_share, 1).reshape(4, share, -1)
    grad_w_up = jnp.zeros((share, hidden_units), F32)
    units = hidden_units // 4
    for bits in range(4):
        grad_w_up = lax.dynamic_update_slice_in_dim(
            grad_w_up, up_share[bits].astype(F32), (mine ^ bits) * units, 1
        )
    return assembled(
        packs,
        grad_tokens,
        grad_w_up,
        down_share[:units].astype(F32),
        down_share[units].astype(F32),
    )


def solution(mesh):
    lines, cycle = mesh.devices.shape
    chips = Mesh(mesh.devices.reshape(lines // 2, 2, cycle), ("z", "core", "seq"))
    return jax.shard_map(
        local,
        mesh=chips,
        in_specs=(
            P(("z", "core", "seq"), None),
            P(("z", "core", "seq"), None),
            P(("z", "core"), None),
        )
        + (P(),) * 17,
        out_specs=(
            P(("z", "core", "seq"), None),
            P(("z", "core", "seq"), None),
            P("seq", None),
            P("seq"),
            P("seq", None),
            P("seq"),
            P("seq", None),
            P("seq"),
            P("seq", None),
            P("seq"),
            P("seq"),
            P("seq"),
            P("seq", None),
            P("seq"),
            P("seq", None),
            P("seq"),
            P("seq"),
            P("seq"),
            P(),
        ),
        check_vma=False,
    )
```

```python
import functools
import math

import jax
import jax.numpy as jnp
from jax import lax
from jax.experimental import pallas as pl
from jax.experimental.pallas import tpu as pltpu
from jax.sharding import Mesh, PartitionSpec as P

D = 768
HEADS = 12
HEAD = 64
SPAN = 256
RELROWS = 512
BLOCK = 128
EXT = RELROWS + 2 * SPAN
PAIRS = HEADS // 2
VECTORS = 2
LATER = 3
DOCS = 4
SCALE = 1.0 / math.sqrt(3 * HEAD)
F32 = jnp.float32
BF16 = jnp.bfloat16
ROLLED = BF16


def normalized(resid):
    center = resid - jnp.mean(resid, axis=-1, keepdims=True)
    inverse = lax.rsqrt(jnp.mean(center * center, axis=-1, keepdims=True) + 1e-07)
    return center * inverse, inverse


def normalized_back(grad, normal, inverse, gain):
    hat = grad * gain
    means = jnp.mean(hat, axis=-1, keepdims=True) + normal * jnp.mean(
        hat * normal, axis=-1, keepdims=True
    )
    total = lambda v: jnp.sum(v, axis=0, keepdims=True)
    return (hat - means) * inverse, total(grad * normal), total(grad)


def product(left, right):
    return jnp.dot(left, right, preferred_element_type=F32)


def product_left(left, right):
    return lax.dot_general(left, right, (((0,), (0,)), ((), ())), preferred_element_type=F32)


def product_right(left, right):
    return lax.dot_general(left, right, (((1,), (1,)), ((), ())), preferred_element_type=F32)


def segment_of(position, place_ref, at):
    passed, bound = jnp.zeros(position.shape, jnp.int32), 0
    for document in range(DOCS):
        bound = bound + place_ref[at + document]
        passed = passed + (position >= bound).astype(jnp.int32)
    return passed


def anti_identity():
    rows = lax.broadcasted_iota(jnp.int32, (BLOCK, BLOCK), 0)
    cols = lax.broadcasted_iota(jnp.int32, (BLOCK, BLOCK), 1)
    return (rows + cols == BLOCK - 1).astype(BF16)


def extend(ext_ref, table_ref):
    ext_ref[SPAN : SPAN + RELROWS, :] = table_ref[...]
    ext_ref[0:SPAN, :] = jnp.broadcast_to(table_ref[0:1, :], (SPAN, BLOCK))
    last = table_ref[RELROWS - 1 : RELROWS, :]
    ext_ref[SPAN + RELROWS :, :] = jnp.broadcast_to(last, (SPAN, BLOCK))


def window_start(offset):
    return pl.multiple_of(jnp.clip(offset, 0, EXT - 2 * BLOCK), BLOCK)


def head_mask(head):
    lane = lax.broadcasted_iota(jnp.int32, (1, BLOCK), 1)
    return (lane >= head * HEAD) & (lane < (head + 1) * HEAD)


def band_roll(wide, shift):
    return pltpu.roll(wide, shift, 1, stride=1, stride_axis=0)


def by_head(pair):
    zero = jnp.zeros_like(pair)
    return jnp.concatenate([jnp.where(head_mask(head), pair, zero) for head in range(2)], axis=0)


def forward_kernel(
    parts, blocks, dist_ref, *refs
):
    part_refs, refs = refs[:parts], refs[parts:]
    wq_ref, wk_ref, wv_ref, bq_ref, bk_ref, bv_ref, pk_ref, pq_ref, *refs = refs
    later, refs = refs[:LATER], refs[LATER:]
    ctx_ref, prob_ref, q_ref, k_ref, v_ref, tok_ref, *refs = refs
    held, refs = refs[:LATER], refs[LATER:]
    score_ref, ek_ref, eq_ref, bias_ref, sems = refs
    copies = [
        pltpu.make_async_copy(later[at], held[at], sems.at[at]) for at in range(LATER)
    ]

    @pl.when(pl.program_id(0) == 0)
    def _():
        for copy in copies:
            copy.start()

    @pl.when(pl.program_id(0) == pl.num_programs(0) - 1)
    def _():
        for copy in copies:
            copy.wait()

    extend(ek_ref, pk_ref)
    extend(eq_ref, pq_ref)

    @pl.when(pl.program_id(0) == 0)
    def _():
        at = 0
        for ref in part_refs:
            tok_ref[at : at + ref.shape[0], :] = ref[...]
            at += ref.shape[0]
        mine = dist_ref[blocks]
        lane = lax.broadcasted_iota(jnp.int32, (1, BLOCK), 1)
        line = lax.broadcasted_iota(jnp.int32, (BLOCK, 1), 0)
        query_segment = segment_of(mine * BLOCK + lane, dist_ref, 2 * blocks)
        for block in range(blocks):
            home = dist_ref[blocks + block]
            allowed = segment_of(home * BLOCK + line, dist_ref, 2 * blocks) == query_segment
            if block > 0:
                allowed = jnp.logical_and(allowed, home != mine)
            rows = slice(block * BLOCK, (block + 1) * BLOCK)
            bias_ref[rows, :] = jnp.where(allowed, 0.0, -1e30)

    both = product(tok_ref[...], jnp.concatenate([wk_ref[...], wv_ref[...]], axis=1))
    k_ref[...] = (both[:, :BLOCK] + bk_ref[...]).astype(BF16)
    v_ref[...] = (both[:, BLOCK:] + bv_ref[...]).astype(BF16)
    q = (product(tok_ref[:BLOCK, :], wq_ref[...]) + bq_ref[...]).astype(BF16)
    q_ref[...] = q
    q_heads = by_head(q)
    tops = [jnp.full((1, BLOCK), -jnp.inf, F32) for head in range(2)]
    for block in range(blocks):
        dist = dist_ref[block]
        rows = slice(block * BLOCK, (block + 1) * BLOCK)
        k_heads = by_head(k_ref[rows, :])
        window_c = ek_ref[pl.ds(window_start(384 - dist * BLOCK), 2 * BLOCK), :]
        window_p = eq_ref[pl.ds(window_start(384 + dist * BLOCK), 2 * BLOCK), :]
        c2p = product_right(q_heads, window_c)
        p2c = product_right(k_heads, window_p)
        direct = product_right(k_heads, q)
        for head in range(2):
            own = slice(head * BLOCK, (head + 1) * BLOCK)
            first = band_roll(c2p[own].astype(BF16), BLOCK + 1)[:, :BLOCK].T
            second = band_roll(p2c[own].astype(BF16), BLOCK + 1)[:, :BLOCK]
            score = (direct[own] + first.astype(F32) + second.astype(F32)) * SCALE + bias_ref[rows, :]
            score_ref[head, rows, :] = score
            tops[head] = jnp.maximum(tops[head], jnp.max(score, axis=0, keepdims=True))
    probs = []
    for head in range(2):
        weight = jnp.exp(score_ref[head] - tops[head])
        total = jnp.sum(weight, axis=0, keepdims=True)
        prob = (weight * (1.0 / total)).astype(BF16)
        prob_ref[head] = prob
        probs.append(prob)
    v = v_ref[...]
    zero = jnp.zeros_like(v)
    out = product_left(probs[0], jnp.where(head_mask(0), v, zero)) + product_left(
        probs[1], jnp.where(head_mask(1), v, zero)
    )
    ctx_ref[...] = out.astype(BF16)


def streamed(*arrays):
    return [pltpu.with_memory_space_constraint(array, pltpu.HBM) for array in arrays]


def once(*shape):
    return pl.BlockSpec(shape, lambda p, *_: (0,) * len(shape), pipeline_mode=pl.Buffered(1))


def attention_forward(dist, token_parts, weights, biases, pos_key, pos_query, later):
    keys = sum(part.shape[0] for part in token_parts)
    blocks = keys // BLOCK
    pair = lambda rows: pl.BlockSpec((rows, BLOCK), lambda p, dist: (0, p))
    return pl.pallas_call(
        functools.partial(forward_kernel, len(token_parts), blocks),
        grid_spec=pltpu.PrefetchScalarGridSpec(
            num_scalar_prefetch=1,
            grid=(PAIRS,),
            in_specs=[once(*part.shape) for part in token_parts]
            + [pair(D)] * 3
            + [pair(1)] * 3
            + [pair(RELROWS), pair(RELROWS)]
            + [pl.BlockSpec(memory_space=pl.ANY)] * LATER,
            out_specs=[
                pair(BLOCK),
                pl.BlockSpec((2, keys, BLOCK), lambda p, dist: (p, 0, 0)),
                pair(BLOCK),
                pair(keys),
                pair(keys),
                once(keys, D),
            ]
            + [pl.BlockSpec(memory_space=pl.ANY)] * LATER,
            scratch_shapes=[
                pltpu.VMEM((2, keys, BLOCK), F32),
                pltpu.VMEM((EXT, BLOCK), BF16),
                pltpu.VMEM((EXT, BLOCK), BF16),
                pltpu.VMEM((keys, BLOCK), F32),
                pltpu.SemaphoreType.DMA((LATER,)),
            ],
        ),
        out_shape=[
            jax.ShapeDtypeStruct((BLOCK, D), BF16),
            pltpu.HBM((HEADS, keys, BLOCK), BF16),
            pltpu.HBM((BLOCK, D), BF16),
            pltpu.HBM((keys, D), BF16),
            pltpu.HBM((keys, D), BF16),
            pltpu.HBM((keys, D), BF16),
        ]
        + [pltpu.VMEM(array.shape, array.dtype) for array in later],
        compiler_params=pltpu.CompilerParams(vmem_limit_bytes=(16 if keys <= 1024 else 40) * 2**20),
        name="attention_forward",
    )(dist, *token_parts, *streamed(*weights), *biases, *streamed(pos_key, pos_query), *streamed(*later))


def fold_edges(acc_ref):
    head_sum = jnp.sum(acc_ref[:, 0:SPAN], axis=1, keepdims=True)
    tail_sum = jnp.sum(acc_ref[:, SPAN + RELROWS :], axis=1, keepdims=True)
    lane = lax.broadcasted_iota(jnp.int32, (BLOCK, RELROWS), 1)
    middle = acc_ref[:, SPAN : SPAN + RELROWS]
    middle = middle + jnp.where(lane == 0, head_sum, 0.0)
    return (middle + jnp.where(lane == RELROWS - 1, tail_sum, 0.0)).astype(BF16)


def flipped_lanes(array, flip):
    parts = array.shape[1] // BLOCK
    return jnp.concatenate(
        [
            product(array[:, part * BLOCK : (part + 1) * BLOCK], flip).astype(BF16)
            for part in reversed(range(parts))
        ],
        axis=1,
    )


def place(order_ref, share, core, shares, each):
    at = (core ^ order_ref[0]) * shares + (share ^ order_ref[1])
    return pl.multiple_of(at * each, 16)


def place_rows(order_ref, into_ref, value, cores, shares):
    each = value.shape[0] // (cores * shares)
    for share in range(shares):
        for core in range(cores):
            at = (share * cores + core) * each
            into_ref[pl.ds(place(order_ref, share, core, shares, each), each), :] = value[
                at : at + each
            ]


def store_pieces(refs, at, value, lanes):
    shares = refs[0].shape[0]
    each = value.shape[0] // (len(refs) * shares)
    for core, ref in enumerate(refs):
        for share in range(shares):
            start = (core * shares + share) * each
            ref[share, at : at + each, lanes] = value[start : start + each]


def backward_kernel(
    blocks,
    cores,
    first,
    last,
    dist_ref,
    order_ref,
    q_ref,
    k_ref,
    v_ref,
    pk_ref,
    pq_ref,
    prob_ref,
    gctx_ref,
    tok_ref,
    rel_ref,
    wq_ref,
    wk_ref,
    wv_ref,
    extra_one_ref,
    extra_two_ref,
    *refs,
):
    vec_refs, refs = refs[:VECTORS], refs[VECTORS:]
    pack_refs, refs = refs[:cores], refs[cores:]
    backward_body(
        blocks, first, last, dist_ref, order_ref, q_ref, k_ref, v_ref, pk_ref, pq_ref, prob_ref, gctx_ref,
        tok_ref, rel_ref, wq_ref, wk_ref, wv_ref, extra_one_ref, extra_two_ref, vec_refs, pack_refs, *refs
    )


def backward_body(
    blocks,
    first,
    last,
    dist_ref,
    order_ref,
    q_ref,
    k_ref,
    v_ref,
    pk_ref,
    pq_ref,
    prob_ref,
    gctx_ref,
    tok_ref,
    rel_ref,
    wq_ref,
    wk_ref,
    wv_ref,
    extra_one_ref,
    extra_two_ref,
    vec_refs,
    pack_refs,
    out_one_ref,
    out_two_ref,
    back_ref,
    gk_ref,
    gv_ref,
    acck_ref,
    accq_ref,
    tokt_ref,
    relt_ref,
    acc_tok_ref,
    acc_rel_ref,
    turn_ref,
    ek_ref,
    eq_ref,
):
    step = pl.program_id(0)
    extend(ek_ref, pk_ref)
    extend(eq_ref, pq_ref)
    cores, shares, half = len(pack_refs), pack_refs[0].shape[0], pack_refs[0].shape[2]
    share = D // cores // shares
    flip = anti_identity()

    @pl.when(step == 0)
    def _():
        place_rows(order_ref, tokt_ref, tok_ref[...].T, cores, shares)
        place_rows(order_ref, relt_ref, rel_ref[...].T, cores, shares)
        if first:
            acc_tok_ref[...] = jnp.zeros_like(acc_tok_ref)
            acc_rel_ref[...] = jnp.zeros_like(acc_rel_ref)
        else:
            acc_tok_ref[...] = extra_one_ref[...]
            acc_rel_ref[...] = extra_two_ref[...]

    acck_ref[...] = jnp.zeros_like(acck_ref)
    accq_ref[...] = jnp.zeros_like(accq_ref)
    g_heads = by_head(gctx_ref[...])
    first_rows = lax.broadcasted_iota(jnp.int32, (BLOCK, 1), 0) < HEAD
    first_lanes = head_mask(0)

    def turned_heads(array):
        turned = array.T
        zero = jnp.zeros_like(turned)
        return jnp.concatenate(
            [jnp.where(first_rows, turned, zero), jnp.where(first_rows, zero, turned)], axis=1
        )

    def of_heads(stacked):
        return jnp.where(first_lanes, stacked[:BLOCK], stacked[BLOCK:])

    q_back = product(flip, q_ref[...]).astype(BF16)
    q_turned = turned_heads(q_back)
    probs = jnp.concatenate([prob_ref[head] for head in range(2)], axis=1)
    g_prob = product_right(v_ref[...], g_heads)
    gv_ref[...] = product(probs, g_heads).astype(BF16)
    probs = probs.astype(F32)
    delta = jnp.sum(probs * g_prob, axis=0, keepdims=True)
    g_score = (probs * (g_prob - delta) * SCALE).astype(BF16)
    for head in range(2):
        lanes = slice(head * BLOCK, (head + 1) * BLOCK)
        back_ref[:, lanes] = product(g_score[:, lanes], flip).astype(BF16)
    g_query = jnp.zeros((2 * BLOCK, BLOCK), F32)
    pad = jnp.zeros((BLOCK, BLOCK), BF16)
    for block in range(blocks):
        rows = slice(block * BLOCK, (block + 1) * BLOCK)
        k_block = k_ref[rows, :]
        at = pl.ds(window_start(384 - dist_ref[block] * BLOCK), 2 * BLOCK)
        window_c = ek_ref[at, :]
        window_p = eq_ref[at, :]
        backs = [back_ref[rows, head * BLOCK : (head + 1) * BLOCK] for head in range(2)]
        turns = [back.T for back in backs]
        bands_c = [band_roll(jnp.concatenate([turn, pad], axis=1), 0) for turn in turns]
        bands_p = [band_roll(jnp.concatenate([back, pad], axis=1), 1) for back in backs]
        bands_c = jnp.concatenate(bands_c, axis=0)
        bands_p = jnp.concatenate(bands_p, axis=0)
        g_query = g_query + product(
            jnp.concatenate([jnp.concatenate(turns, axis=0), bands_c], axis=1),
            jnp.concatenate([k_block, window_c], axis=0),
        )
        g_key = product(
            jnp.concatenate([jnp.concatenate(backs, axis=0), bands_p], axis=1),
            jnp.concatenate([q_back, window_p], axis=0),
        )
        gk_ref[rows, :] = of_heads(g_key).astype(BF16)
        acck_ref[:, at] += product(q_turned, bands_c)
        accq_ref[:, at] += product(turned_heads(k_block), bands_p)

    g_query = product(flip, of_heads(g_query).astype(BF16)).astype(BF16)
    g_pos_key = flipped_lanes(fold_edges(acck_ref), flip)
    g_pos_query = fold_edges(accq_ref)
    g_key = gk_ref[...]
    g_value = gv_ref[...]
    lanes = pl.ds(pl.multiple_of(step * BLOCK, BLOCK), BLOCK)
    ones_tok = jnp.ones((16, tok_ref.shape[0]), BF16)
    ones_rel = jnp.ones((16, RELROWS), BF16)
    row = lax.broadcasted_iota(jnp.int32, (16, BLOCK), 0)
    vec = jnp.zeros((16, BLOCK), F32)
    for at, vec_ref in enumerate(vec_refs):
        for part in range(3):
            vec = vec + jnp.where(row == 3 + 3 * at + part, vec_ref[part : part + 1, :], 0.0)
    g_both = jnp.concatenate([g_key, g_value], axis=1)
    pos_both = jnp.concatenate([g_pos_key, g_pos_query], axis=0)
    from_tok = product(tokt_ref[...], g_both)
    from_rel = product_right(relt_ref[...], pos_both)
    from_own = product(tokt_ref[:, :BLOCK], g_query)
    sum_tok = product(ones_tok, g_both)
    sum_rel = product_right(ones_rel, pos_both)
    sum_own = product(ones_tok[:, :BLOCK], g_query)
    weights = [
        (from_own + from_rel[:, BLOCK:], sum_own + sum_rel[:, BLOCK:]),
        (from_tok[:, :BLOCK] + from_rel[:, :BLOCK], sum_tok[:, :BLOCK] + sum_rel[:, :BLOCK]),
        (from_tok[:, BLOCK:], sum_tok[:, BLOCK:]),
    ]
    for at, (weight, total) in enumerate(weights):
        store_pieces(pack_refs, at * share, weight.astype(BF16), lanes)
        vec = vec + jnp.where(row == at, total, 0.0)
    vec = vec.astype(BF16)
    for pack_ref in pack_refs:
        for part in range(shares):
            pack_ref[part, 3 * share : 3 * share + 16, lanes] = vec
    acc_tok_ref[...] += product_right(
        g_both,
        jnp.concatenate([wk_ref[...], wv_ref[...]], axis=1),
    )
    acc_tok_ref[0:BLOCK, :] += product_right(g_query, wq_ref[...])
    acc_rel_ref[...] += product(
        jnp.concatenate([wk_ref[...], wq_ref[...]], axis=1),
        pos_both,
    )

    @pl.when(step == pl.num_programs(0) - 1)
    def _():
        base = 3 * share + 16
        extra = None
        if last:
            out_one_ref[...] = acc_tok_ref[0:BLOCK, :]
            for block in range(1, blocks):
                out_two_ref[block - 1] = acc_tok_ref[block * BLOCK : (block + 1) * BLOCK].astype(BF16)
            place_rows(order_ref, turn_ref, acc_rel_ref[...].T.astype(BF16), cores, shares)
            extra = turn_ref[...]
        else:
            out_one_ref[...] = acc_tok_ref[...]
            out_two_ref[...] = acc_rel_ref[...]
        if first:
            place_rows(order_ref, turn_ref, extra_one_ref[...].T, cores, shares)
            extra = product(turn_ref[...], extra_two_ref[...]).astype(BF16)
        if extra is not None:
            each = extra.shape[0] // (cores * shares)
            for part in range(D // half):
                columns = extra[:, part * half : (part + 1) * half]
                store_pieces(pack_refs, base + part * each, columns, slice(None))


def attention_backward(
    start, pairs, cores, shares, dist, order, query, key, value, pos_key, pos_query, prob, g_context,
    tokens_row, rel_table, w_query, w_key, w_value, extra_one, extra_two, vectors,
):
    keys = key.shape[0]
    blocks = keys // BLOCK
    first, last = start == 0, start + pairs == PAIRS
    share = D // cores // shares
    half = pairs * BLOCK
    rows_extra = D if first else RELROWS if last else 0
    pack = (shares, 3 * share + 16 + rows_extra // cores // shares * (D // half), half)
    pair = lambda rows: pl.BlockSpec((rows, BLOCK), lambda p, *_: (0, p + start))
    if first:
        extras = [once(BLOCK, D), once(BLOCK, D)]
        turn = (D, BLOCK)
    else:
        extras = [once(keys, D), once(D, RELROWS)]
        turn = (RELROWS, D)
    if last:
        outs = [((BLOCK, D), F32), ((blocks - 1, BLOCK, D), BF16)]
    else:
        outs = [((keys, D), F32), ((D, RELROWS), F32)]
    return pl.pallas_call(
        functools.partial(backward_kernel, blocks, cores, first, last),
        grid_spec=pltpu.PrefetchScalarGridSpec(
            num_scalar_prefetch=2,
            grid=(pairs,),
            in_specs=[
                pair(BLOCK),
                pair(keys),
                pair(keys),
                pair(RELROWS),
                pair(RELROWS),
                pl.BlockSpec((2, keys, BLOCK), lambda p, *_: (p + start, 0, 0)),
                pair(BLOCK),
                once(keys, D),
                once(RELROWS, D),
                pair(D),
                pair(D),
                pair(D),
            ]
            + extras
            + [pair(8)] * VECTORS,
            out_specs=[once(*pack)] * cores + [once(*shape) for shape, _ in outs],
            scratch_shapes=[
                pltpu.VMEM((keys, 2 * BLOCK), BF16),
                pltpu.VMEM((keys, BLOCK), BF16),
                pltpu.VMEM((keys, BLOCK), BF16),
                pltpu.VMEM((BLOCK, EXT), F32),
                pltpu.VMEM((BLOCK, EXT), F32),
                pltpu.VMEM((D, keys), BF16),
                pltpu.VMEM((D, RELROWS), BF16),
                pltpu.VMEM((keys, D), F32),
                pltpu.VMEM((D, RELROWS), F32),
                pltpu.VMEM(turn, BF16),
                pltpu.VMEM((EXT, BLOCK), BF16),
                pltpu.VMEM((EXT, BLOCK), BF16),
            ],
        ),
        out_shape=[jax.ShapeDtypeStruct(pack, BF16)] * cores
        + [jax.ShapeDtypeStruct(shape, dtype) for shape, dtype in outs],
        compiler_params=pltpu.CompilerParams(vmem_limit_bytes=(24 if keys <= 1024 else 58) * 2**20),
        name="attention_backward",
    )(
        dist, order, *streamed(query, key, value, pos_key, pos_query, prob), g_context,
        *streamed(tokens_row, rel_table, w_query, w_key, w_value), extra_one, extra_two, *vectors,
    )


def column_sum(array):
    return jnp.sum(array, axis=0, keepdims=True)


def middle_forward_kernel(
    blocks,
    place_ref,
    ctx_ref,
    tok_ref,
    cot_ref,
    wout_ref,
    bout_ref,
    gain_one_ref,
    shift_one_ref,
    bdown_ref,
    gain_two_ref,
    shift_two_ref,
    wup_ref,
    bup_ref,
    wdown_ref,
    output_ref,
    feed_ref,
    normal_ref,
    inverse_ref,
    resid_ref,
    slope_ref,
    sums_ref,
    hidden_ref,
    down_ref,
):
    step = pl.program_id(0)

    @pl.when(step == 0)
    def _():
        attn = product(ctx_ref[...], wout_ref[...]) + bout_ref[...]
        normal, inverse = normalized(tok_ref[...].astype(F32) + attn)
        normal_ref[...] = normal
        inverse_ref[...] = jnp.broadcast_to(inverse, inverse_ref.shape)
        hidden = normal * gain_one_ref[...] + shift_one_ref[...]
        hidden_ref[...] = hidden
        feed_ref[:, :D] = hidden.astype(BF16)
        down_ref[...] = jnp.zeros_like(down_ref)

    width = bup_ref.shape[1]
    units = pl.ds(pl.multiple_of(step * width, width), width)
    act, slope = gelu_and_slope(product(feed_ref[:, :D], wup_ref[:, units]) + bup_ref[...])
    slope_ref[...] = slope
    down_ref[...] += product(act.astype(BF16), wdown_ref[units, :])

    @pl.when(step == pl.num_programs(0) - 1)
    def _():
        normal, inverse = normalized(hidden_ref[...] + (down_ref[...] + bdown_ref[...]))
        output_ref[...] = (normal * gain_two_ref[...] + shift_two_ref[...]).astype(BF16)
        position = place_ref[blocks] * BLOCK + lax.broadcasted_iota(jnp.int32, (BLOCK, 1), 0)
        valid = segment_of(position, place_ref, 2 * blocks) < DOCS
        g_out = jnp.where(valid, cot_ref[...].astype(F32), 0.0)
        g_resid, g_gain, g_shift = normalized_back(g_out, normal, inverse, gain_two_ref[...])
        resid_ref[...] = g_resid
        g_down = g_resid.astype(BF16)
        feed_ref[:, D:] = g_down
        sums_ref[0:1, :] = column_sum(g_down.astype(F32))
        sums_ref[1:2, :] = g_gain
        sums_ref[2:3, :] = g_shift


def middle_forward(
    place, context, tokens, cotangent, w_out, b_out, gain_one, shift_one, b_down, gain_two, shift_two,
    w_up, b_up, w_down,
):
    units = w_up.shape[1]
    width = 512
    row = lambda v: v.reshape(1, -1)
    return pl.pallas_call(
        functools.partial(middle_forward_kernel, (place.shape[0] - DOCS) // 2),
        grid_spec=pltpu.PrefetchScalarGridSpec(
        num_scalar_prefetch=1,
        grid=(units // width,),
        in_specs=[once(BLOCK, D)] * 3
        + [pl.BlockSpec(memory_space=pltpu.VMEM)]
        + [once(1, D)] * 6
        + [
            pl.BlockSpec(memory_space=pltpu.VMEM),
            pl.BlockSpec((1, width), lambda p, *_: (0, p)),
            pl.BlockSpec(memory_space=pltpu.VMEM),
        ],
        out_specs=[
            once(BLOCK, D),
            once(BLOCK, 2 * D),
            once(BLOCK, D),
            once(BLOCK, BLOCK),
            once(BLOCK, D),
            pl.BlockSpec((BLOCK, width), lambda p, *_: (0, p)),
            once(8, D),
        ],
        scratch_shapes=[pltpu.VMEM((BLOCK, D), F32), pltpu.VMEM((BLOCK, D), F32)],
        ),
        out_shape=[
            jax.ShapeDtypeStruct((BLOCK, D), BF16),
            jax.ShapeDtypeStruct((BLOCK, 2 * D), BF16),
            jax.ShapeDtypeStruct((BLOCK, D), F32),
            jax.ShapeDtypeStruct((BLOCK, BLOCK), F32),
            jax.ShapeDtypeStruct((BLOCK, D), F32),
            jax.ShapeDtypeStruct((BLOCK, units), F32),
            jax.ShapeDtypeStruct((8, D), F32),
        ],
        compiler_params=pltpu.CompilerParams(vmem_limit_bytes=20 * 2**20),
        name="middle_forward",
    )(
        place, context, tokens, cotangent, w_out, row(b_out), row(gain_one), row(shift_one), row(b_down),
        row(gain_two), row(shift_two), w_up, row(b_up), w_down,
    )


def middle_backward_kernel(
    feed_ref,
    resid_ref,
    normal_ref,
    inverse_ref,
    gain_ref,
    wout_ref,
    slope_ref,
    wup_ref,
    wdown_ref,
    g_resid_ref,
    g_attn_ref,
    g_ctx_ref,
    sums_ref,
    g_up_ref,
    acc_ref,
):
    step = pl.program_id(0)

    @pl.when(step == 0)
    def _():
        acc_ref[...] = resid_ref[...]

    width = slope_ref.shape[1]
    units = pl.ds(pl.multiple_of(step * width, width), width)
    g_up = (product_right(feed_ref[:, D:], wdown_ref[units, :]) * slope_ref[...]).astype(BF16)
    g_up_ref[...] = g_up
    acc_ref[...] += product_right(g_up, wup_ref[:, units])

    @pl.when(step == pl.num_programs(0) - 1)
    def _():
        g_resid, g_gain, g_shift = normalized_back(
            acc_ref[...], normal_ref[...], inverse_ref[:, 0:1], gain_ref[...]
        )
        g_resid_ref[...] = g_resid
        g_attn = g_resid.astype(BF16)
        g_attn_ref[...] = g_attn
        g_ctx_ref[...] = product_right(g_attn, wout_ref[...]).astype(BF16)
        sums_ref[0:1, :] = column_sum(g_attn.astype(F32))
        sums_ref[1:2, :] = g_gain
        sums_ref[2:3, :] = g_shift


def middle_backward(feed, g_resid_two, normal, inverse, gain_one, w_out, slope, w_up, w_down):
    units = w_up.shape[1]
    width = 512
    return pl.pallas_call(
        middle_backward_kernel,
        grid=(units // width,),
        in_specs=[
            once(BLOCK, 2 * D),
            once(BLOCK, D),
            once(BLOCK, D),
            once(BLOCK, BLOCK),
            once(1, D),
            pl.BlockSpec(memory_space=pltpu.VMEM),
            pl.BlockSpec((BLOCK, width), lambda p: (0, p)),
            pl.BlockSpec(memory_space=pltpu.VMEM),
            pl.BlockSpec(memory_space=pltpu.VMEM),
        ],
        out_specs=[
            once(BLOCK, D),
            once(BLOCK, D),
            once(BLOCK, D),
            once(8, D),
            pl.BlockSpec((BLOCK, width), lambda p: (0, p)),
        ],
        scratch_shapes=[pltpu.VMEM((BLOCK, D), F32)],
        out_shape=[
            jax.ShapeDtypeStruct((BLOCK, D), F32),
            jax.ShapeDtypeStruct((BLOCK, D), BF16),
            jax.ShapeDtypeStruct((BLOCK, D), BF16),
            jax.ShapeDtypeStruct((8, D), F32),
            jax.ShapeDtypeStruct((BLOCK, units), BF16),
        ],
        compiler_params=pltpu.CompilerParams(vmem_limit_bytes=20 * 2**20),
        name="middle_backward",
    )(
        feed, g_resid_two, normal, inverse, gain_one.reshape(1, -1), w_out, slope,
        w_up, w_down,
    )


def gelu_and_slope(x):
    below = 0.5 + 0.5 * lax.erf(x * math.sqrt(0.5))
    density = jnp.exp(-0.5 * x * x) * (1.0 / math.sqrt(2.0 * math.pi))
    return x * below, below + x * density


def feedforward_kernel(
    parts,
    order_ref,
    *refs,
):
    part_refs, refs = refs[:parts], refs[parts:]
    wup_ref, bup_ref, wdown_ref, down_own_ref, down_other_ref, up_own_ref, up_other_ref, *refs = refs
    hid_ref, gd_ref, hidt_ref, sums_ref = refs
    step = pl.program_id(0)
    shares = up_own_ref.shape[0]
    half = down_own_ref.shape[1]
    width = wup_ref.shape[1]

    @pl.when(step == 0)
    def _():
        for part in range(parts):
            rows = slice(part * BLOCK, (part + 1) * BLOCK)
            hid_ref[rows, :] = part_refs[part][:, :D]
            gd_ref[rows, :] = part_refs[part][:, D:]
        place_rows(order_ref, hidt_ref, hid_ref[...].T, 2, shares)

    lanes = pl.ds(pl.multiple_of(step * width, width), width)
    act, slope = gelu_and_slope(product(hid_ref[...], wup_ref[...]) + bup_ref[...])
    g_up = (product_right(gd_ref[...], wdown_ref[...]) * slope).astype(BF16)
    act_turned = act.astype(BF16).T
    for core, ref in enumerate((down_own_ref, down_other_ref)):
        columns = pl.ds(pl.multiple_of((order_ref[0] ^ core) * half, BLOCK), half)
        ref[lanes, :] = product(act_turned, gd_ref[:, columns]).astype(BF16)
    store_pieces((up_own_ref, up_other_ref), 0, product(hidt_ref[...], g_up).astype(BF16), lanes)
    sums_ref[:, lanes] = product(jnp.ones((16, hid_ref.shape[0]), BF16), g_up)

    @pl.when(step == pl.num_programs(0) - 1)
    def _():
        for core, ref in enumerate((down_own_ref, down_other_ref)):
            columns = pl.ds(pl.multiple_of((order_ref[0] ^ core) * half, BLOCK), half)
            ref[pl.ds(sums_ref.shape[1], 16), :] = sums_ref[:, columns].astype(BF16)


def feedforward_gradients(order, row_parts, w_up, b_up, w_down):
    shares = len(row_parts)
    tokens = shares * BLOCK
    units = w_up.shape[1] // shares
    width = 256
    steps = units // width
    down = (units + 16, D // 2)
    up = (shares, D // shares // 2, units)
    return pl.pallas_call(
        functools.partial(feedforward_kernel, shares),
        grid_spec=pltpu.PrefetchScalarGridSpec(
            num_scalar_prefetch=1,
            grid=(steps,),
            in_specs=[once(BLOCK, 2 * D)] * shares
            + [
                pl.BlockSpec((D, width), lambda p, order: (0, order[1] * steps + p)),
                pl.BlockSpec((1, width), lambda p, order: (0, order[1] * steps + p)),
                pl.BlockSpec((width, D), lambda p, order: (order[1] * steps + p, 0)),
            ],
            out_specs=[once(*down), once(*down), once(*up), once(*up)],
            scratch_shapes=[
                pltpu.VMEM((tokens, D), BF16),
                pltpu.VMEM((tokens, D), BF16),
                pltpu.VMEM((D, tokens), BF16),
                pltpu.VMEM((16, units), F32),
            ],
        ),
        out_shape=[jax.ShapeDtypeStruct(shape, BF16) for shape in (down, down, up, up)],
        compiler_params=pltpu.CompilerParams(vmem_limit_bytes=16 * 2**20),
        name="feedforward_gradients",
    )(order, *row_parts, *streamed(w_up), b_up, *streamed(w_down))


def swapped(array, axis, bits):
    return lax.ppermute(array, axis, [(i, i ^ bits) for i in range(lax.axis_size(axis))])


def from_peers(arrays):
    return [swapped(array, "seq", bits) for bits, array in enumerate(arrays, 1)]


def picked(array, index, axis):
    return lax.dynamic_index_in_dim(array, index, axis, keepdims=False)


def together(*arrays):
    return lax.optimization_barrier(arrays)


def added(*arrays):
    return functools.reduce(jnp.add, [array.astype(F32) for array in arrays]).astype(BF16)


def halves(pack):
    middle = pack.shape[1] // 32 * 16
    return pack[:, :middle], pack[:, middle:]


def in_row_order(pack, mine):
    return jnp.stack([picked(pack, mine ^ at, 0) for at in range(4)], axis=0)


def square_mesh():
    return lax.axis_size("seq") == 4 and lax.axis_size("z") == 4


def scatter(pack):
    return from_peers([pack[1], pack[2], pack[3]])


def inward(share):
    return lax.ppermute(share, "z", [(0, 1), (3, 2)])


def across(share):
    return lax.ppermute(share, "z", [(1, 2), (2, 1)])


def outward(share):
    return lax.ppermute(share, "z", [(1, 0), (2, 3)])


def settled(share, got):
    at_z = lax.axis_index("z")
    return jnp.where((at_z == 1) | (at_z == 2), share, got)


def core_index():
    return lax.axis_index("core")


def both_cores(share, axis):
    other = swapped(share, "core", 1)
    first = core_index() == 0
    return jnp.concatenate(
        [jnp.where(first, share, other), jnp.where(first, other, share)], axis=axis
    )


def reduce_plain(partial):
    share = lax.psum_scatter(partial.astype(BF16), "seq", scatter_dimension=0, tiled=True)
    return lax.psum(share, ("z", "core")).astype(F32)


def local(
    tokens,
    cotangent,
    lengths,
    w_query,
    b_query,
    w_key,
    b_key,
    w_value,
    b_value,
    w_out,
    b_out,
    gain_one,
    shift_one,
    w_up,
    b_up,
    w_down,
    b_down,
    gain_two,
    shift_two,
    rel_table,
):
    rows = tokens.shape[0]
    cycle = lax.axis_size("seq")
    mine = lax.axis_index("seq")
    core = core_index()
    square = square_mesh()
    hidden_units = w_up.shape[1]
    share = D // cycle
    if square:
        token_parts = [tokens] + from_peers([tokens] * 3)
        ids = mine ^ jnp.arange(cycle, dtype=jnp.int32)
        order = jnp.stack([core, mine]).astype(jnp.int32)
        cores = 2
    else:
        token_parts = [tokens, lax.all_gather(tokens, "seq", axis=0, tiled=True)]
        ids = jnp.concatenate([mine[None], jnp.arange(cycle, dtype=jnp.int32)])
        order = jnp.zeros((2,), jnp.int32)
        cores = 1
    dist = jnp.concatenate([mine - ids, ids, lengths[0]]).astype(jnp.int32)

    places = jnp.arange(RELROWS, dtype=jnp.int32)
    turn = (places[:, None] + places[None, :] == RELROWS - 1).astype(BF16)
    rel_back = product(turn, rel_table).astype(BF16)
    pos_key_back = (product(rel_back, w_key) + b_key).astype(BF16)
    pos_query_back = (product(rel_back, w_query) + b_query).astype(BF16)
    pos_query = (product(rel_table, w_query) + b_query).astype(BF16)
    pos_key_back, pos_query_back, pos_query = together(pos_key_back, pos_query_back, pos_query)
    context, prob, query, key, value, tokens_row, *held = attention_forward(
        dist,
        token_parts,
        [w_query, w_key, w_value],
        [v[None] for v in (b_query, b_key, b_value)],
        pos_key_back,
        pos_query_back,
        [w_up, w_down, w_out],
    )
    held_up, held_down, held_out = held

    output, feed, normal_one, inverse_one, g_resid_two, slope, sums_two = middle_forward(
        dist, context, tokens, cotangent, held_out, b_out, gain_one, shift_one, b_down, gain_two,
        shift_two, held_up, b_up, held_down,
    )
    if square:
        row_parts = [feed] + from_peers([feed] * 3)
    g_resid_one, g_attn, g_context, sums_one, g_up = middle_backward(
        feed, g_resid_two, normal_one, inverse_one, gain_one, held_out, slope, held_up, held_down
    )
    vectors = [sums_one, sums_two]

    def backward(start, pairs, g_context, extra_one, extra_two):
        outs = attention_backward(
            start, pairs, cores, cycle, dist, order, query, key, value, pos_key_back, pos_query, prob,
            g_context, tokens_row, rel_table, w_query, w_key, w_value, extra_one, extra_two, vectors,
        )
        return outs[:cores], outs[cores:]

    piece = share // cores
    whole_rows = lambda v, at, each: v[:, at : at + each].reshape(cores * each, -1)

    def unpacked(v, each):
        base = 3 * piece + 16
        parts = D // v.shape[2]
        return jnp.concatenate(
            [whole_rows(v, base + part * each, each) for part in range(parts)], axis=1
        )

    def rel_pieces(pack):
        part = unpacked(pack, RELROWS // cycle // cores)
        if square:
            return [part] + from_peers([part] * 3)
        return [lax.all_gather(part, "seq", axis=0, tiled=True)]

    def assembled(packs, rel_parts, grad_tokens, grad_w_up, grad_w_down, grad_b_up):
        grads = [
            jnp.concatenate([whole_rows(v, at * piece, piece) for v in packs], axis=1).astype(F32)
            for at in range(3)
        ]
        base = 3 * piece
        vector_sums = jnp.concatenate([v[0, base : base + 16] for v in packs], axis=1).astype(F32)
        grad_w_out = unpacked(packs[0], piece).astype(F32)
        if square:
            grad_rel = jnp.zeros((RELROWS, D), F32)
            for bits, part in enumerate(rel_parts):
                grad_rel = lax.dynamic_update_slice_in_dim(
                    grad_rel, part.astype(F32), (mine ^ bits) * (RELROWS // cycle), 0
                )
        else:
            grad_rel = rel_parts[0].astype(F32)
        vector_share = lax.dynamic_slice_in_dim(vector_sums, mine * share, share, 1)
        return (
            output,
            grad_tokens,
            grads[0],
            vector_share[0],
            grads[1],
            vector_share[1],
            grads[2],
            vector_share[2],
            grad_w_out,
            vector_share[3],
            vector_share[4],
            vector_share[5],
            grad_w_up,
            grad_b_up,
            grad_w_down,
            vector_share[6],
            vector_share[7],
            vector_share[8],
            grad_rel,
        )

    if not square:
        act = gelu_and_slope(product(feed[:, :D], w_up) + b_up)[0].astype(BF16)
        (one,), carried = backward(0, 3, g_context, context, g_attn)
        (two,), (home, away) = backward(3, 3, g_context, *carried)
        packs = [
            lax.psum(lax.psum_scatter(v, "seq", scatter_dimension=0, tiled=True), ("z", "core"))
            for v in (one, two)
        ]
        got = lax.psum_scatter(away, "seq", scatter_dimension=0, tiled=False)
        return assembled(
            packs,
            rel_pieces(packs[-1]),
            g_resid_one + home + got.astype(F32),
            reduce_plain(product_left(feed[:, :D], g_up)),
            reduce_plain(product_left(act, feed[:, D:])),
            reduce_plain(jnp.sum(g_up.astype(F32), axis=0)),
        )

    one, carried = backward(0, 3, g_context, context, g_attn)

    row_parts, one, carried = together(row_parts, one, carried)
    one_got = swapped(one[1], "core", 1)
    down_own, down_other, up_own, up_other = feedforward_gradients(
        order, row_parts, w_up, b_up[None], w_down
    )

    one_got, down_own, down_other, up_own, up_other = together(
        one_got, down_own, down_other, up_own, up_other
    )
    down_got = swapped(down_other, "core", 1)
    up_got = swapped(up_other, "core", 1)
    one_share = added(one[0], one_got)
    down_share = added(down_own, down_got)
    up_share = added(up_own, up_got)
    down_got = inward(down_share)
    one_first, one_second = halves(one_share)
    one_first_got = swapped(one_first[1::2], "seq", 1)
    one_second_got = swapped(one_second[2:], "seq", 2)
    g_context, down_share, up_share, one_share = together(g_context, down_share, up_share, one_share)
    two, (home, away) = backward(3, 3, g_context, *carried)

    units = hidden_units // 4
    two, home, away, one_first_got, one_second_got, down_got = together(
        two, home, away, one_first_got, one_second_got, down_got
    )
    two_got = swapped(two[1], "core", 1)
    down_share = added(down_share, down_got)
    down_got = across(down_share)
    up_got = inward(up_share)

    two_got, down_share = together(two_got, down_share)
    two_share = added(two[0], two_got)
    two_first, two_second = halves(two_share)
    two_first_got = swapped(two_first[1::2], "seq", 1)
    two_second_got = swapped(two_second[2:], "seq", 2)

    two_first_got, two_second_got = together(two_first_got, two_second_got)
    two_first = added(two_first[0::2], two_first_got)
    two_second = added(two_second[:2], two_second_got)
    two_first_got = swapped(two_first[1], "seq", 2)
    two_second_got = swapped(two_second[1], "seq", 1)
    one_first = added(one_first[0::2], one_first_got)
    one_second = added(one_second[:2], one_second_got)

    two_first_got, two_second_got, down_got, up_got, one_first, one_second = together(
        two_first_got, two_second_got, down_got, up_got, one_first, one_second
    )
    two_share = jnp.concatenate(
        [added(two_first[0], two_first_got), added(two_second[0], two_second_got)], axis=0
    )
    two_got = inward(two_share)
    down_share = added(down_share, down_got)
    down_got = outward(down_share)
    up_share = added(up_share, up_got)
    up_got = across(up_share)
    one_first_got = swapped(one_first[1], "seq", 2)
    one_second_got = swapped(one_second[1], "seq", 1)

    two_got, one_first_got, one_second_got = together(two_got, one_first_got, one_second_got)
    two_share = added(two_share, two_got)
    two_got = across(two_share)
    one_share = jnp.concatenate(
        [added(one_first[0], one_first_got), added(one_second[0], one_second_got)], axis=0
    )
    one_got = inward(one_share)

    up_got, down_got, away = together(up_got, down_got, away)
    up_share = added(up_share, up_got)
    up_got = outward(up_share)
    down_share = both_cores(settled(down_share, down_got), 1)

    two_got, one_got, down_share, away = together(two_got, one_got, down_share, away)
    two_share = added(two_share, two_got)
    two_got = outward(two_share)
    one_share = added(one_share, one_got)
    one_got = across(one_share)
    grad_w_down = down_share[:units].astype(F32)
    grad_b_up = down_share[units].astype(F32)
    home_got = from_peers([away[0], away[1], away[2]])

    up_got, home_got, grad_w_down = together(up_got, home_got, grad_w_down)
    up_share = settled(up_share, up_got)
    up_got = scatter(up_share)
    grad_tokens = g_resid_one + functools.reduce(jnp.add, [v.astype(F32) for v in home_got], home)

    one_got, two_got, up_got, grad_tokens = together(one_got, two_got, up_got, grad_tokens)
    two_share = both_cores(settled(two_share, two_got)[None], 0)
    one_share = added(one_share, one_got)
    one_got = outward(one_share)
    rel_parts = rel_pieces(two_share)
    up_share = both_cores(jnp.stack([up_share[0]] + up_got, axis=0), 1).reshape(4, share, -1)
    grad_w_up = jnp.zeros((share, hidden_units), F32)
    for bits in range(4):
        grad_w_up = lax.dynamic_update_slice_in_dim(
            grad_w_up, up_share[bits].astype(F32), (mine ^ bits) * units, 1
        )
    one_share = both_cores(settled(one_share, one_got)[None], 0)
    return assembled(
        [one_share, two_share],
        rel_parts,
        grad_tokens,
        grad_w_up,
        grad_w_down,
        grad_b_up,
    )


def solution(mesh):
    lines, cycle = mesh.devices.shape
    chips = Mesh(mesh.devices.reshape(lines // 2, 2, cycle), ("z", "core", "seq"))
    return jax.shard_map(
        local,
        mesh=chips,
        in_specs=(
            P(("z", "core", "seq"), None),
            P(("z", "core", "seq"), None),
            P(("z", "core"), None),
        )
        + (P(),) * 17,
        out_specs=(
            P(("z", "core", "seq"), None),
            P(("z", "core", "seq"), None),
            P("seq", None),
            P("seq"),
            P("seq", None),
            P("seq"),
            P("seq", None),
            P("seq"),
            P("seq", None),
            P("seq"),
            P("seq"),
            P("seq"),
            P("seq", None),
            P("seq"),
            P("seq", None),
            P("seq"),
            P("seq"),
            P("seq"),
            P(),
        ),
        check_vma=False,
    )
```

```python
import functools
import math

import jax
import jax.numpy as jnp
from jax import lax
from jax.experimental import pallas as pl
from jax.experimental.pallas import tpu as pltpu
from jax.sharding import Mesh, PartitionSpec as P

D = 768
HEADS = 12
HEAD = 64
SPAN = 256
RELROWS = 512
BLOCK = 128
EXT = RELROWS + 2 * SPAN
PAIRS = HEADS // 2
VECTORS = 2
LATER = 3
DOCS = 4
SCALE = 1.0 / math.sqrt(3 * HEAD)
F32 = jnp.float32
BF16 = jnp.bfloat16
ROLLED = BF16


def normalized(resid):
    center = resid - jnp.mean(resid, axis=-1, keepdims=True)
    inverse = lax.rsqrt(jnp.mean(center * center, axis=-1, keepdims=True) + 1e-07)
    return center * inverse, inverse


def normalized_back(grad, normal, inverse, gain):
    hat = grad * gain
    means = jnp.mean(hat, axis=-1, keepdims=True) + normal * jnp.mean(
        hat * normal, axis=-1, keepdims=True
    )
    total = lambda v: jnp.sum(v, axis=0, keepdims=True)
    return (hat - means) * inverse, total(grad * normal), total(grad)


def product(left, right):
    return jnp.dot(left, right, preferred_element_type=F32)


def product_left(left, right):
    return lax.dot_general(left, right, (((0,), (0,)), ((), ())), preferred_element_type=F32)


def product_right(left, right):
    return lax.dot_general(left, right, (((1,), (1,)), ((), ())), preferred_element_type=F32)


def segment_of(position, place_ref, at):
    passed, bound = jnp.zeros(position.shape, jnp.int32), 0
    for document in range(DOCS):
        bound = bound + place_ref[at + document]
        passed = passed + (position >= bound).astype(jnp.int32)
    return passed


def anti_identity():
    rows = lax.broadcasted_iota(jnp.int32, (BLOCK, BLOCK), 0)
    cols = lax.broadcasted_iota(jnp.int32, (BLOCK, BLOCK), 1)
    return (rows + cols == BLOCK - 1).astype(BF16)


def extend(ext_ref, table_ref):
    ext_ref[SPAN : SPAN + RELROWS, :] = table_ref[...]
    ext_ref[0:SPAN, :] = jnp.broadcast_to(table_ref[0:1, :], (SPAN, BLOCK))
    last = table_ref[RELROWS - 1 : RELROWS, :]
    ext_ref[SPAN + RELROWS :, :] = jnp.broadcast_to(last, (SPAN, BLOCK))


def window_start(offset):
    return pl.multiple_of(jnp.clip(offset, 0, EXT - 2 * BLOCK), BLOCK)


def head_mask(head):
    lane = lax.broadcasted_iota(jnp.int32, (1, BLOCK), 1)
    return (lane >= head * HEAD) & (lane < (head + 1) * HEAD)


def band_roll(wide, shift):
    return pltpu.roll(wide, shift, 1, stride=1, stride_axis=0)


def by_head(pair):
    zero = jnp.zeros_like(pair)
    return jnp.concatenate([jnp.where(head_mask(head), pair, zero) for head in range(2)], axis=0)


def forward_kernel(
    parts, blocks, dist_ref, *refs
):
    part_refs, refs = refs[:parts], refs[parts:]
    wq_ref, wk_ref, wv_ref, bq_ref, bk_ref, bv_ref, pk_ref, pq_ref, *refs = refs
    later, refs = refs[:LATER], refs[LATER:]
    ctx_ref, prob_ref, q_ref, k_ref, v_ref, tok_ref, *refs = refs
    held, refs = refs[:LATER], refs[LATER:]
    score_ref, ek_ref, eq_ref, bias_ref, sems = refs
    copies = [
        pltpu.make_async_copy(later[at], held[at], sems.at[at]) for at in range(LATER)
    ]

    @pl.when(pl.program_id(0) == 0)
    def _():
        for copy in copies:
            copy.start()

    @pl.when(pl.program_id(0) == pl.num_programs(0) - 1)
    def _():
        for copy in copies:
            copy.wait()

    extend(ek_ref, pk_ref)
    extend(eq_ref, pq_ref)

    @pl.when(pl.program_id(0) == 0)
    def _():
        at = 0
        for ref in part_refs:
            tok_ref[at : at + ref.shape[0], :] = ref[...]
            at += ref.shape[0]
        mine = dist_ref[blocks]
        lane = lax.broadcasted_iota(jnp.int32, (1, BLOCK), 1)
        line = lax.broadcasted_iota(jnp.int32, (BLOCK, 1), 0)
        query_segment = segment_of(mine * BLOCK + lane, dist_ref, 2 * blocks)
        for block in range(blocks):
            home = dist_ref[blocks + block]
            allowed = segment_of(home * BLOCK + line, dist_ref, 2 * blocks) == query_segment
            if block > 0:
                allowed = jnp.logical_and(allowed, home != mine)
            rows = slice(block * BLOCK, (block + 1) * BLOCK)
            bias_ref[rows, :] = jnp.where(allowed, 0.0, -1e30)

    both = product(tok_ref[...], jnp.concatenate([wk_ref[...], wv_ref[...]], axis=1))
    k_ref[...] = (both[:, :BLOCK] + bk_ref[...]).astype(BF16)
    v_ref[...] = (both[:, BLOCK:] + bv_ref[...]).astype(BF16)
    q = (product(tok_ref[:BLOCK, :], wq_ref[...]) + bq_ref[...]).astype(BF16)
    q_ref[...] = q
    q_heads = by_head(q)
    tops = [jnp.full((1, BLOCK), -jnp.inf, F32) for head in range(2)]
    for block in range(blocks):
        dist = dist_ref[block]
        rows = slice(block * BLOCK, (block + 1) * BLOCK)
        k_heads = by_head(k_ref[rows, :])
        window_c = ek_ref[pl.ds(window_start(384 - dist * BLOCK), 2 * BLOCK), :]
        window_p = eq_ref[pl.ds(window_start(384 + dist * BLOCK), 2 * BLOCK), :]
        c2p = product_right(q_heads, window_c)
        p2c = product_right(k_heads, window_p)
        direct = product_right(k_heads, q)
        for head in range(2):
            own = slice(head * BLOCK, (head + 1) * BLOCK)
            first = band_roll(c2p[own].astype(BF16), BLOCK + 1)[:, :BLOCK].T
            second = band_roll(p2c[own].astype(BF16), BLOCK + 1)[:, :BLOCK]
            score = (direct[own] + first.astype(F32) + second.astype(F32)) * SCALE + bias_ref[rows, :]
            score_ref[head, rows, :] = score
            tops[head] = jnp.maximum(tops[head], jnp.max(score, axis=0, keepdims=True))
    probs = []
    for head in range(2):
        weight = jnp.exp(score_ref[head] - tops[head])
        total = jnp.sum(weight, axis=0, keepdims=True)
        prob = (weight * (1.0 / total)).astype(BF16)
        prob_ref[head] = prob
        probs.append(prob)
    v = v_ref[...]
    zero = jnp.zeros_like(v)
    out = product_left(probs[0], jnp.where(head_mask(0), v, zero)) + product_left(
        probs[1], jnp.where(head_mask(1), v, zero)
    )
    ctx_ref[...] = out.astype(BF16)


def streamed(*arrays):
    return [pltpu.with_memory_space_constraint(array, pltpu.HBM) for array in arrays]


def once(*shape):
    return pl.BlockSpec(shape, lambda p, *_: (0,) * len(shape), pipeline_mode=pl.Buffered(1))


def attention_forward(dist, token_parts, weights, biases, pos_key, pos_query, later):
    keys = sum(part.shape[0] for part in token_parts)
    blocks = keys // BLOCK
    pair = lambda rows: pl.BlockSpec((rows, BLOCK), lambda p, dist: (0, p))
    return pl.pallas_call(
        functools.partial(forward_kernel, len(token_parts), blocks),
        grid_spec=pltpu.PrefetchScalarGridSpec(
            num_scalar_prefetch=1,
            grid=(PAIRS,),
            in_specs=[once(*part.shape) for part in token_parts]
            + [pair(D)] * 3
            + [pair(1)] * 3
            + [pair(RELROWS), pair(RELROWS)]
            + [pl.BlockSpec(memory_space=pl.ANY)] * LATER,
            out_specs=[
                pair(BLOCK),
                pl.BlockSpec((2, keys, BLOCK), lambda p, dist: (p, 0, 0)),
                pair(BLOCK),
                pair(keys),
                pair(keys),
                once(keys, D),
            ]
            + [pl.BlockSpec(memory_space=pl.ANY)] * LATER,
            scratch_shapes=[
                pltpu.VMEM((2, keys, BLOCK), F32),
                pltpu.VMEM((EXT, BLOCK), BF16),
                pltpu.VMEM((EXT, BLOCK), BF16),
                pltpu.VMEM((keys, BLOCK), F32),
                pltpu.SemaphoreType.DMA((LATER,)),
            ],
        ),
        out_shape=[
            jax.ShapeDtypeStruct((BLOCK, D), BF16),
            pltpu.HBM((HEADS, keys, BLOCK), BF16),
            pltpu.HBM((BLOCK, D), BF16),
            pltpu.HBM((keys, D), BF16),
            pltpu.HBM((keys, D), BF16),
            pltpu.HBM((keys, D), BF16),
        ]
        + [pltpu.VMEM(array.shape, array.dtype) for array in later],
        compiler_params=pltpu.CompilerParams(vmem_limit_bytes=(16 if keys <= 1024 else 40) * 2**20),
        name="attention_forward",
    )(dist, *token_parts, *streamed(*weights), *biases, *streamed(pos_key, pos_query), *streamed(*later))


def fold_edges(acc_ref):
    head_sum = jnp.sum(acc_ref[:, 0:SPAN], axis=1, keepdims=True)
    tail_sum = jnp.sum(acc_ref[:, SPAN + RELROWS :], axis=1, keepdims=True)
    lane = lax.broadcasted_iota(jnp.int32, (BLOCK, RELROWS), 1)
    middle = acc_ref[:, SPAN : SPAN + RELROWS]
    middle = middle + jnp.where(lane == 0, head_sum, 0.0)
    return (middle + jnp.where(lane == RELROWS - 1, tail_sum, 0.0)).astype(BF16)


def flipped_lanes(array, flip):
    parts = array.shape[1] // BLOCK
    return jnp.concatenate(
        [
            product(array[:, part * BLOCK : (part + 1) * BLOCK], flip).astype(BF16)
            for part in reversed(range(parts))
        ],
        axis=1,
    )


def place(order_ref, share, core, shares, each):
    at = (core ^ order_ref[0]) * shares + (share ^ order_ref[1])
    return pl.multiple_of(at * each, 16)


def place_rows(order_ref, into_ref, value, cores, shares):
    each = value.shape[0] // (cores * shares)
    for share in range(shares):
        for core in range(cores):
            at = (share * cores + core) * each
            into_ref[pl.ds(place(order_ref, share, core, shares, each), each), :] = value[
                at : at + each
            ]


def store_pieces(refs, at, value, lanes):
    shares = refs[0].shape[0]
    each = value.shape[0] // (len(refs) * shares)
    for core, ref in enumerate(refs):
        for share in range(shares):
            start = (core * shares + share) * each
            ref[share, at : at + each, lanes] = value[start : start + each]


def backward_kernel(
    blocks,
    cores,
    first,
    last,
    dist_ref,
    order_ref,
    q_ref,
    k_ref,
    v_ref,
    pk_ref,
    pq_ref,
    prob_ref,
    gctx_ref,
    tok_ref,
    rel_ref,
    wq_ref,
    wk_ref,
    wv_ref,
    extra_one_ref,
    extra_two_ref,
    *refs,
):
    vec_refs, refs = refs[:VECTORS], refs[VECTORS:]
    pack_refs, refs = refs[:cores], refs[cores:]
    backward_body(
        blocks, first, last, dist_ref, order_ref, q_ref, k_ref, v_ref, pk_ref, pq_ref, prob_ref, gctx_ref,
        tok_ref, rel_ref, wq_ref, wk_ref, wv_ref, extra_one_ref, extra_two_ref, vec_refs, pack_refs, *refs
    )


def backward_body(
    blocks,
    first,
    last,
    dist_ref,
    order_ref,
    q_ref,
    k_ref,
    v_ref,
    pk_ref,
    pq_ref,
    prob_ref,
    gctx_ref,
    tok_ref,
    rel_ref,
    wq_ref,
    wk_ref,
    wv_ref,
    extra_one_ref,
    extra_two_ref,
    vec_refs,
    pack_refs,
    out_one_ref,
    out_two_ref,
    back_ref,
    gk_ref,
    gv_ref,
    acck_ref,
    accq_ref,
    tokt_ref,
    relt_ref,
    acc_tok_ref,
    acc_rel_ref,
    turn_ref,
    ek_ref,
    eq_ref,
):
    step = pl.program_id(0)
    extend(ek_ref, pk_ref)
    extend(eq_ref, pq_ref)
    cores, shares, half = len(pack_refs), pack_refs[0].shape[0], pack_refs[0].shape[2]
    share = D // cores // shares
    flip = anti_identity()

    @pl.when(step == 0)
    def _():
        place_rows(order_ref, tokt_ref, tok_ref[...].T, cores, shares)
        place_rows(order_ref, relt_ref, rel_ref[...].T, cores, shares)
        if first:
            acc_tok_ref[...] = jnp.zeros_like(acc_tok_ref)
            acc_rel_ref[...] = jnp.zeros_like(acc_rel_ref)
        else:
            acc_tok_ref[...] = extra_one_ref[...]
            acc_rel_ref[...] = extra_two_ref[...]

    acck_ref[...] = jnp.zeros_like(acck_ref)
    accq_ref[...] = jnp.zeros_like(accq_ref)
    g_heads = by_head(gctx_ref[...])
    first_rows = lax.broadcasted_iota(jnp.int32, (BLOCK, 1), 0) < HEAD
    first_lanes = head_mask(0)

    def turned_heads(array):
        turned = array.T
        zero = jnp.zeros_like(turned)
        return jnp.concatenate(
            [jnp.where(first_rows, turned, zero), jnp.where(first_rows, zero, turned)], axis=1
        )

    def of_heads(stacked):
        return jnp.where(first_lanes, stacked[:BLOCK], stacked[BLOCK:])

    q_back = product(flip, q_ref[...]).astype(BF16)
    q_turned = turned_heads(q_back)
    probs = jnp.concatenate([prob_ref[head] for head in range(2)], axis=1)
    g_prob = product_right(v_ref[...], g_heads)
    gv_ref[...] = product(probs, g_heads).astype(BF16)
    probs = probs.astype(F32)
    delta = jnp.sum(probs * g_prob, axis=0, keepdims=True)
    g_score = (probs * (g_prob - delta) * SCALE).astype(BF16)
    for head in range(2):
        lanes = slice(head * BLOCK, (head + 1) * BLOCK)
        back_ref[:, lanes] = product(g_score[:, lanes], flip).astype(BF16)
    g_query = jnp.zeros((2 * BLOCK, BLOCK), F32)
    pad = jnp.zeros((BLOCK, BLOCK), BF16)
    for block in range(blocks):
        rows = slice(block * BLOCK, (block + 1) * BLOCK)
        k_block = k_ref[rows, :]
        at = pl.ds(window_start(384 - dist_ref[block] * BLOCK), 2 * BLOCK)
        window_c = ek_ref[at, :]
        window_p = eq_ref[at, :]
        backs = [back_ref[rows, head * BLOCK : (head + 1) * BLOCK] for head in range(2)]
        turns = [back.T for back in backs]
        bands_c = [band_roll(jnp.concatenate([turn, pad], axis=1), 0) for turn in turns]
        bands_p = [band_roll(jnp.concatenate([back, pad], axis=1), 1) for back in backs]
        bands_c = jnp.concatenate(bands_c, axis=0)
        bands_p = jnp.concatenate(bands_p, axis=0)
        g_query = g_query + product(
            jnp.concatenate([jnp.concatenate(turns, axis=0), bands_c], axis=1),
            jnp.concatenate([k_block, window_c], axis=0),
        )
        g_key = product(
            jnp.concatenate([jnp.concatenate(backs, axis=0), bands_p], axis=1),
            jnp.concatenate([q_back, window_p], axis=0),
        )
        gk_ref[rows, :] = of_heads(g_key).astype(BF16)
        acck_ref[:, at] += product(q_turned, bands_c)
        accq_ref[:, at] += product(turned_heads(k_block), bands_p)

    g_query = product(flip, of_heads(g_query).astype(BF16)).astype(BF16)
    g_pos_key = flipped_lanes(fold_edges(acck_ref), flip)
    g_pos_query = fold_edges(accq_ref)
    g_key = gk_ref[...]
    g_value = gv_ref[...]
    lanes = pl.ds(pl.multiple_of(step * BLOCK, BLOCK), BLOCK)
    ones_tok = jnp.ones((16, tok_ref.shape[0]), BF16)
    ones_rel = jnp.ones((16, RELROWS), BF16)
    row = lax.broadcasted_iota(jnp.int32, (16, BLOCK), 0)
    vec = jnp.zeros((16, BLOCK), F32)
    for at, vec_ref in enumerate(vec_refs):
        for part in range(3):
            vec = vec + jnp.where(row == 3 + 3 * at + part, vec_ref[part : part + 1, :], 0.0)
    g_both = jnp.concatenate([g_key, g_value], axis=1)
    pos_both = jnp.concatenate([g_pos_key, g_pos_query], axis=0)
    from_tok = product(tokt_ref[...], g_both)
    from_rel = product_right(relt_ref[...], pos_both)
    from_own = product(tokt_ref[:, :BLOCK], g_query)
    sum_tok = product(ones_tok, g_both)
    sum_rel = product_right(ones_rel, pos_both)
    sum_own = product(ones_tok[:, :BLOCK], g_query)
    weights = [
        (from_own + from_rel[:, BLOCK:], sum_own + sum_rel[:, BLOCK:]),
        (from_tok[:, :BLOCK] + from_rel[:, :BLOCK], sum_tok[:, :BLOCK] + sum_rel[:, :BLOCK]),
        (from_tok[:, BLOCK:], sum_tok[:, BLOCK:]),
    ]
    for at, (weight, total) in enumerate(weights):
        store_pieces(pack_refs, at * share, weight.astype(BF16), lanes)
        vec = vec + jnp.where(row == at, total, 0.0)
    vec = vec.astype(BF16)
    for pack_ref in pack_refs:
        for part in range(shares):
            pack_ref[part, 3 * share : 3 * share + 16, lanes] = vec
    acc_tok_ref[...] += product_right(
        g_both,
        jnp.concatenate([wk_ref[...], wv_ref[...]], axis=1),
    )
    acc_tok_ref[0:BLOCK, :] += product_right(g_query, wq_ref[...])
    acc_rel_ref[...] += product(
        jnp.concatenate([wk_ref[...], wq_ref[...]], axis=1),
        pos_both,
    )

    @pl.when(step == pl.num_programs(0) - 1)
    def _():
        base = 3 * share + 16
        extra = None
        if last:
            out_one_ref[...] = acc_tok_ref[0:BLOCK, :]
            for block in range(1, blocks):
                out_two_ref[block - 1] = acc_tok_ref[block * BLOCK : (block + 1) * BLOCK].astype(BF16)
            place_rows(order_ref, turn_ref, acc_rel_ref[...].T.astype(BF16), cores, shares)
            extra = turn_ref[...]
        else:
            out_one_ref[...] = acc_tok_ref[...]
            out_two_ref[...] = acc_rel_ref[...]
        if first:
            place_rows(order_ref, turn_ref, extra_one_ref[...].T, cores, shares)
            extra = product(turn_ref[...], extra_two_ref[...]).astype(BF16)
        if extra is not None:
            each = extra.shape[0] // (cores * shares)
            for part in range(D // half):
                columns = extra[:, part * half : (part + 1) * half]
                store_pieces(pack_refs, base + part * each, columns, slice(None))


def attention_backward(
    start, pairs, cores, shares, dist, order, query, key, value, pos_key, pos_query, prob, g_context,
    tokens_row, rel_table, w_query, w_key, w_value, extra_one, extra_two, vectors,
):
    keys = key.shape[0]
    blocks = keys // BLOCK
    first, last = start == 0, start + pairs == PAIRS
    share = D // cores // shares
    half = pairs * BLOCK
    rows_extra = D if first else RELROWS if last else 0
    pack = (shares, 3 * share + 16 + rows_extra // cores // shares * (D // half), half)
    pair = lambda rows: pl.BlockSpec((rows, BLOCK), lambda p, *_: (0, p + start))
    if first:
        extras = [once(BLOCK, D), once(BLOCK, D)]
        turn = (D, BLOCK)
    else:
        extras = [once(keys, D), once(D, RELROWS)]
        turn = (RELROWS, D)
    if last:
        outs = [((BLOCK, D), F32), ((blocks - 1, BLOCK, D), BF16)]
    else:
        outs = [((keys, D), F32), ((D, RELROWS), F32)]
    return pl.pallas_call(
        functools.partial(backward_kernel, blocks, cores, first, last),
        grid_spec=pltpu.PrefetchScalarGridSpec(
            num_scalar_prefetch=2,
            grid=(pairs,),
            in_specs=[
                pair(BLOCK),
                pair(keys),
                pair(keys),
                pair(RELROWS),
                pair(RELROWS),
                pl.BlockSpec((2, keys, BLOCK), lambda p, *_: (p + start, 0, 0)),
                pair(BLOCK),
                once(keys, D),
                once(RELROWS, D),
                pair(D),
                pair(D),
                pair(D),
            ]
            + extras
            + [pair(8)] * VECTORS,
            out_specs=[once(*pack)] * cores + [once(*shape) for shape, _ in outs],
            scratch_shapes=[
                pltpu.VMEM((keys, 2 * BLOCK), BF16),
                pltpu.VMEM((keys, BLOCK), BF16),
                pltpu.VMEM((keys, BLOCK), BF16),
                pltpu.VMEM((BLOCK, EXT), F32),
                pltpu.VMEM((BLOCK, EXT), F32),
                pltpu.VMEM((D, keys), BF16),
                pltpu.VMEM((D, RELROWS), BF16),
                pltpu.VMEM((keys, D), F32),
                pltpu.VMEM((D, RELROWS), F32),
                pltpu.VMEM(turn, BF16),
                pltpu.VMEM((EXT, BLOCK), BF16),
                pltpu.VMEM((EXT, BLOCK), BF16),
            ],
        ),
        out_shape=[jax.ShapeDtypeStruct(pack, BF16)] * cores
        + [jax.ShapeDtypeStruct(shape, dtype) for shape, dtype in outs],
        compiler_params=pltpu.CompilerParams(vmem_limit_bytes=(24 if keys <= 1024 else 58) * 2**20),
        name="attention_backward",
    )(
        dist, order, *streamed(query, key, value, pos_key, pos_query, prob), g_context,
        *streamed(tokens_row, rel_table, w_query, w_key, w_value), extra_one, extra_two, *vectors,
    )


def column_sum(array):
    return jnp.sum(array, axis=0, keepdims=True)


def middle_forward_kernel(
    blocks,
    place_ref,
    ctx_ref,
    tok_ref,
    cot_ref,
    wout_ref,
    bout_ref,
    gain_one_ref,
    shift_one_ref,
    bdown_ref,
    gain_two_ref,
    shift_two_ref,
    wup_ref,
    bup_ref,
    wdown_ref,
    output_ref,
    feed_ref,
    normal_ref,
    inverse_ref,
    resid_ref,
    slope_ref,
    sums_ref,
    hidden_ref,
    down_ref,
):
    step = pl.program_id(0)

    @pl.when(step == 0)
    def _():
        attn = product(ctx_ref[...], wout_ref[...]) + bout_ref[...]
        normal, inverse = normalized(tok_ref[...].astype(F32) + attn)
        normal_ref[...] = normal
        inverse_ref[...] = jnp.broadcast_to(inverse, inverse_ref.shape)
        hidden = normal * gain_one_ref[...] + shift_one_ref[...]
        hidden_ref[...] = hidden
        feed_ref[:, :D] = hidden.astype(BF16)
        down_ref[...] = jnp.zeros_like(down_ref)

    width = bup_ref.shape[1]
    units = pl.ds(pl.multiple_of(step * width, width), width)
    act, slope = gelu_and_slope(product(feed_ref[:, :D], wup_ref[:, units]) + bup_ref[...])
    slope_ref[...] = slope
    down_ref[...] += product(act.astype(BF16), wdown_ref[units, :])

    @pl.when(step == pl.num_programs(0) - 1)
    def _():
        normal, inverse = normalized(hidden_ref[...] + (down_ref[...] + bdown_ref[...]))
        output_ref[...] = (normal * gain_two_ref[...] + shift_two_ref[...]).astype(BF16)
        position = place_ref[blocks] * BLOCK + lax.broadcasted_iota(jnp.int32, (BLOCK, 1), 0)
        valid = segment_of(position, place_ref, 2 * blocks) < DOCS
        g_out = jnp.where(valid, cot_ref[...].astype(F32), 0.0)
        g_resid, g_gain, g_shift = normalized_back(g_out, normal, inverse, gain_two_ref[...])
        resid_ref[...] = g_resid
        g_down = g_resid.astype(BF16)
        feed_ref[:, D:] = g_down
        sums_ref[0:1, :] = column_sum(g_down.astype(F32))
        sums_ref[1:2, :] = g_gain
        sums_ref[2:3, :] = g_shift


def middle_forward(
    place, context, tokens, cotangent, w_out, b_out, gain_one, shift_one, b_down, gain_two, shift_two,
    w_up, b_up, w_down,
):
    units = w_up.shape[1]
    width = 512
    row = lambda v: v.reshape(1, -1)
    return pl.pallas_call(
        functools.partial(middle_forward_kernel, (place.shape[0] - DOCS) // 2),
        grid_spec=pltpu.PrefetchScalarGridSpec(
        num_scalar_prefetch=1,
        grid=(units // width,),
        in_specs=[once(BLOCK, D)] * 3
        + [pl.BlockSpec(memory_space=pltpu.VMEM)]
        + [once(1, D)] * 6
        + [
            pl.BlockSpec(memory_space=pltpu.VMEM),
            pl.BlockSpec((1, width), lambda p, *_: (0, p)),
            pl.BlockSpec(memory_space=pltpu.VMEM),
        ],
        out_specs=[
            once(BLOCK, D),
            once(BLOCK, 2 * D),
            once(BLOCK, D),
            once(BLOCK, BLOCK),
            once(BLOCK, D),
            pl.BlockSpec((BLOCK, width), lambda p, *_: (0, p)),
            once(8, D),
        ],
        scratch_shapes=[pltpu.VMEM((BLOCK, D), F32), pltpu.VMEM((BLOCK, D), F32)],
        ),
        out_shape=[
            jax.ShapeDtypeStruct((BLOCK, D), BF16),
            jax.ShapeDtypeStruct((BLOCK, 2 * D), BF16),
            jax.ShapeDtypeStruct((BLOCK, D), F32),
            jax.ShapeDtypeStruct((BLOCK, BLOCK), F32),
            jax.ShapeDtypeStruct((BLOCK, D), F32),
            jax.ShapeDtypeStruct((BLOCK, units), F32),
            jax.ShapeDtypeStruct((8, D), F32),
        ],
        compiler_params=pltpu.CompilerParams(vmem_limit_bytes=20 * 2**20),
        name="middle_forward",
    )(
        place, context, tokens, cotangent, w_out, row(b_out), row(gain_one), row(shift_one), row(b_down),
        row(gain_two), row(shift_two), w_up, row(b_up), w_down,
    )


def middle_backward_kernel(
    feed_ref,
    resid_ref,
    normal_ref,
    inverse_ref,
    gain_ref,
    wout_ref,
    slope_ref,
    wup_ref,
    wdown_ref,
    g_resid_ref,
    g_attn_ref,
    g_ctx_ref,
    sums_ref,
    g_up_ref,
    acc_ref,
):
    step = pl.program_id(0)

    @pl.when(step == 0)
    def _():
        acc_ref[...] = resid_ref[...]

    width = slope_ref.shape[1]
    units = pl.ds(pl.multiple_of(step * width, width), width)
    g_up = (product_right(feed_ref[:, D:], wdown_ref[units, :]) * slope_ref[...]).astype(BF16)
    g_up_ref[...] = g_up
    acc_ref[...] += product_right(g_up, wup_ref[:, units])

    @pl.when(step == pl.num_programs(0) - 1)
    def _():
        g_resid, g_gain, g_shift = normalized_back(
            acc_ref[...], normal_ref[...], inverse_ref[:, 0:1], gain_ref[...]
        )
        g_resid_ref[...] = g_resid
        g_attn = g_resid.astype(BF16)
        g_attn_ref[...] = g_attn
        g_ctx_ref[...] = product_right(g_attn, wout_ref[...]).astype(BF16)
        sums_ref[0:1, :] = column_sum(g_attn.astype(F32))
        sums_ref[1:2, :] = g_gain
        sums_ref[2:3, :] = g_shift


def middle_backward(feed, g_resid_two, normal, inverse, gain_one, w_out, slope, w_up, w_down):
    units = w_up.shape[1]
    width = 512
    return pl.pallas_call(
        middle_backward_kernel,
        grid=(units // width,),
        in_specs=[
            once(BLOCK, 2 * D),
            once(BLOCK, D),
            once(BLOCK, D),
            once(BLOCK, BLOCK),
            once(1, D),
            pl.BlockSpec(memory_space=pltpu.VMEM),
            pl.BlockSpec((BLOCK, width), lambda p: (0, p)),
            pl.BlockSpec(memory_space=pltpu.VMEM),
            pl.BlockSpec(memory_space=pltpu.VMEM),
        ],
        out_specs=[
            once(BLOCK, D),
            once(BLOCK, D),
            once(BLOCK, D),
            once(8, D),
            pl.BlockSpec((BLOCK, width), lambda p: (0, p)),
        ],
        scratch_shapes=[pltpu.VMEM((BLOCK, D), F32)],
        out_shape=[
            jax.ShapeDtypeStruct((BLOCK, D), F32),
            jax.ShapeDtypeStruct((BLOCK, D), BF16),
            jax.ShapeDtypeStruct((BLOCK, D), BF16),
            jax.ShapeDtypeStruct((8, D), F32),
            jax.ShapeDtypeStruct((BLOCK, units), BF16),
        ],
        compiler_params=pltpu.CompilerParams(vmem_limit_bytes=20 * 2**20),
        name="middle_backward",
    )(
        feed, g_resid_two, normal, inverse, gain_one.reshape(1, -1), w_out, slope,
        w_up, w_down,
    )


def gelu_and_slope(x):
    below = 0.5 + 0.5 * lax.erf(x * math.sqrt(0.5))
    density = jnp.exp(-0.5 * x * x) * (1.0 / math.sqrt(2.0 * math.pi))
    return x * below, below + x * density


def feedforward_kernel(
    parts,
    order_ref,
    *refs,
):
    part_refs, refs = refs[:parts], refs[parts:]
    wup_ref, bup_ref, wdown_ref, down_own_ref, down_other_ref, up_own_ref, up_other_ref, *refs = refs
    hid_ref, gd_ref, hidt_ref, sums_ref = refs
    step = pl.program_id(0)
    shares = up_own_ref.shape[0]
    half = down_own_ref.shape[1]
    width = wup_ref.shape[1]

    @pl.when(step == 0)
    def _():
        for part in range(parts):
            rows = slice(part * BLOCK, (part + 1) * BLOCK)
            hid_ref[rows, :] = part_refs[part][:, :D]
            gd_ref[rows, :] = part_refs[part][:, D:]
        place_rows(order_ref, hidt_ref, hid_ref[...].T, 2, shares)

    lanes = pl.ds(pl.multiple_of(step * width, width), width)
    act, slope = gelu_and_slope(product(hid_ref[...], wup_ref[...]) + bup_ref[...])
    g_up = (product_right(gd_ref[...], wdown_ref[...]) * slope).astype(BF16)
    act_turned = act.astype(BF16).T
    for core, ref in enumerate((down_own_ref, down_other_ref)):
        columns = pl.ds(pl.multiple_of((order_ref[0] ^ core) * half, BLOCK), half)
        ref[lanes, :] = product(act_turned, gd_ref[:, columns]).astype(BF16)
    store_pieces((up_own_ref, up_other_ref), 0, product(hidt_ref[...], g_up).astype(BF16), lanes)
    sums_ref[:, lanes] = product(jnp.ones((16, hid_ref.shape[0]), BF16), g_up)

    @pl.when(step == pl.num_programs(0) - 1)
    def _():
        for core, ref in enumerate((down_own_ref, down_other_ref)):
            columns = pl.ds(pl.multiple_of((order_ref[0] ^ core) * half, BLOCK), half)
            ref[pl.ds(sums_ref.shape[1], 16), :] = sums_ref[:, columns].astype(BF16)


def feedforward_gradients(order, row_parts, w_up, b_up, w_down):
    shares = len(row_parts)
    tokens = shares * BLOCK
    units = w_up.shape[1] // shares
    width = 256
    steps = units // width
    down = (units + 16, D // 2)
    up = (shares, D // shares // 2, units)
    return pl.pallas_call(
        functools.partial(feedforward_kernel, shares),
        grid_spec=pltpu.PrefetchScalarGridSpec(
            num_scalar_prefetch=1,
            grid=(steps,),
            in_specs=[once(BLOCK, 2 * D)] * shares
            + [
                pl.BlockSpec((D, width), lambda p, order: (0, order[1] * steps + p)),
                pl.BlockSpec((1, width), lambda p, order: (0, order[1] * steps + p)),
                pl.BlockSpec((width, D), lambda p, order: (order[1] * steps + p, 0)),
            ],
            out_specs=[once(*down), once(*down), once(*up), once(*up)],
            scratch_shapes=[
                pltpu.VMEM((tokens, D), BF16),
                pltpu.VMEM((tokens, D), BF16),
                pltpu.VMEM((D, tokens), BF16),
                pltpu.VMEM((16, units), F32),
            ],
        ),
        out_shape=[jax.ShapeDtypeStruct(shape, BF16) for shape in (down, down, up, up)],
        compiler_params=pltpu.CompilerParams(vmem_limit_bytes=16 * 2**20),
        name="feedforward_gradients",
    )(order, *row_parts, *streamed(w_up), b_up, *streamed(w_down))


def swapped(array, axis, bits):
    return lax.ppermute(array, axis, [(i, i ^ bits) for i in range(lax.axis_size(axis))])


def from_peers(arrays):
    return [swapped(array, "seq", bits) for bits, array in enumerate(arrays, 1)]


def picked(array, index, axis):
    return lax.dynamic_index_in_dim(array, index, axis, keepdims=False)


def together(*arrays):
    return lax.optimization_barrier(arrays)


def added(*arrays):
    return functools.reduce(jnp.add, [array.astype(F32) for array in arrays]).astype(BF16)


def halves(pack):
    middle = pack.shape[1] // 32 * 16
    return pack[:, :middle], pack[:, middle:]


def in_row_order(pack, mine):
    return jnp.stack([picked(pack, mine ^ at, 0) for at in range(4)], axis=0)


def square_mesh():
    return lax.axis_size("seq") == 4 and lax.axis_size("z") == 4


def scatter(pack):
    return from_peers([pack[1], pack[2], pack[3]])


def inward(share):
    return lax.ppermute(share, "z", [(0, 1), (3, 2)])


def across(share):
    return lax.ppermute(share, "z", [(1, 2), (2, 1)])


def outward(share):
    return lax.ppermute(share, "z", [(1, 0), (2, 3)])


def settled(share, got):
    at_z = lax.axis_index("z")
    return jnp.where((at_z == 1) | (at_z == 2), share, got)


def core_index():
    return lax.axis_index("core")


def both_cores(share, axis):
    other = swapped(share, "core", 1)
    first = core_index() == 0
    return jnp.concatenate(
        [jnp.where(first, share, other), jnp.where(first, other, share)], axis=axis
    )


def reduce_plain(partial):
    share = lax.psum_scatter(partial.astype(BF16), "seq", scatter_dimension=0, tiled=True)
    return lax.psum(share, ("z", "core")).astype(F32)


def local(
    tokens,
    cotangent,
    lengths,
    w_query,
    b_query,
    w_key,
    b_key,
    w_value,
    b_value,
    w_out,
    b_out,
    gain_one,
    shift_one,
    w_up,
    b_up,
    w_down,
    b_down,
    gain_two,
    shift_two,
    rel_table,
):
    rows = tokens.shape[0]
    cycle = lax.axis_size("seq")
    mine = lax.axis_index("seq")
    core = core_index()
    square = square_mesh()
    hidden_units = w_up.shape[1]
    share = D // cycle
    if square:
        token_parts = [tokens] + from_peers([tokens] * 3)
        ids = mine ^ jnp.arange(cycle, dtype=jnp.int32)
        order = jnp.stack([core, mine]).astype(jnp.int32)
        cores = 2
    else:
        token_parts = [tokens, lax.all_gather(tokens, "seq", axis=0, tiled=True)]
        ids = jnp.concatenate([mine[None], jnp.arange(cycle, dtype=jnp.int32)])
        order = jnp.zeros((2,), jnp.int32)
        cores = 1
    dist = jnp.concatenate([mine - ids, ids, lengths[0]]).astype(jnp.int32)

    places = jnp.arange(RELROWS, dtype=jnp.int32)
    turn = (places[:, None] + places[None, :] == RELROWS - 1).astype(BF16)
    rel_back = product(turn, rel_table).astype(BF16)
    pos_key_back = (product(rel_back, w_key) + b_key).astype(BF16)
    pos_query_back = (product(rel_back, w_query) + b_query).astype(BF16)
    pos_query = (product(rel_table, w_query) + b_query).astype(BF16)
    context, prob, query, key, value, tokens_row, *held = attention_forward(
        dist,
        token_parts,
        [w_query, w_key, w_value],
        [v[None] for v in (b_query, b_key, b_value)],
        pos_key_back,
        pos_query_back,
        [w_up, w_down, w_out],
    )
    held_up, held_down, held_out = held

    output, feed, normal_one, inverse_one, g_resid_two, slope, sums_two = middle_forward(
        dist, context, tokens, cotangent, held_out, b_out, gain_one, shift_one, b_down, gain_two,
        shift_two, held_up, b_up, held_down,
    )
    if square:
        row_parts = [feed] + from_peers([feed] * 3)
    g_resid_one, g_attn, g_context, sums_one, g_up = middle_backward(
        feed, g_resid_two, normal_one, inverse_one, gain_one, held_out, slope, held_up, held_down
    )
    vectors = [sums_one, sums_two]

    def backward(start, pairs, g_context, extra_one, extra_two):
        outs = attention_backward(
            start, pairs, cores, cycle, dist, order, query, key, value, pos_key_back, pos_query, prob,
            g_context, tokens_row, rel_table, w_query, w_key, w_value, extra_one, extra_two, vectors,
        )
        return outs[:cores], outs[cores:]

    piece = share // cores
    whole_rows = lambda v, at, each: v[:, at : at + each].reshape(cores * each, -1)

    def unpacked(v, each):
        base = 3 * piece + 16
        parts = D // v.shape[2]
        return jnp.concatenate(
            [whole_rows(v, base + part * each, each) for part in range(parts)], axis=1
        )

    def rel_pieces(pack):
        part = unpacked(pack, RELROWS // cycle // cores)
        if square:
            return [part] + from_peers([part] * 3)
        return [lax.all_gather(part, "seq", axis=0, tiled=True)]

    def assembled(packs, rel_parts, grad_tokens, grad_w_up, grad_w_down, grad_b_up):
        grads = [
            jnp.concatenate([whole_rows(v, at * piece, piece) for v in packs], axis=1).astype(F32)
            for at in range(3)
        ]
        base = 3 * piece
        vector_sums = jnp.concatenate([v[0, base : base + 16] for v in packs], axis=1).astype(F32)
        grad_w_out = unpacked(packs[0], piece).astype(F32)
        if square:
            grad_rel = jnp.zeros((RELROWS, D), F32)
            for bits, part in enumerate(rel_parts):
                grad_rel = lax.dynamic_update_slice_in_dim(
                    grad_rel, part.astype(F32), (mine ^ bits) * (RELROWS // cycle), 0
                )
        else:
            grad_rel = rel_parts[0].astype(F32)
        vector_share = lax.dynamic_slice_in_dim(vector_sums, mine * share, share, 1)
        return (
            output,
            grad_tokens,
            grads[0],
            vector_share[0],
            grads[1],
            vector_share[1],
            grads[2],
            vector_share[2],
            grad_w_out,
            vector_share[3],
            vector_share[4],
            vector_share[5],
            grad_w_up,
            grad_b_up,
            grad_w_down,
            vector_share[6],
            vector_share[7],
            vector_share[8],
            grad_rel,
        )

    if not square:
        act = gelu_and_slope(product(feed[:, :D], w_up) + b_up)[0].astype(BF16)
        (one,), carried = backward(0, 3, g_context, context, g_attn)
        (two,), (home, away) = backward(3, 3, g_context, *carried)
        packs = [
            lax.psum(lax.psum_scatter(v, "seq", scatter_dimension=0, tiled=True), ("z", "core"))
            for v in (one, two)
        ]
        got = lax.psum_scatter(away, "seq", scatter_dimension=0, tiled=False)
        return assembled(
            packs,
            rel_pieces(packs[-1]),
            g_resid_one + home + got.astype(F32),
            reduce_plain(product_left(feed[:, :D], g_up)),
            reduce_plain(product_left(act, feed[:, D:])),
            reduce_plain(jnp.sum(g_up.astype(F32), axis=0)),
        )

    one, carried = backward(0, 3, g_context, context, g_attn)

    row_parts, one, carried = together(row_parts, one, carried)
    one_got = swapped(one[1], "core", 1)
    down_own, down_other, up_own, up_other = feedforward_gradients(
        order, row_parts, w_up, b_up[None], w_down
    )

    one_got, down_own, down_other, up_own, up_other = together(
        one_got, down_own, down_other, up_own, up_other
    )
    down_got = swapped(down_other, "core", 1)
    up_got = swapped(up_other, "core", 1)
    one_share = added(one[0], one_got)
    down_share = added(down_own, down_got)
    up_share = added(up_own, up_got)
    down_got = inward(down_share)
    one_first, one_second = halves(one_share)
    one_first_got = swapped(one_first[1::2], "seq", 1)
    one_second_got = swapped(one_second[2:], "seq", 2)
    g_context, down_share, up_share, one_share = together(g_context, down_share, up_share, one_share)
    two, (home, away) = backward(3, 3, g_context, *carried)

    units = hidden_units // 4
    two, home, away, one_first_got, one_second_got, down_got = together(
        two, home, away, one_first_got, one_second_got, down_got
    )
    two_got = swapped(two[1], "core", 1)
    down_share = added(down_share, down_got)
    down_got = across(down_share)
    up_got = inward(up_share)

    two_got, down_share = together(two_got, down_share)
    two_share = added(two[0], two_got)
    two_first, two_second = halves(two_share)
    two_first_got = swapped(two_first[1::2], "seq", 1)
    two_second_got = swapped(two_second[2:], "seq", 2)

    two_first_got, two_second_got = together(two_first_got, two_second_got)
    two_first = added(two_first[0::2], two_first_got)
    two_second = added(two_second[:2], two_second_got)
    two_first_got = swapped(two_first[1], "seq", 2)
    two_second_got = swapped(two_second[1], "seq", 1)
    one_first = added(one_first[0::2], one_first_got)
    one_second = added(one_second[:2], one_second_got)

    two_first_got, two_second_got, down_got, up_got, one_first, one_second = together(
        two_first_got, two_second_got, down_got, up_got, one_first, one_second
    )
    two_share = jnp.concatenate(
        [added(two_first[0], two_first_got), added(two_second[0], two_second_got)], axis=0
    )
    two_got = inward(two_share)
    down_share = added(down_share, down_got)
    down_got = outward(down_share)
    up_share = added(up_share, up_got)
    up_got = across(up_share)
    one_first_got = swapped(one_first[1], "seq", 2)
    one_second_got = swapped(one_second[1], "seq", 1)

    two_got, one_first_got, one_second_got = together(two_got, one_first_got, one_second_got)
    two_share = added(two_share, two_got)
    two_got = across(two_share)
    one_share = jnp.concatenate(
        [added(one_first[0], one_first_got), added(one_second[0], one_second_got)], axis=0
    )
    one_got = inward(one_share)

    up_got, down_got, away = together(up_got, down_got, away)
    up_share = added(up_share, up_got)
    up_got = outward(up_share)
    down_share = both_cores(settled(down_share, down_got), 1)

    two_got, one_got, down_share, away = together(two_got, one_got, down_share, away)
    two_share = added(two_share, two_got)
    two_got = outward(two_share)
    one_share = added(one_share, one_got)
    one_got = across(one_share)
    grad_w_down = down_share[:units].astype(F32)
    grad_b_up = down_share[units].astype(F32)
    home_got = from_peers([away[0], away[1], away[2]])

    up_got, home_got, grad_w_down = together(up_got, home_got, grad_w_down)
    up_share = settled(up_share, up_got)
    up_got = scatter(up_share)
    grad_tokens = g_resid_one + functools.reduce(jnp.add, [v.astype(F32) for v in home_got], home)

    one_got, two_got, up_got, grad_tokens = together(one_got, two_got, up_got, grad_tokens)
    two_share = both_cores(settled(two_share, two_got)[None], 0)
    one_share = added(one_share, one_got)
    one_got = outward(one_share)
    rel_parts = rel_pieces(two_share)
    up_share = both_cores(jnp.stack([up_share[0]] + up_got, axis=0), 1).reshape(4, share, -1)
    grad_w_up = jnp.zeros((share, hidden_units), F32)
    for bits in range(4):
        grad_w_up = lax.dynamic_update_slice_in_dim(
            grad_w_up, up_share[bits].astype(F32), (mine ^ bits) * units, 1
        )
    one_share = both_cores(settled(one_share, one_got)[None], 0)
    return assembled(
        [one_share, two_share],
        rel_parts,
        grad_tokens,
        grad_w_up,
        grad_w_down,
        grad_b_up,
    )


def solution(mesh):
    lines, cycle = mesh.devices.shape
    chips = Mesh(mesh.devices.reshape(lines // 2, 2, cycle), ("z", "core", "seq"))
    return jax.shard_map(
        local,
        mesh=chips,
        in_specs=(
            P(("z", "core", "seq"), None),
            P(("z", "core", "seq"), None),
            P(("z", "core"), None),
        )
        + (P(),) * 17,
        out_specs=(
            P(("z", "core", "seq"), None),
            P(("z", "core", "seq"), None),
            P("seq", None),
            P("seq"),
            P("seq", None),
            P("seq"),
            P("seq", None),
            P("seq"),
            P("seq", None),
            P("seq"),
            P("seq"),
            P("seq"),
            P("seq", None),
            P("seq"),
            P("seq", None),
            P("seq"),
            P("seq"),
            P("seq"),
            P(),
        ),
        check_vma=False,
    )
```

```python
import functools
import math

import jax
import jax.numpy as jnp
from jax import lax
from jax.experimental import pallas as pl
from jax.experimental.pallas import tpu as pltpu
from jax.sharding import Mesh, PartitionSpec as P

D = 768
HEADS = 12
HEAD = 64
SPAN = 256
RELROWS = 512
BLOCK = 128
EXT = RELROWS + 2 * SPAN
PAIRS = HEADS // 2
VECTORS = 2
LATER = 3
DOCS = 4
SCALE = 1.0 / math.sqrt(3 * HEAD)
F32 = jnp.float32
BF16 = jnp.bfloat16
ROLLED = BF16


def normalized(resid):
    center = resid - jnp.mean(resid, axis=-1, keepdims=True)
    inverse = lax.rsqrt(jnp.mean(center * center, axis=-1, keepdims=True) + 1e-07)
    return center * inverse, inverse


def normalized_back(grad, normal, inverse, gain):
    hat = grad * gain
    means = jnp.mean(hat, axis=-1, keepdims=True) + normal * jnp.mean(
        hat * normal, axis=-1, keepdims=True
    )
    total = lambda v: jnp.sum(v, axis=0, keepdims=True)
    return (hat - means) * inverse, total(grad * normal), total(grad)


def product(left, right):
    return jnp.dot(left, right, preferred_element_type=F32)


def product_left(left, right):
    return lax.dot_general(left, right, (((0,), (0,)), ((), ())), preferred_element_type=F32)


def product_right(left, right):
    return lax.dot_general(left, right, (((1,), (1,)), ((), ())), preferred_element_type=F32)


def segment_of(position, place_ref, at):
    passed, bound = jnp.zeros(position.shape, jnp.int32), 0
    for document in range(DOCS):
        bound = bound + place_ref[at + document]
        passed = passed + (position >= bound).astype(jnp.int32)
    return passed


def anti_identity():
    rows = lax.broadcasted_iota(jnp.int32, (BLOCK, BLOCK), 0)
    cols = lax.broadcasted_iota(jnp.int32, (BLOCK, BLOCK), 1)
    return (rows + cols == BLOCK - 1).astype(BF16)


def extend(ext_ref, table_ref):
    ext_ref[SPAN : SPAN + RELROWS, :] = table_ref[...]
    ext_ref[0:SPAN, :] = jnp.broadcast_to(table_ref[0:1, :], (SPAN, BLOCK))
    last = table_ref[RELROWS - 1 : RELROWS, :]
    ext_ref[SPAN + RELROWS :, :] = jnp.broadcast_to(last, (SPAN, BLOCK))


def window_start(offset):
    return pl.multiple_of(jnp.clip(offset, 0, EXT - 2 * BLOCK), BLOCK)


def head_mask(head):
    lane = lax.broadcasted_iota(jnp.int32, (1, BLOCK), 1)
    return (lane >= head * HEAD) & (lane < (head + 1) * HEAD)


def band_roll(wide, shift):
    return pltpu.roll(wide, shift, 1, stride=1, stride_axis=0)


def by_head(pair):
    zero = jnp.zeros_like(pair)
    return jnp.concatenate([jnp.where(head_mask(head), pair, zero) for head in range(2)], axis=0)


def forward_kernel(
    parts, blocks, dist_ref, *refs
):
    part_refs, refs = refs[:parts], refs[parts:]
    wq_ref, wk_ref, wv_ref, bq_ref, bk_ref, bv_ref, pk_ref, pq_ref, *refs = refs
    later, refs = refs[:LATER], refs[LATER:]
    ctx_ref, prob_ref, q_ref, k_ref, v_ref, tok_ref, *refs = refs
    held, refs = refs[:LATER], refs[LATER:]
    score_ref, ek_ref, eq_ref, bias_ref, sems = refs
    copies = [
        pltpu.make_async_copy(later[at], held[at], sems.at[at]) for at in range(LATER)
    ]

    @pl.when(pl.program_id(0) == 0)
    def _():
        for copy in copies:
            copy.start()

    @pl.when(pl.program_id(0) == pl.num_programs(0) - 1)
    def _():
        for copy in copies:
            copy.wait()

    extend(ek_ref, pk_ref)
    extend(eq_ref, pq_ref)

    @pl.when(pl.program_id(0) == 0)
    def _():
        at = 0
        for ref in part_refs:
            tok_ref[at : at + ref.shape[0], :] = ref[...]
            at += ref.shape[0]
        mine = dist_ref[blocks]
        lane = lax.broadcasted_iota(jnp.int32, (1, BLOCK), 1)
        line = lax.broadcasted_iota(jnp.int32, (BLOCK, 1), 0)
        query_segment = segment_of(mine * BLOCK + lane, dist_ref, 2 * blocks)
        for block in range(blocks):
            home = dist_ref[blocks + block]
            allowed = segment_of(home * BLOCK + line, dist_ref, 2 * blocks) == query_segment
            if block > 0:
                allowed = jnp.logical_and(allowed, home != mine)
            rows = slice(block * BLOCK, (block + 1) * BLOCK)
            bias_ref[rows, :] = jnp.where(allowed, 0.0, -1e30)

    both = product(tok_ref[...], jnp.concatenate([wk_ref[...], wv_ref[...]], axis=1))
    k_ref[...] = (both[:, :BLOCK] + bk_ref[...]).astype(BF16)
    v_ref[...] = (both[:, BLOCK:] + bv_ref[...]).astype(BF16)
    q = (product(tok_ref[:BLOCK, :], wq_ref[...]) + bq_ref[...]).astype(BF16)
    q_ref[...] = q
    q_heads = by_head(q)
    tops = [jnp.full((1, BLOCK), -jnp.inf, F32) for head in range(2)]
    for block in range(blocks):
        dist = dist_ref[block]
        rows = slice(block * BLOCK, (block + 1) * BLOCK)
        k_heads = by_head(k_ref[rows, :])
        window_c = ek_ref[pl.ds(window_start(384 - dist * BLOCK), 2 * BLOCK), :]
        window_p = eq_ref[pl.ds(window_start(384 + dist * BLOCK), 2 * BLOCK), :]
        c2p = product_right(q_heads, window_c)
        p2c = product_right(k_heads, window_p)
        direct = product_right(k_heads, q)
        for head in range(2):
            own = slice(head * BLOCK, (head + 1) * BLOCK)
            first = band_roll(c2p[own].astype(BF16), BLOCK + 1)[:, :BLOCK].T
            second = band_roll(p2c[own].astype(BF16), BLOCK + 1)[:, :BLOCK]
            score = (direct[own] + first.astype(F32) + second.astype(F32)) * SCALE + bias_ref[rows, :]
            score_ref[head, rows, :] = score
            tops[head] = jnp.maximum(tops[head], jnp.max(score, axis=0, keepdims=True))
    probs = []
    for head in range(2):
        weight = jnp.exp(score_ref[head] - tops[head])
        total = jnp.sum(weight, axis=0, keepdims=True)
        prob = (weight * (1.0 / total)).astype(BF16)
        prob_ref[head] = prob
        probs.append(prob)
    v = v_ref[...]
    zero = jnp.zeros_like(v)
    out = product_left(probs[0], jnp.where(head_mask(0), v, zero)) + product_left(
        probs[1], jnp.where(head_mask(1), v, zero)
    )
    ctx_ref[...] = out.astype(BF16)


def streamed(*arrays):
    return [pltpu.with_memory_space_constraint(array, pltpu.HBM) for array in arrays]


def once(*shape):
    return pl.BlockSpec(shape, lambda p, *_: (0,) * len(shape), pipeline_mode=pl.Buffered(1))


def fits(keys):
    return keys <= 2 * RELROWS


def kept(keys, *shape):
    return pl.BlockSpec(memory_space=pltpu.VMEM) if fits(keys) else once(*shape)


def kept_array(keys, shape, dtype):
    return (pltpu.VMEM if fits(keys) else jax.ShapeDtypeStruct)(shape, dtype)


def attention_forward(dist, token_parts, weights, biases, pos_key, pos_query, later):
    keys = sum(part.shape[0] for part in token_parts)
    blocks = keys // BLOCK
    pair = lambda rows: pl.BlockSpec((rows, BLOCK), lambda p, dist: (0, p))
    return pl.pallas_call(
        functools.partial(forward_kernel, len(token_parts), blocks),
        grid_spec=pltpu.PrefetchScalarGridSpec(
            num_scalar_prefetch=1,
            grid=(PAIRS,),
            in_specs=[once(*part.shape) for part in token_parts]
            + [pair(D)] * 3
            + [pair(1)] * 3
            + [pair(RELROWS), pair(RELROWS)]
            + [pl.BlockSpec(memory_space=pl.ANY)] * LATER,
            out_specs=[
                pair(BLOCK),
                pl.BlockSpec((2, keys, BLOCK), lambda p, dist: (p, 0, 0)),
                pair(BLOCK),
                pair(keys),
                pair(keys),
                kept(keys, keys, D),
            ]
            + [pl.BlockSpec(memory_space=pl.ANY)] * LATER,
            scratch_shapes=[
                pltpu.VMEM((2, keys, BLOCK), F32),
                pltpu.VMEM((EXT, BLOCK), BF16),
                pltpu.VMEM((EXT, BLOCK), BF16),
                pltpu.VMEM((keys, BLOCK), F32),
                pltpu.SemaphoreType.DMA((LATER,)),
            ],
        ),
        out_shape=[
            jax.ShapeDtypeStruct((BLOCK, D), BF16),
            pltpu.HBM((HEADS, keys, BLOCK), BF16),
            pltpu.HBM((BLOCK, D), BF16),
            pltpu.HBM((keys, D), BF16),
            pltpu.HBM((keys, D), BF16),
            kept_array(keys, (keys, D), BF16),
        ]
        + [pltpu.VMEM(array.shape, array.dtype) for array in later],
        compiler_params=pltpu.CompilerParams(vmem_limit_bytes=(16 if fits(keys) else 40) * 2**20),
        name="attention_forward",
    )(dist, *token_parts, *streamed(*weights), *biases, *streamed(pos_key, pos_query), *streamed(*later))


def fold_edges(acc_ref):
    head_sum = jnp.sum(acc_ref[:, 0:SPAN], axis=1, keepdims=True)
    tail_sum = jnp.sum(acc_ref[:, SPAN + RELROWS :], axis=1, keepdims=True)
    lane = lax.broadcasted_iota(jnp.int32, (BLOCK, RELROWS), 1)
    middle = acc_ref[:, SPAN : SPAN + RELROWS]
    middle = middle + jnp.where(lane == 0, head_sum, 0.0)
    return (middle + jnp.where(lane == RELROWS - 1, tail_sum, 0.0)).astype(BF16)


def flipped_lanes(array, flip):
    parts = array.shape[1] // BLOCK
    return jnp.concatenate(
        [
            product(array[:, part * BLOCK : (part + 1) * BLOCK], flip).astype(BF16)
            for part in reversed(range(parts))
        ],
        axis=1,
    )


def place(order_ref, share, core, shares, each):
    at = (core ^ order_ref[0]) * shares + (share ^ order_ref[1])
    return pl.multiple_of(at * each, 16)


def place_rows(order_ref, into_ref, value, cores, shares):
    each = value.shape[0] // (cores * shares)
    for share in range(shares):
        for core in range(cores):
            at = (share * cores + core) * each
            into_ref[pl.ds(place(order_ref, share, core, shares, each), each), :] = value[
                at : at + each
            ]


def store_pieces(refs, at, value, lanes):
    shares = refs[0].shape[0]
    each = value.shape[0] // (len(refs) * shares)
    for core, ref in enumerate(refs):
        for share in range(shares):
            start = (core * shares + share) * each
            ref[share, at : at + each, lanes] = value[start : start + each]


def backward_kernel(
    blocks,
    cores,
    first,
    last,
    dist_ref,
    order_ref,
    q_ref,
    k_ref,
    v_ref,
    pk_ref,
    pq_ref,
    prob_ref,
    gctx_ref,
    tok_ref,
    rel_ref,
    wq_ref,
    wk_ref,
    wv_ref,
    extra_one_ref,
    extra_two_ref,
    *refs,
):
    vec_refs, refs = refs[:VECTORS], refs[VECTORS:]
    pack_refs, refs = refs[:cores], refs[cores:]
    backward_body(
        blocks, first, last, dist_ref, order_ref, q_ref, k_ref, v_ref, pk_ref, pq_ref, prob_ref, gctx_ref,
        tok_ref, rel_ref, wq_ref, wk_ref, wv_ref, extra_one_ref, extra_two_ref, vec_refs, pack_refs, *refs
    )


def backward_body(
    blocks,
    first,
    last,
    dist_ref,
    order_ref,
    q_ref,
    k_ref,
    v_ref,
    pk_ref,
    pq_ref,
    prob_ref,
    gctx_ref,
    tok_ref,
    rel_ref,
    wq_ref,
    wk_ref,
    wv_ref,
    extra_one_ref,
    extra_two_ref,
    vec_refs,
    pack_refs,
    out_one_ref,
    out_two_ref,
    back_ref,
    gk_ref,
    gv_ref,
    acck_ref,
    accq_ref,
    tokt_ref,
    relt_ref,
    acc_tok_ref,
    acc_rel_ref,
    turn_ref,
    ek_ref,
    eq_ref,
):
    step = pl.program_id(0)
    if not last:
        acc_tok_ref, acc_rel_ref = out_one_ref, out_two_ref
    extend(ek_ref, pk_ref)
    extend(eq_ref, pq_ref)
    cores, shares, half = len(pack_refs), pack_refs[0].shape[0], pack_refs[0].shape[2]
    share = D // cores // shares
    flip = anti_identity()

    @pl.when(step == 0)
    def _():
        place_rows(order_ref, tokt_ref, tok_ref[...].T, cores, shares)
        place_rows(order_ref, relt_ref, rel_ref[...].T, cores, shares)
        if first:
            acc_tok_ref[...] = jnp.zeros_like(acc_tok_ref)
            acc_rel_ref[...] = jnp.zeros_like(acc_rel_ref)
        else:
            acc_tok_ref[...] = extra_one_ref[...]
            acc_rel_ref[...] = extra_two_ref[...]

    acck_ref[...] = jnp.zeros_like(acck_ref)
    accq_ref[...] = jnp.zeros_like(accq_ref)
    g_heads = by_head(gctx_ref[...])
    first_rows = lax.broadcasted_iota(jnp.int32, (BLOCK, 1), 0) < HEAD
    first_lanes = head_mask(0)

    def turned_heads(array):
        turned = array.T
        zero = jnp.zeros_like(turned)
        return jnp.concatenate(
            [jnp.where(first_rows, turned, zero), jnp.where(first_rows, zero, turned)], axis=1
        )

    def of_heads(stacked):
        return jnp.where(first_lanes, stacked[:BLOCK], stacked[BLOCK:])

    q_back = product(flip, q_ref[...]).astype(BF16)
    q_turned = turned_heads(q_back)
    probs = jnp.concatenate([prob_ref[head] for head in range(2)], axis=1)
    g_prob = product_right(v_ref[...], g_heads)
    gv_ref[...] = product(probs, g_heads).astype(BF16)
    probs = probs.astype(F32)
    delta = jnp.sum(probs * g_prob, axis=0, keepdims=True)
    g_score = (probs * (g_prob - delta) * SCALE).astype(BF16)
    for head in range(2):
        lanes = slice(head * BLOCK, (head + 1) * BLOCK)
        back_ref[:, lanes] = product(g_score[:, lanes], flip).astype(BF16)
    g_query = jnp.zeros((2 * BLOCK, BLOCK), F32)
    pad = jnp.zeros((BLOCK, BLOCK), BF16)
    for block in range(blocks):
        rows = slice(block * BLOCK, (block + 1) * BLOCK)
        k_block = k_ref[rows, :]
        at = pl.ds(window_start(384 - dist_ref[block] * BLOCK), 2 * BLOCK)
        window_c = ek_ref[at, :]
        window_p = eq_ref[at, :]
        backs = [back_ref[rows, head * BLOCK : (head + 1) * BLOCK] for head in range(2)]
        turns = [back.T for back in backs]
        bands_c = [band_roll(jnp.concatenate([turn, pad], axis=1), 0) for turn in turns]
        bands_p = [band_roll(jnp.concatenate([back, pad], axis=1), 1) for back in backs]
        bands_c = jnp.concatenate(bands_c, axis=0)
        bands_p = jnp.concatenate(bands_p, axis=0)
        g_query = g_query + product(
            jnp.concatenate([jnp.concatenate(turns, axis=0), bands_c], axis=1),
            jnp.concatenate([k_block, window_c], axis=0),
        )
        g_key = product(
            jnp.concatenate([jnp.concatenate(backs, axis=0), bands_p], axis=1),
            jnp.concatenate([q_back, window_p], axis=0),
        )
        gk_ref[rows, :] = of_heads(g_key).astype(BF16)
        acck_ref[:, at] += product(q_turned, bands_c)
        accq_ref[:, at] += product(turned_heads(k_block), bands_p)

    g_query = product(flip, of_heads(g_query).astype(BF16)).astype(BF16)
    g_pos_key = flipped_lanes(fold_edges(acck_ref), flip)
    g_pos_query = fold_edges(accq_ref)
    g_key = gk_ref[...]
    g_value = gv_ref[...]
    lanes = pl.ds(pl.multiple_of(step * BLOCK, BLOCK), BLOCK)
    ones_tok = jnp.ones((16, tok_ref.shape[0]), BF16)
    ones_rel = jnp.ones((16, RELROWS), BF16)
    row = lax.broadcasted_iota(jnp.int32, (16, BLOCK), 0)
    vec = jnp.zeros((16, BLOCK), F32)
    for at, vec_ref in enumerate(vec_refs):
        for part in range(3):
            vec = vec + jnp.where(row == 3 + 3 * at + part, vec_ref[part : part + 1, :], 0.0)
    g_both = jnp.concatenate([g_key, g_value], axis=1)
    pos_both = jnp.concatenate([g_pos_key, g_pos_query], axis=0)
    from_tok = product(tokt_ref[...], g_both)
    from_rel = product_right(relt_ref[...], pos_both)
    from_own = product(tokt_ref[:, :BLOCK], g_query)
    sum_tok = product(ones_tok, g_both)
    sum_rel = product_right(ones_rel, pos_both)
    sum_own = product(ones_tok[:, :BLOCK], g_query)
    weights = [
        (from_own + from_rel[:, BLOCK:], sum_own + sum_rel[:, BLOCK:]),
        (from_tok[:, :BLOCK] + from_rel[:, :BLOCK], sum_tok[:, :BLOCK] + sum_rel[:, :BLOCK]),
        (from_tok[:, BLOCK:], sum_tok[:, BLOCK:]),
    ]
    for at, (weight, total) in enumerate(weights):
        store_pieces(pack_refs, at * share, weight.astype(BF16), lanes)
        vec = vec + jnp.where(row == at, total, 0.0)
    vec = vec.astype(BF16)
    for pack_ref in pack_refs:
        for part in range(shares):
            pack_ref[part, 3 * share : 3 * share + 16, lanes] = vec
    acc_tok_ref[...] += product_right(
        g_both,
        jnp.concatenate([wk_ref[...], wv_ref[...]], axis=1),
    )
    acc_tok_ref[0:BLOCK, :] += product_right(g_query, wq_ref[...])
    acc_rel_ref[...] += product(
        jnp.concatenate([wk_ref[...], wq_ref[...]], axis=1),
        pos_both,
    )

    @pl.when(step == pl.num_programs(0) - 1)
    def _():
        base = 3 * share + 16
        extra = None
        if last:
            out_one_ref[...] = acc_tok_ref[0:BLOCK, :]
            for block in range(1, blocks):
                out_two_ref[block - 1] = acc_tok_ref[block * BLOCK : (block + 1) * BLOCK].astype(BF16)
            place_rows(order_ref, turn_ref, acc_rel_ref[...].T.astype(BF16), cores, shares)
            extra = turn_ref[...]
        if first:
            place_rows(order_ref, turn_ref, extra_one_ref[...].T, cores, shares)
            extra = product(turn_ref[...], extra_two_ref[...]).astype(BF16)
        if extra is not None:
            each = extra.shape[0] // (cores * shares)
            for part in range(D // half):
                columns = extra[:, part * half : (part + 1) * half]
                store_pieces(pack_refs, base + part * each, columns, slice(None))


def attention_backward(
    start, pairs, cores, shares, dist, order, query, key, value, pos_key, pos_query, prob, g_context,
    tokens_row, rel_table, w_query, w_key, w_value, extra_one, extra_two, vectors,
):
    keys = key.shape[0]
    blocks = keys // BLOCK
    first, last = start == 0, start + pairs == PAIRS
    share = D // cores // shares
    half = pairs * BLOCK
    rows_extra = D if first else RELROWS if last else 0
    pack = (shares, 3 * share + 16 + rows_extra // cores // shares * (D // half), half)
    pair = lambda rows: pl.BlockSpec((rows, BLOCK), lambda p, *_: (0, p + start))
    if first:
        extras = [once(BLOCK, D), once(BLOCK, D)]
        turn = (D, BLOCK)
    else:
        extras = [kept(keys, keys, D), kept(keys, D, RELROWS)]
        turn = (RELROWS, D)
    sums = [(keys, D), (D, RELROWS)] if last else [(8, 128), (8, 128)]
    if last:
        outs = [((BLOCK, D), F32), ((blocks - 1, BLOCK, D), BF16)]
    else:
        outs = [((keys, D), F32), ((D, RELROWS), F32)]
    return pl.pallas_call(
        functools.partial(backward_kernel, blocks, cores, first, last),
        grid_spec=pltpu.PrefetchScalarGridSpec(
            num_scalar_prefetch=2,
            grid=(pairs,),
            in_specs=[
                pair(BLOCK),
                pair(keys),
                pair(keys),
                pair(RELROWS),
                pair(RELROWS),
                pl.BlockSpec((2, keys, BLOCK), lambda p, *_: (p + start, 0, 0)),
                pair(BLOCK),
                kept(keys, keys, D),
                once(RELROWS, D),
                pair(D),
                pair(D),
                pair(D),
            ]
            + extras
            + [pair(8)] * VECTORS,
            out_specs=[kept(keys, *pack)] * cores + [kept(keys, *shape) for shape, _ in outs],
            scratch_shapes=[
                pltpu.VMEM((keys, 2 * BLOCK), BF16),
                pltpu.VMEM((keys, BLOCK), BF16),
                pltpu.VMEM((keys, BLOCK), BF16),
                pltpu.VMEM((BLOCK, EXT), F32),
                pltpu.VMEM((BLOCK, EXT), F32),
                pltpu.VMEM((D, keys), BF16),
                pltpu.VMEM((D, RELROWS), BF16),
                pltpu.VMEM(sums[0], F32),
                pltpu.VMEM(sums[1], F32),
                pltpu.VMEM(turn, BF16),
                pltpu.VMEM((EXT, BLOCK), BF16),
                pltpu.VMEM((EXT, BLOCK), BF16),
            ],
        ),
        out_shape=[kept_array(keys, pack, BF16)] * cores
        + [kept_array(keys, shape, dtype) for shape, dtype in outs],
        compiler_params=pltpu.CompilerParams(vmem_limit_bytes=(18 if fits(keys) else 58) * 2**20),
        name="attention_backward",
    )(
        dist, order, *streamed(query, key, value, pos_key, pos_query, prob), g_context,
        tokens_row, *streamed(rel_table, w_query, w_key, w_value), extra_one, extra_two, *vectors,
    )


def column_sum(array):
    return jnp.sum(array, axis=0, keepdims=True)


def middle_forward_kernel(
    blocks,
    place_ref,
    ctx_ref,
    tok_ref,
    cot_ref,
    wout_ref,
    bout_ref,
    gain_one_ref,
    shift_one_ref,
    bdown_ref,
    gain_two_ref,
    shift_two_ref,
    wup_ref,
    bup_ref,
    wdown_ref,
    output_ref,
    feed_ref,
    normal_ref,
    inverse_ref,
    resid_ref,
    slope_ref,
    sums_ref,
    hidden_ref,
    down_ref,
):
    step = pl.program_id(0)

    @pl.when(step == 0)
    def _():
        attn = product(ctx_ref[...], wout_ref[...]) + bout_ref[...]
        normal, inverse = normalized(tok_ref[...].astype(F32) + attn)
        normal_ref[...] = normal
        inverse_ref[...] = jnp.broadcast_to(inverse, inverse_ref.shape)
        hidden = normal * gain_one_ref[...] + shift_one_ref[...]
        hidden_ref[...] = hidden
        feed_ref[:, :D] = hidden.astype(BF16)
        down_ref[...] = jnp.zeros_like(down_ref)

    width = bup_ref.shape[1]
    units = pl.ds(pl.multiple_of(step * width, width), width)
    act, slope = gelu_and_slope(product(feed_ref[:, :D], wup_ref[:, units]) + bup_ref[...])
    slope_ref[...] = slope
    down_ref[...] += product(act.astype(BF16), wdown_ref[units, :])

    @pl.when(step == pl.num_programs(0) - 1)
    def _():
        normal, inverse = normalized(hidden_ref[...] + (down_ref[...] + bdown_ref[...]))
        output_ref[...] = (normal * gain_two_ref[...] + shift_two_ref[...]).astype(BF16)
        position = place_ref[blocks] * BLOCK + lax.broadcasted_iota(jnp.int32, (BLOCK, 1), 0)
        valid = segment_of(position, place_ref, 2 * blocks) < DOCS
        g_out = jnp.where(valid, cot_ref[...].astype(F32), 0.0)
        g_resid, g_gain, g_shift = normalized_back(g_out, normal, inverse, gain_two_ref[...])
        resid_ref[...] = g_resid
        g_down = g_resid.astype(BF16)
        feed_ref[:, D:] = g_down
        sums_ref[0:1, :] = column_sum(g_down.astype(F32))
        sums_ref[1:2, :] = g_gain
        sums_ref[2:3, :] = g_shift


def middle_forward(
    place, context, tokens, cotangent, w_out, b_out, gain_one, shift_one, b_down, gain_two, shift_two,
    w_up, b_up, w_down,
):
    units = w_up.shape[1]
    width = 512
    row = lambda v: v.reshape(1, -1)
    return pl.pallas_call(
        functools.partial(middle_forward_kernel, (place.shape[0] - DOCS) // 2),
        grid_spec=pltpu.PrefetchScalarGridSpec(
        num_scalar_prefetch=1,
        grid=(units // width,),
        in_specs=[once(BLOCK, D)] * 3
        + [pl.BlockSpec(memory_space=pltpu.VMEM)]
        + [once(1, D)] * 6
        + [
            pl.BlockSpec(memory_space=pltpu.VMEM),
            pl.BlockSpec((1, width), lambda p, *_: (0, p)),
            pl.BlockSpec(memory_space=pltpu.VMEM),
        ],
        out_specs=[
            once(BLOCK, D),
            once(BLOCK, 2 * D),
            once(BLOCK, D),
            once(BLOCK, BLOCK),
            once(BLOCK, D),
            pl.BlockSpec((BLOCK, width), lambda p, *_: (0, p)),
            once(8, D),
        ],
        scratch_shapes=[pltpu.VMEM((BLOCK, D), F32), pltpu.VMEM((BLOCK, D), F32)],
        ),
        out_shape=[
            jax.ShapeDtypeStruct((BLOCK, D), BF16),
            jax.ShapeDtypeStruct((BLOCK, 2 * D), BF16),
            jax.ShapeDtypeStruct((BLOCK, D), F32),
            jax.ShapeDtypeStruct((BLOCK, BLOCK), F32),
            jax.ShapeDtypeStruct((BLOCK, D), F32),
            jax.ShapeDtypeStruct((BLOCK, units), F32),
            jax.ShapeDtypeStruct((8, D), F32),
        ],
        compiler_params=pltpu.CompilerParams(vmem_limit_bytes=20 * 2**20),
        name="middle_forward",
    )(
        place, context, tokens, cotangent, w_out, row(b_out), row(gain_one), row(shift_one), row(b_down),
        row(gain_two), row(shift_two), w_up, row(b_up), w_down,
    )


def middle_backward_kernel(
    feed_ref,
    resid_ref,
    normal_ref,
    inverse_ref,
    gain_ref,
    wout_ref,
    slope_ref,
    wup_ref,
    wdown_ref,
    g_resid_ref,
    g_attn_ref,
    g_ctx_ref,
    sums_ref,
    g_up_ref,
    acc_ref,
):
    step = pl.program_id(0)

    @pl.when(step == 0)
    def _():
        acc_ref[...] = resid_ref[...]

    width = slope_ref.shape[1]
    units = pl.ds(pl.multiple_of(step * width, width), width)
    g_up = (product_right(feed_ref[:, D:], wdown_ref[units, :]) * slope_ref[...]).astype(BF16)
    g_up_ref[...] = g_up
    acc_ref[...] += product_right(g_up, wup_ref[:, units])

    @pl.when(step == pl.num_programs(0) - 1)
    def _():
        g_resid, g_gain, g_shift = normalized_back(
            acc_ref[...], normal_ref[...], inverse_ref[:, 0:1], gain_ref[...]
        )
        g_resid_ref[...] = g_resid
        g_attn = g_resid.astype(BF16)
        g_attn_ref[...] = g_attn
        g_ctx_ref[...] = product_right(g_attn, wout_ref[...]).astype(BF16)
        sums_ref[0:1, :] = column_sum(g_attn.astype(F32))
        sums_ref[1:2, :] = g_gain
        sums_ref[2:3, :] = g_shift


def middle_backward(feed, g_resid_two, normal, inverse, gain_one, w_out, slope, w_up, w_down):
    units = w_up.shape[1]
    width = 512
    return pl.pallas_call(
        middle_backward_kernel,
        grid=(units // width,),
        in_specs=[
            once(BLOCK, 2 * D),
            once(BLOCK, D),
            once(BLOCK, D),
            once(BLOCK, BLOCK),
            once(1, D),
            pl.BlockSpec(memory_space=pltpu.VMEM),
            pl.BlockSpec((BLOCK, width), lambda p: (0, p)),
            pl.BlockSpec(memory_space=pltpu.VMEM),
            pl.BlockSpec(memory_space=pltpu.VMEM),
        ],
        out_specs=[
            once(BLOCK, D),
            once(BLOCK, D),
            once(BLOCK, D),
            once(8, D),
            pl.BlockSpec((BLOCK, width), lambda p: (0, p)),
        ],
        scratch_shapes=[pltpu.VMEM((BLOCK, D), F32)],
        out_shape=[
            jax.ShapeDtypeStruct((BLOCK, D), F32),
            jax.ShapeDtypeStruct((BLOCK, D), BF16),
            jax.ShapeDtypeStruct((BLOCK, D), BF16),
            jax.ShapeDtypeStruct((8, D), F32),
            jax.ShapeDtypeStruct((BLOCK, units), BF16),
        ],
        compiler_params=pltpu.CompilerParams(vmem_limit_bytes=20 * 2**20),
        name="middle_backward",
    )(
        feed, g_resid_two, normal, inverse, gain_one.reshape(1, -1), w_out, slope,
        w_up, w_down,
    )


def gelu_and_slope(x):
    below = 0.5 + 0.5 * lax.erf(x * math.sqrt(0.5))
    density = jnp.exp(-0.5 * x * x) * (1.0 / math.sqrt(2.0 * math.pi))
    return x * below, below + x * density


def feedforward_kernel(
    parts,
    order_ref,
    *refs,
):
    part_refs, refs = refs[:parts], refs[parts:]
    wup_ref, bup_ref, wdown_ref, down_own_ref, down_other_ref, up_own_ref, up_other_ref, *refs = refs
    hid_ref, gd_ref, hidt_ref, sums_ref = refs
    step = pl.program_id(0)
    shares = up_own_ref.shape[0]
    half = down_own_ref.shape[1]
    width = wup_ref.shape[1]

    @pl.when(step == 0)
    def _():
        for part in range(parts):
            rows = slice(part * BLOCK, (part + 1) * BLOCK)
            hid_ref[rows, :] = part_refs[part][:, :D]
            gd_ref[rows, :] = part_refs[part][:, D:]
        place_rows(order_ref, hidt_ref, hid_ref[...].T, 2, shares)

    lanes = pl.ds(pl.multiple_of(step * width, width), width)
    act, slope = gelu_and_slope(product(hid_ref[...], wup_ref[...]) + bup_ref[...])
    g_up = (product_right(gd_ref[...], wdown_ref[...]) * slope).astype(BF16)
    act_turned = act.astype(BF16).T
    for core, ref in enumerate((down_own_ref, down_other_ref)):
        columns = pl.ds(pl.multiple_of((order_ref[0] ^ core) * half, BLOCK), half)
        ref[lanes, :] = product(act_turned, gd_ref[:, columns]).astype(BF16)
    store_pieces((up_own_ref, up_other_ref), 0, product(hidt_ref[...], g_up).astype(BF16), lanes)
    sums_ref[:, lanes] = product(jnp.ones((16, hid_ref.shape[0]), BF16), g_up)

    @pl.when(step == pl.num_programs(0) - 1)
    def _():
        for core, ref in enumerate((down_own_ref, down_other_ref)):
            columns = pl.ds(pl.multiple_of((order_ref[0] ^ core) * half, BLOCK), half)
            ref[pl.ds(sums_ref.shape[1], 16), :] = sums_ref[:, columns].astype(BF16)


def feedforward_gradients(order, row_parts, w_up, b_up, w_down):
    shares = len(row_parts)
    tokens = shares * BLOCK
    units = w_up.shape[1] // shares
    width = 256
    steps = units // width
    down = (units + 16, D // 2)
    up = (shares, D // shares // 2, units)
    return pl.pallas_call(
        functools.partial(feedforward_kernel, shares),
        grid_spec=pltpu.PrefetchScalarGridSpec(
            num_scalar_prefetch=1,
            grid=(steps,),
            in_specs=[once(BLOCK, 2 * D)] * shares
            + [
                pl.BlockSpec((D, width), lambda p, order: (0, order[1] * steps + p)),
                pl.BlockSpec((1, width), lambda p, order: (0, order[1] * steps + p)),
                pl.BlockSpec((width, D), lambda p, order: (order[1] * steps + p, 0)),
            ],
            out_specs=[pl.BlockSpec(memory_space=pltpu.VMEM)] * 4,
            scratch_shapes=[
                pltpu.VMEM((tokens, D), BF16),
                pltpu.VMEM((tokens, D), BF16),
                pltpu.VMEM((D, tokens), BF16),
                pltpu.VMEM((16, units), F32),
            ],
        ),
        out_shape=[pltpu.VMEM(shape, BF16) for shape in (down, down, up, up)],
        compiler_params=pltpu.CompilerParams(vmem_limit_bytes=16 * 2**20),
        name="feedforward_gradients",
    )(order, *row_parts, *streamed(w_up), b_up, *streamed(w_down))


def swapped(array, axis, bits):
    return lax.ppermute(array, axis, [(i, i ^ bits) for i in range(lax.axis_size(axis))])


def from_peers(arrays):
    return [swapped(array, "seq", bits) for bits, array in enumerate(arrays, 1)]


def picked(array, index, axis):
    return lax.dynamic_index_in_dim(array, index, axis, keepdims=False)


def together(*arrays):
    return lax.optimization_barrier(arrays)


def added(*arrays):
    return functools.reduce(jnp.add, [array.astype(F32) for array in arrays]).astype(BF16)


def halves(pack):
    middle = pack.shape[1] // 32 * 16
    return pack[:, :middle], pack[:, middle:]


def in_row_order(pack, mine):
    return jnp.stack([picked(pack, mine ^ at, 0) for at in range(4)], axis=0)


def square_mesh():
    return lax.axis_size("seq") == 4 and lax.axis_size("z") == 4


def scatter(pack):
    return from_peers([pack[1], pack[2], pack[3]])


NEXT = [(0, 1), (1, 0), (2, 3), (3, 2)]
ACROSS = [(0, 3), (1, 2), (2, 1), (3, 0)]


def half_of(share, second):
    half = share.shape[0] // 2
    return jnp.where(second, share[half:], share[:half])


def core_index():
    return lax.axis_index("core")


def both_cores(share, axis):
    other = swapped(share, "core", 1)
    first = core_index() == 0
    return jnp.concatenate(
        [jnp.where(first, share, other), jnp.where(first, other, share)], axis=axis
    )


def reduce_plain(partial):
    share = lax.psum_scatter(partial.astype(BF16), "seq", scatter_dimension=0, tiled=True)
    return lax.psum(share, ("z", "core")).astype(F32)


def local(
    tokens,
    cotangent,
    lengths,
    w_query,
    b_query,
    w_key,
    b_key,
    w_value,
    b_value,
    w_out,
    b_out,
    gain_one,
    shift_one,
    w_up,
    b_up,
    w_down,
    b_down,
    gain_two,
    shift_two,
    rel_table,
):
    rows = tokens.shape[0]
    cycle = lax.axis_size("seq")
    mine = lax.axis_index("seq")
    core = core_index()
    square = square_mesh()
    hidden_units = w_up.shape[1]
    share = D // cycle
    if square:
        token_parts = [tokens] + from_peers([tokens] * 3)
        ids = mine ^ jnp.arange(cycle, dtype=jnp.int32)
        order = jnp.stack([core, mine]).astype(jnp.int32)
        cores = 2
    else:
        token_parts = [tokens, lax.all_gather(tokens, "seq", axis=0, tiled=True)]
        ids = jnp.concatenate([mine[None], jnp.arange(cycle, dtype=jnp.int32)])
        order = jnp.zeros((2,), jnp.int32)
        cores = 1
    dist = jnp.concatenate([mine - ids, ids, lengths[0]]).astype(jnp.int32)

    at_z = lax.axis_index("z")
    end = (at_z == 0) | (at_z == 3)
    between = jnp.logical_not(end)
    low = core == 0
    odd_x, odd_y = (mine & 1) == 1, (mine & 2) == 2
    place_of = (dist, order, end, between, low, odd_x, odd_y)
    dist, order, end, between, low, odd_x, odd_y = lax.optimization_barrier(place_of)

    def in_order(pieces):
        first, second, third, fourth = pieces
        pairs = [
            (jnp.where(odd_x, b, a), jnp.where(odd_x, a, b))
            for a, b in ((first, second), (third, fourth))
        ]
        return [jnp.where(odd_y, b, a) for a, b in zip(*pairs)] + [
            jnp.where(odd_y, a, b) for a, b in zip(*pairs)
        ]

    def own_quarter(array):
        half = array.shape[1] // 2
        array = jnp.where(odd_y, array[:, half:], array[:, :half])
        return jnp.where(odd_x, array[:, half // 2 :], array[:, : half // 2])

    places = jnp.arange(RELROWS, dtype=jnp.int32)
    turn = (places[:, None] + places[None, :] == RELROWS - 1).astype(BF16)
    rel_back = product(turn, rel_table).astype(BF16)
    pos_key_back = (product(rel_back, w_key) + b_key).astype(BF16)
    pos_query_back = (product(rel_back, w_query) + b_query).astype(BF16)
    pos_query = (product(rel_table, w_query) + b_query).astype(BF16)
    pos_key_back, (dist, order, end, between, low, odd_x, odd_y) = together(
        pos_key_back, (dist, order, end, between, low, odd_x, odd_y)
    )
    context, prob, query, key, value, tokens_row, *held = attention_forward(
        dist,
        token_parts,
        [w_query, w_key, w_value],
        [v[None] for v in (b_query, b_key, b_value)],
        pos_key_back,
        pos_query_back,
        [w_up, w_down, w_out],
    )
    held_up, held_down, held_out = held

    output, feed, normal_one, inverse_one, g_resid_two, slope, sums_two = middle_forward(
        dist, context, tokens, cotangent, held_out, b_out, gain_one, shift_one, b_down, gain_two,
        shift_two, held_up, b_up, held_down,
    )
    if square:
        row_parts = [feed] + from_peers([feed] * 3)
    g_resid_one, g_attn, g_context, sums_one, g_up = middle_backward(
        feed, g_resid_two, normal_one, inverse_one, gain_one, held_out, slope, held_up, held_down
    )
    vectors = [sums_one, sums_two]

    def backward(start, pairs, g_context, extra_one, extra_two):
        outs = attention_backward(
            start, pairs, cores, cycle, dist, order, query, key, value, pos_key_back, pos_query, prob,
            g_context, tokens_row, rel_table, w_query, w_key, w_value, extra_one, extra_two, vectors,
        )
        return outs[:cores], outs[cores:]

    piece = share // cores
    whole_rows = lambda v, at, each: v[:, at : at + each].reshape(cores * each, -1)

    def unpacked(v, each):
        base = 3 * piece + 16
        parts = D // v.shape[2]
        return jnp.concatenate(
            [whole_rows(v, base + part * each, each) for part in range(parts)], axis=1
        )

    def rel_own(pack):
        return unpacked(pack, RELROWS // cycle // cores)

    def assembled(packs, rel_parts, grad_tokens, grad_w_up, grad_w_down, grad_b_up):
        grads = [
            jnp.concatenate([whole_rows(v, at * piece, piece) for v in packs], axis=1).astype(F32)
            for at in range(3)
        ]
        base = 3 * piece
        vector_sums = jnp.concatenate([v[0, base : base + 16] for v in packs], axis=1).astype(F32)
        grad_w_out = unpacked(packs[0], piece).astype(F32)
        grads, grad_w_out, grad_w_down, grad_b_up, grad_tokens, rel_parts = together(
            grads, grad_w_out, grad_w_down, grad_b_up, grad_tokens, rel_parts
        )
        if square:
            grad_rel = jnp.concatenate(in_order(rel_parts), axis=0).astype(F32)
        else:
            grad_rel = rel_parts[0].astype(F32)
        if square:
            vector_share = own_quarter(vector_sums)
        else:
            vector_share = lax.dynamic_slice_in_dim(vector_sums, mine * share, share, 1)
        return (
            output,
            grad_tokens,
            grads[0],
            vector_share[0],
            grads[1],
            vector_share[1],
            grads[2],
            vector_share[2],
            grad_w_out,
            vector_share[3],
            vector_share[4],
            vector_share[5],
            grad_w_up,
            grad_b_up,
            grad_w_down,
            vector_share[6],
            vector_share[7],
            vector_share[8],
            grad_rel,
        )

    if not square:
        act = gelu_and_slope(product(feed[:, :D], w_up) + b_up)[0].astype(BF16)
        (one,), carried = backward(0, 3, g_context, context, g_attn)
        (two,), (home, away) = backward(3, 3, g_context, *carried)
        packs = [
            lax.psum(lax.psum_scatter(v, "seq", scatter_dimension=0, tiled=True), ("z", "core"))
            for v in (one, two)
        ]
        got = lax.psum_scatter(away, "seq", scatter_dimension=0, tiled=False)
        return assembled(
            packs,
            [lax.all_gather(rel_own(packs[-1]), "seq", axis=0, tiled=True)],
            g_resid_one + home + got.astype(F32),
            reduce_plain(product_left(feed[:, :D], g_up)),
            reduce_plain(product_left(act, feed[:, D:])),
            reduce_plain(jnp.sum(g_up.astype(F32), axis=0)),
        )

    one, carried = backward(0, 3, g_context, context, g_attn)

    row_parts, one, carried = together(row_parts, one, carried)
    one_got = swapped(one[1], "core", 1)
    down_own, down_other, up_own, up_other = feedforward_gradients(
        order, row_parts, w_up, b_up[None], w_down
    )

    one_got, down_own, down_other, up_own, up_other = together(
        one_got, down_own, down_other, up_own, up_other
    )
    down_got = swapped(down_other, "core", 1)
    up_got = swapped(up_other, "core", 1)
    one_share = added(one[0], one_got)
    down_share = added(down_own, down_got)
    up_share = added(up_own, up_got)

    units = hidden_units // 4

    def first_start(v):
        first, second = halves(v)
        return swapped(first[1::2], "seq", 1), swapped(second[2:], "seq", 2)

    def first_end(v, got):
        first, second = halves(v)
        return added(first[0::2], got[0]), added(second[:2], got[1])

    def second_start(v):
        return swapped(v[0][1], "seq", 2), swapped(v[1][1], "seq", 1)

    def second_end(v, got):
        return jnp.concatenate([added(v[0][0], got[0]), added(v[1][0], got[1])], axis=0)

    def core_start(v):
        return swapped(v, "core", 1)

    def joined(axis):
        return lambda v, got: jnp.concatenate(
            [jnp.where(low, v, got), jnp.where(low, got, v)], axis=axis
        )

    core_rows = joined(0)
    moves = {
        "first": (first_start, first_end),
        "second": (second_start, second_end),
        "in": (
            lambda v: lax.ppermute(half_of(v, end), "z", NEXT),
            lambda v, got: added(half_of(v, between), got),
        ),
        "mid": (lambda v: lax.ppermute(v, "z", ACROSS), added),
        "out": (
            lambda v: lax.ppermute(v, "z", NEXT),
            lambda v, got: jnp.concatenate(
                [jnp.where(end, v, got), jnp.where(end, got, v)], axis=0
            ),
        ),
        "pair": (lambda v: swapped(v[1], "core", 1), lambda v, got: added(v[0], got)),
        "rows": (lambda v: core_start(v[None]), lambda v, got: core_rows(v[None], got)),
        "columns": (core_start, joined(1)),
        "give": (scatter, lambda v, got: jnp.stack([v[0]] + got, axis=0)),
        "home": (
            lambda v: from_peers([v[0], v[1], v[2]]),
            lambda v, got: functools.reduce(jnp.add, [part.astype(F32) for part in got]),
        ),
        "spread": (scatter, lambda v, got: added(v[0], *got)),
        "x": (lambda v: swapped(v[1], "seq", 1), lambda v, got: [v[0], got, v[2], v[3]]),
        "y": (lambda v: swapped(v[2], "seq", 2), lambda v, got: [v[0], v[1], got, v[3]]),
        "d": (
            lambda v: swapped(v[3], "seq", 3),
            lambda v, got: jnp.stack([v[0], v[1], v[2], got], axis=0),
        ),
        "dd": (
            lambda v: swapped(v[3], "seq", 3),
            lambda v, got: jnp.stack([v[0], v[1], v[2], got], axis=0),
        ),
        "hx": (lambda v: swapped(v[0], "seq", 1), lambda v, got: [got, v[1], v[2]]),
        "hy": (lambda v: swapped(v[1], "seq", 2), lambda v, got: [v[0], got, v[2]]),
        "hd": (
            lambda v: swapped(v[2], "seq", 3),
            lambda v, got: functools.reduce(
                jnp.add, [part.astype(F32) for part in (v[0], v[1], got)]
            ),
        ),
        "rel": (
            lambda v: from_peers([rel_own(v)] * 3),
            lambda v, got: (v, [rel_own(v)] + got),
        ),
    }
    held_sums = {"down": down_share, "up": up_share, "one": one_share}
    flying = {}

    def begin(*steps):
        for step in steps:
            name, move = step.split(".")
            if move == "share":
                both = zip(held_sums["up"][1:], held_sums["away"])
                flying[step] = from_peers([jnp.concatenate(parts, axis=0) for parts in both])
            else:
                flying[step] = moves[move][0](held_sums[name])

    def meet(done, then):
        names = [step.split(".")[0] for step in then] + [step.split(".")[0] for step in done]
        names += ["away"] if "up.share" in done or "up.share" in then else []
        names = [name for at, name in enumerate(names) if name not in names[:at]]
        gots = {step: flying.pop(step) for step in done}
        kept, gots = together({name: held_sums[name] for name in names}, gots)
        held_sums.update(kept)
        for step in done:
            name, move = step.split(".")
            if move == "share":
                each = held_sums["up"].shape[1]
                parts = [held_sums["up"][0]] + [got[:each] for got in gots[step]]
                held_sums["up"] = jnp.stack(parts, axis=0)
                homes = [got[each:].astype(F32) for got in gots[step]]
                held_sums["away"] = functools.reduce(jnp.add, homes)
            else:
                held_sums[name] = moves[move][1](held_sums[name], gots[step])
        begin(*then)

    stages = (
        ([], ["up.in", "one.spread"]),
        (["up.in", "one.spread"], ["two.pair", "up.mid", "one.in"]),
        (["two.pair"], ["two.first", "down.in"]),
        (["two.first", "up.mid", "one.in"], ["two.second", "up.out", "one.mid"]),
        (["two.second", "down.in", "one.mid"], ["two.in", "down.mid", "one.out"]),
        (["two.in", "up.out", "one.out"], ["two.mid", "up.share", "one.rows"]),
        (["two.mid", "down.mid", "one.rows"], ["two.out", "down.out"]),
        (["two.out", "up.share", "down.out"], ["two.rows", "up.columns", "down.columns"]),
        (["two.rows", "up.columns", "down.columns"], ["two.rel"]),
        (["two.rel"], []),
    )
    begin(*stages[0][1])
    g_context, held_sums = together(g_context, held_sums)
    two, (home, away) = backward(3, 3, g_context, *carried)
    home, held_sums, flying_now = together(
        home, dict(held_sums, two=two, away=away), {step: flying[step] for step in stages[1][0]}
    )
    flying.update(flying_now)
    for done, then in stages[1:]:
        meet(done, then)

    grad_tokens = g_resid_one + home + held_sums["away"]
    down_share = held_sums["down"]
    up_share = held_sums["up"].reshape(4, share, -1)
    grad_w_up = jnp.concatenate(in_order(list(up_share)), axis=1).astype(F32)
    two_share, rel_parts = held_sums["two"]
    return assembled(
        [held_sums["one"], two_share],
        rel_parts,
        grad_tokens,
        grad_w_up,
        down_share[:units].astype(F32),
        down_share[units].astype(F32),
    )


def solution(mesh):
    lines, cycle = mesh.devices.shape
    chips = Mesh(mesh.devices.reshape(lines // 2, 2, cycle), ("z", "core", "seq"))
    return jax.shard_map(
        local,
        mesh=chips,
        in_specs=(
            P(("z", "core", "seq"), None),
            P(("z", "core", "seq"), None),
            P(("z", "core"), None),
        )
        + (P(),) * 17,
        out_specs=(
            P(("z", "core", "seq"), None),
            P(("z", "core", "seq"), None),
            P("seq", None),
            P("seq"),
            P("seq", None),
            P("seq"),
            P("seq", None),
            P("seq"),
            P("seq", None),
            P("seq"),
            P("seq"),
            P("seq"),
            P("seq", None),
            P("seq"),
            P("seq", None),
            P("seq"),
            P("seq"),
            P("seq"),
            P(),
        ),
        check_vma=False,
    )
```

```python
import functools
import math

import jax
import jax.numpy as jnp
from jax import lax
from jax.experimental import pallas as pl
from jax.experimental.pallas import tpu as pltpu
from jax.sharding import Mesh, PartitionSpec as P

D = 768
HEADS = 12
HEAD = 64
SPAN = 256
RELROWS = 512
BLOCK = 128
EXT = RELROWS + 2 * SPAN
PAIRS = HEADS // 2
VECTORS = 2
LATER = 3
DOCS = 4
SCALE = 1.0 / math.sqrt(3 * HEAD)
F32 = jnp.float32
BF16 = jnp.bfloat16
ROLLED = BF16


def normalized(resid):
    center = resid - jnp.mean(resid, axis=-1, keepdims=True)
    inverse = lax.rsqrt(jnp.mean(center * center, axis=-1, keepdims=True) + 1e-07)
    return center * inverse, inverse


def normalized_back(grad, normal, inverse, gain):
    hat = grad * gain
    means = jnp.mean(hat, axis=-1, keepdims=True) + normal * jnp.mean(
        hat * normal, axis=-1, keepdims=True
    )
    total = lambda v: jnp.sum(v, axis=0, keepdims=True)
    return (hat - means) * inverse, total(grad * normal), total(grad)


def product(left, right):
    return jnp.dot(left, right, preferred_element_type=F32)


def product_left(left, right):
    return lax.dot_general(left, right, (((0,), (0,)), ((), ())), preferred_element_type=F32)


def product_right(left, right):
    return lax.dot_general(left, right, (((1,), (1,)), ((), ())), preferred_element_type=F32)


def segment_of(position, place_ref, at):
    passed, bound = jnp.zeros(position.shape, jnp.int32), 0
    for document in range(DOCS):
        bound = bound + place_ref[at + document]
        passed = passed + (position >= bound).astype(jnp.int32)
    return passed


def anti_identity():
    rows = lax.broadcasted_iota(jnp.int32, (BLOCK, BLOCK), 0)
    cols = lax.broadcasted_iota(jnp.int32, (BLOCK, BLOCK), 1)
    return (rows + cols == BLOCK - 1).astype(BF16)


def extend(ext_ref, table_ref):
    ext_ref[SPAN : SPAN + RELROWS, :] = table_ref[...]
    ext_ref[0:SPAN, :] = jnp.broadcast_to(table_ref[0:1, :], (SPAN, BLOCK))
    last = table_ref[RELROWS - 1 : RELROWS, :]
    ext_ref[SPAN + RELROWS :, :] = jnp.broadcast_to(last, (SPAN, BLOCK))


def window_start(offset):
    return pl.multiple_of(jnp.clip(offset, 0, EXT - 2 * BLOCK), BLOCK)


def head_mask(head):
    lane = lax.broadcasted_iota(jnp.int32, (1, BLOCK), 1)
    return (lane >= head * HEAD) & (lane < (head + 1) * HEAD)


def band_roll(wide, shift):
    return pltpu.roll(wide, shift, 1, stride=1, stride_axis=0)


def by_head(pair):
    zero = jnp.zeros_like(pair)
    return jnp.concatenate([jnp.where(head_mask(head), pair, zero) for head in range(2)], axis=0)


def forward_kernel(
    parts, blocks, dist_ref, *refs
):
    part_refs, refs = refs[:parts], refs[parts:]
    wq_ref, wk_ref, wv_ref, bq_ref, bk_ref, bv_ref, pk_ref, pq_ref, *refs = refs
    later, refs = refs[:LATER], refs[LATER:]
    ctx_ref, prob_ref, q_ref, k_ref, v_ref, tok_ref, *refs = refs
    held, refs = refs[:LATER], refs[LATER:]
    score_ref, ek_ref, eq_ref, bias_ref, sems = refs
    copies = [
        pltpu.make_async_copy(later[at], held[at], sems.at[at]) for at in range(LATER)
    ]

    @pl.when(pl.program_id(0) == 0)
    def _():
        for copy in copies:
            copy.start()

    @pl.when(pl.program_id(0) == pl.num_programs(0) - 1)
    def _():
        for copy in copies:
            copy.wait()

    extend(ek_ref, pk_ref)
    extend(eq_ref, pq_ref)

    @pl.when(pl.program_id(0) == 0)
    def _():
        at = 0
        for ref in part_refs:
            tok_ref[at : at + ref.shape[0], :] = ref[...]
            at += ref.shape[0]
        mine = dist_ref[blocks]
        lane = lax.broadcasted_iota(jnp.int32, (1, BLOCK), 1)
        line = lax.broadcasted_iota(jnp.int32, (BLOCK, 1), 0)
        query_segment = segment_of(mine * BLOCK + lane, dist_ref, 2 * blocks)
        for block in range(blocks):
            home = dist_ref[blocks + block]
            allowed = segment_of(home * BLOCK + line, dist_ref, 2 * blocks) == query_segment
            if block > 0:
                allowed = jnp.logical_and(allowed, home != mine)
            rows = slice(block * BLOCK, (block + 1) * BLOCK)
            bias_ref[rows, :] = jnp.where(allowed, 0.0, -1e30)

    at = pl.multiple_of(pl.program_id(0) * BLOCK, BLOCK)
    both = product(tok_ref[...], jnp.concatenate([wk_ref[...], wv_ref[...]], axis=1))
    k_ref[...] = (both[:, :BLOCK] + row_of(bk_ref, at, BLOCK)).astype(BF16)
    v_ref[...] = (both[:, BLOCK:] + row_of(bv_ref, at, BLOCK)).astype(BF16)
    q = (product(tok_ref[:BLOCK, :], wq_ref[...]) + row_of(bq_ref, at, BLOCK)).astype(BF16)
    q_ref[...] = q
    q_heads = by_head(q)
    tops = [jnp.full((1, BLOCK), -jnp.inf, F32) for head in range(2)]
    for block in range(blocks):
        dist = dist_ref[block]
        rows = slice(block * BLOCK, (block + 1) * BLOCK)
        k_heads = by_head(k_ref[rows, :])
        window_c = ek_ref[pl.ds(window_start(384 - dist * BLOCK), 2 * BLOCK), :]
        window_p = eq_ref[pl.ds(window_start(384 + dist * BLOCK), 2 * BLOCK), :]
        c2p = product_right(q_heads, window_c)
        p2c = product_right(k_heads, window_p)
        direct = product_right(k_heads, q)
        for head in range(2):
            own = slice(head * BLOCK, (head + 1) * BLOCK)
            first = band_roll(c2p[own].astype(BF16), BLOCK + 1)[:, :BLOCK].T
            second = band_roll(p2c[own].astype(BF16), BLOCK + 1)[:, :BLOCK]
            score = (direct[own] + first.astype(F32) + second.astype(F32)) * SCALE + bias_ref[rows, :]
            score_ref[head, rows, :] = score
            tops[head] = jnp.maximum(tops[head], jnp.max(score, axis=0, keepdims=True))
    probs = []
    for head in range(2):
        weight = jnp.exp(score_ref[head] - tops[head])
        total = jnp.sum(weight, axis=0, keepdims=True)
        prob = (weight * (1.0 / total)).astype(BF16)
        prob_ref[head] = prob
        probs.append(prob)
    v = v_ref[...]
    zero = jnp.zeros_like(v)
    out = product_left(probs[0], jnp.where(head_mask(0), v, zero)) + product_left(
        probs[1], jnp.where(head_mask(1), v, zero)
    )
    ctx_ref[...] = out.astype(BF16)


def streamed(*arrays):
    return [pltpu.with_memory_space_constraint(array, pltpu.HBM) for array in arrays]


def once(*shape):
    return pl.BlockSpec(shape, lambda p, *_: (0,) * len(shape), pipeline_mode=pl.Buffered(1))


def fits(keys):
    return keys <= 2 * RELROWS


def kept(keys, *shape):
    return pl.BlockSpec(memory_space=pltpu.VMEM) if fits(keys) else once(*shape)


def kept_array(keys, shape, dtype):
    return (pltpu.VMEM if fits(keys) else jax.ShapeDtypeStruct)(shape, dtype)


def attention_forward(dist, token_parts, weights, biases, pos_key, pos_query, later):
    keys = sum(part.shape[0] for part in token_parts)
    blocks = keys // BLOCK
    pair = lambda rows: pl.BlockSpec((rows, BLOCK), lambda p, dist: (0, p))
    return pl.pallas_call(
        functools.partial(forward_kernel, len(token_parts), blocks),
        grid_spec=pltpu.PrefetchScalarGridSpec(
            num_scalar_prefetch=1,
            grid=(PAIRS,),
            in_specs=[once(*part.shape) for part in token_parts]
            + [pair(D)] * 3
            + [pl.BlockSpec(memory_space=pltpu.VMEM)] * 3
            + [pair(RELROWS), pair(RELROWS)]
            + [pl.BlockSpec(memory_space=pl.ANY)] * LATER,
            out_specs=[
                pair(BLOCK),
                pl.BlockSpec((2, keys, BLOCK), lambda p, dist: (p, 0, 0)),
                pair(BLOCK),
                pair(keys),
                pair(keys),
                kept(keys, keys, D),
            ]
            + [pl.BlockSpec(memory_space=pl.ANY)] * LATER,
            scratch_shapes=[
                pltpu.VMEM((2, keys, BLOCK), F32),
                pltpu.VMEM((EXT, BLOCK), BF16),
                pltpu.VMEM((EXT, BLOCK), BF16),
                pltpu.VMEM((keys, BLOCK), F32),
                pltpu.SemaphoreType.DMA((LATER,)),
            ],
        ),
        out_shape=[
            jax.ShapeDtypeStruct((BLOCK, D), BF16),
            pltpu.HBM((HEADS, keys, BLOCK), BF16),
            pltpu.HBM((BLOCK, D), BF16),
            pltpu.HBM((keys, D), BF16),
            pltpu.HBM((keys, D), BF16),
            kept_array(keys, (keys, D), BF16),
        ]
        + [pltpu.VMEM(array.shape, array.dtype) for array in later],
        compiler_params=pltpu.CompilerParams(vmem_limit_bytes=(16 if fits(keys) else 40) * 2**20),
        name="attention_forward",
    )(dist, *token_parts, *streamed(*weights), *biases, *streamed(pos_key, pos_query), *streamed(*later))


def fold_edges(acc_ref):
    head_sum = jnp.sum(acc_ref[:, 0:SPAN], axis=1, keepdims=True)
    tail_sum = jnp.sum(acc_ref[:, SPAN + RELROWS :], axis=1, keepdims=True)
    lane = lax.broadcasted_iota(jnp.int32, (BLOCK, RELROWS), 1)
    middle = acc_ref[:, SPAN : SPAN + RELROWS]
    middle = middle + jnp.where(lane == 0, head_sum, 0.0)
    return (middle + jnp.where(lane == RELROWS - 1, tail_sum, 0.0)).astype(BF16)


def flipped_lanes(array, flip):
    parts = array.shape[1] // BLOCK
    return jnp.concatenate(
        [
            product(array[:, part * BLOCK : (part + 1) * BLOCK], flip).astype(BF16)
            for part in reversed(range(parts))
        ],
        axis=1,
    )


def place(order_ref, share, core, shares, each):
    at = (core ^ order_ref[0]) * shares + (share ^ order_ref[1])
    return pl.multiple_of(at * each, 16)


def place_rows(order_ref, into_ref, value, cores, shares):
    each = value.shape[0] // (cores * shares)
    for share in range(shares):
        for core in range(cores):
            at = (share * cores + core) * each
            into_ref[pl.ds(place(order_ref, share, core, shares, each), each), :] = value[
                at : at + each
            ]


def store_pieces(refs, at, value, lanes):
    shares = refs[0].shape[0]
    each = value.shape[0] // (len(refs) * shares)
    for core, ref in enumerate(refs):
        for share in range(shares):
            start = (core * shares + share) * each
            ref[share, at : at + each, lanes] = value[start : start + each]


def backward_kernel(
    blocks,
    cores,
    first,
    last,
    dist_ref,
    order_ref,
    q_ref,
    k_ref,
    v_ref,
    pk_ref,
    pq_ref,
    prob_ref,
    gctx_ref,
    tok_ref,
    rel_ref,
    wq_ref,
    wk_ref,
    wv_ref,
    extra_one_ref,
    extra_two_ref,
    *refs,
):
    vec_refs, refs = refs[:VECTORS], refs[VECTORS:]
    pack_refs, refs = refs[:cores], refs[cores:]
    backward_body(
        blocks, first, last, dist_ref, order_ref, q_ref, k_ref, v_ref, pk_ref, pq_ref, prob_ref, gctx_ref,
        tok_ref, rel_ref, wq_ref, wk_ref, wv_ref, extra_one_ref, extra_two_ref, vec_refs, pack_refs, *refs
    )


def backward_body(
    blocks,
    first,
    last,
    dist_ref,
    order_ref,
    q_ref,
    k_ref,
    v_ref,
    pk_ref,
    pq_ref,
    prob_ref,
    gctx_ref,
    tok_ref,
    rel_ref,
    wq_ref,
    wk_ref,
    wv_ref,
    extra_one_ref,
    extra_two_ref,
    vec_refs,
    pack_refs,
    out_one_ref,
    out_two_ref,
    back_ref,
    gk_ref,
    gv_ref,
    acck_ref,
    accq_ref,
    tokt_ref,
    relt_ref,
    acc_tok_ref,
    acc_rel_ref,
    turn_ref,
    ek_ref,
    eq_ref,
):
    step = pl.program_id(0)
    if not last:
        acc_tok_ref, acc_rel_ref = out_one_ref, out_two_ref
    extend(ek_ref, pk_ref)
    extend(eq_ref, pq_ref)
    cores, shares, half = len(pack_refs), pack_refs[0].shape[0], pack_refs[0].shape[2]
    share = D // cores // shares
    flip = anti_identity()

    @pl.when(step == 0)
    def _():
        place_rows(order_ref, tokt_ref, tok_ref[...].T, cores, shares)
        place_rows(order_ref, relt_ref, rel_ref[...].T, cores, shares)
        if first:
            acc_tok_ref[...] = jnp.zeros_like(acc_tok_ref)
            acc_rel_ref[...] = jnp.zeros_like(acc_rel_ref)
        else:
            acc_tok_ref[...] = extra_one_ref[...]
            acc_rel_ref[...] = extra_two_ref[...]

    acck_ref[...] = jnp.zeros_like(acck_ref)
    accq_ref[...] = jnp.zeros_like(accq_ref)
    g_heads = by_head(gctx_ref[...])
    first_rows = lax.broadcasted_iota(jnp.int32, (BLOCK, 1), 0) < HEAD
    first_lanes = head_mask(0)

    def turned_heads(array):
        turned = array.T
        zero = jnp.zeros_like(turned)
        return jnp.concatenate(
            [jnp.where(first_rows, turned, zero), jnp.where(first_rows, zero, turned)], axis=1
        )

    def of_heads(stacked):
        return jnp.where(first_lanes, stacked[:BLOCK], stacked[BLOCK:])

    q_back = product(flip, q_ref[...]).astype(BF16)
    q_turned = turned_heads(q_back)
    probs = jnp.concatenate([prob_ref[head] for head in range(2)], axis=1)
    g_prob = product_right(v_ref[...], g_heads)
    gv_ref[...] = product(probs, g_heads).astype(BF16)
    probs = probs.astype(F32)
    delta = jnp.sum(probs * g_prob, axis=0, keepdims=True)
    g_score = (probs * (g_prob - delta) * SCALE).astype(BF16)
    for head in range(2):
        lanes = slice(head * BLOCK, (head + 1) * BLOCK)
        back_ref[:, lanes] = product(g_score[:, lanes], flip).astype(BF16)
    g_query = jnp.zeros((2 * BLOCK, BLOCK), F32)
    pad = jnp.zeros((BLOCK, BLOCK), BF16)
    for block in range(blocks):
        rows = slice(block * BLOCK, (block + 1) * BLOCK)
        k_block = k_ref[rows, :]
        at = pl.ds(window_start(384 - dist_ref[block] * BLOCK), 2 * BLOCK)
        window_c = ek_ref[at, :]
        window_p = eq_ref[at, :]
        backs = [back_ref[rows, head * BLOCK : (head + 1) * BLOCK] for head in range(2)]
        turns = [back.T for back in backs]
        bands_c = [band_roll(jnp.concatenate([turn, pad], axis=1), 0) for turn in turns]
        bands_p = [band_roll(jnp.concatenate([back, pad], axis=1), 1) for back in backs]
        bands_c = jnp.concatenate(bands_c, axis=0)
        bands_p = jnp.concatenate(bands_p, axis=0)
        g_query = g_query + product(
            jnp.concatenate([jnp.concatenate(turns, axis=0), bands_c], axis=1),
            jnp.concatenate([k_block, window_c], axis=0),
        )
        g_key = product(
            jnp.concatenate([jnp.concatenate(backs, axis=0), bands_p], axis=1),
            jnp.concatenate([q_back, window_p], axis=0),
        )
        gk_ref[rows, :] = of_heads(g_key).astype(BF16)
        acck_ref[:, at] += product(q_turned, bands_c)
        accq_ref[:, at] += product(turned_heads(k_block), bands_p)

    g_query = product(flip, of_heads(g_query).astype(BF16)).astype(BF16)
    g_pos_key = flipped_lanes(fold_edges(acck_ref), flip)
    g_pos_query = fold_edges(accq_ref)
    g_key = gk_ref[...]
    g_value = gv_ref[...]
    lanes = pl.ds(pl.multiple_of(step * BLOCK, BLOCK), BLOCK)
    ones_tok = jnp.ones((16, tok_ref.shape[0]), BF16)
    ones_rel = jnp.ones((16, RELROWS), BF16)
    row = lax.broadcasted_iota(jnp.int32, (16, BLOCK), 0)
    vec = jnp.zeros((16, BLOCK), F32)
    for at, vec_ref in enumerate(vec_refs):
        for part in range(3):
            vec = vec + jnp.where(row == 3 + 3 * at + part, vec_ref[part : part + 1, :], 0.0)
    g_both = jnp.concatenate([g_key, g_value], axis=1)
    pos_both = jnp.concatenate([g_pos_key, g_pos_query], axis=0)
    from_tok = product(tokt_ref[...], g_both)
    from_rel = product_right(relt_ref[...], pos_both)
    from_own = product(tokt_ref[:, :BLOCK], g_query)
    sum_tok = product(ones_tok, g_both)
    sum_rel = product_right(ones_rel, pos_both)
    sum_own = product(ones_tok[:, :BLOCK], g_query)
    weights = [
        (from_own + from_rel[:, BLOCK:], sum_own + sum_rel[:, BLOCK:]),
        (from_tok[:, :BLOCK] + from_rel[:, :BLOCK], sum_tok[:, :BLOCK] + sum_rel[:, :BLOCK]),
        (from_tok[:, BLOCK:], sum_tok[:, BLOCK:]),
    ]
    for at, (weight, total) in enumerate(weights):
        store_pieces(pack_refs, at * share, weight.astype(BF16), lanes)
        vec = vec + jnp.where(row == at, total, 0.0)
    vec = vec.astype(BF16)
    for pack_ref in pack_refs:
        for part in range(shares):
            pack_ref[part, 3 * share : 3 * share + 16, lanes] = vec
    acc_tok_ref[...] += product_right(
        g_both,
        jnp.concatenate([wk_ref[...], wv_ref[...]], axis=1),
    )
    acc_tok_ref[0:BLOCK, :] += product_right(g_query, wq_ref[...])
    acc_rel_ref[...] += product(
        jnp.concatenate([wk_ref[...], wq_ref[...]], axis=1),
        pos_both,
    )

    @pl.when(step == pl.num_programs(0) - 1)
    def _():
        base = 3 * share + 16
        extra = None
        if last:
            out_one_ref[...] = acc_tok_ref[0:BLOCK, :]
            for block in range(1, blocks):
                out_two_ref[block - 1] = acc_tok_ref[block * BLOCK : (block + 1) * BLOCK].astype(BF16)
            place_rows(order_ref, turn_ref, acc_rel_ref[...].T.astype(BF16), cores, shares)
            extra = turn_ref[...]
        if first:
            place_rows(order_ref, turn_ref, extra_one_ref[...].T, cores, shares)
            extra = product(turn_ref[...], extra_two_ref[...]).astype(BF16)
        if extra is not None:
            each = extra.shape[0] // (cores * shares)
            for part in range(D // half):
                columns = extra[:, part * half : (part + 1) * half]
                store_pieces(pack_refs, base + part * each, columns, slice(None))


def attention_backward(
    start, pairs, cores, shares, dist, order, query, key, value, pos_key, pos_query, prob, g_context,
    tokens_row, rel_table, w_query, w_key, w_value, extra_one, extra_two, vectors,
):
    keys = key.shape[0]
    blocks = keys // BLOCK
    first, last = start == 0, start + pairs == PAIRS
    share = D // cores // shares
    half = pairs * BLOCK
    rows_extra = D if first else RELROWS if last else 0
    pack = (shares, 3 * share + 16 + rows_extra // cores // shares * (D // half), half)
    pair = lambda rows: pl.BlockSpec((rows, BLOCK), lambda p, *_: (0, p + start))
    if first:
        extras = [once(BLOCK, D), once(BLOCK, D)]
        turn = (D, BLOCK)
    else:
        extras = [kept(keys, keys, D), kept(keys, D, RELROWS)]
        turn = (RELROWS, D)
    sums = [(keys, D), (D, RELROWS)] if last else [(8, 128), (8, 128)]
    if last:
        outs = [((BLOCK, D), F32), ((blocks - 1, BLOCK, D), BF16)]
    else:
        outs = [((keys, D), F32), ((D, RELROWS), F32)]
    return pl.pallas_call(
        functools.partial(backward_kernel, blocks, cores, first, last),
        grid_spec=pltpu.PrefetchScalarGridSpec(
            num_scalar_prefetch=2,
            grid=(pairs,),
            in_specs=[
                pair(BLOCK),
                pair(keys),
                pair(keys),
                pair(RELROWS),
                pl.BlockSpec((RELROWS, BLOCK), lambda p, *_: (1, p + start)),
                pl.BlockSpec((2, keys, BLOCK), lambda p, *_: (p + start, 0, 0)),
                pair(BLOCK),
                kept(keys, keys, D),
                once(RELROWS, D),
                pair(D),
                pair(D),
                pair(D),
            ]
            + extras
            + [pair(8)] * VECTORS,
            out_specs=[kept(keys, *pack)] * cores + [kept(keys, *shape) for shape, _ in outs],
            scratch_shapes=[
                pltpu.VMEM((keys, 2 * BLOCK), BF16),
                pltpu.VMEM((keys, BLOCK), BF16),
                pltpu.VMEM((keys, BLOCK), BF16),
                pltpu.VMEM((BLOCK, EXT), F32),
                pltpu.VMEM((BLOCK, EXT), F32),
                pltpu.VMEM((D, keys), BF16),
                pltpu.VMEM((D, RELROWS), BF16),
                pltpu.VMEM(sums[0], F32),
                pltpu.VMEM(sums[1], F32),
                pltpu.VMEM(turn, BF16),
                pltpu.VMEM((EXT, BLOCK), BF16),
                pltpu.VMEM((EXT, BLOCK), BF16),
            ],
        ),
        out_shape=[kept_array(keys, pack, BF16)] * cores
        + [kept_array(keys, shape, dtype) for shape, dtype in outs],
        compiler_params=pltpu.CompilerParams(vmem_limit_bytes=(18 if fits(keys) else 58) * 2**20),
        name="attention_backward",
    )(
        dist, order, *streamed(query, key, value, pos_key, pos_query, prob), g_context,
        tokens_row, *streamed(rel_table, w_query, w_key, w_value), extra_one, extra_two, *vectors,
    )


def column_sum(array):
    return jnp.sum(array, axis=0, keepdims=True)


def middle_forward_kernel(
    blocks,
    place_ref,
    ctx_ref,
    tok_ref,
    cot_ref,
    wout_ref,
    bout_ref,
    gain_one_ref,
    shift_one_ref,
    bdown_ref,
    gain_two_ref,
    shift_two_ref,
    wup_ref,
    bup_ref,
    wdown_ref,
    output_ref,
    feed_ref,
    normal_ref,
    inverse_ref,
    resid_ref,
    slope_ref,
    sums_ref,
    hidden_ref,
    down_ref,
):
    step = pl.program_id(0)

    @pl.when(step == 0)
    def _():
        attn = product(ctx_ref[...], wout_ref[...]) + row_of(bout_ref)
        normal, inverse = normalized(tok_ref[...].astype(F32) + attn)
        normal_ref[...] = normal
        inverse_ref[...] = jnp.broadcast_to(inverse, inverse_ref.shape)
        hidden = normal * row_of(gain_one_ref) + row_of(shift_one_ref)
        hidden_ref[...] = hidden
        feed_ref[:, :D] = hidden.astype(BF16)
        down_ref[...] = jnp.zeros_like(down_ref)

    width = slope_ref.shape[1]
    at = pl.multiple_of(step * width, width)
    units = pl.ds(at, width)
    act, slope = gelu_and_slope(
        product(feed_ref[:, :D], wup_ref[:, units]) + row_of(bup_ref, at, width)
    )
    slope_ref[...] = slope
    down_ref[...] += product(act.astype(BF16), wdown_ref[units, :])

    @pl.when(step == pl.num_programs(0) - 1)
    def _():
        normal, inverse = normalized(hidden_ref[...] + (down_ref[...] + row_of(bdown_ref)))
        output_ref[...] = (normal * row_of(gain_two_ref) + row_of(shift_two_ref)).astype(BF16)
        position = place_ref[blocks] * BLOCK + lax.broadcasted_iota(jnp.int32, (BLOCK, 1), 0)
        valid = segment_of(position, place_ref, 2 * blocks) < DOCS
        g_out = jnp.where(valid, cot_ref[...].astype(F32), 0.0)
        g_resid, g_gain, g_shift = normalized_back(g_out, normal, inverse, row_of(gain_two_ref))
        resid_ref[...] = g_resid
        g_down = g_resid.astype(BF16)
        feed_ref[:, D:] = g_down
        sums_ref[0:1, :] = column_sum(g_down.astype(F32))
        sums_ref[1:2, :] = g_gain
        sums_ref[2:3, :] = g_shift


def middle_forward(
    place, context, tokens, cotangent, w_out, b_out, gain_one, shift_one, b_down, gain_two, shift_two,
    w_up, b_up, w_down,
):
    units = w_up.shape[1]
    width = 512
    return pl.pallas_call(
        functools.partial(middle_forward_kernel, (place.shape[0] - DOCS) // 2),
        grid_spec=pltpu.PrefetchScalarGridSpec(
        num_scalar_prefetch=1,
        grid=(units // width,),
        in_specs=[once(BLOCK, D)] * 3
        + [pl.BlockSpec(memory_space=pltpu.VMEM)]
        + [pl.BlockSpec(memory_space=pltpu.VMEM)] * 6
        + [
            pl.BlockSpec(memory_space=pltpu.VMEM),
            pl.BlockSpec(memory_space=pltpu.VMEM),
            pl.BlockSpec(memory_space=pltpu.VMEM),
        ],
        out_specs=[
            once(BLOCK, D),
            once(BLOCK, 2 * D),
            once(BLOCK, D),
            once(BLOCK, BLOCK),
            once(BLOCK, D),
            pl.BlockSpec((BLOCK, width), lambda p, *_: (0, p)),
            once(8, D),
        ],
        scratch_shapes=[pltpu.VMEM((BLOCK, D), F32), pltpu.VMEM((BLOCK, D), F32)],
        ),
        out_shape=[
            jax.ShapeDtypeStruct((BLOCK, D), BF16),
            jax.ShapeDtypeStruct((BLOCK, 2 * D), BF16),
            jax.ShapeDtypeStruct((BLOCK, D), F32),
            jax.ShapeDtypeStruct((BLOCK, BLOCK), F32),
            jax.ShapeDtypeStruct((BLOCK, D), F32),
            jax.ShapeDtypeStruct((BLOCK, units), F32),
            jax.ShapeDtypeStruct((8, D), F32),
        ],
        compiler_params=pltpu.CompilerParams(vmem_limit_bytes=20 * 2**20),
        name="middle_forward",
    )(
        place, context, tokens, cotangent, w_out, b_out, gain_one, shift_one, b_down,
        gain_two, shift_two, w_up, b_up, w_down,
    )


def middle_backward_kernel(
    feed_ref,
    resid_ref,
    normal_ref,
    inverse_ref,
    gain_ref,
    wout_ref,
    slope_ref,
    wup_ref,
    wdown_ref,
    g_resid_ref,
    g_attn_ref,
    g_ctx_ref,
    sums_ref,
    g_up_ref,
    acc_ref,
):
    step = pl.program_id(0)

    @pl.when(step == 0)
    def _():
        acc_ref[...] = resid_ref[...]

    width = slope_ref.shape[1]
    units = pl.ds(pl.multiple_of(step * width, width), width)
    g_up = (product_right(feed_ref[:, D:], wdown_ref[units, :]) * slope_ref[...]).astype(BF16)
    g_up_ref[...] = g_up
    acc_ref[...] += product_right(g_up, wup_ref[:, units])

    @pl.when(step == pl.num_programs(0) - 1)
    def _():
        g_resid, g_gain, g_shift = normalized_back(
            acc_ref[...], normal_ref[...], inverse_ref[:, 0:1], row_of(gain_ref)
        )
        g_resid_ref[...] = g_resid
        g_attn = g_resid.astype(BF16)
        g_attn_ref[...] = g_attn
        g_ctx_ref[...] = product_right(g_attn, wout_ref[...]).astype(BF16)
        sums_ref[0:1, :] = column_sum(g_attn.astype(F32))
        sums_ref[1:2, :] = g_gain
        sums_ref[2:3, :] = g_shift


def middle_backward(feed, g_resid_two, normal, inverse, gain_one, w_out, slope, w_up, w_down):
    units = w_up.shape[1]
    width = 512
    return pl.pallas_call(
        middle_backward_kernel,
        grid=(units // width,),
        in_specs=[
            once(BLOCK, 2 * D),
            once(BLOCK, D),
            once(BLOCK, D),
            once(BLOCK, BLOCK),
            pl.BlockSpec(memory_space=pltpu.VMEM),
            pl.BlockSpec(memory_space=pltpu.VMEM),
            pl.BlockSpec((BLOCK, width), lambda p: (0, p)),
            pl.BlockSpec(memory_space=pltpu.VMEM),
            pl.BlockSpec(memory_space=pltpu.VMEM),
        ],
        out_specs=[
            once(BLOCK, D),
            once(BLOCK, D),
            once(BLOCK, D),
            once(8, D),
            pl.BlockSpec((BLOCK, width), lambda p: (0, p)),
        ],
        scratch_shapes=[pltpu.VMEM((BLOCK, D), F32)],
        out_shape=[
            jax.ShapeDtypeStruct((BLOCK, D), F32),
            jax.ShapeDtypeStruct((BLOCK, D), BF16),
            jax.ShapeDtypeStruct((BLOCK, D), BF16),
            jax.ShapeDtypeStruct((8, D), F32),
            jax.ShapeDtypeStruct((BLOCK, units), BF16),
        ],
        compiler_params=pltpu.CompilerParams(vmem_limit_bytes=20 * 2**20),
        name="middle_backward",
    )(
        feed, g_resid_two, normal, inverse, gain_one, w_out, slope,
        w_up, w_down,
    )


def row_of(ref, at=None, width=None):
    return (ref[...] if at is None else ref[pl.ds(at, width)]).reshape(1, -1)


def gelu_and_slope(x):
    below = 0.5 + 0.5 * lax.erf(x * math.sqrt(0.5))
    density = jnp.exp(-0.5 * x * x) * (1.0 / math.sqrt(2.0 * math.pi))
    return x * below, below + x * density


def feedforward_kernel(
    parts,
    order_ref,
    *refs,
):
    part_refs, refs = refs[:parts], refs[parts:]
    wup_ref, bup_ref, wdown_ref, down_own_ref, down_other_ref, up_own_ref, up_other_ref, *refs = refs
    hid_ref, gd_ref, hidt_ref, sums_ref = refs
    step = pl.program_id(0)
    shares = up_own_ref.shape[0]
    half = down_own_ref.shape[1]
    width = wup_ref.shape[1]

    @pl.when(step == 0)
    def _():
        for part in range(parts):
            rows = slice(part * BLOCK, (part + 1) * BLOCK)
            hid_ref[rows, :] = part_refs[part][:, :D]
            gd_ref[rows, :] = part_refs[part][:, D:]
        place_rows(order_ref, hidt_ref, hid_ref[...].T, 2, shares)

    lanes = pl.ds(pl.multiple_of(step * width, width), width)
    at = pl.multiple_of(order_ref[1] * sums_ref.shape[1] + step * width, width)
    act, slope = gelu_and_slope(product(hid_ref[...], wup_ref[...]) + row_of(bup_ref, at, width))
    g_up = (product_right(gd_ref[...], wdown_ref[...]) * slope).astype(BF16)
    act_turned = act.astype(BF16).T
    for core, ref in enumerate((down_own_ref, down_other_ref)):
        columns = pl.ds(pl.multiple_of((order_ref[0] ^ core) * half, BLOCK), half)
        ref[lanes, :] = product(act_turned, gd_ref[:, columns]).astype(BF16)
    store_pieces((up_own_ref, up_other_ref), 0, product(hidt_ref[...], g_up).astype(BF16), lanes)
    sums_ref[:, lanes] = product(jnp.ones((16, hid_ref.shape[0]), BF16), g_up)

    @pl.when(step == pl.num_programs(0) - 1)
    def _():
        for core, ref in enumerate((down_own_ref, down_other_ref)):
            columns = pl.ds(pl.multiple_of((order_ref[0] ^ core) * half, BLOCK), half)
            ref[pl.ds(sums_ref.shape[1], 16), :] = sums_ref[:, columns].astype(BF16)


def feedforward_gradients(order, row_parts, w_up, b_up, w_down):
    shares = len(row_parts)
    tokens = shares * BLOCK
    units = w_up.shape[1] // shares
    width = 256
    steps = units // width
    down = (units + 16, D // 2)
    up = (shares, D // shares // 2, units)
    return pl.pallas_call(
        functools.partial(feedforward_kernel, shares),
        grid_spec=pltpu.PrefetchScalarGridSpec(
            num_scalar_prefetch=1,
            grid=(steps,),
            in_specs=[once(BLOCK, 2 * D)] * shares
            + [
                pl.BlockSpec((D, width), lambda p, order: (0, order[1] * steps + p)),
                pl.BlockSpec(memory_space=pltpu.VMEM),
                pl.BlockSpec((width, D), lambda p, order: (order[1] * steps + p, 0)),
            ],
            out_specs=[pl.BlockSpec(memory_space=pltpu.VMEM)] * 4,
            scratch_shapes=[
                pltpu.VMEM((tokens, D), BF16),
                pltpu.VMEM((tokens, D), BF16),
                pltpu.VMEM((D, tokens), BF16),
                pltpu.VMEM((16, units), F32),
            ],
        ),
        out_shape=[pltpu.VMEM(shape, BF16) for shape in (down, down, up, up)],
        compiler_params=pltpu.CompilerParams(vmem_limit_bytes=16 * 2**20),
        name="feedforward_gradients",
    )(order, *row_parts, *streamed(w_up), b_up, *streamed(w_down))


def assemble_kernel(
    place_ref,
    one_ref,
    one_other_ref,
    two_ref,
    two_other_ref,
    down_ref,
    down_other_ref,
    up_ref,
    up_other_ref,
    *refs,
):
    outs, refs = refs[:8], refs[8:]
    held, sems = refs[:8], refs[8]
    query_ref, key_ref, value_ref, out_ref, wide_ref, narrow_ref, sums_ref, vec_ref = held
    piece = query_ref.shape[0] // 2
    half = one_ref.shape[1]
    units = up_ref.shape[2]
    copies = [pltpu.make_async_copy(held[at], outs[at], sems.at[at]) for at in range(8)]

    def write(cores):
        for core, (one, two, down, up) in enumerate(cores):
            rows = slice(core * piece, (core + 1) * piece)
            for bits in range(4):
                at = pl.multiple_of((place_ref[1] ^ bits) * units, units)
                wide_ref[rows, pl.ds(at, units)] = up[bits].astype(F32)
        copies[4].start()
        for core, (one, two, down, up) in enumerate(cores):
            columns = slice(core * half, (core + 1) * half)
            narrow_ref[:, columns] = down[:units, :].astype(F32)
            sums_ref[:, columns] = down[units:, :].astype(F32)
        copies[5].start()
        copies[6].start()
        for at, ref in enumerate((query_ref, key_ref, value_ref)):
            for core, (one, two, down, up) in enumerate(cores):
                rows = slice(core * piece, (core + 1) * piece)
                ref[rows, :half] = one[at * piece : (at + 1) * piece, :].astype(F32)
                ref[rows, half:] = two[at * piece : (at + 1) * piece, :].astype(F32)
            copies[at].start()
        base = 3 * piece
        vec_ref[:, :half] = one_ref[base : base + 16, :].astype(F32)
        vec_ref[:, half:] = two_ref[base : base + 16, :].astype(F32)
        copies[7].start()
        base += 16
        for core, (one, two, down, up) in enumerate(cores):
            rows = slice(core * piece, (core + 1) * piece)
            out_ref[rows, :half] = one[base : base + piece, :].astype(F32)
            out_ref[rows, half:] = one[base + piece : base + 2 * piece, :].astype(F32)
        copies[3].start()
        for copy in copies:
            copy.wait()

    own = (one_ref, two_ref, down_ref, up_ref)
    other = (one_other_ref, two_other_ref, down_other_ref, up_other_ref)

    @pl.when(place_ref[0] == 0)
    def _():
        write((own, other))

    @pl.when(place_ref[0] != 0)
    def _():
        write((other, own))


def assemble(order, one, two, down, up):
    share = D // up[0].shape[0]
    units = up[0].shape[2]
    shapes = [(share, D)] * 4 + [(share, units * up[0].shape[0]), (units, D), (16, D), (16, D)]
    whole = pl.BlockSpec(memory_space=pltpu.VMEM)
    return pl.pallas_call(
        assemble_kernel,
        grid_spec=pltpu.PrefetchScalarGridSpec(
            num_scalar_prefetch=1,
            grid=(1,),
            in_specs=[whole] * 8,
            out_specs=[pl.BlockSpec(memory_space=pl.ANY)] * 8,
            scratch_shapes=[pltpu.VMEM(shape, F32) for shape in shapes]
            + [pltpu.SemaphoreType.DMA((8,))],
        ),
        out_shape=[pltpu.HBM(shape, F32) for shape in shapes],
        compiler_params=pltpu.CompilerParams(vmem_limit_bytes=16 * 2**20),
        cost_estimate=pl.CostEstimate(flops=0, bytes_accessed=24 * 2**20, transcendentals=0),
        name="assemble",
    )(order, *one, *two, *down, *up)


def swapped(array, axis, bits):
    return lax.ppermute(array, axis, [(i, i ^ bits) for i in range(lax.axis_size(axis))])


def from_peers(arrays):
    return [swapped(array, "seq", bits) for bits, array in enumerate(arrays, 1)]


def picked(array, index, axis):
    return lax.dynamic_index_in_dim(array, index, axis, keepdims=False)


def together(*arrays):
    return lax.optimization_barrier(arrays)


def added(*arrays):
    return functools.reduce(jnp.add, [array.astype(F32) for array in arrays]).astype(BF16)


def halves(pack):
    middle = pack.shape[1] // 32 * 16
    return pack[:, :middle], pack[:, middle:]


def in_row_order(pack, mine):
    return jnp.stack([picked(pack, mine ^ at, 0) for at in range(4)], axis=0)


def square_mesh():
    return lax.axis_size("seq") == 4 and lax.axis_size("z") == 4


def scatter(pack):
    return from_peers([pack[1], pack[2], pack[3]])


NEXT = [(0, 1), (1, 0), (2, 3), (3, 2)]
ACROSS = [(0, 3), (1, 2), (2, 1), (3, 0)]


def half_of(share, second):
    half = share.shape[0] // 2
    return jnp.where(second, share[half:], share[:half])


def core_index():
    return lax.axis_index("core")


def both_cores(share, axis):
    other = swapped(share, "core", 1)
    first = core_index() == 0
    return jnp.concatenate(
        [jnp.where(first, share, other), jnp.where(first, other, share)], axis=axis
    )


def reduce_plain(partial):
    share = lax.psum_scatter(partial.astype(BF16), "seq", scatter_dimension=0, tiled=True)
    return lax.psum(share, ("z", "core")).astype(F32)


def local(
    tokens,
    cotangent,
    lengths,
    w_query,
    b_query,
    w_key,
    b_key,
    w_value,
    b_value,
    w_out,
    b_out,
    gain_one,
    shift_one,
    w_up,
    b_up,
    w_down,
    b_down,
    gain_two,
    shift_two,
    rel_table,
):
    rows = tokens.shape[0]
    cycle = lax.axis_size("seq")
    mine = lax.axis_index("seq")
    core = core_index()
    square = square_mesh()
    hidden_units = w_up.shape[1]
    share = D // cycle
    if square:
        token_parts = [tokens] + from_peers([tokens] * 3)
        ids = mine ^ jnp.arange(cycle, dtype=jnp.int32)
        order = jnp.stack([core, mine]).astype(jnp.int32)
        cores = 2
    else:
        token_parts = [tokens, lax.all_gather(tokens, "seq", axis=0, tiled=True)]
        ids = jnp.concatenate([mine[None], jnp.arange(cycle, dtype=jnp.int32)])
        order = jnp.zeros((2,), jnp.int32)
        cores = 1
    dist = jnp.concatenate([mine - ids, ids, lengths[0]]).astype(jnp.int32)

    at_z = lax.axis_index("z")
    end = (at_z == 0) | (at_z == 3)
    between = jnp.logical_not(end)
    low = core == 0
    odd_x, odd_y = (mine & 1) == 1, (mine & 2) == 2
    place_of = (dist, order, end, between, low, odd_x, odd_y)
    dist, order, end, between, low, odd_x, odd_y = lax.optimization_barrier(place_of)

    def in_order(pieces):
        first, second, third, fourth = pieces
        pairs = [
            (jnp.where(odd_x, b, a), jnp.where(odd_x, a, b))
            for a, b in ((first, second), (third, fourth))
        ]
        return [jnp.where(odd_y, b, a) for a, b in zip(*pairs)] + [
            jnp.where(odd_y, a, b) for a, b in zip(*pairs)
        ]

    def own_quarter(array):
        half = array.shape[1] // 2
        array = jnp.where(odd_y, array[:, half:], array[:, :half])
        return jnp.where(odd_x, array[:, half // 2 :], array[:, : half // 2])

    places = jnp.arange(RELROWS, dtype=jnp.int32)
    turn = (places[:, None] + places[None, :] == RELROWS - 1).astype(BF16)
    stay = (places[:, None] == places[None, :]).astype(BF16)
    rel_both = product(jnp.concatenate([turn, stay], axis=0), rel_table).astype(BF16)
    pos_key_back = (product(rel_both[:RELROWS], w_key) + b_key).astype(BF16)
    pos_query = (product(rel_both, w_query) + b_query).astype(BF16)
    pos_key_back, (dist, order, end, between, low, odd_x, odd_y) = together(
        pos_key_back, (dist, order, end, between, low, odd_x, odd_y)
    )
    context, prob, query, key, value, tokens_row, *held = attention_forward(
        dist,
        token_parts,
        [w_query, w_key, w_value],
        [b_query, b_key, b_value],
        pos_key_back,
        pos_query,
        [w_up, w_down, w_out],
    )
    held_up, held_down, held_out = held

    output, feed, normal_one, inverse_one, g_resid_two, slope, sums_two = middle_forward(
        dist, context, tokens, cotangent, held_out, b_out, gain_one, shift_one, b_down, gain_two,
        shift_two, held_up, b_up, held_down,
    )
    if square:
        row_parts = [feed] + from_peers([feed] * 3)
    g_resid_one, g_attn, g_context, sums_one, g_up = middle_backward(
        feed, g_resid_two, normal_one, inverse_one, gain_one, held_out, slope, held_up, held_down
    )
    vectors = [sums_one, sums_two]

    def backward(start, pairs, g_context, extra_one, extra_two):
        outs = attention_backward(
            start, pairs, cores, cycle, dist, order, query, key, value, pos_key_back, pos_query, prob,
            g_context, tokens_row, rel_table, w_query, w_key, w_value, extra_one, extra_two, vectors,
        )
        return outs[:cores], outs[cores:]

    piece = share // cores
    whole_rows = lambda v, at, each: v[:, at : at + each].reshape(cores * each, -1)

    def unpacked(v, each):
        base = 3 * piece + 16
        parts = D // v.shape[2]
        return jnp.concatenate(
            [whole_rows(v, base + part * each, each) for part in range(parts)], axis=1
        )

    def rel_own(pack):
        return unpacked(pack, RELROWS // cycle // cores)

    def results(grads, grad_w_out, vectors, grad_rel, grad_tokens, grad_w_up, grad_w_down, grad_b_up):
        return (
            output,
            grad_tokens,
            grads[0],
            vectors[0],
            grads[1],
            vectors[1],
            grads[2],
            vectors[2],
            grad_w_out,
            vectors[3],
            vectors[4],
            vectors[5],
            grad_w_up,
            grad_b_up,
            grad_w_down,
            vectors[6],
            vectors[7],
            vectors[8],
            grad_rel,
        )

    if not square:
        act = gelu_and_slope(product(feed[:, :D], w_up) + b_up)[0].astype(BF16)
        (one,), carried = backward(0, 3, g_context, context, g_attn)
        (two,), (home, away) = backward(3, 3, g_context, *carried)
        packs = [
            lax.psum(lax.psum_scatter(v, "seq", scatter_dimension=0, tiled=True), ("z", "core"))
            for v in (one, two)
        ]
        got = lax.psum_scatter(away, "seq", scatter_dimension=0, tiled=False)
        grads = [
            jnp.concatenate([whole_rows(v, at * piece, piece) for v in packs], axis=1).astype(F32)
            for at in range(3)
        ]
        base = 3 * piece
        sums = jnp.concatenate([v[0, base : base + 16] for v in packs], axis=1).astype(F32)
        return results(
            grads,
            unpacked(packs[0], piece).astype(F32),
            lax.dynamic_slice_in_dim(sums, mine * share, share, 1),
            lax.all_gather(rel_own(packs[-1]), "seq", axis=0, tiled=True).astype(F32),
            g_resid_one + home + got.astype(F32),
            reduce_plain(product_left(feed[:, :D], g_up)),
            reduce_plain(product_left(act, feed[:, D:])),
            reduce_plain(jnp.sum(g_up.astype(F32), axis=0)),
        )

    one, carried = backward(0, 3, g_context, context, g_attn)

    row_parts, one, carried = together(row_parts, one, carried)
    one_got = swapped(one[1], "core", 1)
    down_own, down_other, up_own, up_other = feedforward_gradients(
        order, row_parts, w_up, b_up, w_down
    )

    one_got, down_own, down_other, up_own, up_other = together(
        one_got, down_own, down_other, up_own, up_other
    )
    down_got = swapped(down_other, "core", 1)
    up_got = swapped(up_other, "core", 1)
    one_share = added(one[0], one_got)
    down_share = added(down_own, down_got)
    up_share = added(up_own, up_got)

    units = hidden_units // 4

    def first_start(v):
        first, second = halves(v)
        return swapped(first[1::2], "seq", 1), swapped(second[2:], "seq", 2)

    def first_end(v, got):
        first, second = halves(v)
        return added(first[0::2], got[0]), added(second[:2], got[1])

    def second_start(v):
        return swapped(v[0][1], "seq", 2), swapped(v[1][1], "seq", 1)

    def second_end(v, got):
        return jnp.concatenate([added(v[0][0], got[0]), added(v[1][0], got[1])], axis=0)

    def core_start(v):
        return swapped(v, "core", 1)

    def rel_rows(pair):
        base, each = 3 * share // 2 + 16, RELROWS // 8
        own, other = [
            jnp.concatenate([v[base : base + each], v[base + each : base + 2 * each]], axis=1)
            for v in pair
        ]
        return jnp.concatenate(
            [jnp.where(low, own, other), jnp.where(low, other, own)], axis=0
        )

    moves = {
        "first": (first_start, first_end),
        "second": (second_start, second_end),
        "in": (
            lambda v: lax.ppermute(half_of(v, end), "z", NEXT),
            lambda v, got: added(half_of(v, between), got),
        ),
        "mid": (lambda v: lax.ppermute(v, "z", ACROSS), added),
        "out": (
            lambda v: lax.ppermute(v, "z", NEXT),
            lambda v, got: jnp.concatenate(
                [jnp.where(end, v, got), jnp.where(end, got, v)], axis=0
            ),
        ),
        "pair": (lambda v: swapped(v[1], "core", 1), lambda v, got: added(v[0], got)),
        "rows": (core_start, lambda v, got: (v, got)),
        "columns": (core_start, lambda v, got: (v, got)),
        "give": (scatter, lambda v, got: jnp.stack([v[0]] + got, axis=0)),
        "home": (
            lambda v: from_peers([v[0], v[1], v[2]]),
            lambda v, got: functools.reduce(jnp.add, [part.astype(F32) for part in got]),
        ),
        "spread": (scatter, lambda v, got: added(v[0], *got)),
        "x": (lambda v: swapped(v[1], "seq", 1), lambda v, got: [v[0], got, v[2], v[3]]),
        "y": (lambda v: swapped(v[2], "seq", 2), lambda v, got: [v[0], v[1], got, v[3]]),
        "d": (
            lambda v: swapped(v[3], "seq", 3),
            lambda v, got: jnp.stack([v[0], v[1], v[2], got], axis=0),
        ),
        "dd": (
            lambda v: swapped(v[3], "seq", 3),
            lambda v, got: jnp.stack([v[0], v[1], v[2], got], axis=0),
        ),
        "hx": (lambda v: swapped(v[0], "seq", 1), lambda v, got: [got, v[1], v[2]]),
        "hy": (lambda v: swapped(v[1], "seq", 2), lambda v, got: [v[0], got, v[2]]),
        "hd": (
            lambda v: swapped(v[2], "seq", 3),
            lambda v, got: functools.reduce(
                jnp.add, [part.astype(F32) for part in (v[0], v[1], got)]
            ),
        ),
        "rel": (
            lambda v: from_peers([rel_rows(v)] * 3),
            lambda v, got: (v, [rel_rows(v)] + got),
        ),
    }
    held_sums = {"down": down_share, "up": up_share, "one": one_share}
    flying = {}

    def begin(*steps):
        for step in steps:
            name, move = step.split(".")
            if move == "share":
                both = zip(held_sums["up"][1:], held_sums["away"])
                flying[step] = from_peers([jnp.concatenate(parts, axis=0) for parts in both])
            else:
                flying[step] = moves[move][0](held_sums[name])

    def meet(done, then):
        names = [step.split(".")[0] for step in then] + [step.split(".")[0] for step in done]
        names += ["away"] if "up.share" in done or "up.share" in then else []
        names = [name for at, name in enumerate(names) if name not in names[:at]]
        gots = {step: flying.pop(step) for step in done}
        kept, gots = together({name: held_sums[name] for name in names}, gots)
        held_sums.update(kept)
        for step in done:
            name, move = step.split(".")
            if move == "share":
                each = held_sums["up"].shape[1]
                parts = [held_sums["up"][0]] + [got[:each] for got in gots[step]]
                held_sums["up"] = jnp.stack(parts, axis=0)
                homes = [got[each:].astype(F32) for got in gots[step]]
                held_sums["away"] = functools.reduce(jnp.add, homes)
            else:
                held_sums[name] = moves[move][1](held_sums[name], gots[step])
        begin(*then)

    stages = (
        ([], ["up.in", "one.spread"]),
        (["up.in", "one.spread"], ["two.pair", "up.mid", "one.in"]),
        (["two.pair"], ["two.first", "down.in"]),
        (["two.first", "up.mid", "one.in"], ["two.second", "up.out", "one.mid"]),
        (["two.second", "down.in", "one.mid"], ["two.in", "down.mid", "one.out"]),
        (["two.in", "up.out", "one.out"], ["two.mid", "up.share", "one.rows"]),
        (["two.mid", "down.mid", "one.rows"], ["two.out", "down.out"]),
        (["two.out", "up.share", "down.out"], ["two.rows", "up.columns", "down.columns"]),
        (["two.rows", "up.columns", "down.columns"], []),
    )
    begin(*stages[0][1])
    g_context, held_sums = together(g_context, held_sums)
    two, (home, away) = backward(3, 3, g_context, *carried)
    home, held_sums, flying_now = together(
        home, dict(held_sums, two=two, away=away), {step: flying[step] for step in stages[1][0]}
    )
    flying.update(flying_now)
    for done, then in stages[1:]:
        meet(done, then)

    grad_tokens = g_resid_one + home + held_sums["away"]
    rel = rel_rows(held_sums["two"])
    from_y, from_both = swapped(rel, "seq", 2), swapped(rel, "seq", 3)
    *grads, grad_w_up, grad_w_down, sums_up, sums = assemble(
        order, held_sums["one"], held_sums["two"], held_sums["down"], held_sums["up"]
    )
    rel, sums = together(rel, sums)
    rel_parts = [rel, swapped(rel, "seq", 1), from_y, from_both]
    return results(
        grads[:3],
        grads[3],
        own_quarter(sums),
        jnp.concatenate(in_order(rel_parts), axis=0).astype(F32),
        grad_tokens,
        grad_w_up,
        grad_w_down,
        sums_up[0],
    )


def solution(mesh):
    lines, cycle = mesh.devices.shape
    chips = Mesh(mesh.devices.reshape(lines // 2, 2, cycle), ("z", "core", "seq"))
    return jax.shard_map(
        local,
        mesh=chips,
        in_specs=(
            P(("z", "core", "seq"), None),
            P(("z", "core", "seq"), None),
            P(("z", "core"), None),
        )
        + (P(),) * 17,
        out_specs=(
            P(("z", "core", "seq"), None),
            P(("z", "core", "seq"), None),
            P("seq", None),
            P("seq"),
            P("seq", None),
            P("seq"),
            P("seq", None),
            P("seq"),
            P("seq", None),
            P("seq"),
            P("seq"),
            P("seq"),
            P("seq", None),
            P("seq"),
            P("seq", None),
            P("seq"),
            P("seq"),
            P("seq"),
            P(),
        ),
        check_vma=False,
    )
```

```python
import functools
import math

import jax
import jax.numpy as jnp
from jax import lax
from jax.experimental import pallas as pl
from jax.experimental.pallas import tpu as pltpu
from jax.sharding import Mesh, PartitionSpec as P

D = 768
HEADS = 12
HEAD = 64
SPAN = 256
RELROWS = 512
BLOCK = 128
EXT = RELROWS + 2 * SPAN
PAIRS = HEADS // 2
VECTORS = 2
LATER = 3
DOCS = 4
SCALE = 1.0 / math.sqrt(3 * HEAD)
F32 = jnp.float32
BF16 = jnp.bfloat16
ROLLED = BF16


def normalized(resid):
    center = resid - jnp.mean(resid, axis=-1, keepdims=True)
    inverse = lax.rsqrt(jnp.mean(center * center, axis=-1, keepdims=True) + 1e-07)
    return center * inverse, inverse


def normalized_back(grad, normal, inverse, gain):
    hat = grad * gain
    means = jnp.mean(hat, axis=-1, keepdims=True) + normal * jnp.mean(
        hat * normal, axis=-1, keepdims=True
    )
    total = lambda v: jnp.sum(v, axis=0, keepdims=True)
    return (hat - means) * inverse, total(grad * normal), total(grad)


def product(left, right):
    return jnp.dot(left, right, preferred_element_type=F32)


def product_left(left, right):
    return lax.dot_general(left, right, (((0,), (0,)), ((), ())), preferred_element_type=F32)


def product_right(left, right):
    return lax.dot_general(left, right, (((1,), (1,)), ((), ())), preferred_element_type=F32)


def segment_of(position, place_ref, at):
    passed, bound = jnp.zeros(position.shape, jnp.int32), 0
    for document in range(DOCS):
        bound = bound + place_ref[at + document]
        passed = passed + (position >= bound).astype(jnp.int32)
    return passed


def anti_identity():
    rows = lax.broadcasted_iota(jnp.int32, (BLOCK, BLOCK), 0)
    cols = lax.broadcasted_iota(jnp.int32, (BLOCK, BLOCK), 1)
    return (rows + cols == BLOCK - 1).astype(BF16)


def extend(ext_ref, table_ref):
    ext_ref[SPAN : SPAN + RELROWS, :] = table_ref[...]
    ext_ref[0:SPAN, :] = jnp.broadcast_to(table_ref[0:1, :], (SPAN, BLOCK))
    last = table_ref[RELROWS - 1 : RELROWS, :]
    ext_ref[SPAN + RELROWS :, :] = jnp.broadcast_to(last, (SPAN, BLOCK))


def window_start(offset):
    return pl.multiple_of(jnp.clip(offset, 0, EXT - 2 * BLOCK), BLOCK)


def head_mask(head):
    lane = lax.broadcasted_iota(jnp.int32, (1, BLOCK), 1)
    return (lane >= head * HEAD) & (lane < (head + 1) * HEAD)


def band_roll(wide, shift):
    return pltpu.roll(wide, shift, 1, stride=1, stride_axis=0)


def by_head(pair):
    zero = jnp.zeros_like(pair)
    return jnp.concatenate([jnp.where(head_mask(head), pair, zero) for head in range(2)], axis=0)


def forward_kernel(
    parts, blocks, dist_ref, *refs
):
    part_refs, refs = refs[:parts], refs[parts:]
    wq_ref, wk_ref, wv_ref, bq_ref, bk_ref, bv_ref, pk_ref, pq_ref, *refs = refs
    later, refs = refs[:LATER], refs[LATER:]
    ctx_ref, prob_ref, q_ref, k_ref, v_ref, tok_ref, *refs = refs
    held, refs = refs[:LATER], refs[LATER:]
    score_ref, ek_ref, eq_ref, bias_ref, sems = refs
    copies = [
        pltpu.make_async_copy(later[at], held[at], sems.at[at]) for at in range(LATER)
    ]

    @pl.when(pl.program_id(0) == 0)
    def _():
        for copy in copies:
            copy.start()

    @pl.when(pl.program_id(0) == pl.num_programs(0) - 1)
    def _():
        for copy in copies:
            copy.wait()

    extend(ek_ref, pk_ref)
    extend(eq_ref, pq_ref)

    @pl.when(pl.program_id(0) == 0)
    def _():
        at = 0
        for ref in part_refs:
            tok_ref[at : at + ref.shape[0], :] = ref[...]
            at += ref.shape[0]
        mine = dist_ref[blocks]
        lane = lax.broadcasted_iota(jnp.int32, (1, BLOCK), 1)
        line = lax.broadcasted_iota(jnp.int32, (BLOCK, 1), 0)
        query_segment = segment_of(mine * BLOCK + lane, dist_ref, 2 * blocks)
        for block in range(blocks):
            home = dist_ref[blocks + block]
            allowed = segment_of(home * BLOCK + line, dist_ref, 2 * blocks) == query_segment
            if block > 0:
                allowed = jnp.logical_and(allowed, home != mine)
            rows = slice(block * BLOCK, (block + 1) * BLOCK)
            bias_ref[rows, :] = jnp.where(allowed, 0.0, -1e30)

    at = pl.multiple_of(pl.program_id(0) * BLOCK, BLOCK)
    both = product(tok_ref[...], jnp.concatenate([wk_ref[...], wv_ref[...]], axis=1))
    k_ref[...] = (both[:, :BLOCK] + row_of(bk_ref, at, BLOCK)).astype(BF16)
    v_ref[...] = (both[:, BLOCK:] + row_of(bv_ref, at, BLOCK)).astype(BF16)
    q = (product(tok_ref[:BLOCK, :], wq_ref[...]) + row_of(bq_ref, at, BLOCK)).astype(BF16)
    q_ref[...] = q
    q_heads = by_head(q)
    tops = [jnp.full((1, BLOCK), -jnp.inf, F32) for head in range(2)]
    for block in range(blocks):
        dist = dist_ref[block]
        rows = slice(block * BLOCK, (block + 1) * BLOCK)
        k_heads = by_head(k_ref[rows, :])
        window_c = ek_ref[pl.ds(window_start(384 - dist * BLOCK), 2 * BLOCK), :]
        window_p = eq_ref[pl.ds(window_start(384 + dist * BLOCK), 2 * BLOCK), :]
        c2p = product_right(q_heads, window_c)
        p2c = product_right(k_heads, window_p)
        direct = product_right(k_heads, q)
        for head in range(2):
            own = slice(head * BLOCK, (head + 1) * BLOCK)
            first = band_roll(c2p[own].astype(BF16), BLOCK + 1)[:, :BLOCK].T
            second = band_roll(p2c[own].astype(BF16), BLOCK + 1)[:, :BLOCK]
            score = (direct[own] + first.astype(F32) + second.astype(F32)) * SCALE + bias_ref[rows, :]
            score_ref[head, rows, :] = score
            tops[head] = jnp.maximum(tops[head], jnp.max(score, axis=0, keepdims=True))
    probs = []
    for head in range(2):
        weight = jnp.exp(score_ref[head] - tops[head])
        total = jnp.sum(weight, axis=0, keepdims=True)
        prob = (weight * (1.0 / total)).astype(BF16)
        prob_ref[head] = prob
        probs.append(prob)
    v = v_ref[...]
    zero = jnp.zeros_like(v)
    out = product_left(probs[0], jnp.where(head_mask(0), v, zero)) + product_left(
        probs[1], jnp.where(head_mask(1), v, zero)
    )
    ctx_ref[...] = out.astype(BF16)


def streamed(*arrays):
    return [pltpu.with_memory_space_constraint(array, pltpu.HBM) for array in arrays]


def once(*shape):
    return pl.BlockSpec(shape, lambda p, *_: (0,) * len(shape), pipeline_mode=pl.Buffered(1))


def fits(keys):
    return keys <= 2 * RELROWS


def kept(keys, *shape):
    return pl.BlockSpec(memory_space=pltpu.VMEM) if fits(keys) else once(*shape)


def kept_array(keys, shape, dtype):
    return (pltpu.VMEM if fits(keys) else jax.ShapeDtypeStruct)(shape, dtype)


def attention_forward(dist, token_parts, weights, biases, pos_key, pos_query, later):
    keys = sum(part.shape[0] for part in token_parts)
    blocks = keys // BLOCK
    pair = lambda rows: pl.BlockSpec((rows, BLOCK), lambda p, dist: (0, p))
    return pl.pallas_call(
        functools.partial(forward_kernel, len(token_parts), blocks),
        grid_spec=pltpu.PrefetchScalarGridSpec(
            num_scalar_prefetch=1,
            grid=(PAIRS,),
            in_specs=[once(*part.shape) for part in token_parts]
            + [pair(D)] * 3
            + [pl.BlockSpec(memory_space=pltpu.VMEM)] * 3
            + [pair(RELROWS), pair(RELROWS)]
            + [pl.BlockSpec(memory_space=pl.ANY)] * LATER,
            out_specs=[
                pair(BLOCK),
                pl.BlockSpec((2, keys, BLOCK), lambda p, dist: (p, 0, 0)),
                pair(BLOCK),
                pair(keys),
                pair(keys),
                kept(keys, keys, D),
            ]
            + [pl.BlockSpec(memory_space=pl.ANY)] * LATER,
            scratch_shapes=[
                pltpu.VMEM((2, keys, BLOCK), F32),
                pltpu.VMEM((EXT, BLOCK), BF16),
                pltpu.VMEM((EXT, BLOCK), BF16),
                pltpu.VMEM((keys, BLOCK), F32),
                pltpu.SemaphoreType.DMA((LATER,)),
            ],
        ),
        out_shape=[
            jax.ShapeDtypeStruct((BLOCK, D), BF16),
            pltpu.HBM((HEADS, keys, BLOCK), BF16),
            pltpu.HBM((BLOCK, D), BF16),
            pltpu.HBM((keys, D), BF16),
            pltpu.HBM((keys, D), BF16),
            kept_array(keys, (keys, D), BF16),
        ]
        + [pltpu.VMEM(array.shape, array.dtype) for array in later],
        compiler_params=pltpu.CompilerParams(vmem_limit_bytes=(16 if fits(keys) else 40) * 2**20),
        name="attention_forward",
    )(dist, *token_parts, *streamed(*weights), *biases, *streamed(pos_key, pos_query), *streamed(*later))


def fold_edges(acc_ref):
    head_sum = jnp.sum(acc_ref[:, 0:SPAN], axis=1, keepdims=True)
    tail_sum = jnp.sum(acc_ref[:, SPAN + RELROWS :], axis=1, keepdims=True)
    lane = lax.broadcasted_iota(jnp.int32, (BLOCK, RELROWS), 1)
    middle = acc_ref[:, SPAN : SPAN + RELROWS]
    middle = middle + jnp.where(lane == 0, head_sum, 0.0)
    return (middle + jnp.where(lane == RELROWS - 1, tail_sum, 0.0)).astype(BF16)


def flipped_lanes(array, flip):
    parts = array.shape[1] // BLOCK
    return jnp.concatenate(
        [
            product(array[:, part * BLOCK : (part + 1) * BLOCK], flip).astype(BF16)
            for part in reversed(range(parts))
        ],
        axis=1,
    )


def place(order_ref, share, core, shares, each):
    at = (core ^ order_ref[0]) * shares + (share ^ order_ref[1])
    return pl.multiple_of(at * each, 16)


def place_rows(order_ref, into_ref, value, cores, shares):
    each = value.shape[0] // (cores * shares)
    for share in range(shares):
        for core in range(cores):
            at = (share * cores + core) * each
            into_ref[pl.ds(place(order_ref, share, core, shares, each), each), :] = value[
                at : at + each
            ]


def store_pieces(refs, at, value, lanes):
    shares = refs[0].shape[0]
    each = value.shape[0] // (len(refs) * shares)
    for core, ref in enumerate(refs):
        for share in range(shares):
            start = (core * shares + share) * each
            ref[share, at : at + each, lanes] = value[start : start + each]


def backward_kernel(
    blocks,
    cores,
    first,
    last,
    dist_ref,
    order_ref,
    q_ref,
    k_ref,
    v_ref,
    pk_ref,
    pq_ref,
    prob_ref,
    gctx_ref,
    tok_ref,
    rel_ref,
    wq_ref,
    wk_ref,
    wv_ref,
    extra_one_ref,
    extra_two_ref,
    *refs,
):
    vec_refs, refs = refs[:VECTORS], refs[VECTORS:]
    pack_refs, refs = refs[:cores], refs[cores:]
    backward_body(
        blocks, first, last, dist_ref, order_ref, q_ref, k_ref, v_ref, pk_ref, pq_ref, prob_ref, gctx_ref,
        tok_ref, rel_ref, wq_ref, wk_ref, wv_ref, extra_one_ref, extra_two_ref, vec_refs, pack_refs, *refs
    )


def backward_body(
    blocks,
    first,
    last,
    dist_ref,
    order_ref,
    q_ref,
    k_ref,
    v_ref,
    pk_ref,
    pq_ref,
    prob_ref,
    gctx_ref,
    tok_ref,
    rel_ref,
    wq_ref,
    wk_ref,
    wv_ref,
    extra_one_ref,
    extra_two_ref,
    vec_refs,
    pack_refs,
    out_one_ref,
    out_two_ref,
    back_ref,
    gk_ref,
    gv_ref,
    acck_ref,
    accq_ref,
    tokt_ref,
    relt_ref,
    acc_tok_ref,
    acc_rel_ref,
    turn_ref,
    ek_ref,
    eq_ref,
):
    step = pl.program_id(0)
    if not last:
        acc_tok_ref, acc_rel_ref = out_one_ref, out_two_ref
    extend(ek_ref, pk_ref)
    extend(eq_ref, pq_ref)
    cores, shares, half = len(pack_refs), pack_refs[0].shape[0], pack_refs[0].shape[2]
    share = D // cores // shares
    flip = anti_identity()

    @pl.when(step == 0)
    def _():
        place_rows(order_ref, tokt_ref, tok_ref[...].T, cores, shares)
        place_rows(order_ref, relt_ref, rel_ref[...].T, cores, shares)
        if first:
            acc_tok_ref[...] = jnp.zeros_like(acc_tok_ref)
            acc_rel_ref[...] = jnp.zeros_like(acc_rel_ref)
        else:
            acc_tok_ref[...] = extra_one_ref[...]
            acc_rel_ref[...] = extra_two_ref[...]

    acck_ref[...] = jnp.zeros_like(acck_ref)
    accq_ref[...] = jnp.zeros_like(accq_ref)
    g_heads = by_head(gctx_ref[...])
    first_rows = lax.broadcasted_iota(jnp.int32, (BLOCK, 1), 0) < HEAD
    first_lanes = head_mask(0)

    def turned_heads(array):
        turned = array.T
        zero = jnp.zeros_like(turned)
        return jnp.concatenate(
            [jnp.where(first_rows, turned, zero), jnp.where(first_rows, zero, turned)], axis=1
        )

    def of_heads(stacked):
        return jnp.where(first_lanes, stacked[:BLOCK], stacked[BLOCK:])

    q_back = product(flip, q_ref[...]).astype(BF16)
    q_turned = turned_heads(q_back)
    probs = jnp.concatenate([prob_ref[head] for head in range(2)], axis=1)
    g_prob = product_right(v_ref[...], g_heads)
    gv_ref[...] = product(probs, g_heads).astype(BF16)
    probs = probs.astype(F32)
    delta = jnp.sum(probs * g_prob, axis=0, keepdims=True)
    g_score = (probs * (g_prob - delta) * SCALE).astype(BF16)
    for head in range(2):
        lanes = slice(head * BLOCK, (head + 1) * BLOCK)
        back_ref[:, lanes] = product(g_score[:, lanes], flip).astype(BF16)
    g_query = jnp.zeros((2 * BLOCK, BLOCK), F32)
    pad = jnp.zeros((BLOCK, BLOCK), BF16)
    for block in range(blocks):
        rows = slice(block * BLOCK, (block + 1) * BLOCK)
        k_block = k_ref[rows, :]
        at = pl.ds(window_start(384 - dist_ref[block] * BLOCK), 2 * BLOCK)
        window_c = ek_ref[at, :]
        window_p = eq_ref[at, :]
        backs = [back_ref[rows, head * BLOCK : (head + 1) * BLOCK] for head in range(2)]
        turns = [back.T for back in backs]
        bands_c = [band_roll(jnp.concatenate([turn, pad], axis=1), 0) for turn in turns]
        bands_p = [band_roll(jnp.concatenate([back, pad], axis=1), 1) for back in backs]
        bands_c = jnp.concatenate(bands_c, axis=0)
        bands_p = jnp.concatenate(bands_p, axis=0)
        g_query = g_query + product(
            jnp.concatenate([jnp.concatenate(turns, axis=0), bands_c], axis=1),
            jnp.concatenate([k_block, window_c], axis=0),
        )
        g_key = product(
            jnp.concatenate([jnp.concatenate(backs, axis=0), bands_p], axis=1),
            jnp.concatenate([q_back, window_p], axis=0),
        )
        gk_ref[rows, :] = of_heads(g_key).astype(BF16)
        acck_ref[:, at] += product(q_turned, bands_c)
        accq_ref[:, at] += product(turned_heads(k_block), bands_p)

    g_query = product(flip, of_heads(g_query).astype(BF16)).astype(BF16)
    g_pos_key = flipped_lanes(fold_edges(acck_ref), flip)
    g_pos_query = fold_edges(accq_ref)
    g_key = gk_ref[...]
    g_value = gv_ref[...]
    lanes = pl.ds(pl.multiple_of(step * BLOCK, BLOCK), BLOCK)
    ones_tok = jnp.ones((16, tok_ref.shape[0]), BF16)
    ones_rel = jnp.ones((16, RELROWS), BF16)
    row = lax.broadcasted_iota(jnp.int32, (16, BLOCK), 0)
    vec = jnp.zeros((16, BLOCK), F32)
    for at, vec_ref in enumerate(vec_refs):
        for part in range(3):
            vec = vec + jnp.where(row == 3 + 3 * at + part, vec_ref[part : part + 1, :], 0.0)
    g_both = jnp.concatenate([g_key, g_value], axis=1)
    pos_both = jnp.concatenate([g_pos_key, g_pos_query], axis=0)
    from_tok = product(tokt_ref[...], g_both)
    from_rel = product_right(relt_ref[...], pos_both)
    from_own = product(tokt_ref[:, :BLOCK], g_query)
    sum_tok = product(ones_tok, g_both)
    sum_rel = product_right(ones_rel, pos_both)
    sum_own = product(ones_tok[:, :BLOCK], g_query)
    weights = [
        (from_own + from_rel[:, BLOCK:], sum_own + sum_rel[:, BLOCK:]),
        (from_tok[:, :BLOCK] + from_rel[:, :BLOCK], sum_tok[:, :BLOCK] + sum_rel[:, :BLOCK]),
        (from_tok[:, BLOCK:], sum_tok[:, BLOCK:]),
    ]
    for at, (weight, total) in enumerate(weights):
        store_pieces(pack_refs, at * share, weight.astype(BF16), lanes)
        vec = vec + jnp.where(row == at, total, 0.0)
    vec = vec.astype(BF16)
    for pack_ref in pack_refs:
        for part in range(shares):
            pack_ref[part, 3 * share : 3 * share + 16, lanes] = vec
    acc_tok_ref[...] += product_right(
        g_both,
        jnp.concatenate([wk_ref[...], wv_ref[...]], axis=1),
    )
    acc_tok_ref[0:BLOCK, :] += product_right(g_query, wq_ref[...])
    acc_rel_ref[...] += product(
        jnp.concatenate([wk_ref[...], wq_ref[...]], axis=1),
        pos_both,
    )

    @pl.when(step == pl.num_programs(0) - 1)
    def _():
        base = 3 * share + 16
        extra = None
        if last:
            out_one_ref[...] = acc_tok_ref[0:BLOCK, :]
            for block in range(1, blocks):
                out_two_ref[block - 1] = acc_tok_ref[block * BLOCK : (block + 1) * BLOCK].astype(BF16)
            place_rows(order_ref, turn_ref, acc_rel_ref[...].T.astype(BF16), cores, shares)
            extra = turn_ref[...]
        if first:
            place_rows(order_ref, turn_ref, extra_one_ref[...].T, cores, shares)
            extra = product(turn_ref[...], extra_two_ref[...]).astype(BF16)
        if extra is not None:
            each = extra.shape[0] // (cores * shares)
            for part in range(D // half):
                columns = extra[:, part * half : (part + 1) * half]
                store_pieces(pack_refs, base + part * each, columns, slice(None))


def attention_backward(
    start, pairs, cores, shares, dist, order, query, key, value, pos_key, pos_query, prob, g_context,
    tokens_row, rel_table, w_query, w_key, w_value, extra_one, extra_two, vectors,
):
    keys = key.shape[0]
    blocks = keys // BLOCK
    first, last = start == 0, start + pairs == PAIRS
    share = D // cores // shares
    half = pairs * BLOCK
    rows_extra = D if first else RELROWS if last else 0
    pack = (shares, 3 * share + 16 + rows_extra // cores // shares * (D // half), half)
    pair = lambda rows: pl.BlockSpec((rows, BLOCK), lambda p, *_: (0, p + start))
    if first:
        extras = [once(BLOCK, D), once(BLOCK, D)]
        turn = (D, BLOCK)
    else:
        extras = [kept(keys, keys, D), kept(keys, D, RELROWS)]
        turn = (RELROWS, D)
    sums = [(keys, D), (D, RELROWS)] if last else [(8, 128), (8, 128)]
    if last:
        outs = [((BLOCK, D), F32), ((blocks - 1, BLOCK, D), BF16)]
    else:
        outs = [((keys, D), F32), ((D, RELROWS), F32)]
    return pl.pallas_call(
        functools.partial(backward_kernel, blocks, cores, first, last),
        grid_spec=pltpu.PrefetchScalarGridSpec(
            num_scalar_prefetch=2,
            grid=(pairs,),
            in_specs=[
                pair(BLOCK),
                pair(keys),
                pair(keys),
                pair(RELROWS),
                pl.BlockSpec((RELROWS, BLOCK), lambda p, *_: (1, p + start)),
                pl.BlockSpec((2, keys, BLOCK), lambda p, *_: (p + start, 0, 0)),
                pair(BLOCK),
                kept(keys, keys, D),
                once(RELROWS, D),
                pair(D),
                pair(D),
                pair(D),
            ]
            + extras
            + [pair(8)] * VECTORS,
            out_specs=[kept(keys, *pack)] * cores + [kept(keys, *shape) for shape, _ in outs],
            scratch_shapes=[
                pltpu.VMEM((keys, 2 * BLOCK), BF16),
                pltpu.VMEM((keys, BLOCK), BF16),
                pltpu.VMEM((keys, BLOCK), BF16),
                pltpu.VMEM((BLOCK, EXT), F32),
                pltpu.VMEM((BLOCK, EXT), F32),
                pltpu.VMEM((D, keys), BF16),
                pltpu.VMEM((D, RELROWS), BF16),
                pltpu.VMEM(sums[0], F32),
                pltpu.VMEM(sums[1], F32),
                pltpu.VMEM(turn, BF16),
                pltpu.VMEM((EXT, BLOCK), BF16),
                pltpu.VMEM((EXT, BLOCK), BF16),
            ],
        ),
        out_shape=[kept_array(keys, pack, BF16)] * cores
        + [kept_array(keys, shape, dtype) for shape, dtype in outs],
        compiler_params=pltpu.CompilerParams(vmem_limit_bytes=(18 if fits(keys) else 58) * 2**20),
        name="attention_backward",
    )(
        dist, order, *streamed(query, key, value, pos_key, pos_query, prob), g_context,
        tokens_row, *streamed(rel_table, w_query, w_key, w_value), extra_one, extra_two, *vectors,
    )


def column_sum(array):
    return jnp.sum(array, axis=0, keepdims=True)


def middle_forward_kernel(
    blocks,
    place_ref,
    ctx_ref,
    tok_ref,
    cot_ref,
    wout_ref,
    bout_ref,
    gain_one_ref,
    shift_one_ref,
    bdown_ref,
    gain_two_ref,
    shift_two_ref,
    wup_ref,
    bup_ref,
    wdown_ref,
    output_ref,
    feed_ref,
    normal_ref,
    inverse_ref,
    resid_ref,
    slope_ref,
    sums_ref,
    hidden_ref,
    down_ref,
):
    step = pl.program_id(0)

    @pl.when(step == 0)
    def _():
        attn = product(ctx_ref[...], wout_ref[...]) + row_of(bout_ref)
        normal, inverse = normalized(tok_ref[...].astype(F32) + attn)
        normal_ref[...] = normal
        inverse_ref[...] = jnp.broadcast_to(inverse, inverse_ref.shape)
        hidden = normal * row_of(gain_one_ref) + row_of(shift_one_ref)
        hidden_ref[...] = hidden
        feed_ref[:, :D] = hidden.astype(BF16)
        down_ref[...] = jnp.zeros_like(down_ref)

    width = slope_ref.shape[1]
    at = pl.multiple_of(step * width, width)
    units = pl.ds(at, width)
    act, slope = gelu_and_slope(
        product(feed_ref[:, :D], wup_ref[:, units]) + row_of(bup_ref, at, width)
    )
    slope_ref[...] = slope
    down_ref[...] += product(act.astype(BF16), wdown_ref[units, :])

    @pl.when(step == pl.num_programs(0) - 1)
    def _():
        normal, inverse = normalized(hidden_ref[...] + (down_ref[...] + row_of(bdown_ref)))
        output_ref[...] = (normal * row_of(gain_two_ref) + row_of(shift_two_ref)).astype(BF16)
        position = place_ref[blocks] * BLOCK + lax.broadcasted_iota(jnp.int32, (BLOCK, 1), 0)
        valid = segment_of(position, place_ref, 2 * blocks) < DOCS
        g_out = jnp.where(valid, cot_ref[...].astype(F32), 0.0)
        g_resid, g_gain, g_shift = normalized_back(g_out, normal, inverse, row_of(gain_two_ref))
        resid_ref[...] = g_resid
        g_down = g_resid.astype(BF16)
        feed_ref[:, D:] = g_down
        sums_ref[0:1, :] = column_sum(g_down.astype(F32))
        sums_ref[1:2, :] = g_gain
        sums_ref[2:3, :] = g_shift


def middle_forward(
    place, context, tokens, cotangent, w_out, b_out, gain_one, shift_one, b_down, gain_two, shift_two,
    w_up, b_up, w_down,
):
    units = w_up.shape[1]
    width = 512
    return pl.pallas_call(
        functools.partial(middle_forward_kernel, (place.shape[0] - DOCS) // 2),
        grid_spec=pltpu.PrefetchScalarGridSpec(
        num_scalar_prefetch=1,
        grid=(units // width,),
        in_specs=[once(BLOCK, D)] * 3
        + [pl.BlockSpec(memory_space=pltpu.VMEM)]
        + [pl.BlockSpec(memory_space=pltpu.VMEM)] * 6
        + [
            pl.BlockSpec(memory_space=pltpu.VMEM),
            pl.BlockSpec(memory_space=pltpu.VMEM),
            pl.BlockSpec(memory_space=pltpu.VMEM),
        ],
        out_specs=[
            once(BLOCK, D),
            once(BLOCK, 2 * D),
            once(BLOCK, D),
            once(BLOCK, BLOCK),
            once(BLOCK, D),
            pl.BlockSpec((BLOCK, width), lambda p, *_: (0, p)),
            once(8, D),
        ],
        scratch_shapes=[pltpu.VMEM((BLOCK, D), F32), pltpu.VMEM((BLOCK, D), F32)],
        ),
        out_shape=[
            jax.ShapeDtypeStruct((BLOCK, D), BF16),
            jax.ShapeDtypeStruct((BLOCK, 2 * D), BF16),
            jax.ShapeDtypeStruct((BLOCK, D), F32),
            jax.ShapeDtypeStruct((BLOCK, BLOCK), F32),
            jax.ShapeDtypeStruct((BLOCK, D), F32),
            jax.ShapeDtypeStruct((BLOCK, units), F32),
            jax.ShapeDtypeStruct((8, D), F32),
        ],
        compiler_params=pltpu.CompilerParams(vmem_limit_bytes=20 * 2**20),
        name="middle_forward",
    )(
        place, context, tokens, cotangent, w_out, b_out, gain_one, shift_one, b_down,
        gain_two, shift_two, w_up, b_up, w_down,
    )


def middle_backward_kernel(
    feed_ref,
    resid_ref,
    normal_ref,
    inverse_ref,
    gain_ref,
    wout_ref,
    slope_ref,
    wup_ref,
    wdown_ref,
    g_resid_ref,
    g_attn_ref,
    g_ctx_ref,
    sums_ref,
    g_up_ref,
    acc_ref,
):
    step = pl.program_id(0)

    @pl.when(step == 0)
    def _():
        acc_ref[...] = resid_ref[...]

    width = slope_ref.shape[1]
    units = pl.ds(pl.multiple_of(step * width, width), width)
    g_up = (product_right(feed_ref[:, D:], wdown_ref[units, :]) * slope_ref[...]).astype(BF16)
    g_up_ref[...] = g_up
    acc_ref[...] += product_right(g_up, wup_ref[:, units])

    @pl.when(step == pl.num_programs(0) - 1)
    def _():
        g_resid, g_gain, g_shift = normalized_back(
            acc_ref[...], normal_ref[...], inverse_ref[:, 0:1], row_of(gain_ref)
        )
        g_resid_ref[...] = g_resid
        g_attn = g_resid.astype(BF16)
        g_attn_ref[...] = g_attn
        g_ctx_ref[...] = product_right(g_attn, wout_ref[...]).astype(BF16)
        sums_ref[0:1, :] = column_sum(g_attn.astype(F32))
        sums_ref[1:2, :] = g_gain
        sums_ref[2:3, :] = g_shift


def middle_backward(feed, g_resid_two, normal, inverse, gain_one, w_out, slope, w_up, w_down):
    units = w_up.shape[1]
    width = 512
    return pl.pallas_call(
        middle_backward_kernel,
        grid=(units // width,),
        in_specs=[
            once(BLOCK, 2 * D),
            once(BLOCK, D),
            once(BLOCK, D),
            once(BLOCK, BLOCK),
            pl.BlockSpec(memory_space=pltpu.VMEM),
            pl.BlockSpec(memory_space=pltpu.VMEM),
            pl.BlockSpec((BLOCK, width), lambda p: (0, p)),
            pl.BlockSpec(memory_space=pltpu.VMEM),
            pl.BlockSpec(memory_space=pltpu.VMEM),
        ],
        out_specs=[
            once(BLOCK, D),
            once(BLOCK, D),
            once(BLOCK, D),
            once(8, D),
            pl.BlockSpec((BLOCK, width), lambda p: (0, p)),
        ],
        scratch_shapes=[pltpu.VMEM((BLOCK, D), F32)],
        out_shape=[
            jax.ShapeDtypeStruct((BLOCK, D), F32),
            jax.ShapeDtypeStruct((BLOCK, D), BF16),
            jax.ShapeDtypeStruct((BLOCK, D), BF16),
            jax.ShapeDtypeStruct((8, D), F32),
            jax.ShapeDtypeStruct((BLOCK, units), BF16),
        ],
        compiler_params=pltpu.CompilerParams(vmem_limit_bytes=20 * 2**20),
        name="middle_backward",
    )(
        feed, g_resid_two, normal, inverse, gain_one, w_out, slope,
        w_up, w_down,
    )


def row_of(ref, at=None, width=None):
    return (ref[...] if at is None else ref[pl.ds(at, width)]).reshape(1, -1)


def gelu_and_slope(x):
    below = 0.5 + 0.5 * lax.erf(x * math.sqrt(0.5))
    density = jnp.exp(-0.5 * x * x) * (1.0 / math.sqrt(2.0 * math.pi))
    return x * below, below + x * density


def feedforward_kernel(
    parts,
    order_ref,
    *refs,
):
    part_refs, refs = refs[:parts], refs[parts:]
    wup_ref, bup_ref, wdown_ref, down_own_ref, down_other_ref, up_own_ref, up_other_ref, *refs = refs
    hid_ref, gd_ref, hidt_ref, sums_ref = refs
    step = pl.program_id(0)
    shares = up_own_ref.shape[0]
    half = down_own_ref.shape[1]
    width = wup_ref.shape[1]

    @pl.when(step == 0)
    def _():
        for part in range(parts):
            rows = slice(part * BLOCK, (part + 1) * BLOCK)
            hid_ref[rows, :] = part_refs[part][:, :D]
            gd_ref[rows, :] = part_refs[part][:, D:]
        place_rows(order_ref, hidt_ref, hid_ref[...].T, 2, shares)

    lanes = pl.ds(pl.multiple_of(step * width, width), width)
    at = pl.multiple_of(order_ref[1] * sums_ref.shape[1] + step * width, width)
    act, slope = gelu_and_slope(product(hid_ref[...], wup_ref[...]) + row_of(bup_ref, at, width))
    g_up = (product_right(gd_ref[...], wdown_ref[...]) * slope).astype(BF16)
    act_turned = act.astype(BF16).T
    for core, ref in enumerate((down_own_ref, down_other_ref)):
        columns = pl.ds(pl.multiple_of((order_ref[0] ^ core) * half, BLOCK), half)
        ref[lanes, :] = product(act_turned, gd_ref[:, columns]).astype(BF16)
    store_pieces((up_own_ref, up_other_ref), 0, product(hidt_ref[...], g_up).astype(BF16), lanes)
    sums_ref[:, lanes] = product(jnp.ones((16, hid_ref.shape[0]), BF16), g_up)

    @pl.when(step == pl.num_programs(0) - 1)
    def _():
        for core, ref in enumerate((down_own_ref, down_other_ref)):
            columns = pl.ds(pl.multiple_of((order_ref[0] ^ core) * half, BLOCK), half)
            ref[pl.ds(sums_ref.shape[1], 16), :] = sums_ref[:, columns].astype(BF16)


def feedforward_gradients(order, row_parts, w_up, b_up, w_down):
    shares = len(row_parts)
    tokens = shares * BLOCK
    units = w_up.shape[1] // shares
    width = 256
    steps = units // width
    down = (units + 16, D // 2)
    up = (shares, D // shares // 2, units)
    return pl.pallas_call(
        functools.partial(feedforward_kernel, shares),
        grid_spec=pltpu.PrefetchScalarGridSpec(
            num_scalar_prefetch=1,
            grid=(steps,),
            in_specs=[once(BLOCK, 2 * D)] * shares
            + [
                pl.BlockSpec((D, width), lambda p, order: (0, order[1] * steps + p)),
                pl.BlockSpec(memory_space=pltpu.VMEM),
                pl.BlockSpec((width, D), lambda p, order: (order[1] * steps + p, 0)),
            ],
            out_specs=[pl.BlockSpec(memory_space=pltpu.VMEM)] * 4,
            scratch_shapes=[
                pltpu.VMEM((tokens, D), BF16),
                pltpu.VMEM((tokens, D), BF16),
                pltpu.VMEM((D, tokens), BF16),
                pltpu.VMEM((16, units), F32),
            ],
        ),
        out_shape=[pltpu.VMEM(shape, BF16) for shape in (down, down, up, up)],
        compiler_params=pltpu.CompilerParams(vmem_limit_bytes=16 * 2**20),
        name="feedforward_gradients",
    )(order, *row_parts, *streamed(w_up), b_up, *streamed(w_down))


def assemble_kernel(
    place_ref,
    one_ref,
    one_other_ref,
    two_ref,
    two_other_ref,
    down_ref,
    down_other_ref,
    up_ref,
    up_other_ref,
    *refs,
):
    outs, refs = refs[:8], refs[8:]
    held, sems = refs[:8], refs[8]
    query_ref, key_ref, value_ref, out_ref, wide_ref, narrow_ref, sums_ref, vec_ref = held
    piece = query_ref.shape[0] // 2
    half = one_ref.shape[1]
    units = up_ref.shape[2]
    copies = [pltpu.make_async_copy(held[at], outs[at], sems.at[at]) for at in range(8)]

    def write(cores):
        for core, (one, two, down, up) in enumerate(cores):
            rows = slice(core * piece, (core + 1) * piece)
            for bits in range(4):
                at = pl.multiple_of((place_ref[1] ^ bits) * units, units)
                wide_ref[rows, pl.ds(at, units)] = up[bits].astype(F32)
        copies[4].start()
        for core, (one, two, down, up) in enumerate(cores):
            columns = slice(core * half, (core + 1) * half)
            narrow_ref[:, columns] = down[:units, :].astype(F32)
            sums_ref[:, columns] = down[units:, :].astype(F32)
        copies[5].start()
        copies[6].start()
        for at, ref in enumerate((query_ref, key_ref, value_ref)):
            for core, (one, two, down, up) in enumerate(cores):
                rows = slice(core * piece, (core + 1) * piece)
                ref[rows, :half] = one[at * piece : (at + 1) * piece, :].astype(F32)
                ref[rows, half:] = two[at * piece : (at + 1) * piece, :].astype(F32)
            copies[at].start()
        base = 3 * piece
        vec_ref[:, :half] = one_ref[base : base + 16, :].astype(F32)
        vec_ref[:, half:] = two_ref[base : base + 16, :].astype(F32)
        copies[7].start()
        base += 16
        for core, (one, two, down, up) in enumerate(cores):
            rows = slice(core * piece, (core + 1) * piece)
            out_ref[rows, :half] = one[base : base + piece, :].astype(F32)
            out_ref[rows, half:] = one[base + piece : base + 2 * piece, :].astype(F32)
        copies[3].start()
        for copy in copies:
            copy.wait()

    own = (one_ref, two_ref, down_ref, up_ref)
    other = (one_other_ref, two_other_ref, down_other_ref, up_other_ref)

    @pl.when(place_ref[0] == 0)
    def _():
        write((own, other))

    @pl.when(place_ref[0] != 0)
    def _():
        write((other, own))


def assemble(order, one, two, down, up):
    share = D // up[0].shape[0]
    units = up[0].shape[2]
    shapes = [(share, D)] * 4 + [(share, units * up[0].shape[0]), (units, D), (16, D), (16, D)]
    whole = pl.BlockSpec(memory_space=pltpu.VMEM)
    return pl.pallas_call(
        assemble_kernel,
        grid_spec=pltpu.PrefetchScalarGridSpec(
            num_scalar_prefetch=1,
            grid=(1,),
            in_specs=[whole] * 8,
            out_specs=[pl.BlockSpec(memory_space=pl.ANY)] * 8,
            scratch_shapes=[pltpu.VMEM(shape, F32) for shape in shapes]
            + [pltpu.SemaphoreType.DMA((8,))],
        ),
        out_shape=[pltpu.HBM(shape, F32) for shape in shapes],
        compiler_params=pltpu.CompilerParams(vmem_limit_bytes=16 * 2**20),
        cost_estimate=pl.CostEstimate(flops=0, bytes_accessed=24 * 2**20, transcendentals=0),
        name="assemble",
    )(order, *one, *two, *down, *up)


def swapped(array, axis, bits):
    return lax.ppermute(array, axis, [(i, i ^ bits) for i in range(lax.axis_size(axis))])


def from_peers(arrays):
    return [swapped(array, "seq", bits) for bits, array in enumerate(arrays, 1)]


def picked(array, index, axis):
    return lax.dynamic_index_in_dim(array, index, axis, keepdims=False)


def together(*arrays):
    return lax.optimization_barrier(arrays)


def added(*arrays):
    return functools.reduce(jnp.add, [array.astype(F32) for array in arrays]).astype(BF16)


def halves(pack):
    middle = pack.shape[1] // 32 * 16
    return pack[:, :middle], pack[:, middle:]


def in_row_order(pack, mine):
    return jnp.stack([picked(pack, mine ^ at, 0) for at in range(4)], axis=0)


def square_mesh():
    return lax.axis_size("seq") == 4 and lax.axis_size("z") == 4


def scatter(pack):
    return from_peers([pack[1], pack[2], pack[3]])


NEXT = [(0, 1), (1, 0), (2, 3), (3, 2)]
ACROSS = [(0, 3), (1, 2), (2, 1), (3, 0)]


def half_of(share, second):
    half = share.shape[0] // 2
    return jnp.where(second, share[half:], share[:half])


def core_index():
    return lax.axis_index("core")


def both_cores(share, axis):
    other = swapped(share, "core", 1)
    first = core_index() == 0
    return jnp.concatenate(
        [jnp.where(first, share, other), jnp.where(first, other, share)], axis=axis
    )


def reduce_plain(partial):
    share = lax.psum_scatter(partial.astype(BF16), "seq", scatter_dimension=0, tiled=True)
    return lax.psum(share, ("z", "core")).astype(F32)


def local(
    tokens,
    cotangent,
    lengths,
    w_query,
    b_query,
    w_key,
    b_key,
    w_value,
    b_value,
    w_out,
    b_out,
    gain_one,
    shift_one,
    w_up,
    b_up,
    w_down,
    b_down,
    gain_two,
    shift_two,
    rel_table,
):
    rows = tokens.shape[0]
    cycle = lax.axis_size("seq")
    mine = lax.axis_index("seq")
    core = core_index()
    square = square_mesh()
    hidden_units = w_up.shape[1]
    share = D // cycle
    if square:
        token_parts = [tokens] + from_peers([tokens] * 3)
        ids = mine ^ jnp.arange(cycle, dtype=jnp.int32)
        order = jnp.stack([core, mine]).astype(jnp.int32)
        cores = 2
    else:
        token_parts = [tokens, lax.all_gather(tokens, "seq", axis=0, tiled=True)]
        ids = jnp.concatenate([mine[None], jnp.arange(cycle, dtype=jnp.int32)])
        order = jnp.zeros((2,), jnp.int32)
        cores = 1
    dist = jnp.concatenate([mine - ids, ids, lengths[0]]).astype(jnp.int32)

    at_z = lax.axis_index("z")
    end = (at_z == 0) | (at_z == 3)
    between = jnp.logical_not(end)
    low = core == 0
    odd_x, odd_y = (mine & 1) == 1, (mine & 2) == 2
    place_of = (dist, order, end, between, low, odd_x, odd_y)
    dist, order, end, between, low, odd_x, odd_y = lax.optimization_barrier(place_of)

    def in_order(pieces):
        first, second, third, fourth = pieces
        pairs = [
            (jnp.where(odd_x, b, a), jnp.where(odd_x, a, b))
            for a, b in ((first, second), (third, fourth))
        ]
        return [jnp.where(odd_y, b, a) for a, b in zip(*pairs)] + [
            jnp.where(odd_y, a, b) for a, b in zip(*pairs)
        ]

    def own_quarter(array):
        half = array.shape[1] // 2
        array = jnp.where(odd_y, array[:, half:], array[:, :half])
        return jnp.where(odd_x, array[:, half // 2 :], array[:, : half // 2])

    places = jnp.arange(RELROWS, dtype=jnp.int32)
    turn = (places[:, None] + places[None, :] == RELROWS - 1).astype(BF16)
    stay = (places[:, None] == places[None, :]).astype(BF16)
    rel_both = product(jnp.concatenate([turn, stay], axis=0), rel_table).astype(BF16)
    pos_key_back = (product(rel_both[:RELROWS], w_key) + b_key).astype(BF16)
    pos_query = (product(rel_both, w_query) + b_query).astype(BF16)
    pos_key_back, (dist, order, end, between, low, odd_x, odd_y) = together(
        pos_key_back, (dist, order, end, between, low, odd_x, odd_y)
    )
    context, prob, query, key, value, tokens_row, *held = attention_forward(
        dist,
        token_parts,
        [w_query, w_key, w_value],
        [b_query, b_key, b_value],
        pos_key_back,
        pos_query,
        [w_up, w_down, w_out],
    )
    held_up, held_down, held_out = held

    output, feed, normal_one, inverse_one, g_resid_two, slope, sums_two = middle_forward(
        dist, context, tokens, cotangent, held_out, b_out, gain_one, shift_one, b_down, gain_two,
        shift_two, held_up, b_up, held_down,
    )
    if square:
        row_parts = [feed] + from_peers([feed] * 3)
    g_resid_one, g_attn, g_context, sums_one, g_up = middle_backward(
        feed, g_resid_two, normal_one, inverse_one, gain_one, held_out, slope, held_up, held_down
    )
    vectors = [sums_one, sums_two]

    def backward(start, pairs, g_context, extra_one, extra_two):
        outs = attention_backward(
            start, pairs, cores, cycle, dist, order, query, key, value, pos_key_back, pos_query, prob,
            g_context, tokens_row, rel_table, w_query, w_key, w_value, extra_one, extra_two, vectors,
        )
        return outs[:cores], outs[cores:]

    piece = share // cores
    whole_rows = lambda v, at, each: v[:, at : at + each].reshape(cores * each, -1)

    def unpacked(v, each):
        base = 3 * piece + 16
        parts = D // v.shape[2]
        return jnp.concatenate(
            [whole_rows(v, base + part * each, each) for part in range(parts)], axis=1
        )

    def rel_own(pack):
        return unpacked(pack, RELROWS // cycle // cores)

    def results(grads, grad_w_out, vectors, grad_rel, grad_tokens, grad_w_up, grad_w_down, grad_b_up):
        return (
            output,
            grad_tokens,
            grads[0],
            vectors[0],
            grads[1],
            vectors[1],
            grads[2],
            vectors[2],
            grad_w_out,
            vectors[3],
            vectors[4],
            vectors[5],
            grad_w_up,
            grad_b_up,
            grad_w_down,
            vectors[6],
            vectors[7],
            vectors[8],
            grad_rel,
        )

    if not square:
        act = gelu_and_slope(product(feed[:, :D], w_up) + b_up)[0].astype(BF16)
        (one,), carried = backward(0, 3, g_context, context, g_attn)
        (two,), (home, away) = backward(3, 3, g_context, *carried)
        packs = [
            lax.psum(lax.psum_scatter(v, "seq", scatter_dimension=0, tiled=True), ("z", "core"))
            for v in (one, two)
        ]
        got = lax.psum_scatter(away, "seq", scatter_dimension=0, tiled=False)
        grads = [
            jnp.concatenate([whole_rows(v, at * piece, piece) for v in packs], axis=1).astype(F32)
            for at in range(3)
        ]
        base = 3 * piece
        sums = jnp.concatenate([v[0, base : base + 16] for v in packs], axis=1).astype(F32)
        return results(
            grads,
            unpacked(packs[0], piece).astype(F32),
            lax.dynamic_slice_in_dim(sums, mine * share, share, 1),
            lax.all_gather(rel_own(packs[-1]), "seq", axis=0, tiled=True).astype(F32),
            g_resid_one + home + got.astype(F32),
            reduce_plain(product_left(feed[:, :D], g_up)),
            reduce_plain(product_left(act, feed[:, D:])),
            reduce_plain(jnp.sum(g_up.astype(F32), axis=0)),
        )

    one, carried = backward(0, 3, g_context, context, g_attn)

    row_parts, one, carried = together(row_parts, one, carried)
    one_got = swapped(one[1], "core", 1)
    down_own, down_other, up_own, up_other = feedforward_gradients(
        order, row_parts, w_up, b_up, w_down
    )

    one_got, down_own, down_other, up_own, up_other = together(
        one_got, down_own, down_other, up_own, up_other
    )
    down_got = swapped(down_other, "core", 1)
    up_got = swapped(up_other, "core", 1)
    one_share = added(one[0], one_got)
    down_share = added(down_own, down_got)
    up_share = added(up_own, up_got)

    units = hidden_units // 4

    def first_start(v):
        first, second = halves(v)
        return swapped(first[1::2], "seq", 1), swapped(second[2:], "seq", 2)

    def first_end(v, got):
        first, second = halves(v)
        return added(first[0::2], got[0]), added(second[:2], got[1])

    def second_start(v):
        return swapped(v[0][1], "seq", 2), swapped(v[1][1], "seq", 1)

    def second_end(v, got):
        return jnp.concatenate([added(v[0][0], got[0]), added(v[1][0], got[1])], axis=0)

    def core_start(v):
        return swapped(v, "core", 1)

    def rel_rows(pair):
        base, each = 3 * share // 2 + 16, RELROWS // 8
        own, other = [
            jnp.concatenate([v[base : base + each], v[base + each : base + 2 * each]], axis=1)
            for v in pair
        ]
        return jnp.concatenate(
            [jnp.where(low, own, other), jnp.where(low, other, own)], axis=0
        )

    moves = {
        "first": (first_start, first_end),
        "second": (second_start, second_end),
        "in": (
            lambda v: lax.ppermute(half_of(v, end), "z", NEXT),
            lambda v, got: added(half_of(v, between), got),
        ),
        "mid": (lambda v: lax.ppermute(v, "z", ACROSS), added),
        "out": (
            lambda v: lax.ppermute(v, "z", NEXT),
            lambda v, got: jnp.concatenate(
                [jnp.where(end, v, got), jnp.where(end, got, v)], axis=0
            ),
        ),
        "pair": (lambda v: swapped(v[1], "core", 1), lambda v, got: added(v[0], got)),
        "rows": (core_start, lambda v, got: (v, got)),
        "columns": (core_start, lambda v, got: (v, got)),
        "give": (scatter, lambda v, got: jnp.stack([v[0]] + got, axis=0)),
        "home": (
            lambda v: from_peers([v[0], v[1], v[2]]),
            lambda v, got: functools.reduce(jnp.add, [part.astype(F32) for part in got]),
        ),
        "spread": (scatter, lambda v, got: added(v[0], *got)),
        "x": (lambda v: swapped(v[1], "seq", 1), lambda v, got: [v[0], got, v[2], v[3]]),
        "y": (lambda v: swapped(v[2], "seq", 2), lambda v, got: [v[0], v[1], got, v[3]]),
        "d": (
            lambda v: swapped(v[3], "seq", 3),
            lambda v, got: jnp.stack([v[0], v[1], v[2], got], axis=0),
        ),
        "dd": (
            lambda v: swapped(v[3], "seq", 3),
            lambda v, got: jnp.stack([v[0], v[1], v[2], got], axis=0),
        ),
        "hx": (lambda v: swapped(v[0], "seq", 1), lambda v, got: [got, v[1], v[2]]),
        "hy": (lambda v: swapped(v[1], "seq", 2), lambda v, got: [v[0], got, v[2]]),
        "hd": (
            lambda v: swapped(v[2], "seq", 3),
            lambda v, got: functools.reduce(
                jnp.add, [part.astype(F32) for part in (v[0], v[1], got)]
            ),
        ),
        "rel": (
            lambda v: from_peers([rel_rows(v)] * 3),
            lambda v, got: (v, [rel_rows(v)] + got),
        ),
    }
    held_sums = {"down": down_share, "up": up_share, "one": one_share}
    flying = {}

    def begin(*steps):
        for step in steps:
            name, move = step.split(".")
            if move == "share":
                both = zip(held_sums["up"][1:], held_sums["away"])
                flying[step] = from_peers([jnp.concatenate(parts, axis=0) for parts in both])
            else:
                flying[step] = moves[move][0](held_sums[name])

    def meet(done, then):
        names = [step.split(".")[0] for step in then] + [step.split(".")[0] for step in done]
        names += ["away"] if "up.share" in done or "up.share" in then else []
        names = [name for at, name in enumerate(names) if name not in names[:at]]
        gots = {step: flying.pop(step) for step in done}
        kept, gots = together({name: held_sums[name] for name in names}, gots)
        held_sums.update(kept)
        for step in done:
            name, move = step.split(".")
            if move == "share":
                each = held_sums["up"].shape[1]
                parts = [held_sums["up"][0]] + [got[:each] for got in gots[step]]
                held_sums["up"] = jnp.stack(parts, axis=0)
                homes = [got[each:].astype(F32) for got in gots[step]]
                held_sums["away"] = functools.reduce(jnp.add, homes)
            else:
                held_sums[name] = moves[move][1](held_sums[name], gots[step])
        begin(*then)

    stages = (
        ([], ["up.in", "one.first"]),
        (["up.in", "one.first"], ["two.pair", "up.mid", "one.second"]),
        (["two.pair"], ["two.first"]),
        (["one.second"], ["one.in", "down.in"]),
        (["two.first", "up.mid"], ["two.second", "up.out"]),
        (["one.in"], ["one.mid"]),
        (["two.second", "down.in", "one.mid"], ["two.in", "down.mid", "one.out"]),
        (["two.in", "up.out", "one.out"], ["two.mid", "up.share"]),
        (["down.mid"], ["down.out"]),
        (["two.mid"], ["two.out"]),
        (["two.out", "down.out", "up.share"], ["two.rows", "one.rows", "up.columns", "down.columns"]),
        (["two.rows", "one.rows", "up.columns", "down.columns"], []),
    )
    begin(*stages[0][1])
    g_context, held_sums = together(g_context, held_sums)
    two, (home, away) = backward(3, 3, g_context, *carried)
    home, held_sums, flying_now = together(
        home, dict(held_sums, two=two, away=away), {step: flying[step] for step in stages[1][0]}
    )
    flying.update(flying_now)
    for done, then in stages[1:]:
        meet(done, then)

    grad_tokens = g_resid_one + home + held_sums["away"]
    rel = rel_rows(held_sums["two"])
    from_y, from_both = swapped(rel, "seq", 2), swapped(rel, "seq", 3)
    *grads, grad_w_up, grad_w_down, sums_up, sums = assemble(
        order, held_sums["one"], held_sums["two"], held_sums["down"], held_sums["up"]
    )
    rel, sums = together(rel, sums)
    rel_parts = [rel, swapped(rel, "seq", 1), from_y, from_both]
    return results(
        grads[:3],
        grads[3],
        own_quarter(sums),
        jnp.concatenate(in_order(rel_parts), axis=0).astype(F32),
        grad_tokens,
        grad_w_up,
        grad_w_down,
        sums_up[0],
    )


def solution(mesh):
    lines, cycle = mesh.devices.shape
    chips = Mesh(mesh.devices.reshape(lines // 2, 2, cycle), ("z", "core", "seq"))
    return jax.shard_map(
        local,
        mesh=chips,
        in_specs=(
            P(("z", "core", "seq"), None),
            P(("z", "core", "seq"), None),
            P(("z", "core"), None),
        )
        + (P(),) * 17,
        out_specs=(
            P(("z", "core", "seq"), None),
            P(("z", "core", "seq"), None),
            P("seq", None),
            P("seq"),
            P("seq", None),
            P("seq"),
            P("seq", None),
            P("seq"),
            P("seq", None),
            P("seq"),
            P("seq"),
            P("seq"),
            P("seq", None),
            P("seq"),
            P("seq", None),
            P("seq"),
            P("seq"),
            P("seq"),
            P(),
        ),
        check_vma=False,
    )
```

```python
import functools
import math

import jax
import jax.numpy as jnp
from jax import lax
from jax.experimental import pallas as pl
from jax.experimental.pallas import tpu as pltpu
from jax.sharding import Mesh, PartitionSpec as P

D = 768
HEADS = 12
HEAD = 64
SPAN = 256
RELROWS = 512
BLOCK = 128
EXT = RELROWS + 2 * SPAN
PAIRS = HEADS // 2
VECTORS = 2
LATER = 3
DOCS = 4
SCALE = 1.0 / math.sqrt(3 * HEAD)
F32 = jnp.float32
BF16 = jnp.bfloat16
ROLLED = BF16


def normalized(resid):
    center = resid - jnp.mean(resid, axis=-1, keepdims=True)
    inverse = lax.rsqrt(jnp.mean(center * center, axis=-1, keepdims=True) + 1e-07)
    return center * inverse, inverse


def normalized_back(grad, normal, inverse, gain):
    hat = grad * gain
    means = jnp.mean(hat, axis=-1, keepdims=True) + normal * jnp.mean(
        hat * normal, axis=-1, keepdims=True
    )
    total = lambda v: jnp.sum(v, axis=0, keepdims=True)
    return (hat - means) * inverse, total(grad * normal), total(grad)


def product(left, right):
    return jnp.dot(left, right, preferred_element_type=F32)


def product_left(left, right):
    return lax.dot_general(left, right, (((0,), (0,)), ((), ())), preferred_element_type=F32)


def product_right(left, right):
    return lax.dot_general(left, right, (((1,), (1,)), ((), ())), preferred_element_type=F32)


def segment_of(position, place_ref, at):
    passed, bound = jnp.zeros(position.shape, jnp.int32), 0
    for document in range(DOCS):
        bound = bound + place_ref[at + document]
        passed = passed + (position >= bound).astype(jnp.int32)
    return passed


def anti_identity():
    rows = lax.broadcasted_iota(jnp.int32, (BLOCK, BLOCK), 0)
    cols = lax.broadcasted_iota(jnp.int32, (BLOCK, BLOCK), 1)
    return (rows + cols == BLOCK - 1).astype(BF16)


def extend(ext_ref, table_ref):
    ext_ref[SPAN : SPAN + RELROWS, :] = table_ref[...]
    ext_ref[0:SPAN, :] = jnp.broadcast_to(table_ref[0:1, :], (SPAN, BLOCK))
    last = table_ref[RELROWS - 1 : RELROWS, :]
    ext_ref[SPAN + RELROWS :, :] = jnp.broadcast_to(last, (SPAN, BLOCK))


def window_start(offset):
    return pl.multiple_of(jnp.clip(offset, 0, EXT - 2 * BLOCK), BLOCK)


def head_mask(head):
    lane = lax.broadcasted_iota(jnp.int32, (1, BLOCK), 1)
    return (lane >= head * HEAD) & (lane < (head + 1) * HEAD)


def band_roll(wide, shift):
    return pltpu.roll(wide, shift, 1, stride=1, stride_axis=0)


def by_head(pair):
    zero = jnp.zeros_like(pair)
    return jnp.concatenate([jnp.where(head_mask(head), pair, zero) for head in range(2)], axis=0)


def forward_kernel(
    parts, blocks, dist_ref, *refs
):
    part_refs, refs = refs[:parts], refs[parts:]
    wq_ref, wk_ref, wv_ref, bq_ref, bk_ref, bv_ref, pk_ref, pq_ref, *refs = refs
    later, refs = refs[:LATER], refs[LATER:]
    ctx_ref, prob_ref, q_ref, k_ref, v_ref, tok_ref, *refs = refs
    held, refs = refs[:LATER], refs[LATER:]
    score_ref, ek_ref, eq_ref, bias_ref, sems = refs
    copies = [
        pltpu.make_async_copy(later[at], held[at], sems.at[at]) for at in range(LATER)
    ]

    @pl.when(pl.program_id(0) == 0)
    def _():
        for copy in copies:
            copy.start()

    @pl.when(pl.program_id(0) == pl.num_programs(0) - 1)
    def _():
        for copy in copies:
            copy.wait()

    extend(ek_ref, pk_ref)
    extend(eq_ref, pq_ref)

    @pl.when(pl.program_id(0) == 0)
    def _():
        at = 0
        for ref in part_refs:
            tok_ref[at : at + ref.shape[0], :] = ref[...]
            at += ref.shape[0]
        mine = dist_ref[blocks]
        lane = lax.broadcasted_iota(jnp.int32, (1, BLOCK), 1)
        line = lax.broadcasted_iota(jnp.int32, (BLOCK, 1), 0)
        query_segment = segment_of(mine * BLOCK + lane, dist_ref, 2 * blocks)
        for block in range(blocks):
            home = dist_ref[blocks + block]
            allowed = segment_of(home * BLOCK + line, dist_ref, 2 * blocks) == query_segment
            if block > 0:
                allowed = jnp.logical_and(allowed, home != mine)
            rows = slice(block * BLOCK, (block + 1) * BLOCK)
            bias_ref[rows, :] = jnp.where(allowed, 0.0, -1e30)

    at = pl.multiple_of(pl.program_id(0) * BLOCK, BLOCK)
    both = product(tok_ref[...], jnp.concatenate([wk_ref[...], wv_ref[...]], axis=1))
    k_ref[...] = (both[:, :BLOCK] + row_of(bk_ref, at, BLOCK)).astype(BF16)
    v_ref[...] = (both[:, BLOCK:] + row_of(bv_ref, at, BLOCK)).astype(BF16)
    q = (product(tok_ref[:BLOCK, :], wq_ref[...]) + row_of(bq_ref, at, BLOCK)).astype(BF16)
    q_ref[...] = q
    q_heads = by_head(q)
    tops = [jnp.full((1, BLOCK), -jnp.inf, F32) for head in range(2)]
    for block in range(blocks):
        dist = dist_ref[block]
        rows = slice(block * BLOCK, (block + 1) * BLOCK)
        k_heads = by_head(k_ref[rows, :])
        window_c = ek_ref[pl.ds(window_start(384 - dist * BLOCK), 2 * BLOCK), :]
        window_p = eq_ref[pl.ds(window_start(384 + dist * BLOCK), 2 * BLOCK), :]
        c2p = product_right(q_heads, window_c)
        p2c = product_right(k_heads, window_p)
        direct = product_right(k_heads, q)
        for head in range(2):
            own = slice(head * BLOCK, (head + 1) * BLOCK)
            first = band_roll(c2p[own].astype(BF16), BLOCK + 1)[:, :BLOCK].T
            second = band_roll(p2c[own].astype(BF16), BLOCK + 1)[:, :BLOCK]
            score = (direct[own] + first.astype(F32) + second.astype(F32)) * SCALE + bias_ref[rows, :]
            score_ref[head, rows, :] = score
            tops[head] = jnp.maximum(tops[head], jnp.max(score, axis=0, keepdims=True))
    probs = []
    for head in range(2):
        weight = jnp.exp(score_ref[head] - tops[head])
        total = jnp.sum(weight, axis=0, keepdims=True)
        prob = (weight * (1.0 / total)).astype(BF16)
        prob_ref[head] = prob
        probs.append(prob)
    v = v_ref[...]
    zero = jnp.zeros_like(v)
    out = product_left(probs[0], jnp.where(head_mask(0), v, zero)) + product_left(
        probs[1], jnp.where(head_mask(1), v, zero)
    )
    ctx_ref[...] = out.astype(BF16)


def streamed(*arrays):
    return [pltpu.with_memory_space_constraint(array, pltpu.HBM) for array in arrays]


def once(*shape):
    return pl.BlockSpec(shape, lambda p, *_: (0,) * len(shape), pipeline_mode=pl.Buffered(1))


def fits(keys):
    return keys <= 2 * RELROWS


def kept(keys, *shape):
    return pl.BlockSpec(memory_space=pltpu.VMEM) if fits(keys) else once(*shape)


def kept_array(keys, shape, dtype):
    return (pltpu.VMEM if fits(keys) else jax.ShapeDtypeStruct)(shape, dtype)


def attention_forward(dist, token_parts, weights, biases, pos_key, pos_query, later):
    keys = sum(part.shape[0] for part in token_parts)
    blocks = keys // BLOCK
    pair = lambda rows: pl.BlockSpec((rows, BLOCK), lambda p, dist: (0, p))
    return pl.pallas_call(
        functools.partial(forward_kernel, len(token_parts), blocks),
        grid_spec=pltpu.PrefetchScalarGridSpec(
            num_scalar_prefetch=1,
            grid=(PAIRS,),
            in_specs=[once(*part.shape) for part in token_parts]
            + [pair(D)] * 3
            + [pl.BlockSpec(memory_space=pltpu.VMEM)] * 3
            + [pair(RELROWS), pair(RELROWS)]
            + [pl.BlockSpec(memory_space=pl.ANY)] * LATER,
            out_specs=[
                pair(BLOCK),
                pl.BlockSpec((2, keys, BLOCK), lambda p, dist: (p, 0, 0)),
                pair(BLOCK),
                pair(keys),
                pair(keys),
                kept(keys, keys, D),
            ]
            + [pl.BlockSpec(memory_space=pl.ANY)] * LATER,
            scratch_shapes=[
                pltpu.VMEM((2, keys, BLOCK), F32),
                pltpu.VMEM((EXT, BLOCK), BF16),
                pltpu.VMEM((EXT, BLOCK), BF16),
                pltpu.VMEM((keys, BLOCK), F32),
                pltpu.SemaphoreType.DMA((LATER,)),
            ],
        ),
        out_shape=[
            jax.ShapeDtypeStruct((BLOCK, D), BF16),
            pltpu.HBM((HEADS, keys, BLOCK), BF16),
            pltpu.HBM((BLOCK, D), BF16),
            pltpu.HBM((keys, D), BF16),
            pltpu.HBM((keys, D), BF16),
            kept_array(keys, (keys, D), BF16),
        ]
        + [pltpu.VMEM(array.shape, array.dtype) for array in later],
        compiler_params=pltpu.CompilerParams(vmem_limit_bytes=(16 if fits(keys) else 40) * 2**20),
        name="attention_forward",
    )(dist, *token_parts, *streamed(*weights), *biases, *streamed(pos_key, pos_query), *streamed(*later))


def fold_edges(acc_ref):
    head_sum = jnp.sum(acc_ref[:, 0:SPAN], axis=1, keepdims=True)
    tail_sum = jnp.sum(acc_ref[:, SPAN + RELROWS :], axis=1, keepdims=True)
    lane = lax.broadcasted_iota(jnp.int32, (BLOCK, RELROWS), 1)
    middle = acc_ref[:, SPAN : SPAN + RELROWS]
    middle = middle + jnp.where(lane == 0, head_sum, 0.0)
    return (middle + jnp.where(lane == RELROWS - 1, tail_sum, 0.0)).astype(BF16)


def flipped_lanes(array, flip):
    parts = array.shape[1] // BLOCK
    return jnp.concatenate(
        [
            product(array[:, part * BLOCK : (part + 1) * BLOCK], flip).astype(BF16)
            for part in reversed(range(parts))
        ],
        axis=1,
    )


def place(order_ref, share, core, shares, each):
    at = (core ^ order_ref[0]) * shares + (share ^ order_ref[1])
    return pl.multiple_of(at * each, 16)


def place_rows(order_ref, into_ref, value, cores, shares):
    each = value.shape[0] // (cores * shares)
    for share in range(shares):
        for core in range(cores):
            at = (share * cores + core) * each
            into_ref[pl.ds(place(order_ref, share, core, shares, each), each), :] = value[
                at : at + each
            ]


def store_pieces(refs, at, value, lanes):
    shares = refs[0].shape[0]
    each = value.shape[0] // (len(refs) * shares)
    for core, ref in enumerate(refs):
        for share in range(shares):
            start = (core * shares + share) * each
            ref[share, at : at + each, lanes] = value[start : start + each]


def backward_kernel(
    blocks,
    cores,
    first,
    last,
    dist_ref,
    order_ref,
    q_ref,
    k_ref,
    v_ref,
    pk_ref,
    pq_ref,
    prob_ref,
    gctx_ref,
    tok_ref,
    rel_ref,
    wq_ref,
    wk_ref,
    wv_ref,
    extra_one_ref,
    extra_two_ref,
    *refs,
):
    vec_refs, refs = refs[:VECTORS], refs[VECTORS:]
    pack_refs, refs = refs[:cores], refs[cores:]
    backward_body(
        blocks, first, last, dist_ref, order_ref, q_ref, k_ref, v_ref, pk_ref, pq_ref, prob_ref, gctx_ref,
        tok_ref, rel_ref, wq_ref, wk_ref, wv_ref, extra_one_ref, extra_two_ref, vec_refs, pack_refs, *refs
    )


def backward_body(
    blocks,
    first,
    last,
    dist_ref,
    order_ref,
    q_ref,
    k_ref,
    v_ref,
    pk_ref,
    pq_ref,
    prob_ref,
    gctx_ref,
    tok_ref,
    rel_ref,
    wq_ref,
    wk_ref,
    wv_ref,
    extra_one_ref,
    extra_two_ref,
    vec_refs,
    pack_refs,
    out_one_ref,
    out_two_ref,
    back_ref,
    gk_ref,
    gv_ref,
    acck_ref,
    accq_ref,
    tokt_ref,
    relt_ref,
    acc_tok_ref,
    acc_rel_ref,
    turn_ref,
    ek_ref,
    eq_ref,
):
    step = pl.program_id(0)
    if not last:
        acc_tok_ref, acc_rel_ref = out_one_ref, out_two_ref
    extend(ek_ref, pk_ref)
    extend(eq_ref, pq_ref)
    cores, shares, half = len(pack_refs), pack_refs[0].shape[0], pack_refs[0].shape[2]
    share = D // cores // shares
    flip = anti_identity()

    @pl.when(step == 0)
    def _():
        place_rows(order_ref, tokt_ref, tok_ref[...].T, cores, shares)
        place_rows(order_ref, relt_ref, rel_ref[...].T, cores, shares)
        if first:
            acc_tok_ref[...] = jnp.zeros_like(acc_tok_ref)
            acc_rel_ref[...] = jnp.zeros_like(acc_rel_ref)
        else:
            acc_tok_ref[...] = extra_one_ref[...]
            acc_rel_ref[...] = extra_two_ref[...]

    acck_ref[...] = jnp.zeros_like(acck_ref)
    accq_ref[...] = jnp.zeros_like(accq_ref)
    g_heads = by_head(gctx_ref[...])
    first_rows = lax.broadcasted_iota(jnp.int32, (BLOCK, 1), 0) < HEAD
    first_lanes = head_mask(0)

    def turned_heads(array):
        turned = array.T
        zero = jnp.zeros_like(turned)
        return jnp.concatenate(
            [jnp.where(first_rows, turned, zero), jnp.where(first_rows, zero, turned)], axis=1
        )

    def of_heads(stacked):
        return jnp.where(first_lanes, stacked[:BLOCK], stacked[BLOCK:])

    q_back = product(flip, q_ref[...]).astype(BF16)
    q_turned = turned_heads(q_back)
    probs = jnp.concatenate([prob_ref[head] for head in range(2)], axis=1)
    g_prob = product_right(v_ref[...], g_heads)
    gv_ref[...] = product(probs, g_heads).astype(BF16)
    probs = probs.astype(F32)
    delta = jnp.sum(probs * g_prob, axis=0, keepdims=True)
    g_score = (probs * (g_prob - delta) * SCALE).astype(BF16)
    for head in range(2):
        lanes = slice(head * BLOCK, (head + 1) * BLOCK)
        back_ref[:, lanes] = product(g_score[:, lanes], flip).astype(BF16)
    g_query = jnp.zeros((2 * BLOCK, BLOCK), F32)
    pad = jnp.zeros((BLOCK, BLOCK), BF16)
    for block in range(blocks):
        rows = slice(block * BLOCK, (block + 1) * BLOCK)
        k_block = k_ref[rows, :]
        at = pl.ds(window_start(384 - dist_ref[block] * BLOCK), 2 * BLOCK)
        window_c = ek_ref[at, :]
        window_p = eq_ref[at, :]
        backs = [back_ref[rows, head * BLOCK : (head + 1) * BLOCK] for head in range(2)]
        turns = [back.T for back in backs]
        bands_c = [band_roll(jnp.concatenate([turn, pad], axis=1), 0) for turn in turns]
        bands_p = [band_roll(jnp.concatenate([back, pad], axis=1), 1) for back in backs]
        bands_c = jnp.concatenate(bands_c, axis=0)
        bands_p = jnp.concatenate(bands_p, axis=0)
        g_query = g_query + product(
            jnp.concatenate([jnp.concatenate(turns, axis=0), bands_c], axis=1),
            jnp.concatenate([k_block, window_c], axis=0),
        )
        g_key = product(
            jnp.concatenate([jnp.concatenate(backs, axis=0), bands_p], axis=1),
            jnp.concatenate([q_back, window_p], axis=0),
        )
        gk_ref[rows, :] = of_heads(g_key).astype(BF16)
        acck_ref[:, at] += product(q_turned, bands_c)
        accq_ref[:, at] += product(turned_heads(k_block), bands_p)

    g_query = product(flip, of_heads(g_query).astype(BF16)).astype(BF16)
    g_pos_key = flipped_lanes(fold_edges(acck_ref), flip)
    g_pos_query = fold_edges(accq_ref)
    g_key = gk_ref[...]
    g_value = gv_ref[...]
    lanes = pl.ds(pl.multiple_of(step * BLOCK, BLOCK), BLOCK)
    ones_tok = jnp.ones((16, tok_ref.shape[0]), BF16)
    ones_rel = jnp.ones((16, RELROWS), BF16)
    row = lax.broadcasted_iota(jnp.int32, (16, BLOCK), 0)
    vec = jnp.zeros((16, BLOCK), F32)
    for at, vec_ref in enumerate(vec_refs):
        for part in range(3):
            vec = vec + jnp.where(row == 3 + 3 * at + part, vec_ref[part : part + 1, :], 0.0)
    g_both = jnp.concatenate([g_key, g_value], axis=1)
    pos_both = jnp.concatenate([g_pos_key, g_pos_query], axis=0)
    from_tok = product(tokt_ref[...], g_both)
    from_rel = product_right(relt_ref[...], pos_both)
    from_own = product(tokt_ref[:, :BLOCK], g_query)
    sum_tok = product(ones_tok, g_both)
    sum_rel = product_right(ones_rel, pos_both)
    sum_own = product(ones_tok[:, :BLOCK], g_query)
    weights = [
        (from_own + from_rel[:, BLOCK:], sum_own + sum_rel[:, BLOCK:]),
        (from_tok[:, :BLOCK] + from_rel[:, :BLOCK], sum_tok[:, :BLOCK] + sum_rel[:, :BLOCK]),
        (from_tok[:, BLOCK:], sum_tok[:, BLOCK:]),
    ]
    for at, (weight, total) in enumerate(weights):
        store_pieces(pack_refs, at * share, weight.astype(BF16), lanes)
        vec = vec + jnp.where(row == at, total, 0.0)
    vec = vec.astype(BF16)
    for pack_ref in pack_refs:
        for part in range(shares):
            pack_ref[part, 3 * share : 3 * share + 16, lanes] = vec
    acc_tok_ref[...] += product_right(
        g_both,
        jnp.concatenate([wk_ref[...], wv_ref[...]], axis=1),
    )
    acc_tok_ref[0:BLOCK, :] += product_right(g_query, wq_ref[...])
    acc_rel_ref[...] += product(
        jnp.concatenate([wk_ref[...], wq_ref[...]], axis=1),
        pos_both,
    )

    @pl.when(step == pl.num_programs(0) - 1)
    def _():
        base = 3 * share + 16
        extra = None
        if last:
            out_one_ref[...] = acc_tok_ref[0:BLOCK, :]
            for block in range(1, blocks):
                out_two_ref[block - 1] = acc_tok_ref[block * BLOCK : (block + 1) * BLOCK].astype(BF16)
            place_rows(order_ref, turn_ref, acc_rel_ref[...].T.astype(BF16), cores, shares)
            extra = turn_ref[...]
        if first:
            place_rows(order_ref, turn_ref, extra_one_ref[...].T, cores, shares)
            extra = product(turn_ref[...], extra_two_ref[...]).astype(BF16)
        if extra is not None:
            each = extra.shape[0] // (cores * shares)
            for part in range(D // half):
                columns = extra[:, part * half : (part + 1) * half]
                store_pieces(pack_refs, base + part * each, columns, slice(None))


def attention_backward(
    start, pairs, cores, shares, dist, order, query, key, value, pos_key, pos_query, prob, g_context,
    tokens_row, rel_table, w_query, w_key, w_value, extra_one, extra_two, vectors,
):
    keys = key.shape[0]
    blocks = keys // BLOCK
    first, last = start == 0, start + pairs == PAIRS
    share = D // cores // shares
    half = pairs * BLOCK
    rows_extra = D if first else RELROWS if last else 0
    pack = (shares, 3 * share + 16 + rows_extra // cores // shares * (D // half), half)
    pair = lambda rows: pl.BlockSpec((rows, BLOCK), lambda p, *_: (0, p + start))
    if first:
        extras = [once(BLOCK, D), once(BLOCK, D)]
        turn = (D, BLOCK)
    else:
        extras = [kept(keys, keys, D), kept(keys, D, RELROWS)]
        turn = (RELROWS, D)
    sums = [(keys, D), (D, RELROWS)] if last else [(8, 128), (8, 128)]
    if last:
        outs = [((BLOCK, D), F32), ((blocks - 1, BLOCK, D), BF16)]
    else:
        outs = [((keys, D), F32), ((D, RELROWS), F32)]
    return pl.pallas_call(
        functools.partial(backward_kernel, blocks, cores, first, last),
        grid_spec=pltpu.PrefetchScalarGridSpec(
            num_scalar_prefetch=2,
            grid=(pairs,),
            in_specs=[
                pair(BLOCK),
                pair(keys),
                pair(keys),
                pair(RELROWS),
                pl.BlockSpec((RELROWS, BLOCK), lambda p, *_: (1, p + start)),
                pl.BlockSpec((2, keys, BLOCK), lambda p, *_: (p + start, 0, 0)),
                pair(BLOCK),
                kept(keys, keys, D),
                once(RELROWS, D),
                pair(D),
                pair(D),
                pair(D),
            ]
            + extras
            + [pair(8)] * VECTORS,
            out_specs=[kept(keys, *pack)] * cores + [kept(keys, *shape) for shape, _ in outs],
            scratch_shapes=[
                pltpu.VMEM((keys, 2 * BLOCK), BF16),
                pltpu.VMEM((keys, BLOCK), BF16),
                pltpu.VMEM((keys, BLOCK), BF16),
                pltpu.VMEM((BLOCK, EXT), F32),
                pltpu.VMEM((BLOCK, EXT), F32),
                pltpu.VMEM((D, keys), BF16),
                pltpu.VMEM((D, RELROWS), BF16),
                pltpu.VMEM(sums[0], F32),
                pltpu.VMEM(sums[1], F32),
                pltpu.VMEM(turn, BF16),
                pltpu.VMEM((EXT, BLOCK), BF16),
                pltpu.VMEM((EXT, BLOCK), BF16),
            ],
        ),
        out_shape=[kept_array(keys, pack, BF16)] * cores
        + [kept_array(keys, shape, dtype) for shape, dtype in outs],
        compiler_params=pltpu.CompilerParams(vmem_limit_bytes=(18 if fits(keys) else 58) * 2**20),
        name="attention_backward",
    )(
        dist, order, *streamed(query, key, value, pos_key, pos_query, prob), g_context,
        tokens_row, *streamed(rel_table, w_query, w_key, w_value), extra_one, extra_two, *vectors,
    )


def column_sum(array):
    return jnp.sum(array, axis=0, keepdims=True)


def middle_forward_kernel(
    blocks,
    place_ref,
    ctx_ref,
    tok_ref,
    cot_ref,
    wout_ref,
    bout_ref,
    gain_one_ref,
    shift_one_ref,
    bdown_ref,
    gain_two_ref,
    shift_two_ref,
    wup_ref,
    bup_ref,
    wdown_ref,
    output_ref,
    feed_ref,
    normal_ref,
    inverse_ref,
    resid_ref,
    slope_ref,
    sums_ref,
    hidden_ref,
    down_ref,
):
    step = pl.program_id(0)

    @pl.when(step == 0)
    def _():
        attn = product(ctx_ref[...], wout_ref[...]) + row_of(bout_ref)
        normal, inverse = normalized(tok_ref[...].astype(F32) + attn)
        normal_ref[...] = normal
        inverse_ref[...] = jnp.broadcast_to(inverse, inverse_ref.shape)
        hidden = normal * row_of(gain_one_ref) + row_of(shift_one_ref)
        hidden_ref[...] = hidden
        feed_ref[:, :D] = hidden.astype(BF16)
        down_ref[...] = jnp.zeros_like(down_ref)

    width = slope_ref.shape[1]
    at = pl.multiple_of(step * width, width)
    units = pl.ds(at, width)
    act, slope = gelu_and_slope(
        product(feed_ref[:, :D], wup_ref[:, units]) + row_of(bup_ref, at, width)
    )
    slope_ref[...] = slope
    down_ref[...] += product(act.astype(BF16), wdown_ref[units, :])

    @pl.when(step == pl.num_programs(0) - 1)
    def _():
        normal, inverse = normalized(hidden_ref[...] + (down_ref[...] + row_of(bdown_ref)))
        output_ref[...] = (normal * row_of(gain_two_ref) + row_of(shift_two_ref)).astype(BF16)
        position = place_ref[blocks] * BLOCK + lax.broadcasted_iota(jnp.int32, (BLOCK, 1), 0)
        valid = segment_of(position, place_ref, 2 * blocks) < DOCS
        g_out = jnp.where(valid, cot_ref[...].astype(F32), 0.0)
        g_resid, g_gain, g_shift = normalized_back(g_out, normal, inverse, row_of(gain_two_ref))
        resid_ref[...] = g_resid
        g_down = g_resid.astype(BF16)
        feed_ref[:, D:] = g_down
        sums_ref[0:1, :] = column_sum(g_down.astype(F32))
        sums_ref[1:2, :] = g_gain
        sums_ref[2:3, :] = g_shift


def middle_forward(
    place, context, tokens, cotangent, w_out, b_out, gain_one, shift_one, b_down, gain_two, shift_two,
    w_up, b_up, w_down,
):
    units = w_up.shape[1]
    width = 512
    return pl.pallas_call(
        functools.partial(middle_forward_kernel, (place.shape[0] - DOCS) // 2),
        grid_spec=pltpu.PrefetchScalarGridSpec(
        num_scalar_prefetch=1,
        grid=(units // width,),
        in_specs=[once(BLOCK, D)] * 3
        + [pl.BlockSpec(memory_space=pltpu.VMEM)]
        + [pl.BlockSpec(memory_space=pltpu.VMEM)] * 6
        + [
            pl.BlockSpec(memory_space=pltpu.VMEM),
            pl.BlockSpec(memory_space=pltpu.VMEM),
            pl.BlockSpec(memory_space=pltpu.VMEM),
        ],
        out_specs=[
            once(BLOCK, D),
            once(BLOCK, 2 * D),
            once(BLOCK, D),
            once(BLOCK, BLOCK),
            once(BLOCK, D),
            pl.BlockSpec((BLOCK, width), lambda p, *_: (0, p)),
            once(8, D),
        ],
        scratch_shapes=[pltpu.VMEM((BLOCK, D), F32), pltpu.VMEM((BLOCK, D), F32)],
        ),
        out_shape=[
            jax.ShapeDtypeStruct((BLOCK, D), BF16),
            jax.ShapeDtypeStruct((BLOCK, 2 * D), BF16),
            jax.ShapeDtypeStruct((BLOCK, D), F32),
            jax.ShapeDtypeStruct((BLOCK, BLOCK), F32),
            jax.ShapeDtypeStruct((BLOCK, D), F32),
            jax.ShapeDtypeStruct((BLOCK, units), F32),
            jax.ShapeDtypeStruct((8, D), F32),
        ],
        compiler_params=pltpu.CompilerParams(vmem_limit_bytes=20 * 2**20),
        name="middle_forward",
    )(
        place, context, tokens, cotangent, w_out, b_out, gain_one, shift_one, b_down,
        gain_two, shift_two, w_up, b_up, w_down,
    )


def middle_backward_kernel(
    feed_ref,
    resid_ref,
    normal_ref,
    inverse_ref,
    gain_ref,
    wout_ref,
    slope_ref,
    wup_ref,
    wdown_ref,
    g_resid_ref,
    g_attn_ref,
    g_ctx_ref,
    sums_ref,
    g_up_ref,
    acc_ref,
):
    step = pl.program_id(0)

    @pl.when(step == 0)
    def _():
        acc_ref[...] = resid_ref[...]

    width = slope_ref.shape[1]
    units = pl.ds(pl.multiple_of(step * width, width), width)
    g_up = (product_right(feed_ref[:, D:], wdown_ref[units, :]) * slope_ref[...]).astype(BF16)
    g_up_ref[...] = g_up
    acc_ref[...] += product_right(g_up, wup_ref[:, units])

    @pl.when(step == pl.num_programs(0) - 1)
    def _():
        g_resid, g_gain, g_shift = normalized_back(
            acc_ref[...], normal_ref[...], inverse_ref[:, 0:1], row_of(gain_ref)
        )
        g_resid_ref[...] = g_resid
        g_attn = g_resid.astype(BF16)
        g_attn_ref[...] = g_attn
        g_ctx_ref[...] = product_right(g_attn, wout_ref[...]).astype(BF16)
        sums_ref[0:1, :] = column_sum(g_attn.astype(F32))
        sums_ref[1:2, :] = g_gain
        sums_ref[2:3, :] = g_shift


def middle_backward(feed, g_resid_two, normal, inverse, gain_one, w_out, slope, w_up, w_down):
    units = w_up.shape[1]
    width = 512
    return pl.pallas_call(
        middle_backward_kernel,
        grid=(units // width,),
        in_specs=[
            once(BLOCK, 2 * D),
            once(BLOCK, D),
            once(BLOCK, D),
            once(BLOCK, BLOCK),
            pl.BlockSpec(memory_space=pltpu.VMEM),
            pl.BlockSpec(memory_space=pltpu.VMEM),
            pl.BlockSpec((BLOCK, width), lambda p: (0, p)),
            pl.BlockSpec(memory_space=pltpu.VMEM),
            pl.BlockSpec(memory_space=pltpu.VMEM),
        ],
        out_specs=[
            once(BLOCK, D),
            once(BLOCK, D),
            once(BLOCK, D),
            once(8, D),
            pl.BlockSpec((BLOCK, width), lambda p: (0, p)),
        ],
        scratch_shapes=[pltpu.VMEM((BLOCK, D), F32)],
        out_shape=[
            jax.ShapeDtypeStruct((BLOCK, D), F32),
            jax.ShapeDtypeStruct((BLOCK, D), BF16),
            jax.ShapeDtypeStruct((BLOCK, D), BF16),
            jax.ShapeDtypeStruct((8, D), F32),
            jax.ShapeDtypeStruct((BLOCK, units), BF16),
        ],
        compiler_params=pltpu.CompilerParams(vmem_limit_bytes=20 * 2**20),
        name="middle_backward",
    )(
        feed, g_resid_two, normal, inverse, gain_one, w_out, slope,
        w_up, w_down,
    )


def row_of(ref, at=None, width=None):
    return (ref[...] if at is None else ref[pl.ds(at, width)]).reshape(1, -1)


def gelu_and_slope(x):
    below = 0.5 + 0.5 * lax.erf(x * math.sqrt(0.5))
    density = jnp.exp(-0.5 * x * x) * (1.0 / math.sqrt(2.0 * math.pi))
    return x * below, below + x * density


def feedforward_kernel(
    parts,
    order_ref,
    *refs,
):
    part_refs, refs = refs[:parts], refs[parts:]
    wup_ref, bup_ref, wdown_ref, down_own_ref, down_other_ref, up_own_ref, up_other_ref, *refs = refs
    hid_ref, gd_ref, hidt_ref, sums_ref = refs
    step = pl.program_id(0)
    shares = up_own_ref.shape[0]
    half = down_own_ref.shape[1]
    width = wup_ref.shape[1]

    @pl.when(step == 0)
    def _():
        for part in range(parts):
            rows = slice(part * BLOCK, (part + 1) * BLOCK)
            hid_ref[rows, :] = part_refs[part][:, :D]
            gd_ref[rows, :] = part_refs[part][:, D:]
        place_rows(order_ref, hidt_ref, hid_ref[...].T, 2, shares)

    lanes = pl.ds(pl.multiple_of(step * width, width), width)
    at = pl.multiple_of(order_ref[1] * sums_ref.shape[1] + step * width, width)
    act, slope = gelu_and_slope(product(hid_ref[...], wup_ref[...]) + row_of(bup_ref, at, width))
    g_up = (product_right(gd_ref[...], wdown_ref[...]) * slope).astype(BF16)
    act_turned = act.astype(BF16).T
    for core, ref in enumerate((down_own_ref, down_other_ref)):
        columns = pl.ds(pl.multiple_of((order_ref[0] ^ core) * half, BLOCK), half)
        ref[lanes, :] = product(act_turned, gd_ref[:, columns]).astype(BF16)
    store_pieces((up_own_ref, up_other_ref), 0, product(hidt_ref[...], g_up).astype(BF16), lanes)
    sums_ref[:, lanes] = product(jnp.ones((16, hid_ref.shape[0]), BF16), g_up)

    @pl.when(step == pl.num_programs(0) - 1)
    def _():
        for core, ref in enumerate((down_own_ref, down_other_ref)):
            columns = pl.ds(pl.multiple_of((order_ref[0] ^ core) * half, BLOCK), half)
            ref[pl.ds(sums_ref.shape[1], 16), :] = sums_ref[:, columns].astype(BF16)


def feedforward_gradients(order, row_parts, w_up, b_up, w_down):
    shares = len(row_parts)
    tokens = shares * BLOCK
    units = w_up.shape[1] // shares
    width = 256
    steps = units // width
    down = (units + 16, D // 2)
    up = (shares, D // shares // 2, units)
    return pl.pallas_call(
        functools.partial(feedforward_kernel, shares),
        grid_spec=pltpu.PrefetchScalarGridSpec(
            num_scalar_prefetch=1,
            grid=(steps,),
            in_specs=[once(BLOCK, 2 * D)] * shares
            + [
                pl.BlockSpec((D, width), lambda p, order: (0, order[1] * steps + p)),
                pl.BlockSpec(memory_space=pltpu.VMEM),
                pl.BlockSpec((width, D), lambda p, order: (order[1] * steps + p, 0)),
            ],
            out_specs=[pl.BlockSpec(memory_space=pltpu.VMEM)] * 4,
            scratch_shapes=[
                pltpu.VMEM((tokens, D), BF16),
                pltpu.VMEM((tokens, D), BF16),
                pltpu.VMEM((D, tokens), BF16),
                pltpu.VMEM((16, units), F32),
            ],
        ),
        out_shape=[pltpu.VMEM(shape, BF16) for shape in (down, down, up, up)],
        compiler_params=pltpu.CompilerParams(vmem_limit_bytes=16 * 2**20),
        name="feedforward_gradients",
    )(order, *row_parts, *streamed(w_up), b_up, *streamed(w_down))


def assemble_kernel(
    place_ref,
    one_ref,
    one_other_ref,
    two_ref,
    two_other_ref,
    down_ref,
    down_other_ref,
    up_ref,
    up_other_ref,
    *refs,
):
    outs, refs = refs[:8], refs[8:]
    held, sems = refs[:8], refs[8]
    query_ref, key_ref, value_ref, out_ref, wide_ref, narrow_ref, sums_ref, vec_ref = held
    piece = query_ref.shape[0] // 2
    half = one_ref.shape[1]
    units = up_ref.shape[2]
    copies = [pltpu.make_async_copy(held[at], outs[at], sems.at[at]) for at in range(8)]

    def write(cores):
        for core, (one, two, down, up) in enumerate(cores):
            rows = slice(core * piece, (core + 1) * piece)
            for bits in range(4):
                at = pl.multiple_of((place_ref[1] ^ bits) * units, units)
                wide_ref[rows, pl.ds(at, units)] = up[bits].astype(F32)
        copies[4].start()
        for core, (one, two, down, up) in enumerate(cores):
            columns = slice(core * half, (core + 1) * half)
            narrow_ref[:, columns] = down[:units, :].astype(F32)
            sums_ref[:, columns] = down[units:, :].astype(F32)
        copies[5].start()
        copies[6].start()
        for at, ref in enumerate((query_ref, key_ref, value_ref)):
            for core, (one, two, down, up) in enumerate(cores):
                rows = slice(core * piece, (core + 1) * piece)
                ref[rows, :half] = one[at * piece : (at + 1) * piece, :].astype(F32)
                ref[rows, half:] = two[at * piece : (at + 1) * piece, :].astype(F32)
            copies[at].start()
        base = 3 * piece
        vec_ref[:, :half] = one_ref[base : base + 16, :].astype(F32)
        vec_ref[:, half:] = two_ref[base : base + 16, :].astype(F32)
        copies[7].start()
        base += 16
        for core, (one, two, down, up) in enumerate(cores):
            rows = slice(core * piece, (core + 1) * piece)
            out_ref[rows, :half] = one[base : base + piece, :].astype(F32)
            out_ref[rows, half:] = one[base + piece : base + 2 * piece, :].astype(F32)
        copies[3].start()
        for copy in copies:
            copy.wait()

    own = (one_ref, two_ref, down_ref, up_ref)
    other = (one_other_ref, two_other_ref, down_other_ref, up_other_ref)

    @pl.when(place_ref[0] == 0)
    def _():
        write((own, other))

    @pl.when(place_ref[0] != 0)
    def _():
        write((other, own))


def assemble(order, one, two, down, up):
    share = D // up[0].shape[0]
    units = up[0].shape[2]
    shapes = [(share, D)] * 4 + [(share, units * up[0].shape[0]), (units, D), (16, D), (16, D)]
    whole = pl.BlockSpec(memory_space=pltpu.VMEM)
    return pl.pallas_call(
        assemble_kernel,
        grid_spec=pltpu.PrefetchScalarGridSpec(
            num_scalar_prefetch=1,
            grid=(1,),
            in_specs=[whole] * 8,
            out_specs=[pl.BlockSpec(memory_space=pl.ANY)] * 8,
            scratch_shapes=[pltpu.VMEM(shape, F32) for shape in shapes]
            + [pltpu.SemaphoreType.DMA((8,))],
        ),
        out_shape=[pltpu.HBM(shape, F32) for shape in shapes],
        compiler_params=pltpu.CompilerParams(vmem_limit_bytes=16 * 2**20),
        cost_estimate=pl.CostEstimate(flops=0, bytes_accessed=24 * 2**20, transcendentals=0),
        name="assemble",
    )(order, *one, *two, *down, *up)


def swapped(array, axis, bits):
    return lax.ppermute(array, axis, [(i, i ^ bits) for i in range(lax.axis_size(axis))])


def from_peers(arrays):
    return [swapped(array, "seq", bits) for bits, array in enumerate(arrays, 1)]


def picked(array, index, axis):
    return lax.dynamic_index_in_dim(array, index, axis, keepdims=False)


def together(*arrays):
    return lax.optimization_barrier(arrays)


def added(*arrays):
    return functools.reduce(jnp.add, [array.astype(F32) for array in arrays]).astype(BF16)


def halves(pack):
    middle = pack.shape[1] // 32 * 16
    return pack[:, :middle], pack[:, middle:]


def in_row_order(pack, mine):
    return jnp.stack([picked(pack, mine ^ at, 0) for at in range(4)], axis=0)


def square_mesh():
    return lax.axis_size("seq") == 4 and lax.axis_size("z") == 4


def scatter(pack):
    return from_peers([pack[1], pack[2], pack[3]])


NEXT = [(0, 1), (1, 0), (2, 3), (3, 2)]
ACROSS = [(0, 3), (1, 2), (2, 1), (3, 0)]


def half_of(share, second):
    half = share.shape[0] // 2
    return jnp.where(second, share[half:], share[:half])


def core_index():
    return lax.axis_index("core")


def both_cores(share, axis):
    other = swapped(share, "core", 1)
    first = core_index() == 0
    return jnp.concatenate(
        [jnp.where(first, share, other), jnp.where(first, other, share)], axis=axis
    )


def reduce_plain(partial):
    share = lax.psum_scatter(partial.astype(BF16), "seq", scatter_dimension=0, tiled=True)
    return lax.psum(share, ("z", "core")).astype(F32)


def local(
    tokens,
    cotangent,
    lengths,
    w_query,
    b_query,
    w_key,
    b_key,
    w_value,
    b_value,
    w_out,
    b_out,
    gain_one,
    shift_one,
    w_up,
    b_up,
    w_down,
    b_down,
    gain_two,
    shift_two,
    rel_table,
):
    rows = tokens.shape[0]
    cycle = lax.axis_size("seq")
    mine = lax.axis_index("seq")
    core = core_index()
    square = square_mesh()
    hidden_units = w_up.shape[1]
    share = D // cycle
    if square:
        token_parts = [tokens] + from_peers([tokens] * 3)
        ids = mine ^ jnp.arange(cycle, dtype=jnp.int32)
        order = jnp.stack([core, mine]).astype(jnp.int32)
        cores = 2
    else:
        token_parts = [tokens, lax.all_gather(tokens, "seq", axis=0, tiled=True)]
        ids = jnp.concatenate([mine[None], jnp.arange(cycle, dtype=jnp.int32)])
        order = jnp.zeros((2,), jnp.int32)
        cores = 1
    dist = jnp.concatenate([mine - ids, ids, lengths[0]]).astype(jnp.int32)

    at_z = lax.axis_index("z")
    end = (at_z == 0) | (at_z == 3)
    between = jnp.logical_not(end)
    low = core == 0
    odd_x, odd_y = (mine & 1) == 1, (mine & 2) == 2
    place_of = (dist, order, end, between, low, odd_x, odd_y)
    dist, order, end, between, low, odd_x, odd_y = lax.optimization_barrier(place_of)

    def in_order(pieces):
        first, second, third, fourth = pieces
        pairs = [
            (jnp.where(odd_x, b, a), jnp.where(odd_x, a, b))
            for a, b in ((first, second), (third, fourth))
        ]
        return [jnp.where(odd_y, b, a) for a, b in zip(*pairs)] + [
            jnp.where(odd_y, a, b) for a, b in zip(*pairs)
        ]

    def own_quarter(array):
        half = array.shape[1] // 2
        array = jnp.where(odd_y, array[:, half:], array[:, :half])
        return jnp.where(odd_x, array[:, half // 2 :], array[:, : half // 2])

    places = jnp.arange(RELROWS, dtype=jnp.int32)
    turn = (places[:, None] + places[None, :] == RELROWS - 1).astype(BF16)
    stay = (places[:, None] == places[None, :]).astype(BF16)
    rel_both = product(jnp.concatenate([turn, stay], axis=0), rel_table).astype(BF16)
    pos_key_back = (product(rel_both[:RELROWS], w_key) + b_key).astype(BF16)
    pos_query = (product(rel_both, w_query) + b_query).astype(BF16)
    pos_key_back, (dist, order, end, between, low, odd_x, odd_y) = together(
        pos_key_back, (dist, order, end, between, low, odd_x, odd_y)
    )
    context, prob, query, key, value, tokens_row, *held = attention_forward(
        dist,
        token_parts,
        [w_query, w_key, w_value],
        [b_query, b_key, b_value],
        pos_key_back,
        pos_query,
        [w_up, w_down, w_out],
    )
    held_up, held_down, held_out = held

    output, feed, normal_one, inverse_one, g_resid_two, slope, sums_two = middle_forward(
        dist, context, tokens, cotangent, held_out, b_out, gain_one, shift_one, b_down, gain_two,
        shift_two, held_up, b_up, held_down,
    )
    if square:
        row_parts = [feed] + from_peers([feed] * 3)
    g_resid_one, g_attn, g_context, sums_one, g_up = middle_backward(
        feed, g_resid_two, normal_one, inverse_one, gain_one, held_out, slope, held_up, held_down
    )
    vectors = [sums_one, sums_two]

    def backward(start, pairs, g_context, extra_one, extra_two):
        outs = attention_backward(
            start, pairs, cores, cycle, dist, order, query, key, value, pos_key_back, pos_query, prob,
            g_context, tokens_row, rel_table, w_query, w_key, w_value, extra_one, extra_two, vectors,
        )
        return outs[:cores], outs[cores:]

    piece = share // cores
    whole_rows = lambda v, at, each: v[:, at : at + each].reshape(cores * each, -1)

    def unpacked(v, each):
        base = 3 * piece + 16
        parts = D // v.shape[2]
        return jnp.concatenate(
            [whole_rows(v, base + part * each, each) for part in range(parts)], axis=1
        )

    def rel_own(pack):
        return unpacked(pack, RELROWS // cycle // cores)

    def results(grads, grad_w_out, vectors, grad_rel, grad_tokens, grad_w_up, grad_w_down, grad_b_up):
        return (
            output,
            grad_tokens,
            grads[0],
            vectors[0],
            grads[1],
            vectors[1],
            grads[2],
            vectors[2],
            grad_w_out,
            vectors[3],
            vectors[4],
            vectors[5],
            grad_w_up,
            grad_b_up,
            grad_w_down,
            vectors[6],
            vectors[7],
            vectors[8],
            grad_rel,
        )

    if not square:
        act = gelu_and_slope(product(feed[:, :D], w_up) + b_up)[0].astype(BF16)
        (one,), carried = backward(0, 3, g_context, context, g_attn)
        (two,), (home, away) = backward(3, 3, g_context, *carried)
        packs = [
            lax.psum(lax.psum_scatter(v, "seq", scatter_dimension=0, tiled=True), ("z", "core"))
            for v in (one, two)
        ]
        got = lax.psum_scatter(away, "seq", scatter_dimension=0, tiled=False)
        grads = [
            jnp.concatenate([whole_rows(v, at * piece, piece) for v in packs], axis=1).astype(F32)
            for at in range(3)
        ]
        base = 3 * piece
        sums = jnp.concatenate([v[0, base : base + 16] for v in packs], axis=1).astype(F32)
        return results(
            grads,
            unpacked(packs[0], piece).astype(F32),
            lax.dynamic_slice_in_dim(sums, mine * share, share, 1),
            lax.all_gather(rel_own(packs[-1]), "seq", axis=0, tiled=True).astype(F32),
            g_resid_one + home + got.astype(F32),
            reduce_plain(product_left(feed[:, :D], g_up)),
            reduce_plain(product_left(act, feed[:, D:])),
            reduce_plain(jnp.sum(g_up.astype(F32), axis=0)),
        )

    one, carried = backward(0, 3, g_context, context, g_attn)

    row_parts, one, carried = together(row_parts, one, carried)
    one_got = swapped(one[1], "core", 1)
    down_own, down_other, up_own, up_other = feedforward_gradients(
        order, row_parts, w_up, b_up, w_down
    )

    one_got, down_own, down_other, up_own, up_other = together(
        one_got, down_own, down_other, up_own, up_other
    )
    down_got = swapped(down_other, "core", 1)
    up_got = swapped(up_other, "core", 1)
    one_share = added(one[0], one_got)
    down_share = added(down_own, down_got)
    up_share = added(up_own, up_got)

    units = hidden_units // 4

    def first_start(v):
        first, second = halves(v)
        return swapped(first[1::2], "seq", 1), swapped(second[2:], "seq", 2)

    def first_end(v, got):
        first, second = halves(v)
        return added(first[0::2], got[0]), added(second[:2], got[1])

    def second_start(v):
        return swapped(v[0][1], "seq", 2), swapped(v[1][1], "seq", 1)

    def second_end(v, got):
        return jnp.concatenate([added(v[0][0], got[0]), added(v[1][0], got[1])], axis=0)

    def core_start(v):
        return swapped(v, "core", 1)

    def rel_rows(pair):
        base, each = 3 * share // 2 + 16, RELROWS // 8
        own, other = [
            jnp.concatenate([v[base : base + each], v[base + each : base + 2 * each]], axis=1)
            for v in pair
        ]
        return jnp.concatenate(
            [jnp.where(low, own, other), jnp.where(low, other, own)], axis=0
        )

    moves = {
        "first": (first_start, first_end),
        "second": (second_start, second_end),
        "in": (
            lambda v: lax.ppermute(half_of(v, end), "z", NEXT),
            lambda v, got: added(half_of(v, between), got),
        ),
        "mid": (lambda v: lax.ppermute(v, "z", ACROSS), added),
        "out": (
            lambda v: lax.ppermute(v, "z", NEXT),
            lambda v, got: jnp.concatenate(
                [jnp.where(end, v, got), jnp.where(end, got, v)], axis=0
            ),
        ),
        "pair": (lambda v: swapped(v[1], "core", 1), lambda v, got: added(v[0], got)),
        "rows": (core_start, lambda v, got: (v, got)),
        "columns": (core_start, lambda v, got: (v, got)),
        "give": (scatter, lambda v, got: jnp.stack([v[0]] + got, axis=0)),
        "home": (
            lambda v: from_peers([v[0], v[1], v[2]]),
            lambda v, got: functools.reduce(jnp.add, [part.astype(F32) for part in got]),
        ),
        "spread": (scatter, lambda v, got: added(v[0], *got)),
        "x": (lambda v: swapped(v[1], "seq", 1), lambda v, got: [v[0], got, v[2], v[3]]),
        "y": (lambda v: swapped(v[2], "seq", 2), lambda v, got: [v[0], v[1], got, v[3]]),
        "d": (
            lambda v: swapped(v[3], "seq", 3),
            lambda v, got: jnp.stack([v[0], v[1], v[2], got], axis=0),
        ),
        "dd": (
            lambda v: swapped(v[3], "seq", 3),
            lambda v, got: jnp.stack([v[0], v[1], v[2], got], axis=0),
        ),
        "hx": (lambda v: swapped(v[0], "seq", 1), lambda v, got: [got, v[1], v[2]]),
        "hy": (lambda v: swapped(v[1], "seq", 2), lambda v, got: [v[0], got, v[2]]),
        "hd": (
            lambda v: swapped(v[2], "seq", 3),
            lambda v, got: functools.reduce(
                jnp.add, [part.astype(F32) for part in (v[0], v[1], got)]
            ),
        ),
        "rel": (
            lambda v: from_peers([rel_rows(v)] * 3),
            lambda v, got: (v, [rel_rows(v)] + got),
        ),
    }
    held_sums = {"down": down_share, "up": up_share, "one": one_share}
    flying = {}

    def begin(*steps):
        for step in steps:
            name, move = step.split(".")
            if move == "share":
                both = zip(held_sums["up"][1:], held_sums["away"])
                flying[step] = from_peers([jnp.concatenate(parts, axis=0) for parts in both])
            else:
                flying[step] = moves[move][0](held_sums[name])

    def meet(done, then):
        names = [step.split(".")[0] for step in then] + [step.split(".")[0] for step in done]
        names += ["away"] if "up.share" in done or "up.share" in then else []
        names = [name for at, name in enumerate(names) if name not in names[:at]]
        gots = {step: flying.pop(step) for step in done}
        kept, gots = together({name: held_sums[name] for name in names}, gots)
        held_sums.update(kept)
        for step in done:
            name, move = step.split(".")
            if move == "share":
                each = held_sums["up"].shape[1]
                parts = [held_sums["up"][0]] + [got[:each] for got in gots[step]]
                held_sums["up"] = jnp.stack(parts, axis=0)
                homes = [got[each:].astype(F32) for got in gots[step]]
                held_sums["away"] = functools.reduce(jnp.add, homes)
            else:
                held_sums[name] = moves[move][1](held_sums[name], gots[step])
        begin(*then)

    stages = (
        ([], ["up.in", "one.first"]),
        (["up.in", "one.first"], ["two.pair", "up.mid", "one.second"]),
        (["two.pair"], ["two.first"]),
        (["one.second"], ["one.in", "down.in"]),
        (["two.first", "up.mid"], ["two.second", "up.out"]),
        (["one.in"], ["one.mid"]),
        (["two.second", "down.in", "one.mid"], ["two.in", "down.mid", "one.out"]),
        (["two.in", "up.out"], ["two.mid"]),
        (["one.out"], ["up.share"]),
        (["down.mid"], ["down.out"]),
        (["two.mid"], ["two.out"]),
        (["two.out", "down.out", "up.share"], ["two.rows", "one.rows", "up.columns", "down.columns"]),
        (["two.rows", "one.rows", "up.columns", "down.columns"], []),
    )
    begin(*stages[0][1])
    g_context, held_sums = together(g_context, held_sums)
    two, (home, away) = backward(3, 3, g_context, *carried)
    home, held_sums, flying_now = together(
        home, dict(held_sums, two=two, away=away), {step: flying[step] for step in stages[1][0]}
    )
    flying.update(flying_now)
    for done, then in stages[1:]:
        meet(done, then)

    grad_tokens = g_resid_one + home + held_sums["away"]
    rel = rel_rows(held_sums["two"])
    from_y, from_both = swapped(rel, "seq", 2), swapped(rel, "seq", 3)
    *grads, grad_w_up, grad_w_down, sums_up, sums = assemble(
        order, held_sums["one"], held_sums["two"], held_sums["down"], held_sums["up"]
    )
    rel, sums = together(rel, sums)
    rel_parts = [rel, swapped(rel, "seq", 1), from_y, from_both]
    return results(
        grads[:3],
        grads[3],
        own_quarter(sums),
        jnp.concatenate(in_order(rel_parts), axis=0).astype(F32),
        grad_tokens,
        grad_w_up,
        grad_w_down,
        sums_up[0],
    )


def solution(mesh):
    lines, cycle = mesh.devices.shape
    chips = Mesh(mesh.devices.reshape(lines // 2, 2, cycle), ("z", "core", "seq"))
    return jax.shard_map(
        local,
        mesh=chips,
        in_specs=(
            P(("z", "core", "seq"), None),
            P(("z", "core", "seq"), None),
            P(("z", "core"), None),
        )
        + (P(),) * 17,
        out_specs=(
            P(("z", "core", "seq"), None),
            P(("z", "core", "seq"), None),
            P("seq", None),
            P("seq"),
            P("seq", None),
            P("seq"),
            P("seq", None),
            P("seq"),
            P("seq", None),
            P("seq"),
            P("seq"),
            P("seq"),
            P("seq", None),
            P("seq"),
            P("seq", None),
            P("seq"),
            P("seq"),
            P("seq"),
            P(),
        ),
        check_vma=False,
    )
```

```python
import functools
import math

import jax
import jax.numpy as jnp
from jax import lax
from jax.experimental import pallas as pl
from jax.experimental.pallas import tpu as pltpu
from jax.sharding import Mesh, PartitionSpec as P

D = 768
HEADS = 12
HEAD = 64
SPAN = 256
RELROWS = 512
BLOCK = 128
EXT = RELROWS + 2 * SPAN
PAIRS = HEADS // 2
VECTORS = 2
LATER = 3
DOCS = 4
SCALE = 1.0 / math.sqrt(3 * HEAD)
F32 = jnp.float32
BF16 = jnp.bfloat16
ROLLED = BF16


def normalized(resid):
    center = resid - jnp.mean(resid, axis=-1, keepdims=True)
    inverse = lax.rsqrt(jnp.mean(center * center, axis=-1, keepdims=True) + 1e-07)
    return center * inverse, inverse


def normalized_back(grad, normal, inverse, gain):
    hat = grad * gain
    means = jnp.mean(hat, axis=-1, keepdims=True) + normal * jnp.mean(
        hat * normal, axis=-1, keepdims=True
    )
    total = lambda v: jnp.sum(v, axis=0, keepdims=True)
    return (hat - means) * inverse, total(grad * normal), total(grad)


def product(left, right):
    return jnp.dot(left, right, preferred_element_type=F32)


def product_left(left, right):
    return lax.dot_general(left, right, (((0,), (0,)), ((), ())), preferred_element_type=F32)


def product_right(left, right):
    return lax.dot_general(left, right, (((1,), (1,)), ((), ())), preferred_element_type=F32)


def segment_of(position, place_ref, at):
    passed, bound = jnp.zeros(position.shape, jnp.int32), 0
    for document in range(DOCS):
        bound = bound + place_ref[at + document]
        passed = passed + (position >= bound).astype(jnp.int32)
    return passed


def anti_identity():
    rows = lax.broadcasted_iota(jnp.int32, (BLOCK, BLOCK), 0)
    cols = lax.broadcasted_iota(jnp.int32, (BLOCK, BLOCK), 1)
    return (rows + cols == BLOCK - 1).astype(BF16)


def extend(ext_ref, table_ref):
    ext_ref[SPAN : SPAN + RELROWS, :] = table_ref[...]
    ext_ref[0:SPAN, :] = jnp.broadcast_to(table_ref[0:1, :], (SPAN, BLOCK))
    last = table_ref[RELROWS - 1 : RELROWS, :]
    ext_ref[SPAN + RELROWS :, :] = jnp.broadcast_to(last, (SPAN, BLOCK))


def window_start(offset):
    return pl.multiple_of(jnp.clip(offset, 0, EXT - 2 * BLOCK), BLOCK)


def head_mask(head):
    lane = lax.broadcasted_iota(jnp.int32, (1, BLOCK), 1)
    return (lane >= head * HEAD) & (lane < (head + 1) * HEAD)


def band_roll(wide, shift):
    return pltpu.roll(wide, shift, 1, stride=1, stride_axis=0)


def by_head(pair):
    zero = jnp.zeros_like(pair)
    return jnp.concatenate([jnp.where(head_mask(head), pair, zero) for head in range(2)], axis=0)


def forward_kernel(
    parts, blocks, dist_ref, *refs
):
    part_refs, refs = refs[:parts], refs[parts:]
    wq_ref, wk_ref, wv_ref, bq_ref, bk_ref, bv_ref, pk_ref, pq_ref, *refs = refs
    later, refs = refs[:LATER], refs[LATER:]
    ctx_ref, prob_ref, q_ref, k_ref, v_ref, tok_ref, *refs = refs
    held, refs = refs[:LATER], refs[LATER:]
    score_ref, ek_ref, eq_ref, bias_ref, sems = refs
    copies = [
        pltpu.make_async_copy(later[at], held[at], sems.at[at]) for at in range(LATER)
    ]

    @pl.when(pl.program_id(0) == 0)
    def _():
        for copy in copies:
            copy.start()

    @pl.when(pl.program_id(0) == pl.num_programs(0) - 1)
    def _():
        for copy in copies:
            copy.wait()

    extend(ek_ref, pk_ref)
    extend(eq_ref, pq_ref)

    @pl.when(pl.program_id(0) == 0)
    def _():
        at = 0
        for ref in part_refs:
            tok_ref[at : at + ref.shape[0], :] = ref[...]
            at += ref.shape[0]
        mine = dist_ref[blocks]
        lane = lax.broadcasted_iota(jnp.int32, (1, BLOCK), 1)
        line = lax.broadcasted_iota(jnp.int32, (BLOCK, 1), 0)
        query_segment = segment_of(mine * BLOCK + lane, dist_ref, 2 * blocks)
        for block in range(blocks):
            home = dist_ref[blocks + block]
            allowed = segment_of(home * BLOCK + line, dist_ref, 2 * blocks) == query_segment
            if block > 0:
                allowed = jnp.logical_and(allowed, home != mine)
            rows = slice(block * BLOCK, (block + 1) * BLOCK)
            bias_ref[rows, :] = jnp.where(allowed, 0.0, -1e30)

    at = pl.multiple_of(pl.program_id(0) * BLOCK, BLOCK)
    both = product(tok_ref[...], jnp.concatenate([wk_ref[...], wv_ref[...]], axis=1))
    k_ref[...] = (both[:, :BLOCK] + row_of(bk_ref, at, BLOCK)).astype(BF16)
    v_ref[...] = (both[:, BLOCK:] + row_of(bv_ref, at, BLOCK)).astype(BF16)
    q = (product(tok_ref[:BLOCK, :], wq_ref[...]) + row_of(bq_ref, at, BLOCK)).astype(BF16)
    q_ref[...] = q
    q_heads = by_head(q)
    tops = [jnp.full((1, BLOCK), -jnp.inf, F32) for head in range(2)]
    for block in range(blocks):
        dist = dist_ref[block]
        rows = slice(block * BLOCK, (block + 1) * BLOCK)
        k_heads = by_head(k_ref[rows, :])
        window_c = ek_ref[pl.ds(window_start(384 - dist * BLOCK), 2 * BLOCK), :]
        window_p = eq_ref[pl.ds(window_start(384 + dist * BLOCK), 2 * BLOCK), :]
        c2p = product_right(q_heads, window_c)
        p2c = product_right(k_heads, window_p)
        direct = product_right(k_heads, q)
        for head in range(2):
            own = slice(head * BLOCK, (head + 1) * BLOCK)
            first = band_roll(c2p[own].astype(BF16), BLOCK + 1)[:, :BLOCK].T
            second = band_roll(p2c[own].astype(BF16), BLOCK + 1)[:, :BLOCK]
            score = (direct[own] + first.astype(F32) + second.astype(F32)) * SCALE + bias_ref[rows, :]
            score_ref[head, rows, :] = score
            tops[head] = jnp.maximum(tops[head], jnp.max(score, axis=0, keepdims=True))
    probs = []
    for head in range(2):
        weight = jnp.exp(score_ref[head] - tops[head])
        total = jnp.sum(weight, axis=0, keepdims=True)
        prob = (weight * (1.0 / total)).astype(BF16)
        prob_ref[head] = prob
        probs.append(prob)
    v = v_ref[...]
    zero = jnp.zeros_like(v)
    out = product_left(probs[0], jnp.where(head_mask(0), v, zero)) + product_left(
        probs[1], jnp.where(head_mask(1), v, zero)
    )
    ctx_ref[...] = out.astype(BF16)


def streamed(*arrays):
    return [pltpu.with_memory_space_constraint(array, pltpu.HBM) for array in arrays]


def once(*shape):
    return pl.BlockSpec(shape, lambda p, *_: (0,) * len(shape), pipeline_mode=pl.Buffered(1))


def fits(keys):
    return keys <= 2 * RELROWS


def kept(keys, *shape):
    return pl.BlockSpec(memory_space=pltpu.VMEM) if fits(keys) else once(*shape)


def kept_array(keys, shape, dtype):
    return (pltpu.VMEM if fits(keys) else jax.ShapeDtypeStruct)(shape, dtype)


def attention_forward(dist, token_parts, weights, biases, pos_key, pos_query, later):
    keys = sum(part.shape[0] for part in token_parts)
    blocks = keys // BLOCK
    pair = lambda rows: pl.BlockSpec((rows, BLOCK), lambda p, dist: (0, p))
    return pl.pallas_call(
        functools.partial(forward_kernel, len(token_parts), blocks),
        grid_spec=pltpu.PrefetchScalarGridSpec(
            num_scalar_prefetch=1,
            grid=(PAIRS,),
            in_specs=[once(*part.shape) for part in token_parts]
            + [pair(D)] * 3
            + [pl.BlockSpec(memory_space=pltpu.VMEM)] * 3
            + [pair(RELROWS), pair(RELROWS)]
            + [pl.BlockSpec(memory_space=pl.ANY)] * LATER,
            out_specs=[
                pair(BLOCK),
                pl.BlockSpec((2, keys, BLOCK), lambda p, dist: (p, 0, 0)),
                pair(BLOCK),
                pair(keys),
                pair(keys),
                kept(keys, keys, D),
            ]
            + [pl.BlockSpec(memory_space=pl.ANY)] * LATER,
            scratch_shapes=[
                pltpu.VMEM((2, keys, BLOCK), F32),
                pltpu.VMEM((EXT, BLOCK), BF16),
                pltpu.VMEM((EXT, BLOCK), BF16),
                pltpu.VMEM((keys, BLOCK), F32),
                pltpu.SemaphoreType.DMA((LATER,)),
            ],
        ),
        out_shape=[
            jax.ShapeDtypeStruct((BLOCK, D), BF16),
            pltpu.HBM((HEADS, keys, BLOCK), BF16),
            pltpu.HBM((BLOCK, D), BF16),
            pltpu.HBM((keys, D), BF16),
            pltpu.HBM((keys, D), BF16),
            kept_array(keys, (keys, D), BF16),
        ]
        + [pltpu.VMEM(array.shape, array.dtype) for array in later],
        compiler_params=pltpu.CompilerParams(vmem_limit_bytes=(16 if fits(keys) else 40) * 2**20),
        name="attention_forward",
    )(dist, *token_parts, *streamed(*weights), *biases, *streamed(pos_key, pos_query), *streamed(*later))


def fold_edges(acc_ref):
    head_sum = jnp.sum(acc_ref[:, 0:SPAN], axis=1, keepdims=True)
    tail_sum = jnp.sum(acc_ref[:, SPAN + RELROWS :], axis=1, keepdims=True)
    lane = lax.broadcasted_iota(jnp.int32, (BLOCK, RELROWS), 1)
    middle = acc_ref[:, SPAN : SPAN + RELROWS]
    middle = middle + jnp.where(lane == 0, head_sum, 0.0)
    return (middle + jnp.where(lane == RELROWS - 1, tail_sum, 0.0)).astype(BF16)


def flipped_lanes(array, flip):
    parts = array.shape[1] // BLOCK
    return jnp.concatenate(
        [
            product(array[:, part * BLOCK : (part + 1) * BLOCK], flip).astype(BF16)
            for part in reversed(range(parts))
        ],
        axis=1,
    )


def place(order_ref, share, core, shares, each):
    at = (core ^ order_ref[0]) * shares + (share ^ order_ref[1])
    return pl.multiple_of(at * each, 16)


def place_rows(order_ref, into_ref, value, cores, shares):
    each = value.shape[0] // (cores * shares)
    for share in range(shares):
        for core in range(cores):
            at = (share * cores + core) * each
            into_ref[pl.ds(place(order_ref, share, core, shares, each), each), :] = value[
                at : at + each
            ]


def store_pieces(refs, at, value, lanes):
    shares = refs[0].shape[0]
    each = value.shape[0] // (len(refs) * shares)
    for core, ref in enumerate(refs):
        for share in range(shares):
            start = (core * shares + share) * each
            ref[share, at : at + each, lanes] = value[start : start + each]


def backward_kernel(
    blocks,
    cores,
    first,
    last,
    dist_ref,
    order_ref,
    q_ref,
    k_ref,
    v_ref,
    pk_ref,
    pq_ref,
    prob_ref,
    gctx_ref,
    tok_ref,
    rel_ref,
    wq_ref,
    wk_ref,
    wv_ref,
    extra_one_ref,
    extra_two_ref,
    *refs,
):
    vec_refs, refs = refs[:VECTORS], refs[VECTORS:]
    pack_refs, refs = refs[:cores], refs[cores:]
    backward_body(
        blocks, first, last, dist_ref, order_ref, q_ref, k_ref, v_ref, pk_ref, pq_ref, prob_ref, gctx_ref,
        tok_ref, rel_ref, wq_ref, wk_ref, wv_ref, extra_one_ref, extra_two_ref, vec_refs, pack_refs, *refs
    )


def backward_body(
    blocks,
    first,
    last,
    dist_ref,
    order_ref,
    q_ref,
    k_ref,
    v_ref,
    pk_ref,
    pq_ref,
    prob_ref,
    gctx_ref,
    tok_ref,
    rel_ref,
    wq_ref,
    wk_ref,
    wv_ref,
    extra_one_ref,
    extra_two_ref,
    vec_refs,
    pack_refs,
    out_one_ref,
    out_two_ref,
    back_ref,
    gk_ref,
    gv_ref,
    acck_ref,
    accq_ref,
    tokt_ref,
    relt_ref,
    acc_tok_ref,
    acc_rel_ref,
    turn_ref,
    ek_ref,
    eq_ref,
):
    step = pl.program_id(0)
    if not last:
        acc_tok_ref, acc_rel_ref = out_one_ref, out_two_ref
    extend(ek_ref, pk_ref)
    extend(eq_ref, pq_ref)
    cores, shares, half = len(pack_refs), pack_refs[0].shape[0], pack_refs[0].shape[2]
    share = D // cores // shares
    flip = anti_identity()

    @pl.when(step == 0)
    def _():
        place_rows(order_ref, tokt_ref, tok_ref[...].T, cores, shares)
        place_rows(order_ref, relt_ref, rel_ref[...].T, cores, shares)
        if first:
            acc_tok_ref[...] = jnp.zeros_like(acc_tok_ref)
            acc_rel_ref[...] = jnp.zeros_like(acc_rel_ref)
        else:
            acc_tok_ref[...] = extra_one_ref[...]
            acc_rel_ref[...] = extra_two_ref[...]

    acck_ref[...] = jnp.zeros_like(acck_ref)
    accq_ref[...] = jnp.zeros_like(accq_ref)
    g_heads = by_head(gctx_ref[...])
    first_rows = lax.broadcasted_iota(jnp.int32, (BLOCK, 1), 0) < HEAD
    first_lanes = head_mask(0)

    def turned_heads(array):
        turned = array.T
        zero = jnp.zeros_like(turned)
        return jnp.concatenate(
            [jnp.where(first_rows, turned, zero), jnp.where(first_rows, zero, turned)], axis=1
        )

    def of_heads(stacked):
        return jnp.where(first_lanes, stacked[:BLOCK], stacked[BLOCK:])

    q_back = product(flip, q_ref[...]).astype(BF16)
    q_turned = turned_heads(q_back)
    probs = jnp.concatenate([prob_ref[head] for head in range(2)], axis=1)
    g_prob = product_right(v_ref[...], g_heads)
    gv_ref[...] = product(probs, g_heads).astype(BF16)
    probs = probs.astype(F32)
    delta = jnp.sum(probs * g_prob, axis=0, keepdims=True)
    g_score = (probs * (g_prob - delta) * SCALE).astype(BF16)
    for head in range(2):
        lanes = slice(head * BLOCK, (head + 1) * BLOCK)
        back_ref[:, lanes] = product(g_score[:, lanes], flip).astype(BF16)
    g_query = jnp.zeros((2 * BLOCK, BLOCK), F32)
    pad = jnp.zeros((BLOCK, BLOCK), BF16)
    for block in range(blocks):
        rows = slice(block * BLOCK, (block + 1) * BLOCK)
        k_block = k_ref[rows, :]
        at = pl.ds(window_start(384 - dist_ref[block] * BLOCK), 2 * BLOCK)
        window_c = ek_ref[at, :]
        window_p = eq_ref[at, :]
        backs = [back_ref[rows, head * BLOCK : (head + 1) * BLOCK] for head in range(2)]
        turns = [back.T for back in backs]
        bands_c = [band_roll(jnp.concatenate([turn, pad], axis=1), 0) for turn in turns]
        bands_p = [band_roll(jnp.concatenate([back, pad], axis=1), 1) for back in backs]
        bands_c = jnp.concatenate(bands_c, axis=0)
        bands_p = jnp.concatenate(bands_p, axis=0)
        g_query = g_query + product(
            jnp.concatenate([jnp.concatenate(turns, axis=0), bands_c], axis=1),
            jnp.concatenate([k_block, window_c], axis=0),
        )
        g_key = product(
            jnp.concatenate([jnp.concatenate(backs, axis=0), bands_p], axis=1),
            jnp.concatenate([q_back, window_p], axis=0),
        )
        gk_ref[rows, :] = of_heads(g_key).astype(BF16)
        acck_ref[:, at] += product(q_turned, bands_c)
        accq_ref[:, at] += product(turned_heads(k_block), bands_p)

    g_query = product(flip, of_heads(g_query).astype(BF16)).astype(BF16)
    g_pos_key = flipped_lanes(fold_edges(acck_ref), flip)
    g_pos_query = fold_edges(accq_ref)
    g_key = gk_ref[...]
    g_value = gv_ref[...]
    lanes = pl.ds(pl.multiple_of(step * BLOCK, BLOCK), BLOCK)
    ones_tok = jnp.ones((16, tok_ref.shape[0]), BF16)
    ones_rel = jnp.ones((16, RELROWS), BF16)
    row = lax.broadcasted_iota(jnp.int32, (16, BLOCK), 0)
    vec = jnp.zeros((16, BLOCK), F32)
    for at, vec_ref in enumerate(vec_refs):
        for part in range(3):
            vec = vec + jnp.where(row == 3 + 3 * at + part, vec_ref[part : part + 1, :], 0.0)
    g_both = jnp.concatenate([g_key, g_value], axis=1)
    pos_both = jnp.concatenate([g_pos_key, g_pos_query], axis=0)
    from_tok = product(tokt_ref[...], g_both)
    from_rel = product_right(relt_ref[...], pos_both)
    from_own = product(tokt_ref[:, :BLOCK], g_query)
    sum_tok = product(ones_tok, g_both)
    sum_rel = product_right(ones_rel, pos_both)
    sum_own = product(ones_tok[:, :BLOCK], g_query)
    weights = [
        (from_own + from_rel[:, BLOCK:], sum_own + sum_rel[:, BLOCK:]),
        (from_tok[:, :BLOCK] + from_rel[:, :BLOCK], sum_tok[:, :BLOCK] + sum_rel[:, :BLOCK]),
        (from_tok[:, BLOCK:], sum_tok[:, BLOCK:]),
    ]
    for at, (weight, total) in enumerate(weights):
        store_pieces(pack_refs, at * share, weight.astype(BF16), lanes)
        vec = vec + jnp.where(row == at, total, 0.0)
    vec = vec.astype(BF16)
    for pack_ref in pack_refs:
        for part in range(shares):
            pack_ref[part, 3 * share : 3 * share + 16, lanes] = vec
    acc_tok_ref[...] += product_right(
        g_both,
        jnp.concatenate([wk_ref[...], wv_ref[...]], axis=1),
    )
    acc_tok_ref[0:BLOCK, :] += product_right(g_query, wq_ref[...])
    acc_rel_ref[...] += product(
        jnp.concatenate([wk_ref[...], wq_ref[...]], axis=1),
        pos_both,
    )

    @pl.when(step == pl.num_programs(0) - 1)
    def _():
        base = 3 * share + 16
        extra = None
        if last:
            out_one_ref[...] = acc_tok_ref[0:BLOCK, :]
            for block in range(1, blocks):
                out_two_ref[block - 1] = acc_tok_ref[block * BLOCK : (block + 1) * BLOCK].astype(BF16)
            place_rows(order_ref, turn_ref, acc_rel_ref[...].T.astype(BF16), cores, shares)
            extra = turn_ref[...]
        if first:
            place_rows(order_ref, turn_ref, extra_one_ref[...].T, cores, shares)
            extra = product(turn_ref[...], extra_two_ref[...]).astype(BF16)
        if extra is not None:
            each = extra.shape[0] // (cores * shares)
            for part in range(D // half):
                columns = extra[:, part * half : (part + 1) * half]
                store_pieces(pack_refs, base + part * each, columns, slice(None))


def attention_backward(
    start, pairs, cores, shares, dist, order, query, key, value, pos_key, pos_query, prob, g_context,
    tokens_row, rel_table, w_query, w_key, w_value, extra_one, extra_two, vectors,
):
    keys = key.shape[0]
    blocks = keys // BLOCK
    first, last = start == 0, start + pairs == PAIRS
    share = D // cores // shares
    half = pairs * BLOCK
    rows_extra = D if first else RELROWS if last else 0
    pack = (shares, 3 * share + 16 + rows_extra // cores // shares * (D // half), half)
    pair = lambda rows: pl.BlockSpec((rows, BLOCK), lambda p, *_: (0, p + start))
    if first:
        extras = [once(BLOCK, D), once(BLOCK, D)]
        turn = (D, BLOCK)
    else:
        extras = [kept(keys, keys, D), kept(keys, D, RELROWS)]
        turn = (RELROWS, D)
    sums = [(keys, D), (D, RELROWS)] if last else [(8, 128), (8, 128)]
    if last:
        outs = [((BLOCK, D), F32), ((blocks - 1, BLOCK, D), BF16)]
    else:
        outs = [((keys, D), F32), ((D, RELROWS), F32)]
    return pl.pallas_call(
        functools.partial(backward_kernel, blocks, cores, first, last),
        grid_spec=pltpu.PrefetchScalarGridSpec(
            num_scalar_prefetch=2,
            grid=(pairs,),
            in_specs=[
                pair(BLOCK),
                pair(keys),
                pair(keys),
                pair(RELROWS),
                pl.BlockSpec((RELROWS, BLOCK), lambda p, *_: (1, p + start)),
                pl.BlockSpec((2, keys, BLOCK), lambda p, *_: (p + start, 0, 0)),
                pair(BLOCK),
                kept(keys, keys, D),
                once(RELROWS, D),
                pair(D),
                pair(D),
                pair(D),
            ]
            + extras
            + [pair(8)] * VECTORS,
            out_specs=[kept(keys, *pack)] * cores + [kept(keys, *shape) for shape, _ in outs],
            scratch_shapes=[
                pltpu.VMEM((keys, 2 * BLOCK), BF16),
                pltpu.VMEM((keys, BLOCK), BF16),
                pltpu.VMEM((keys, BLOCK), BF16),
                pltpu.VMEM((BLOCK, EXT), F32),
                pltpu.VMEM((BLOCK, EXT), F32),
                pltpu.VMEM((D, keys), BF16),
                pltpu.VMEM((D, RELROWS), BF16),
                pltpu.VMEM(sums[0], F32),
                pltpu.VMEM(sums[1], F32),
                pltpu.VMEM(turn, BF16),
                pltpu.VMEM((EXT, BLOCK), BF16),
                pltpu.VMEM((EXT, BLOCK), BF16),
            ],
        ),
        out_shape=[kept_array(keys, pack, BF16)] * cores
        + [kept_array(keys, shape, dtype) for shape, dtype in outs],
        compiler_params=pltpu.CompilerParams(vmem_limit_bytes=(18 if fits(keys) else 58) * 2**20),
        name="attention_backward",
    )(
        dist, order, *streamed(query, key, value, pos_key, pos_query, prob), g_context,
        tokens_row, *streamed(rel_table, w_query, w_key, w_value), extra_one, extra_two, *vectors,
    )


def column_sum(array):
    return jnp.sum(array, axis=0, keepdims=True)


def middle_forward_kernel(
    blocks,
    place_ref,
    ctx_ref,
    tok_ref,
    cot_ref,
    wout_ref,
    bout_ref,
    gain_one_ref,
    shift_one_ref,
    bdown_ref,
    gain_two_ref,
    shift_two_ref,
    wup_ref,
    bup_ref,
    wdown_ref,
    output_ref,
    feed_ref,
    normal_ref,
    inverse_ref,
    resid_ref,
    slope_ref,
    sums_ref,
    hidden_ref,
    down_ref,
):
    step = pl.program_id(0)

    @pl.when(step == 0)
    def _():
        attn = product(ctx_ref[...], wout_ref[...]) + row_of(bout_ref)
        normal, inverse = normalized(tok_ref[...].astype(F32) + attn)
        normal_ref[...] = normal
        inverse_ref[...] = jnp.broadcast_to(inverse, inverse_ref.shape)
        hidden = normal * row_of(gain_one_ref) + row_of(shift_one_ref)
        hidden_ref[...] = hidden
        feed_ref[:, :D] = hidden.astype(BF16)
        down_ref[...] = jnp.zeros_like(down_ref)

    width = slope_ref.shape[1]
    at = pl.multiple_of(step * width, width)
    units = pl.ds(at, width)
    act, slope = gelu_and_slope(
        product(feed_ref[:, :D], wup_ref[:, units]) + row_of(bup_ref, at, width)
    )
    slope_ref[...] = slope
    down_ref[...] += product(act.astype(BF16), wdown_ref[units, :])

    @pl.when(step == pl.num_programs(0) - 1)
    def _():
        normal, inverse = normalized(hidden_ref[...] + (down_ref[...] + row_of(bdown_ref)))
        output_ref[...] = (normal * row_of(gain_two_ref) + row_of(shift_two_ref)).astype(BF16)
        position = place_ref[blocks] * BLOCK + lax.broadcasted_iota(jnp.int32, (BLOCK, 1), 0)
        valid = segment_of(position, place_ref, 2 * blocks) < DOCS
        g_out = jnp.where(valid, cot_ref[...].astype(F32), 0.0)
        g_resid, g_gain, g_shift = normalized_back(g_out, normal, inverse, row_of(gain_two_ref))
        resid_ref[...] = g_resid
        g_down = g_resid.astype(BF16)
        feed_ref[:, D:] = g_down
        sums_ref[0:1, :] = column_sum(g_down.astype(F32))
        sums_ref[1:2, :] = g_gain
        sums_ref[2:3, :] = g_shift


def middle_forward(
    place, context, tokens, cotangent, w_out, b_out, gain_one, shift_one, b_down, gain_two, shift_two,
    w_up, b_up, w_down,
):
    units = w_up.shape[1]
    width = 512
    return pl.pallas_call(
        functools.partial(middle_forward_kernel, (place.shape[0] - DOCS) // 2),
        grid_spec=pltpu.PrefetchScalarGridSpec(
        num_scalar_prefetch=1,
        grid=(units // width,),
        in_specs=[once(BLOCK, D)] * 3
        + [pl.BlockSpec(memory_space=pltpu.VMEM)]
        + [pl.BlockSpec(memory_space=pltpu.VMEM)] * 6
        + [
            pl.BlockSpec(memory_space=pltpu.VMEM),
            pl.BlockSpec(memory_space=pltpu.VMEM),
            pl.BlockSpec(memory_space=pltpu.VMEM),
        ],
        out_specs=[
            once(BLOCK, D),
            once(BLOCK, 2 * D),
            once(BLOCK, D),
            once(BLOCK, BLOCK),
            once(BLOCK, D),
            pl.BlockSpec((BLOCK, width), lambda p, *_: (0, p)),
            once(8, D),
        ],
        scratch_shapes=[pltpu.VMEM((BLOCK, D), F32), pltpu.VMEM((BLOCK, D), F32)],
        ),
        out_shape=[
            jax.ShapeDtypeStruct((BLOCK, D), BF16),
            jax.ShapeDtypeStruct((BLOCK, 2 * D), BF16),
            jax.ShapeDtypeStruct((BLOCK, D), F32),
            jax.ShapeDtypeStruct((BLOCK, BLOCK), F32),
            jax.ShapeDtypeStruct((BLOCK, D), F32),
            jax.ShapeDtypeStruct((BLOCK, units), F32),
            jax.ShapeDtypeStruct((8, D), F32),
        ],
        compiler_params=pltpu.CompilerParams(vmem_limit_bytes=20 * 2**20),
        name="middle_forward",
    )(
        place, context, tokens, cotangent, w_out, b_out, gain_one, shift_one, b_down,
        gain_two, shift_two, w_up, b_up, w_down,
    )


def middle_backward_kernel(
    feed_ref,
    resid_ref,
    normal_ref,
    inverse_ref,
    gain_ref,
    wout_ref,
    slope_ref,
    wup_ref,
    wdown_ref,
    g_resid_ref,
    g_attn_ref,
    g_ctx_ref,
    sums_ref,
    g_up_ref,
    acc_ref,
):
    step = pl.program_id(0)

    @pl.when(step == 0)
    def _():
        acc_ref[...] = resid_ref[...]

    width = slope_ref.shape[1]
    units = pl.ds(pl.multiple_of(step * width, width), width)
    g_up = (product_right(feed_ref[:, D:], wdown_ref[units, :]) * slope_ref[...]).astype(BF16)
    g_up_ref[...] = g_up
    acc_ref[...] += product_right(g_up, wup_ref[:, units])

    @pl.when(step == pl.num_programs(0) - 1)
    def _():
        g_resid, g_gain, g_shift = normalized_back(
            acc_ref[...], normal_ref[...], inverse_ref[:, 0:1], row_of(gain_ref)
        )
        g_resid_ref[...] = g_resid
        g_attn = g_resid.astype(BF16)
        g_attn_ref[...] = g_attn
        g_ctx_ref[...] = product_right(g_attn, wout_ref[...]).astype(BF16)
        sums_ref[0:1, :] = column_sum(g_attn.astype(F32))
        sums_ref[1:2, :] = g_gain
        sums_ref[2:3, :] = g_shift


def middle_backward(feed, g_resid_two, normal, inverse, gain_one, w_out, slope, w_up, w_down):
    units = w_up.shape[1]
    width = 512
    return pl.pallas_call(
        middle_backward_kernel,
        grid=(units // width,),
        in_specs=[
            once(BLOCK, 2 * D),
            once(BLOCK, D),
            once(BLOCK, D),
            once(BLOCK, BLOCK),
            pl.BlockSpec(memory_space=pltpu.VMEM),
            pl.BlockSpec(memory_space=pltpu.VMEM),
            pl.BlockSpec((BLOCK, width), lambda p: (0, p)),
            pl.BlockSpec(memory_space=pltpu.VMEM),
            pl.BlockSpec(memory_space=pltpu.VMEM),
        ],
        out_specs=[
            once(BLOCK, D),
            once(BLOCK, D),
            once(BLOCK, D),
            once(8, D),
            pl.BlockSpec((BLOCK, width), lambda p: (0, p)),
        ],
        scratch_shapes=[pltpu.VMEM((BLOCK, D), F32)],
        out_shape=[
            jax.ShapeDtypeStruct((BLOCK, D), F32),
            jax.ShapeDtypeStruct((BLOCK, D), BF16),
            jax.ShapeDtypeStruct((BLOCK, D), BF16),
            jax.ShapeDtypeStruct((8, D), F32),
            jax.ShapeDtypeStruct((BLOCK, units), BF16),
        ],
        compiler_params=pltpu.CompilerParams(vmem_limit_bytes=20 * 2**20),
        name="middle_backward",
    )(
        feed, g_resid_two, normal, inverse, gain_one, w_out, slope,
        w_up, w_down,
    )


def row_of(ref, at=None, width=None):
    return (ref[...] if at is None else ref[pl.ds(at, width)]).reshape(1, -1)


def gelu_and_slope(x):
    below = 0.5 + 0.5 * lax.erf(x * math.sqrt(0.5))
    density = jnp.exp(-0.5 * x * x) * (1.0 / math.sqrt(2.0 * math.pi))
    return x * below, below + x * density


def feedforward_kernel(
    parts,
    order_ref,
    *refs,
):
    part_refs, refs = refs[:parts], refs[parts:]
    wup_ref, bup_ref, wdown_ref, down_own_ref, down_other_ref, up_own_ref, up_other_ref, *refs = refs
    hid_ref, gd_ref, hidt_ref, sums_ref = refs
    step = pl.program_id(0)
    shares = up_own_ref.shape[0]
    half = down_own_ref.shape[1]
    width = wup_ref.shape[1]

    @pl.when(step == 0)
    def _():
        for part in range(parts):
            rows = slice(part * BLOCK, (part + 1) * BLOCK)
            hid_ref[rows, :] = part_refs[part][:, :D]
            gd_ref[rows, :] = part_refs[part][:, D:]
        place_rows(order_ref, hidt_ref, hid_ref[...].T, 2, shares)

    lanes = pl.ds(pl.multiple_of(step * width, width), width)
    at = pl.multiple_of(order_ref[1] * sums_ref.shape[1] + step * width, width)
    act, slope = gelu_and_slope(product(hid_ref[...], wup_ref[...]) + row_of(bup_ref, at, width))
    g_up = (product_right(gd_ref[...], wdown_ref[...]) * slope).astype(BF16)
    act_turned = act.astype(BF16).T
    for core, ref in enumerate((down_own_ref, down_other_ref)):
        columns = pl.ds(pl.multiple_of((order_ref[0] ^ core) * half, BLOCK), half)
        ref[lanes, :] = product(act_turned, gd_ref[:, columns]).astype(BF16)
    store_pieces((up_own_ref, up_other_ref), 0, product(hidt_ref[...], g_up).astype(BF16), lanes)
    sums_ref[:, lanes] = product(jnp.ones((16, hid_ref.shape[0]), BF16), g_up)

    @pl.when(step == pl.num_programs(0) - 1)
    def _():
        for core, ref in enumerate((down_own_ref, down_other_ref)):
            columns = pl.ds(pl.multiple_of((order_ref[0] ^ core) * half, BLOCK), half)
            ref[pl.ds(sums_ref.shape[1], 16), :] = sums_ref[:, columns].astype(BF16)


def feedforward_gradients(order, row_parts, w_up, b_up, w_down):
    shares = len(row_parts)
    tokens = shares * BLOCK
    units = w_up.shape[1] // shares
    width = 256
    steps = units // width
    down = (units + 16, D // 2)
    up = (shares, D // shares // 2, units)
    return pl.pallas_call(
        functools.partial(feedforward_kernel, shares),
        grid_spec=pltpu.PrefetchScalarGridSpec(
            num_scalar_prefetch=1,
            grid=(steps,),
            in_specs=[once(BLOCK, 2 * D)] * shares
            + [
                pl.BlockSpec((D, width), lambda p, order: (0, order[1] * steps + p)),
                pl.BlockSpec(memory_space=pltpu.VMEM),
                pl.BlockSpec((width, D), lambda p, order: (order[1] * steps + p, 0)),
            ],
            out_specs=[pl.BlockSpec(memory_space=pltpu.VMEM)] * 4,
            scratch_shapes=[
                pltpu.VMEM((tokens, D), BF16),
                pltpu.VMEM((tokens, D), BF16),
                pltpu.VMEM((D, tokens), BF16),
                pltpu.VMEM((16, units), F32),
            ],
        ),
        out_shape=[pltpu.VMEM(shape, BF16) for shape in (down, down, up, up)],
        compiler_params=pltpu.CompilerParams(vmem_limit_bytes=16 * 2**20),
        name="feedforward_gradients",
    )(order, *row_parts, *streamed(w_up), b_up, *streamed(w_down))


def assemble_kernel(
    place_ref,
    one_ref,
    one_other_ref,
    two_ref,
    two_other_ref,
    down_ref,
    down_other_ref,
    up_ref,
    up_other_ref,
    *refs,
):
    outs, refs = refs[:8], refs[8:]
    held, sems = refs[:8], refs[8]
    query_ref, key_ref, value_ref, out_ref, wide_ref, narrow_ref, sums_ref, vec_ref = held
    piece = query_ref.shape[0] // 2
    half = one_ref.shape[1]
    units = up_ref.shape[2]
    copies = [pltpu.make_async_copy(held[at], outs[at], sems.at[at]) for at in range(8)]

    def write(cores):
        for core, (one, two, down, up) in enumerate(cores):
            rows = slice(core * piece, (core + 1) * piece)
            for bits in range(4):
                at = pl.multiple_of((place_ref[1] ^ bits) * units, units)
                wide_ref[rows, pl.ds(at, units)] = up[bits].astype(F32)
        copies[4].start()
        for core, (one, two, down, up) in enumerate(cores):
            columns = slice(core * half, (core + 1) * half)
            narrow_ref[:, columns] = down[:units, :].astype(F32)
            sums_ref[:, columns] = down[units:, :].astype(F32)
        copies[5].start()
        copies[6].start()
        for at, ref in enumerate((query_ref, key_ref, value_ref)):
            for core, (one, two, down, up) in enumerate(cores):
                rows = slice(core * piece, (core + 1) * piece)
                ref[rows, :half] = one[at * piece : (at + 1) * piece, :].astype(F32)
                ref[rows, half:] = two[at * piece : (at + 1) * piece, :].astype(F32)
            copies[at].start()
        base = 3 * piece
        vec_ref[:, :half] = one_ref[base : base + 16, :].astype(F32)
        vec_ref[:, half:] = two_ref[base : base + 16, :].astype(F32)
        copies[7].start()
        base += 16
        for core, (one, two, down, up) in enumerate(cores):
            rows = slice(core * piece, (core + 1) * piece)
            out_ref[rows, :half] = one[base : base + piece, :].astype(F32)
            out_ref[rows, half:] = one[base + piece : base + 2 * piece, :].astype(F32)
        copies[3].start()
        for copy in copies:
            copy.wait()

    own = (one_ref, two_ref, down_ref, up_ref)
    other = (one_other_ref, two_other_ref, down_other_ref, up_other_ref)

    @pl.when(place_ref[0] == 0)
    def _():
        write((own, other))

    @pl.when(place_ref[0] != 0)
    def _():
        write((other, own))


def assemble(order, one, two, down, up):
    share = D // up[0].shape[0]
    units = up[0].shape[2]
    shapes = [(share, D)] * 4 + [(share, units * up[0].shape[0]), (units, D), (16, D), (16, D)]
    whole = pl.BlockSpec(memory_space=pltpu.VMEM)
    return pl.pallas_call(
        assemble_kernel,
        grid_spec=pltpu.PrefetchScalarGridSpec(
            num_scalar_prefetch=1,
            grid=(1,),
            in_specs=[whole] * 8,
            out_specs=[pl.BlockSpec(memory_space=pl.ANY)] * 8,
            scratch_shapes=[pltpu.VMEM(shape, F32) for shape in shapes]
            + [pltpu.SemaphoreType.DMA((8,))],
        ),
        out_shape=[pltpu.HBM(shape, F32) for shape in shapes],
        compiler_params=pltpu.CompilerParams(vmem_limit_bytes=16 * 2**20),
        cost_estimate=pl.CostEstimate(flops=0, bytes_accessed=24 * 2**20, transcendentals=0),
        name="assemble",
    )(order, *one, *two, *down, *up)


def swapped(array, axis, bits):
    return lax.ppermute(array, axis, [(i, i ^ bits) for i in range(lax.axis_size(axis))])


def from_peers(arrays):
    return [swapped(array, "seq", bits) for bits, array in enumerate(arrays, 1)]


def picked(array, index, axis):
    return lax.dynamic_index_in_dim(array, index, axis, keepdims=False)


def together(*arrays):
    return lax.optimization_barrier(arrays)


def added(*arrays):
    return functools.reduce(jnp.add, [array.astype(F32) for array in arrays]).astype(BF16)


def halves(pack):
    middle = pack.shape[1] // 32 * 16
    return pack[:, :middle], pack[:, middle:]


def in_row_order(pack, mine):
    return jnp.stack([picked(pack, mine ^ at, 0) for at in range(4)], axis=0)


def square_mesh():
    return lax.axis_size("seq") == 4 and lax.axis_size("z") == 4


def scatter(pack):
    return from_peers([pack[1], pack[2], pack[3]])


NEXT = [(0, 1), (1, 0), (2, 3), (3, 2)]
ACROSS = [(0, 3), (1, 2), (2, 1), (3, 0)]


def half_of(share, second):
    half = share.shape[0] // 2
    return jnp.where(second, share[half:], share[:half])


def core_index():
    return lax.axis_index("core")


def both_cores(share, axis):
    other = swapped(share, "core", 1)
    first = core_index() == 0
    return jnp.concatenate(
        [jnp.where(first, share, other), jnp.where(first, other, share)], axis=axis
    )


def reduce_plain(partial):
    share = lax.psum_scatter(partial.astype(BF16), "seq", scatter_dimension=0, tiled=True)
    return lax.psum(share, ("z", "core")).astype(F32)


def local(
    tokens,
    cotangent,
    lengths,
    w_query,
    b_query,
    w_key,
    b_key,
    w_value,
    b_value,
    w_out,
    b_out,
    gain_one,
    shift_one,
    w_up,
    b_up,
    w_down,
    b_down,
    gain_two,
    shift_two,
    rel_table,
):
    rows = tokens.shape[0]
    cycle = lax.axis_size("seq")
    mine = lax.axis_index("seq")
    core = core_index()
    square = square_mesh()
    hidden_units = w_up.shape[1]
    share = D // cycle
    if square:
        token_parts = [tokens] + from_peers([tokens] * 3)
        ids = mine ^ jnp.arange(cycle, dtype=jnp.int32)
        order = jnp.stack([core, mine]).astype(jnp.int32)
        cores = 2
    else:
        token_parts = [tokens, lax.all_gather(tokens, "seq", axis=0, tiled=True)]
        ids = jnp.concatenate([mine[None], jnp.arange(cycle, dtype=jnp.int32)])
        order = jnp.zeros((2,), jnp.int32)
        cores = 1
    dist = jnp.concatenate([mine - ids, ids, lengths[0]]).astype(jnp.int32)

    at_z = lax.axis_index("z")
    end = (at_z == 0) | (at_z == 3)
    between = jnp.logical_not(end)
    low = core == 0
    odd_x, odd_y = (mine & 1) == 1, (mine & 2) == 2
    place_of = (dist, order, end, between, low, odd_x, odd_y)
    dist, order, end, between, low, odd_x, odd_y = lax.optimization_barrier(place_of)

    def in_order(pieces):
        first, second, third, fourth = pieces
        pairs = [
            (jnp.where(odd_x, b, a), jnp.where(odd_x, a, b))
            for a, b in ((first, second), (third, fourth))
        ]
        return [jnp.where(odd_y, b, a) for a, b in zip(*pairs)] + [
            jnp.where(odd_y, a, b) for a, b in zip(*pairs)
        ]

    def own_quarter(array):
        half = array.shape[1] // 2
        array = jnp.where(odd_y, array[:, half:], array[:, :half])
        return jnp.where(odd_x, array[:, half // 2 :], array[:, : half // 2])

    places = jnp.arange(RELROWS, dtype=jnp.int32)
    turn = (places[:, None] + places[None, :] == RELROWS - 1).astype(BF16)
    stay = (places[:, None] == places[None, :]).astype(BF16)
    rel_both = product(jnp.concatenate([turn, stay], axis=0), rel_table).astype(BF16)
    pos_key_back = (product(rel_both[:RELROWS], w_key) + b_key).astype(BF16)
    pos_query = (product(rel_both, w_query) + b_query).astype(BF16)
    pos_key_back, (dist, order, end, between, low, odd_x, odd_y) = together(
        pos_key_back, (dist, order, end, between, low, odd_x, odd_y)
    )
    context, prob, query, key, value, tokens_row, *held = attention_forward(
        dist,
        token_parts,
        [w_query, w_key, w_value],
        [b_query, b_key, b_value],
        pos_key_back,
        pos_query,
        [w_up, w_down, w_out],
    )
    held_up, held_down, held_out = held

    output, feed, normal_one, inverse_one, g_resid_two, slope, sums_two = middle_forward(
        dist, context, tokens, cotangent, held_out, b_out, gain_one, shift_one, b_down, gain_two,
        shift_two, held_up, b_up, held_down,
    )
    if square:
        row_parts = [feed] + from_peers([feed] * 3)
    g_resid_one, g_attn, g_context, sums_one, g_up = middle_backward(
        feed, g_resid_two, normal_one, inverse_one, gain_one, held_out, slope, held_up, held_down
    )
    vectors = [sums_one, sums_two]

    def backward(start, pairs, g_context, extra_one, extra_two):
        outs = attention_backward(
            start, pairs, cores, cycle, dist, order, query, key, value, pos_key_back, pos_query, prob,
            g_context, tokens_row, rel_table, w_query, w_key, w_value, extra_one, extra_two, vectors,
        )
        return outs[:cores], outs[cores:]

    piece = share // cores
    whole_rows = lambda v, at, each: v[:, at : at + each].reshape(cores * each, -1)

    def unpacked(v, each):
        base = 3 * piece + 16
        parts = D // v.shape[2]
        return jnp.concatenate(
            [whole_rows(v, base + part * each, each) for part in range(parts)], axis=1
        )

    def rel_own(pack):
        return unpacked(pack, RELROWS // cycle // cores)

    def results(grads, grad_w_out, vectors, grad_rel, grad_tokens, grad_w_up, grad_w_down, grad_b_up):
        return (
            output,
            grad_tokens,
            grads[0],
            vectors[0],
            grads[1],
            vectors[1],
            grads[2],
            vectors[2],
            grad_w_out,
            vectors[3],
            vectors[4],
            vectors[5],
            grad_w_up,
            grad_b_up,
            grad_w_down,
            vectors[6],
            vectors[7],
            vectors[8],
            grad_rel,
        )

    if not square:
        act = gelu_and_slope(product(feed[:, :D], w_up) + b_up)[0].astype(BF16)
        (one,), carried = backward(0, 3, g_context, context, g_attn)
        (two,), (home, away) = backward(3, 3, g_context, *carried)
        packs = [
            lax.psum(lax.psum_scatter(v, "seq", scatter_dimension=0, tiled=True), ("z", "core"))
            for v in (one, two)
        ]
        got = lax.psum_scatter(away, "seq", scatter_dimension=0, tiled=False)
        grads = [
            jnp.concatenate([whole_rows(v, at * piece, piece) for v in packs], axis=1).astype(F32)
            for at in range(3)
        ]
        base = 3 * piece
        sums = jnp.concatenate([v[0, base : base + 16] for v in packs], axis=1).astype(F32)
        return results(
            grads,
            unpacked(packs[0], piece).astype(F32),
            lax.dynamic_slice_in_dim(sums, mine * share, share, 1),
            lax.all_gather(rel_own(packs[-1]), "seq", axis=0, tiled=True).astype(F32),
            g_resid_one + home + got.astype(F32),
            reduce_plain(product_left(feed[:, :D], g_up)),
            reduce_plain(product_left(act, feed[:, D:])),
            reduce_plain(jnp.sum(g_up.astype(F32), axis=0)),
        )

    one, carried = backward(0, 3, g_context, context, g_attn)

    row_parts, one, carried = together(row_parts, one, carried)
    one_got = swapped(one[1], "core", 1)
    down_own, down_other, up_own, up_other = feedforward_gradients(
        order, row_parts, w_up, b_up, w_down
    )

    one_got, down_own, down_other, up_own, up_other = together(
        one_got, down_own, down_other, up_own, up_other
    )
    down_got = swapped(down_other, "core", 1)
    up_got = swapped(up_other, "core", 1)
    one_share = added(one[0], one_got)
    down_share = added(down_own, down_got)
    up_share = added(up_own, up_got)

    units = hidden_units // 4

    def first_start(v):
        first, second = halves(v)
        return swapped(first[1::2], "seq", 1), swapped(second[2:], "seq", 2)

    def first_end(v, got):
        first, second = halves(v)
        return added(first[0::2], got[0]), added(second[:2], got[1])

    def second_start(v):
        return swapped(v[0][1], "seq", 2), swapped(v[1][1], "seq", 1)

    def second_end(v, got):
        return jnp.concatenate([added(v[0][0], got[0]), added(v[1][0], got[1])], axis=0)

    def core_start(v):
        return swapped(v, "core", 1)

    def rel_rows(pair):
        base, each = 3 * share // 2 + 16, RELROWS // 8
        own, other = [
            jnp.concatenate([v[base : base + each], v[base + each : base + 2 * each]], axis=1)
            for v in pair
        ]
        return jnp.concatenate(
            [jnp.where(low, own, other), jnp.where(low, other, own)], axis=0
        )

    moves = {
        "first": (first_start, first_end),
        "second": (second_start, second_end),
        "in": (
            lambda v: lax.ppermute(half_of(v, end), "z", NEXT),
            lambda v, got: added(half_of(v, between), got),
        ),
        "mid": (lambda v: lax.ppermute(v, "z", ACROSS), added),
        "out": (
            lambda v: lax.ppermute(v, "z", NEXT),
            lambda v, got: jnp.concatenate(
                [jnp.where(end, v, got), jnp.where(end, got, v)], axis=0
            ),
        ),
        "pair": (lambda v: swapped(v[1], "core", 1), lambda v, got: added(v[0], got)),
        "rows": (core_start, lambda v, got: (v, got)),
        "columns": (core_start, lambda v, got: (v, got)),
        "give": (scatter, lambda v, got: jnp.stack([v[0]] + got, axis=0)),
        "home": (
            lambda v: from_peers([v[0], v[1], v[2]]),
            lambda v, got: functools.reduce(jnp.add, [part.astype(F32) for part in got]),
        ),
        "spread": (scatter, lambda v, got: added(v[0], *got)),
        "x": (lambda v: swapped(v[1], "seq", 1), lambda v, got: [v[0], got, v[2], v[3]]),
        "y": (lambda v: swapped(v[2], "seq", 2), lambda v, got: [v[0], v[1], got, v[3]]),
        "d": (
            lambda v: swapped(v[3], "seq", 3),
            lambda v, got: jnp.stack([v[0], v[1], v[2], got], axis=0),
        ),
        "dd": (
            lambda v: swapped(v[3], "seq", 3),
            lambda v, got: jnp.stack([v[0], v[1], v[2], got], axis=0),
        ),
        "hx": (lambda v: swapped(v[0], "seq", 1), lambda v, got: [got, v[1], v[2]]),
        "hy": (lambda v: swapped(v[1], "seq", 2), lambda v, got: [v[0], got, v[2]]),
        "hd": (
            lambda v: swapped(v[2], "seq", 3),
            lambda v, got: functools.reduce(
                jnp.add, [part.astype(F32) for part in (v[0], v[1], got)]
            ),
        ),
        "rel": (
            lambda v: from_peers([rel_rows(v)] * 3),
            lambda v, got: (v, [rel_rows(v)] + got),
        ),
    }
    held_sums = {"down": down_share, "up": up_share, "one": one_share}
    flying = {}

    def begin(*steps):
        for step in steps:
            name, move = step.split(".")
            if move == "share":
                both = zip(held_sums["up"][1:], held_sums["away"])
                flying[step] = from_peers([jnp.concatenate(parts, axis=0) for parts in both])
            else:
                flying[step] = moves[move][0](held_sums[name])

    def meet(done, then):
        names = [step.split(".")[0] for step in then] + [step.split(".")[0] for step in done]
        names += ["away"] if "up.share" in done or "up.share" in then else []
        names = [name for at, name in enumerate(names) if name not in names[:at]]
        gots = {step: flying.pop(step) for step in done}
        kept, gots = together({name: held_sums[name] for name in names}, gots)
        held_sums.update(kept)
        for step in done:
            name, move = step.split(".")
            if move == "share":
                each = held_sums["up"].shape[1]
                parts = [held_sums["up"][0]] + [got[:each] for got in gots[step]]
                held_sums["up"] = jnp.stack(parts, axis=0)
                homes = [got[each:].astype(F32) for got in gots[step]]
                held_sums["away"] = functools.reduce(jnp.add, homes)
            else:
                held_sums[name] = moves[move][1](held_sums[name], gots[step])
        begin(*then)

    stages = (
        ([], ["up.in", "one.first"]),
        (["up.in", "one.first"], ["two.pair", "up.mid", "one.second"]),
        (["two.pair"], ["two.first"]),
        (["one.second"], ["one.in", "down.in"]),
        (["two.first", "up.mid"], ["two.second", "up.out"]),
        (["one.in"], ["one.mid"]),
        (["two.second", "down.in", "one.mid"], ["two.in", "down.mid", "one.out"]),
        (["two.in", "up.out"], ["two.mid"]),
        (["one.out"], ["up.share"]),
        (["down.mid"], ["down.out"]),
        (["two.mid"], ["two.out"]),
        (["two.out", "down.out", "up.share"], ["two.rows", "one.rows", "up.columns", "down.columns"]),
        (["two.rows", "one.rows", "up.columns", "down.columns"], []),
    )
    begin(*stages[0][1])
    g_context, held_sums = together(g_context, held_sums)
    two, (home, away) = backward(3, 3, g_context, *carried)
    home, held_sums, flying_now = together(
        home, dict(held_sums, two=two, away=away), {step: flying[step] for step in stages[1][0]}
    )
    flying.update(flying_now)
    for done, then in stages[1:]:
        meet(done, then)

    grad_tokens = g_resid_one + home + held_sums["away"]
    rel = rel_rows(held_sums["two"])
    from_y, from_both = swapped(rel, "seq", 2), swapped(rel, "seq", 3)
    *grads, grad_w_up, grad_w_down, sums_up, sums = assemble(
        order, held_sums["one"], held_sums["two"], held_sums["down"], held_sums["up"]
    )
    rel, grads[3] = together(rel, grads[3])
    from_y, sums, sums_up = together(from_y, sums, sums_up)
    rel_parts = [rel, swapped(rel, "seq", 1), from_y, from_both]
    return results(
        grads[:3],
        grads[3],
        own_quarter(sums),
        jnp.concatenate(in_order(rel_parts), axis=0).astype(F32),
        grad_tokens,
        grad_w_up,
        grad_w_down,
        sums_up[0],
    )


def solution(mesh):
    lines, cycle = mesh.devices.shape
    chips = Mesh(mesh.devices.reshape(lines // 2, 2, cycle), ("z", "core", "seq"))
    return jax.shard_map(
        local,
        mesh=chips,
        in_specs=(
            P(("z", "core", "seq"), None),
            P(("z", "core", "seq"), None),
            P(("z", "core"), None),
        )
        + (P(),) * 17,
        out_specs=(
            P(("z", "core", "seq"), None),
            P(("z", "core", "seq"), None),
            P("seq", None),
            P("seq"),
            P("seq", None),
            P("seq"),
            P("seq", None),
            P("seq"),
            P("seq", None),
            P("seq"),
            P("seq"),
            P("seq"),
            P("seq", None),
            P("seq"),
            P("seq", None),
            P("seq"),
            P("seq"),
            P("seq"),
            P(),
        ),
        check_vma=False,
    )
```
